32 devices in a mesh: beam: 8 (over z, y), slab: 4 (over x, core).
Axes of the slice: x: 2, y: 2, z: 4, core: 2. Of those that a mesh axis runs over, the one named last changes fastest.
Arguments:
- pot_first: bfloat16 [4096, 4096], P('beam'), may hold values from -3.140625 to 3.140625
- pot_second: bfloat16 [4096, 4096], P('beam'), may hold values from -3.140625 to 3.140625
- beam_index: int32 [4, 2], replicated, may hold values from -3 to 3
- aberration: float32 [4], replicated, may hold values from -3.140625 to 3.140625
- tile_table: int32 [32, 4], replicated, may hold values from 0 to 4095, as said below
- tile_count: int32 [32], replicated, may hold values from 1 to 4, as said below
Outputs:
- detector_sums: float32 [32, 4, 3, 16], P(('beam', 'slab'))
The draws below stay inside these ranges and needn't reach their ends.
Inputs may be any that keep to these rules, and one draw needn't show every extreme that they name: `tile_table`: group the blocks by the beam index of their device, block // 4; among the 16 slots of one group, active or not, exactly 2 name a tile of row band b, for every band b = ty // 8. The first tile_count[block] slots of a block are active; some block has all 4 active.
All inputs are finite; a program needn't handle non-finite values.
Results may differ from the reference program's by a relative error of at most 0.012.
The reference program's roundings to bfloat16 on the way count: a program that leaves them out, or rounds other values in their place, can miss the bound.
Values may be sent and summed in bfloat16 or wider, within the bound.
No kernel may reach another device: no remote copies, remote signals or barrier semaphores. Data moves between devices by JAX's collectives and lax.ppermute only.
A program may use at most 192 MiB of HBM per device.

```python
import math
import jax
import jax.numpy as jnp
from jax import lax

A = 64
N = 4096
F = 64
QMAX = 3
G = 3
NDET = 16
TMAX = 4
BLK_DEV = 1
BEAMS = 4
BLOCKS = 32
N_BEAM = 8
N_SLAB = 4


def draw_tile_table(key, part):
    key = jax.random.fold_in(key, 11)
    across = N // A
    band_tiles = N // N_BEAM // A
    length = N_SLAB * BLK_DEV * TMAX
    capacity = length // N_BEAM
    key_list = jax.random.split(key, 3)
    orders = jax.vmap(lambda subkey: jax.random.permutation(subkey, length))(jax.random.split(key_list[0], N_BEAM))
    band_ids = orders // capacity
    row_in = jax.random.randint(key_list[1], (N_BEAM, length), 0, band_tiles)
    col_ids = jax.random.randint(key_list[2], (N_BEAM, length), 0, across)
    tile_ids = (band_ids * band_tiles + row_in) * across + col_ids
    return tile_ids.reshape(N_BEAM * N_SLAB * BLK_DEV, TMAX).astype(jnp.int32)


def draw_tile_count(key, part):
    key = jax.random.fold_in(key, 23)
    first_key, second_key = jax.random.split(key)
    counts = jax.random.randint(first_key, (BLOCKS,), 1, TMAX + 1)
    full_block = jax.random.randint(second_key, (), 0, BLOCKS)
    return counts.at[full_block].set(TMAX).astype(jnp.int32)


def touch_ends(drawn, key, least, top_value):
    spot = [jax.random.randint(jax.random.fold_in(key, axis), (), 0, length) for axis, length in enumerate(drawn.shape)]
    main_axis = drawn.shape.index(max(drawn.shape))
    next_to = spot[:main_axis] + [(spot[main_axis] + 1) % drawn.shape[main_axis]] + spot[main_axis + 1:]
    return drawn.at[tuple(spot)].set(least).at[tuple(next_to)].set(top_value)


def setup_inputs(seed: int = 0) -> dict:
    seeds = jax.random.split(jax.random.key(seed), 7)
    return {
        "pot_first": jnp.clip(jax.random.uniform(seeds[0], (N, N), jnp.float32, -3.140625, 3.140625), -3.140625, 3.140625).astype(jnp.bfloat16),
        "pot_second": jnp.clip(jax.random.uniform(seeds[1], (N, N), jnp.float32, -3.140625, 3.140625), -3.140625, 3.140625).astype(jnp.bfloat16),
        "beam_index": touch_ends(jax.random.randint(seeds[2], (BEAMS, 2), -QMAX, QMAX + 1), jax.random.fold_in(seeds[2], 1), -QMAX, QMAX).astype(jnp.int32),
        "aberration": jnp.clip(jax.random.uniform(seeds[3], (BEAMS,), jnp.float32, -3.140625, 3.140625), -3.140625, 3.140625),
        "tile_table": draw_tile_table(jax.random.fold_in(seeds[6], 71), 0),
        "tile_count": draw_tile_count(jax.random.fold_in(seeds[6], 71), 0),
    }


def rounded(values):
    return lax.optimization_barrier(values.astype(jnp.bfloat16)).astype(jnp.float32)


def radix_pair(factor):
    digits = jnp.arange(A, dtype=jnp.int32)
    product = (digits[:, None] * digits[None, :]) % A
    angles = (2.0 * math.pi / A) * product.astype(jnp.float32)
    cosine = rounded(jnp.cos(angles)) * factor
    sine_tab = rounded(jnp.sin(angles)) * factor
    return cosine, sine_tab


def mix_lines(real_part, imag_part, cosine, sine_tab, orient, pattern):
    highest = lax.Precision.HIGHEST
    out_real = jnp.einsum(pattern, real_part, cosine, precision=highest) + orient * jnp.einsum(pattern, imag_part, sine_tab, precision=highest)
    out_imag = jnp.einsum(pattern, imag_part, cosine, precision=highest) - orient * jnp.einsum(pattern, real_part, sine_tab, precision=highest)
    return out_real, out_imag


def twist_lines(real_part, imag_part, orient):
    digits = jnp.arange(A, dtype=jnp.int32)
    product = (digits[:, None] * digits[None, :]) % N
    angles = (2.0 * math.pi / N) * product.astype(jnp.float32)
    cosine = jnp.cos(angles)
    turned = orient * jnp.sin(angles)
    return real_part * cosine + imag_part * turned, imag_part * cosine - real_part * turned


def forward_line(real_part, imag_part):
    full_shape = real_part.shape
    leading = full_shape[:-1]
    cosine, sine_tab = radix_pair(1.0 / A)
    real_part = rounded(real_part).reshape(leading + (A, A))
    imag_part = rounded(imag_part).reshape(leading + (A, A))
    real_part, imag_part = mix_lines(real_part, imag_part, cosine, sine_tab, 1.0, "...nm,nk->...km")
    real_part, imag_part = twist_lines(real_part, imag_part, 1.0)
    real_part, imag_part = rounded(real_part), rounded(imag_part)
    real_part, imag_part = mix_lines(real_part, imag_part, cosine, sine_tab, 1.0, "...km,mj->...kj")
    return jnp.swapaxes(real_part, -1, -2).reshape(full_shape), jnp.swapaxes(imag_part, -1, -2).reshape(full_shape)


def inverse_line(real_part, imag_part):
    full_shape = real_part.shape
    leading = full_shape[:-1]
    cosine, sine_tab = radix_pair(1.0)
    real_part = rounded(real_part).reshape(leading + (A, A))
    imag_part = rounded(imag_part).reshape(leading + (A, A))
    real_part, imag_part = mix_lines(real_part, imag_part, cosine, sine_tab, -1.0, "...jk,jb->...kb")
    real_part, imag_part = twist_lines(real_part, imag_part, -1.0)
    real_part, imag_part = rounded(real_part), rounded(imag_part)
    real_part, imag_part = mix_lines(real_part, imag_part, cosine, sine_tab, -1.0, "...kb,ka->...ab")
    return real_part.reshape(full_shape), imag_part.reshape(full_shape)


def exit_wave(pot_first, pot_second, beam_row):
    places = jnp.arange(N, dtype=jnp.int32)
    wave_y = jnp.remainder(F * beam_row[0], N)
    wave_x = jnp.remainder(F * beam_row[1], N)
    windings = (wave_y * places[:, None] + wave_x * places[None, :]) % N
    angles = (2.0 * math.pi / N) * windings.astype(jnp.float32)
    plane_cos, plane_sin = jnp.cos(angles), jnp.sin(angles)
    potential = pot_first.astype(jnp.float32)
    trans_cos, trans_sin = jnp.cos(potential), jnp.sin(potential)
    real_part = plane_cos * trans_cos - plane_sin * trans_sin
    imag_part = plane_cos * trans_sin + plane_sin * trans_cos
    real_part, imag_part = forward_line(real_part, imag_part)
    real_part, imag_part = forward_line(real_part.T, imag_part.T)
    signed = jnp.where(places < N // 2, places, places - N)
    radius = signed[:, None] ** 2 + signed[None, :] ** 2
    phases = (-math.pi / N) * (radius % (2 * N)).astype(jnp.float32)
    inside = radius <= (N // 3) ** 2
    prop_cos = jnp.where(inside, jnp.cos(phases), 0.0)
    prop_sin = jnp.where(inside, jnp.sin(phases), 0.0)
    real_part, imag_part = real_part * prop_cos - imag_part * prop_sin, real_part * prop_sin + imag_part * prop_cos
    real_part, imag_part = inverse_line(real_part, imag_part)
    real_part, imag_part = inverse_line(real_part.T, imag_part.T)
    potential = pot_second.astype(jnp.float32)
    trans_cos, trans_sin = jnp.cos(potential), jnp.sin(potential)
    return real_part * trans_cos - imag_part * trans_sin, real_part * trans_sin + imag_part * trans_cos


def coefficients(tile_ids, beam_rows, shifts):
    across = N // A
    offsets = jnp.arange(G, dtype=jnp.int32)
    spot_y = (tile_ids // across)[:, None] * A + A // 2 + offsets[None, :]
    spot_x = (tile_ids % across)[:, None] * A + A // 2 + 2 * offsets[None, :]
    wave_y = jnp.remainder(F * beam_rows[:, 0], N)[:, None, None]
    wave_x = jnp.remainder(F * beam_rows[:, 1], N)[:, None, None]
    windings = (wave_y * spot_y[None] % N + wave_x * spot_x[None] % N) % N
    phases = shifts[:, None, None] + (2.0 * math.pi / N) * windings.astype(jnp.float32)
    return jnp.cos(phases), -jnp.sin(phases)


def detector_weights(beam_total):
    digits = jnp.arange(A, dtype=jnp.int32)
    signed = jnp.where(digits < A // 2, digits, digits - A)
    radius = (signed[:, None] ** 2 + signed[None, :] ** 2).reshape(A * A)
    step_width = A // (2 * NDET)
    bin_index = jnp.arange(NDET, dtype=jnp.int32)
    member = (radius[:, None] >= (step_width * bin_index[None, :]) ** 2) & (radius[:, None] < (step_width * (bin_index[None, :] + 1)) ** 2)
    counts = jnp.sum(member.astype(jnp.float32), axis=0)
    return jnp.where(member, (A * A) / (beam_total * counts), 0.0)


def reference(pot_first, pot_second, beam_index, aberration, tile_table, tile_count):
    across = N // A
    tile_ids = tile_table.reshape(-1)
    tile_rows = tile_ids // across
    tile_cols = tile_ids % across
    slot_total = tile_ids.shape[0]

    def beam_step(running, inputs):
        beam_row, shift = inputs
        exit_real, exit_imag = exit_wave(pot_first, pot_second, beam_row)
        crop_real = exit_real.reshape(across, A, across, A)[tile_rows, :, tile_cols, :]
        crop_imag = exit_imag.reshape(across, A, across, A)[tile_rows, :, tile_cols, :]
        coef_cos, coef_sin = coefficients(tile_ids, beam_row[None, :], shift[None])
        coef_cos = coef_cos[0][:, :, None, None]
        coef_sin = coef_sin[0][:, :, None, None]
        probe_real = running[0] + (coef_cos * crop_real[:, None] - coef_sin * crop_imag[:, None])
        probe_imag = running[1] + (coef_cos * crop_imag[:, None] + coef_sin * crop_real[:, None])
        return (probe_real, probe_imag), None

    zeros = jnp.zeros((slot_total, G, A, A), jnp.float32)
    (probe_real, probe_imag), _ = lax.scan(beam_step, (zeros, zeros), (beam_index, aberration))
    cosine, sine_tab = radix_pair(1.0 / A)
    real_part, imag_part = mix_lines(rounded(probe_real), rounded(probe_imag), cosine, sine_tab, 1.0, "...yx,xk->...yk")
    real_part, imag_part = mix_lines(rounded(real_part), rounded(imag_part), cosine, sine_tab, 1.0, "...yk,yj->...jk")
    intensity = (real_part ** 2 + imag_part ** 2).reshape(slot_total * G, A * A)
    weights = detector_weights(BEAMS)
    binned = jnp.dot(intensity, weights, precision=lax.Precision.HIGHEST).reshape(tile_table.shape[0], TMAX, G, NDET)
    active = jnp.arange(TMAX, dtype=jnp.int32)[None, :] < tile_count[:, None]
    return jnp.where(active[:, :, None, None], binned, 0.0)
```

```python
import functools
import math

import jax
import jax.numpy as jnp
import ml_dtypes
import numpy as np
from jax import lax
from jax.experimental import pallas as pl
from jax.experimental.pallas import tpu as pltpu
from jax.sharding import PartitionSpec as P

A = 64
N = 4096
F = 64
G = 3
NDET = 16
QMAX = 3
LIMIT = N // 3
K2_LOW = -(LIMIT // A + 1 + QMAX)
K2_COUNT = 2 * (LIMIT // A + 1 + QMAX)
PART = 104
ROWS = 2 * PART
LANES = 128
SUB = 16
HIGH = A // SUB
HALF = A // 2
PAIRS = A // 2
PARTS = 2
VMEM = 60 * 1024 * 1024
PITCH = A + 1
BF = jnp.bfloat16
F32 = jnp.float32


def low(values):
    return np.asarray(values, dtype=np.float32).astype(ml_dtypes.bfloat16)


def turn(numerator, period):
    return np.exp(2j * np.pi * (numerator % period) / period)


def digits_k2():
    return K2_LOW + np.arange(K2_COUNT)


def spread(table):
    both = np.stack([table.real, table.imag])
    eye = np.eye(SUB)
    out = both[:, :, None, :, None] * eye[None, None, :, None, :]
    return low(out.reshape(2 * table.shape[0] * SUB, table.shape[1] * SUB))


def real_rows(table):
    return np.block([[table.real, -table.imag], [table.imag, table.real]])


def section_forward(k1):
    n1 = np.arange(A)
    return spread(np.conj(turn(k1[:, None] * n1[None, :], A)) / A)


def last_forward_x(k1_pair):
    n2 = np.arange(A)
    out = np.zeros((2, PART, 2, 2, A))
    for ks, k1 in enumerate(k1_pair):
        freq = k1 + A * digits_k2()
        table = np.conj(turn(freq[:, None] * n2[None, :], N)) / A
        block = real_rows(table).reshape(2, K2_COUNT, 2, A)
        out[:, ks * K2_COUNT : (ks + 1) * K2_COUNT, ks] = block
    return low(out.reshape(ROWS, 4 * A))


def last_forward_y(k1_pair):
    n2 = np.arange(A)
    out = np.zeros((ROWS, 2, 2 * A))
    for e, k1 in enumerate(k1_pair):
        freq = k1 + A * digits_k2()
        table = np.conj(turn(freq[:, None] * n2[None, :], N)) / A
        out[e * 2 * K2_COUNT : (e + 1) * 2 * K2_COUNT, e] = real_rows(table)
    return low(out.reshape(ROWS, 4 * A))


def first_inverse(k1):
    n2 = np.arange(A)
    freq = k1 + A * digits_k2()
    return turn(n2[:, None] * freq[None, :], N) * np.conj(turn(freq * freq, 2 * N))[None, :]


def first_inverse_y(k1_pair):
    out = np.zeros((2, 2 * A, ROWS))
    for e, k1 in enumerate(k1_pair):
        out[e, :, e * 2 * K2_COUNT : (e + 1) * 2 * K2_COUNT] = real_rows(first_inverse(k1))
    return low(out.reshape(4 * A, ROWS))


def first_inverse_x(k1_pair):
    out = np.zeros((LANES, 2, 2, A))
    for ks, k1 in enumerate(k1_pair):
        table = first_inverse(k1).T
        out[ks * K2_COUNT : (ks + 1) * K2_COUNT, 0, ks] = table.real
        out[ks * K2_COUNT : (ks + 1) * K2_COUNT, 1, ks] = table.imag
    return low(out.reshape(LANES, 4 * A))


def sine_cosine(x):
    u = x * x
    s = F32(SIN_FIT[-1])
    for c in SIN_FIT[-2::-1]:
        s = s * u + F32(c)
    q = F32(COS_FIT[-1])
    for c in COS_FIT[-2::-1]:
        q = q * u + F32(c)
    return s * x, q


def fit(function, degree):
    top = 3.1421**2
    nodes = 0.5 * top * (1 - np.cos(np.pi * (np.arange(64) + 0.5) / 64))
    cheb = np.polynomial.chebyshev.Chebyshev.fit(
        nodes, function(np.sqrt(nodes)), degree, domain=[0, top]
    )
    return [float(c) for c in cheb.convert(kind=np.polynomial.Polynomial).coef]


SIN_FIT = fit(lambda x: np.sinc(x / np.pi), 5)
COS_FIT = fit(np.cos, 5)


def dot(a, b):
    return jnp.dot(a, b, preferred_element_type=F32)


def cost(micros):
    return pl.CostEstimate(flops=int(micros * 1.1e9), bytes_accessed=0, transcendentals=0)


def forward_x_kernel(sel, pot, section, last, *rest):
    *outs, cos_ref, sin_ref, twisted = rest
    fields = len(outs)
    lanes = cos_ref.shape[2]
    half = section.shape[1] // 2

    def chunk(t, carry):
        block = pot[:, 0, :, pl.ds(pl.multiple_of(t * LANES, LANES), LANES)]
        values = block.reshape(lanes, LANES).astype(F32).T
        sine, cosine = sine_cosine(values)
        cos_ref[pl.ds(2 * t, 2)] = cosine.astype(BF).reshape(2, A, lanes)
        sin_ref[pl.ds(2 * t, 2)] = sine.astype(BF).reshape(2, A, lanes)
        return carry

    lax.fori_loop(0, N // LANES, chunk, 0, unroll=4)
    table = section[0]
    for m in range(HIGH):
        span = slice(m * SUB, (m + 1) * SUB)
        part_cos = cos_ref[:, span, :].reshape(A * SUB, lanes)
        part_sin = sin_ref[:, span, :].reshape(A * SUB, lanes)
        if lanes % LANES == 0:
            both = dot(table, jnp.concatenate([part_cos, part_sin], axis=1))
            of_cos, of_sin = both[:, :lanes], both[:, lanes:]
        else:
            of_cos, of_sin = dot(table, part_cos), dot(table, part_sin)
        real = of_cos[:half] - of_sin[half:]
        imag = of_cos[half:] + of_sin[:half]
        twisted[:, m * SUB : (m + 1) * SUB, :] = real.astype(BF).reshape(2 * fields, SUB, lanes)
        twisted[:, A + m * SUB : A + (m + 1) * SUB, :] = imag.astype(BF).reshape(
            2 * fields, SUB, lanes
        )
    for o in range(fields):
        d = sel[1] ^ o
        lines = twisted[pl.ds(2 * d, 2)].reshape(4 * A, lanes)
        outs[o][0] = dot(last[0, d], lines).astype(BF)


def forward_x(sel, pot, section, last, fields, part):
    groups = pot.shape[0] // A
    lanes = groups * SUB
    steps = HIGH // PARTS
    return pl.pallas_call(
        forward_x_kernel,
        grid_spec=pltpu.PrefetchScalarGridSpec(
            num_scalar_prefetch=1,
            grid=(steps,),
            in_specs=[
                pl.BlockSpec((groups, 1, SUB, N), lambda i, s: (0, part * steps + i, 0, 0)),
                pl.BlockSpec((1,) + section.shape[1:], lambda i, s: (s[0], 0, 0)),
                pl.BlockSpec((1,) + last.shape[1:], lambda i, s: (s[0], 0, 0, 0)),
            ],
            out_specs=[pl.BlockSpec((1, ROWS, lanes), lambda i, s: (i, 0, 0))] * fields,
            scratch_shapes=[
                pltpu.VMEM((A, A, lanes), BF),
                pltpu.VMEM((A, A, lanes), BF),
                pltpu.VMEM((2 * fields, 2 * A, lanes), BF),
            ],
        ),
        out_shape=[jax.ShapeDtypeStruct((steps, ROWS, lanes), BF)] * fields,
        compiler_params=pltpu.CompilerParams(vmem_limit_bytes=VMEM),
        cost_estimate=cost(9),
        name="forward_x",
    )(sel, pot.reshape(groups, HIGH, SUB, N), section, last)


def section_step(sel, groups, section, gathered, twisted, start):
    chunk_rows = 16 * SUB
    for g, group in enumerate(groups):
        block = group[0].astype(F32)
        zeros = jnp.zeros((LANES - PART, LANES), F32)
        both = jnp.concatenate([block[:PART], zeros, block[PART:], zeros], axis=0)
        spot = pl.multiple_of(sel[g] * LANES, LANES)
        gathered[:, pl.ds(spot, LANES)] = both.astype(BF)
    values = gathered[...]
    for c in range(A // 16):
        rows = slice(c * chunk_rows, (c + 1) * chunk_rows)
        turned = slice(A * SUB + c * chunk_rows, A * SUB + (c + 1) * chunk_rows)
        dims = (((1,), (1,)), ((), ()))
        by_cos = lax.dot_general(section[rows, :], values, dims, preferred_element_type=F32)
        by_sin = lax.dot_general(section[turned, :], values, dims, preferred_element_type=F32)
        real = by_cos[:, :LANES] - by_sin[:, LANES:]
        imag = by_cos[:, LANES:] + by_sin[:, :LANES]
        spot = slice(c * 16, (c + 1) * 16)
        twisted[spot, 0, pl.ds(start, SUB), :] = real.astype(BF).reshape(16, SUB, LANES)
        twisted[spot, 1, pl.ds(start, SUB), :] = imag.astype(BF).reshape(16, SUB, LANES)


def forward_y_first_kernel(sel, *refs):
    *groups, section, twisted, gathered = refs
    start = pl.multiple_of(pl.program_id(0) * SUB, SUB)
    section_step(sel, groups, section, gathered, twisted, start)


def forward_y_first(sel, groups, section):
    steps = HIGH // PARTS
    return pl.pallas_call(
        forward_y_first_kernel,
        grid_spec=pltpu.PrefetchScalarGridSpec(
            num_scalar_prefetch=1,
            grid=(steps,),
            in_specs=[pl.BlockSpec((1, ROWS, LANES), lambda i, s: (i, 0, 0))] * len(groups)
            + [pl.BlockSpec(section.shape, lambda i, s: (0, 0))],
            out_specs=pl.BlockSpec((A, 2, A // PARTS, LANES), lambda i, s: (0, 0, 0, 0)),
            scratch_shapes=[pltpu.VMEM((2 * LANES, A * SUB), BF)],
        ),
        out_shape=jax.ShapeDtypeStruct((A, 2, A // PARTS, LANES), BF),
        compiler_params=pltpu.CompilerParams(vmem_limit_bytes=VMEM),
        cost_estimate=cost(4),
        name="forward_y_first",
    )(sel, *groups, section)


def forward_y_kernel(steps, sel, *refs):
    *groups, section, earlier, last, out, gathered, twisted = refs
    step = pl.program_id(0)
    first = HIGH // PARTS

    @pl.when(step < first)
    def _():
        start = pl.multiple_of(step * SUB, SUB)
        section_step(sel, groups, section, gathered, twisted, start)

    @pl.when(step >= first)
    def _():
        count = PAIRS // steps
        base = (step - first) * count
        for q in range(count):
            rows = []
            for e in range(2):
                for part in range(2):
                    rows.append(earlier[2 * (base + q) + e, part])
                    rows.append(twisted[2 * (base + q) + e, part])
            out[q] = dot(last[q], jnp.concatenate(rows, axis=0)).astype(BF)


def forward_y(sel, groups, section, earlier, last):
    steps = 2
    first = HIGH // PARTS
    count = PAIRS // steps

    def late(i, s):
        return (jnp.maximum(i - first, 0), 0, 0)

    return pl.pallas_call(
        functools.partial(forward_y_kernel, steps),
        grid_spec=pltpu.PrefetchScalarGridSpec(
            num_scalar_prefetch=1,
            grid=(first + steps,),
            in_specs=[
                pl.BlockSpec((1, ROWS, LANES), lambda i, s: (jnp.minimum(i, first - 1), 0, 0))
            ]
            * len(groups)
            + [
                pl.BlockSpec(section.shape, lambda i, s: (0, 0)),
                pl.BlockSpec(earlier.shape, lambda i, s: (0, 0, 0, 0)),
                pl.BlockSpec((count, ROWS, 4 * A), late),
            ],
            out_specs=pl.BlockSpec((count, ROWS, LANES), late),
            scratch_shapes=[
                pltpu.VMEM((2 * LANES, A * SUB), BF),
                pltpu.VMEM((A, 2, A // PARTS, LANES), BF),
            ],
        ),
        out_shape=jax.ShapeDtypeStruct((PAIRS, ROWS, LANES), BF),
        compiler_params=pltpu.CompilerParams(vmem_limit_bytes=VMEM),
        cost_estimate=cost(8),
        name="forward_y",
    )(sel, *groups, section, earlier, last)


def inverse_kernel(steps, sel, spec, freq_y, square_x, table_y, table_x, after, out, mid):
    step = pl.program_id(0)
    count = PAIRS // steps
    each = HALF // steps
    limit = F32(LIMIT * LIMIT)

    @pl.when(step < steps)
    def _():
        def pair(q, carry):
            pair_id = step * count + q
            offset = (2 * pair_id + sel[2]).astype(F32)
            row_freq = freq_y[...] + offset
            inside = row_freq * row_freq + square_x[...] <= limit
            values = jnp.where(inside, spec[q].astype(F32), 0.0).astype(BF)
            mixed = dot(table_y[q], values)
            for e in range(2):
                for part in range(2):
                    rows = slice((2 * e + part) * A, (2 * e + part + 1) * A)
                    spot = part * A * PITCH + 2 * pair_id + e
                    mid[pl.ds(spot, A, stride=PITCH), :] = mixed[rows]
            return carry

        lax.fori_loop(0, count, pair, 0, unroll=4)

    @pl.when(step >= steps)
    def _():
        def line(i, carry):
            by = (step - steps) * each + i
            rows = []
            for b in range(2):
                for part in range(2):
                    start = part * A * PITCH + (by + b * HALF) * PITCH
                    rows.append(mid[pl.ds(start, A), :].astype(BF))
            product = dot(jnp.concatenate(rows, axis=0), table_x[0, 0])
            for b in range(2):
                re = product[2 * b * A : (2 * b + 1) * A]
                im = product[(2 * b + 1) * A : (2 * b + 2) * A]
                span = slice(b * LANES, (b + 1) * LANES)
                out[i, :A, span] = (re[:, :LANES] - im[:, LANES:]).astype(BF)
                out[i, A:, span] = (re[:, LANES:] + im[:, :LANES]).astype(BF)
            return carry

        lax.fori_loop(0, each, line, 0, unroll=4)


def inverse(sel, spec, freq_y, square_x, table_y, table_x, after):
    steps = 2
    count = PAIRS // steps
    each = HALF // steps

    def early(i, s):
        return jnp.minimum(i, steps - 1)

    return pl.pallas_call(
        functools.partial(inverse_kernel, steps),
        grid_spec=pltpu.PrefetchScalarGridSpec(
            num_scalar_prefetch=1,
            grid=(2 * steps,),
            in_specs=[
                pl.BlockSpec((count, ROWS, LANES), lambda i, s: (early(i, s), 0, 0)),
                pl.BlockSpec((ROWS, LANES), lambda i, s: (0, 0)),
                pl.BlockSpec((1, LANES), lambda i, s: (0, 0)),
                pl.BlockSpec((count, 4 * A, ROWS), lambda i, s: (early(i, s), 0, 0)),
                pl.BlockSpec((1, 1) + table_x.shape[2:], lambda i, s: (s[0], s[1], 0, 0)),
                pl.BlockSpec(memory_space=pl.ANY),
            ],
            out_specs=pl.BlockSpec(
                (each, 2 * A, 2 * LANES), lambda i, s: (jnp.maximum(i - steps, 0), 0, 0)
            ),
            scratch_shapes=[pltpu.VMEM((2 * A * PITCH, LANES), F32)],
        ),
        out_shape=jax.ShapeDtypeStruct((HALF, 2 * A, 2 * LANES), BF),
        compiler_params=pltpu.CompilerParams(vmem_limit_bytes=VMEM),
        cost_estimate=cost(8.5),
        name="inverse",
    )(sel, spec, freq_y, square_x, table_y, table_x, after)


def collect_kernel(sheet_count, *refs):
    sheets, weights, outs = refs[:sheet_count], refs[sheet_count], refs[sheet_count + 1 :]
    tiles = weights.shape[0] // 4
    group = tiles // len(outs)
    lane = lax.broadcasted_iota(jnp.int32, (tiles, LANES), 1)
    lower = lane < A

    def line(i, carry):
        stacked = sheets[0][i]
        if len(sheets) > 1:
            stacked = jnp.concatenate([sheet[i] for sheet in sheets], axis=0)
        sums = dot(weights[...], stacked)
        for part in range(2):
            even = sums[2 * part * tiles : (2 * part + 1) * tiles]
            odd = sums[(2 * part + 1) * tiles : (2 * part + 2) * tiles]
            keep = jnp.where(lower, even[:, :LANES], odd[:, LANES:])
            move = jnp.where(lower, even[:, LANES:], odd[:, :LANES])
            total = (keep + pltpu.roll(move, A, 1)).astype(BF)
            for o, out in enumerate(outs):
                out[part, i] = total[o * group : (o + 1) * group]
        return carry

    lax.fori_loop(0, outs[0].shape[1], line, 0, unroll=2)


def collect(sheets, weights, fields, part):
    tiles = weights.shape[0] // 4
    group = tiles // fields
    lines = HALF // PARTS
    steps = 2
    each = lines // steps
    sheet_spec = pl.BlockSpec((each, 2 * A, 2 * LANES), lambda i: (part * steps + i, 0, 0))
    return pl.pallas_call(
        functools.partial(collect_kernel, len(sheets)),
        grid=(steps,),
        in_specs=[sheet_spec] * len(sheets) + [pl.BlockSpec(weights.shape, lambda i: (0, 0))],
        out_specs=[pl.BlockSpec((2, each, group, LANES), lambda i: (0, i, 0, 0))] * fields,
        out_shape=[jax.ShapeDtypeStruct((2, lines, group, LANES), BF)] * fields,
        compiler_params=pltpu.CompilerParams(vmem_limit_bytes=VMEM),
        cost_estimate=cost(6),
        name="collect",
    )(*sheets, weights)


def crop_kernel(rows, cols, odd, mine, pot, after, out, held, sems):
    slots = out.shape[0]

    def copy(i):
        return pltpu.make_async_copy(
            pot.at[
                pl.ds(pl.multiple_of(rows[i] * A, A), A),
                pl.ds(pl.multiple_of(cols[i] * LANES, LANES), LANES),
            ],
            held.at[i],
            sems.at[i],
        )

    def begin(i, carry):
        copy(i).start()
        return carry

    def finish(i, carry):
        copy(i).wait()
        block = held[i].astype(F32)
        block = jnp.where(odd[i] == 1, pltpu.roll(block, A, 1), block)
        lane = lax.broadcasted_iota(jnp.int32, (HALF, LANES), 1)
        packed = jnp.where(lane < A, block[:HALF], pltpu.roll(block[HALF:], A, 1))
        out[i] = jnp.where(mine[i] == 1, packed, 0.0).astype(BF)
        return carry

    lax.fori_loop(0, slots, begin, 0)
    lax.fori_loop(0, slots, finish, 0)


def crop(rows, cols, odd, mine, pot, after):
    slots = rows.shape[0]
    return pl.pallas_call(
        crop_kernel,
        in_specs=[pl.BlockSpec(memory_space=pltpu.SMEM)] * 4
        + [pl.BlockSpec(memory_space=pl.ANY)] * 2,
        out_specs=pl.BlockSpec(memory_space=pltpu.VMEM),
        out_shape=jax.ShapeDtypeStruct((slots, HALF, LANES), BF),
        scratch_shapes=[pltpu.VMEM((slots, A, LANES), BF), pltpu.SemaphoreType.DMA((slots,))],
        compiler_params=pltpu.CompilerParams(vmem_limit_bytes=VMEM),
        cost_estimate=cost(7),
        name="crop",
    )(rows, cols, odd, mine, pot, after)


def detect_kernel(alpha, counts, fields, pot, plane, across, down, bins, out, lines):
    beams, slots = fields.shape[0], fields.shape[1]
    for s in range(slots):
        waves = []
        for j in range(beams):
            re, im = fields[j, s, 0].astype(F32), fields[j, s, 1].astype(F32)
            cos, sin = plane[j, 0], plane[j, 1]
            waves.append((re * cos - im * sin, re * sin + im * cos))
        turned, level = sine_cosine(pot[s].astype(F32))
        for g in range(G):
            real = jnp.zeros((HALF, LANES), F32)
            imag = jnp.zeros((HALF, LANES), F32)
            for j in range(beams):
                cos, sin = alpha[0, j, s * G + g], alpha[1, j, s * G + g]
                re, im = waves[j]
                real = real + cos * re - sin * im
                imag = imag + cos * im + sin * re
            lines[2 * (s * G + g)] = (real * level - imag * turned).astype(BF)
            lines[2 * (s * G + g) + 1] = (real * turned + imag * level).astype(BF)
    total = slots * G
    first = dot(lines[...].reshape(2 * total * HALF, LANES), across[...])
    first = first.reshape(total, 2, HALF, 2 * LANES)
    real = (first[:, 0, :, :LANES] + first[:, 1, :, LANES:]).astype(BF)
    imag = (first[:, 1, :, :LANES] - first[:, 0, :, LANES:]).astype(BF)
    lane = lax.broadcasted_iota(jnp.int32, (A, LANES), 1)
    for i in range(total):
        both = jnp.concatenate([real[i], imag[i]], axis=1)
        mixed = dot(down[...], both)
        even, odd = mixed[: 2 * A], mixed[2 * A :]
        re_cos = even[:A, :LANES] + pltpu.roll(odd[:A, :LANES], A, 1)
        re_sin = even[A:, :LANES] + pltpu.roll(odd[A:, :LANES], A, 1)
        im_cos = even[:A, LANES:] + pltpu.roll(odd[:A, LANES:], A, 1)
        im_sin = even[A:, LANES:] + pltpu.roll(odd[A:, LANES:], A, 1)
        re = re_cos + im_sin
        im = im_cos - re_sin
        power = jnp.where(lane < A, re * re + im * im, 0.0)
        sums = jnp.sum(power[None] * bins[...], axis=1)
        block, slot = divmod(i // G, slots // counts.shape[0])
        active = slot < counts[block]
        out[i] = jnp.where(active, sums, 0.0)


def detect(alpha, counts, fields, pot, plane, across, down, bins):
    slots = fields.shape[1]
    smem = pl.BlockSpec(memory_space=pltpu.SMEM)
    vmem = pl.BlockSpec(memory_space=pltpu.VMEM)
    return pl.pallas_call(
        detect_kernel,
        in_specs=[smem, smem] + [vmem] * 6,
        out_specs=vmem,
        out_shape=jax.ShapeDtypeStruct((slots * G, NDET, LANES), F32),
        scratch_shapes=[pltpu.VMEM((2 * slots * G, HALF, LANES), BF)],
        compiler_params=pltpu.CompilerParams(vmem_limit_bytes=VMEM),
        name="detect",
    )(alpha, counts, fields, pot, plane, across, down, bins)


def detect_tables(beam_total):
    n = np.arange(A)
    table = turn(n[:, None] * n[None, :], A) / A
    cos, sin = table.real, table.imag
    zero = np.zeros((A, A))
    across = np.block([[cos, zero, sin, zero], [zero, cos, zero, sin]])
    rows = np.concatenate([cos, sin], axis=0)
    down = np.concatenate([rows[:, :HALF], rows[:, HALF:]], axis=0)
    signed = np.where(n < A // 2, n, n - A)
    radius = signed[:, None] ** 2 + signed[None, :] ** 2
    width = A // (2 * NDET)
    bins = np.zeros((NDET, A, LANES))
    for d in range(NDET):
        member = (radius >= (width * d) ** 2) & (radius < (width * (d + 1)) ** 2)
        bins[d, :, :A] = member * (A * A / (beam_total * member.sum()))
    return low(across), low(down), bins.astype(np.float32)


def coefficients(tile_ids, beam_rows, shifts):
    across = N // A
    offsets = jnp.arange(G, dtype=jnp.int32)
    spot_y = (tile_ids // across)[:, None] * A + A // 2 + offsets[None, :]
    spot_x = (tile_ids % across)[:, None] * A + A // 2 + 2 * offsets[None, :]
    wave_y = jnp.remainder(F * beam_rows[:, 0], N)[:, None, None]
    wave_x = jnp.remainder(F * beam_rows[:, 1], N)[:, None, None]
    windings = (wave_y * spot_y[None] % N + wave_x * spot_x[None] % N) % N
    phases = shifts[:, None, None] + 2.0 * math.pi / N * windings.astype(F32)
    return jnp.stack([jnp.cos(phases), -jnp.sin(phases)])


def tile_weights(tile_ids, beam_row, k1_pairs):
    across = N // A
    ty = tile_ids // across - beam_row[0]
    tx = tile_ids % across - beam_row[1]
    k1y = jnp.arange(A, dtype=jnp.int32)
    k1x = k1_pairs[:, None] + jnp.arange(2, dtype=jnp.int32)[None, :]
    winding = (
        k1y[None, None, None, :] * ty[None, :, None, None]
        + (k1x.T[:, None, :] * tx[None, :, None])[..., None]
    )
    angle = 2.0 * math.pi / A * (winding % A).astype(F32)
    cos, sin = jnp.cos(angle), jnp.sin(angle)
    upper = jnp.stack([cos, -sin], axis=3)
    under = jnp.stack([sin, cos], axis=3)
    both = jnp.stack([upper, under]).astype(BF)
    return both.reshape(4 * tile_ids.shape[0], k1_pairs.shape[0] * 2 * A)


def plane_waves(beam_index):
    by = jnp.arange(HALF, dtype=jnp.int32)[:, None] + HALF * (jnp.arange(LANES) // A)[None, :]
    bx = jnp.broadcast_to((jnp.arange(LANES, dtype=jnp.int32) % A)[None, :], by.shape)
    row_y = beam_index[:, 0][:, None, None]
    row_x = beam_index[:, 1][:, None, None]
    winding = (row_y * by[None] + row_x * bx[None] + HALF * (row_y + row_x)) % A
    angle = 2.0 * math.pi / A * winding.astype(F32)
    return jnp.stack([jnp.cos(angle), jnp.sin(angle)], axis=1)


def shards(pot_first, pot_second, beam_index, aberration, tile_table, tile_count):
    field_count = lax.axis_size("beam")
    hold_count = lax.axis_size("slab")
    field_pos = lax.axis_index("beam")
    hold_pos = lax.axis_index("slab")
    band_rows = pot_first.shape[0]
    band_tiles = band_rows // A
    width_k = A // field_count
    sheets = width_k // 2
    across = N // A
    beam_total = beam_index.shape[0]
    share = hold_pos % sheets

    section_x = np.stack(
        [
            section_forward(
                np.array(
                    [width_k * p + 2 * t + ks for p in range(field_count) for ks in range(2)]
                )
            )
            for t in range(sheets)
        ]
    )
    last_x = np.stack(
        [
            np.stack(
                [
                    last_forward_x([width_k * p + 2 * t, width_k * p + 2 * t + 1])
                    for p in range(field_count)
                ]
            )
            for t in range(sheets)
        ]
    )
    section_y = section_forward(np.arange(A))
    last_y = np.stack([last_forward_y([2 * q, 2 * q + 1]) for q in range(PAIRS)])
    inverse_y = np.stack([first_inverse_y([2 * q, 2 * q + 1]) for q in range(PAIRS)])
    inverse_x = np.stack(
        [
            np.stack(
                [
                    first_inverse_x([width_k * p + 2 * t, width_k * p + 2 * t + 1])
                    for t in range(sheets)
                ]
            )
            for p in range(field_count)
        ]
    )

    blocks_dev = tile_table.shape[0] // (field_count * hold_count)
    slot_count = tile_table.shape[1]
    own_slots = blocks_dev * slot_count
    table = tile_table.reshape(field_count, hold_count, own_slots)
    others = field_pos ^ jnp.arange(field_count, dtype=jnp.int32)
    mates = hold_pos ^ jnp.arange(hold_count, dtype=jnp.int32)

    def trade(arrays, axis, count):
        out = [arrays[0]]
        for o in range(1, count):
            out.append(lax.ppermute(arrays[o], axis, [(i, i ^ o) for i in range(count)]))
        return out

    sel = jnp.stack([share, field_pos]).astype(jnp.int32)
    received = []
    for part in range(PARTS):
        lines = forward_x(sel, pot_first, section_x, last_x, field_count, part)
        lines = trade(lines, "beam", field_count)
        if lines[0].shape[2] != LANES:
            ratio = LANES // lines[0].shape[2]
            stacked = jnp.stack(lines)[others]
            stacked = stacked.reshape((field_count // ratio, ratio) + lines[0].shape)
            stacked = stacked.transpose(0, 2, 3, 1, 4).reshape(
                field_count // ratio, lines[0].shape[0], ROWS, LANES
            )
            lines = [stacked[g] for g in range(stacked.shape[0])]
            places = jnp.arange(len(lines), dtype=jnp.int32)
        else:
            places = others
        received.append(lines)
    earlier = forward_y_first(places, received[0], section_y)
    spec = forward_y(places, received[1], section_y, earlier, last_y)
    specs = [spec]
    for x in range(1, sheets):
        top = 1 << (x.bit_length() - 1)
        bit, source = (top, 0) if x == top else (x ^ top, top)
        swap = [(i, i ^ bit) for i in range(hold_count)]
        specs.append(lax.ppermute(specs[source], "slab", swap))

    ids = lax.dynamic_index_in_dim(table, hold_pos, 1, keepdims=False)[others].reshape(-1)
    tile_y, tile_x = ids // across, ids % across
    mine = (tile_y // band_tiles == field_pos).astype(jnp.int32)
    rows = jnp.clip(tile_y - field_pos * band_tiles, 0, band_tiles - 1)
    crops = crop(rows, tile_x // 2, tile_x % 2, mine, pot_second, spec)
    crops = crops.reshape(field_count, own_slots, HALF, LANES)
    crops = trade([crops[o] for o in range(field_count)], "beam", field_count)
    crop_total = functools.reduce(jnp.add, [c.astype(F32) for c in crops]).astype(BF)

    beam_row = lax.dynamic_index_in_dim(beam_index, hold_pos, 0, keepdims=False)
    pair_ids = share ^ jnp.arange(sheets, dtype=jnp.int32)
    k1_pairs = field_pos * width_k + 2 * pair_ids
    ordered = table[others][:, mates].reshape(-1)
    weights = tile_weights(ordered, beam_row, k1_pairs)
    row = np.arange(ROWS)
    base = (row // (2 * K2_COUNT)) + A * (K2_LOW + row % K2_COUNT)
    base = np.where(row < 4 * K2_COUNT, base, 0)
    freq_y = np.broadcast_to(base[:, None], (ROWS, LANES)).astype(np.float32)
    lane = jnp.arange(LANES, dtype=jnp.int32)[None, None, :]
    freq_x = (
        k1_pairs[:, None, None]
        + lane // K2_COUNT
        + A * (K2_LOW + lane % K2_COUNT)
        + F * beam_row[1]
    )
    square_x = jnp.where(lane < 2 * K2_COUNT, freq_x * freq_x, N * N).astype(F32)
    waves = []
    for x in range(sheets):
        sel = jnp.stack([field_pos, pair_ids[x], F * beam_row[0]]).astype(jnp.int32)
        after = crops[0] if x >= 2 else spec
        waves.append(inverse(sel, specs[x], freq_y, square_x[x], inverse_y, inverse_x, after))
    halves = []
    for part in range(PARTS):
        partial = trade(collect(waves, weights, field_count, part), "beam", field_count)
        total = functools.reduce(jnp.add, [t.astype(F32) for t in partial])
        halves.append(total.astype(BF).transpose(2, 0, 1, 3))
    tiles = jnp.concatenate(halves, axis=2).reshape(hold_count, own_slots, 2, HALF, LANES)
    fields = jnp.stack(trade([tiles[x] for x in range(hold_count)], "slab", hold_count))

    own = lax.dynamic_index_in_dim(
        lax.dynamic_index_in_dim(table, field_pos, 0, keepdims=False), hold_pos, 0, keepdims=False
    )
    beams = beam_index[mates]
    alpha = coefficients(own, beams, aberration[mates]).reshape(2, beam_total, own_slots * G)
    first_block = (field_pos * hold_count + hold_pos) * blocks_dev
    counts = lax.dynamic_slice_in_dim(tile_count, first_block, blocks_dev, 0)
    bins = detect_tables(beam_total)
    sums = detect(alpha, counts, fields, crop_total, plane_waves(beams), *bins)
    return jnp.sum(sums, axis=2).reshape(blocks_dev, slot_count, G, NDET)


def solution(mesh):
    return jax.shard_map(
        shards,
        mesh=mesh,
        in_specs=(P("beam", None), P("beam", None), P(), P(), P(), P()),
        out_specs=P(("beam", "slab"), None, None, None),
        check_vma=False,
    )
```

```python
import functools
import math

import jax
import jax.numpy as jnp
import ml_dtypes
import numpy as np
from jax import lax
from jax.experimental import pallas as pl
from jax.experimental.pallas import tpu as pltpu
from jax.sharding import PartitionSpec as P

A = 64
N = 4096
F = 64
G = 3
NDET = 16
QMAX = 3
LIMIT = N // 3
K2_LOW = -(LIMIT // A + 1 + QMAX)
K2_COUNT = 2 * (LIMIT // A + 1 + QMAX)
PART = 104
ROWS = 2 * PART
LANES = 128
SUB = 16
HIGH = A // SUB
HALF = A // 2
PAIRS = A // 2
PARTS = 2
VMEM = 60 * 1024 * 1024
PITCH = A + 1
BF = jnp.bfloat16
F32 = jnp.float32


def low(values):
    return np.asarray(values, dtype=np.float32).astype(ml_dtypes.bfloat16)


def turn(numerator, period):
    return np.exp(2j * np.pi * (numerator % period) / period)


def digits_k2():
    return K2_LOW + np.arange(K2_COUNT)


def spread(table):
    both = np.stack([table.real, table.imag])
    eye = np.eye(SUB)
    out = both[:, :, None, :, None] * eye[None, None, :, None, :]
    return low(out.reshape(2 * table.shape[0] * SUB, table.shape[1] * SUB))


def real_rows(table):
    return np.block([[table.real, -table.imag], [table.imag, table.real]])


def section_forward(k1):
    n1 = np.arange(A)
    return spread(np.conj(turn(k1[:, None] * n1[None, :], A)) / A)


def last_forward_x(k1_pair):
    n2 = np.arange(A)
    out = np.zeros((2, PART, 2, 2, A))
    for ks, k1 in enumerate(k1_pair):
        freq = k1 + A * digits_k2()
        table = np.conj(turn(freq[:, None] * n2[None, :], N)) / A
        block = real_rows(table).reshape(2, K2_COUNT, 2, A)
        out[:, ks * K2_COUNT : (ks + 1) * K2_COUNT, ks] = block
    return low(out.reshape(ROWS, 4 * A))


def last_forward_y(k1_pair):
    n2 = np.arange(A)
    out = np.zeros((ROWS, 2, 2 * A))
    for e, k1 in enumerate(k1_pair):
        freq = k1 + A * digits_k2()
        table = np.conj(turn(freq[:, None] * n2[None, :], N)) / A
        out[e * 2 * K2_COUNT : (e + 1) * 2 * K2_COUNT, e] = real_rows(table)
    return low(out.reshape(ROWS, 4 * A))


def first_inverse(k1):
    n2 = np.arange(A)
    freq = k1 + A * digits_k2()
    return turn(n2[:, None] * freq[None, :], N) * np.conj(turn(freq * freq, 2 * N))[None, :]


def first_inverse_y(k1_pair):
    out = np.zeros((2, 2 * A, ROWS))
    for e, k1 in enumerate(k1_pair):
        out[e, :, e * 2 * K2_COUNT : (e + 1) * 2 * K2_COUNT] = real_rows(first_inverse(k1))
    return low(out.reshape(4 * A, ROWS))


def first_inverse_x(k1_pair):
    out = np.zeros((LANES, 2, 2, A))
    for ks, k1 in enumerate(k1_pair):
        table = first_inverse(k1).T
        out[ks * K2_COUNT : (ks + 1) * K2_COUNT, 0, ks] = table.real
        out[ks * K2_COUNT : (ks + 1) * K2_COUNT, 1, ks] = table.imag
    return low(out.reshape(LANES, 4 * A))


def sine_cosine(x):
    u = x * x
    s = F32(SIN_FIT[-1])
    for c in SIN_FIT[-2::-1]:
        s = s * u + F32(c)
    q = F32(COS_FIT[-1])
    for c in COS_FIT[-2::-1]:
        q = q * u + F32(c)
    return s * x, q


def fit(function, degree):
    top = 3.1421**2
    nodes = 0.5 * top * (1 - np.cos(np.pi * (np.arange(64) + 0.5) / 64))
    cheb = np.polynomial.chebyshev.Chebyshev.fit(
        nodes, function(np.sqrt(nodes)), degree, domain=[0, top]
    )
    return [float(c) for c in cheb.convert(kind=np.polynomial.Polynomial).coef]


SIN_FIT = fit(lambda x: np.sinc(x / np.pi), 5)
COS_FIT = fit(np.cos, 5)


def dot(a, b):
    return jnp.dot(a, b, preferred_element_type=F32)


def cost(micros):
    return pl.CostEstimate(flops=int(micros * 1.1e9), bytes_accessed=0, transcendentals=0)


def forward_x_kernel(sel, pot, section, last, out, cos_ref, sin_ref, twisted):
    fields = out.shape[0]
    lanes = out.shape[3]
    half = section.shape[1] // 2

    def chunk(t, carry):
        block = pot[:, 0, :, pl.ds(pl.multiple_of(t * LANES, LANES), LANES)]
        values = block.reshape(lanes, LANES).astype(F32).T
        sine, cosine = sine_cosine(values)
        cos_ref[pl.ds(2 * t, 2)] = cosine.astype(BF).reshape(2, A, lanes)
        sin_ref[pl.ds(2 * t, 2)] = sine.astype(BF).reshape(2, A, lanes)
        return carry

    lax.fori_loop(0, N // LANES, chunk, 0, unroll=4)
    table = section[0]
    for m in range(HIGH):
        span = slice(m * SUB, (m + 1) * SUB)
        part_cos = cos_ref[:, span, :].reshape(A * SUB, lanes)
        part_sin = sin_ref[:, span, :].reshape(A * SUB, lanes)
        if lanes % LANES == 0:
            both = dot(table, jnp.concatenate([part_cos, part_sin], axis=1))
            of_cos, of_sin = both[:, :lanes], both[:, lanes:]
        else:
            of_cos, of_sin = dot(table, part_cos), dot(table, part_sin)
        real = of_cos[:half] - of_sin[half:]
        imag = of_cos[half:] + of_sin[:half]
        twisted[:, m * SUB : (m + 1) * SUB, :] = real.astype(BF).reshape(2 * fields, SUB, lanes)
        twisted[:, A + m * SUB : A + (m + 1) * SUB, :] = imag.astype(BF).reshape(
            2 * fields, SUB, lanes
        )
    for d in range(fields):
        lines = twisted[2 * d : 2 * d + 2].reshape(4 * A, lanes)
        out[d, 0] = dot(last[0, d], lines).astype(BF)


def forward_x(sel, pot, section, last, fields, part):
    groups = pot.shape[0] // A
    lanes = groups * SUB
    steps = HIGH // PARTS
    return pl.pallas_call(
        forward_x_kernel,
        grid_spec=pltpu.PrefetchScalarGridSpec(
            num_scalar_prefetch=1,
            grid=(steps,),
            in_specs=[
                pl.BlockSpec((groups, 1, SUB, N), lambda i, s: (0, part * steps + i, 0, 0)),
                pl.BlockSpec((1,) + section.shape[1:], lambda i, s: (s[0], 0, 0)),
                pl.BlockSpec((1,) + last.shape[1:], lambda i, s: (s[0], 0, 0, 0)),
            ],
            out_specs=pl.BlockSpec((fields, 1, ROWS, lanes), lambda i, s: (0, i, 0, 0)),
            scratch_shapes=[
                pltpu.VMEM((A, A, lanes), BF),
                pltpu.VMEM((A, A, lanes), BF),
                pltpu.VMEM((2 * fields, 2 * A, lanes), BF),
            ],
        ),
        out_shape=jax.ShapeDtypeStruct((fields, steps, ROWS, lanes), BF),
        compiler_params=pltpu.CompilerParams(vmem_limit_bytes=VMEM),
        cost_estimate=cost(9),
        name="forward_x",
    )(sel, pot.reshape(groups, HIGH, SUB, N), section, last)


def section_step(lines, section, gathered, twisted, start):
    chunk_rows = 16 * SUB
    for g in range(lines.shape[0]):
        block = lines[g, 0].astype(F32)
        zeros = jnp.zeros((LANES - PART, LANES), F32)
        both = jnp.concatenate([block[:PART], zeros, block[PART:], zeros], axis=0)
        gathered[:, g * LANES : (g + 1) * LANES] = both.astype(BF)
    values = gathered[...]
    for c in range(A // 16):
        rows = slice(c * chunk_rows, (c + 1) * chunk_rows)
        turned = slice(A * SUB + c * chunk_rows, A * SUB + (c + 1) * chunk_rows)
        dims = (((1,), (1,)), ((), ()))
        by_cos = lax.dot_general(section[rows, :], values, dims, preferred_element_type=F32)
        by_sin = lax.dot_general(section[turned, :], values, dims, preferred_element_type=F32)
        real = by_cos[:, :LANES] - by_sin[:, LANES:]
        imag = by_cos[:, LANES:] + by_sin[:, :LANES]
        spot = slice(c * 16, (c + 1) * 16)
        twisted[spot, 0, pl.ds(start, SUB), :] = real.astype(BF).reshape(16, SUB, LANES)
        twisted[spot, 1, pl.ds(start, SUB), :] = imag.astype(BF).reshape(16, SUB, LANES)


def forward_y_first_kernel(lines, section, twisted, gathered):
    start = pl.multiple_of(pl.program_id(0) * SUB, SUB)
    section_step(lines, section, gathered, twisted, start)


def forward_y_first(lines, section):
    groups, steps = lines.shape[:2]
    return pl.pallas_call(
        forward_y_first_kernel,
        grid=(steps,),
        in_specs=[
            pl.BlockSpec((groups, 1, ROWS, LANES), lambda i: (0, i, 0, 0)),
            pl.BlockSpec(section.shape, lambda i: (0, 0)),
        ],
        out_specs=pl.BlockSpec((A, 2, A // PARTS, LANES), lambda i: (0, 0, 0, 0)),
        out_shape=jax.ShapeDtypeStruct((A, 2, A // PARTS, LANES), BF),
        scratch_shapes=[pltpu.VMEM((2 * LANES, A * SUB), BF)],
        compiler_params=pltpu.CompilerParams(vmem_limit_bytes=VMEM),
        cost_estimate=cost(7),
        name="forward_y_first",
    )(lines, section)


def forward_y_kernel(steps, lines, section, earlier, last, after, out, gathered, twisted):
    step = pl.program_id(0)
    first = HIGH // PARTS

    @pl.when(step < first)
    def _():
        start = pl.multiple_of(step * SUB, SUB)
        section_step(lines, section, gathered, twisted, start)

    @pl.when(step >= first)
    def _():
        count = PAIRS // steps
        base = (step - first) * count
        for q in range(count):
            rows = []
            for e in range(2):
                for part in range(2):
                    rows.append(earlier[2 * (base + q) + e, part])
                    rows.append(twisted[2 * (base + q) + e, part])
            out[q] = dot(last[q], jnp.concatenate(rows, axis=0)).astype(BF)


def forward_y(lines, section, earlier, last, after):
    groups, first = lines.shape[:2]
    steps = 2
    count = PAIRS // steps

    def late(i):
        return (jnp.maximum(i - first, 0), 0, 0)

    return pl.pallas_call(
        functools.partial(forward_y_kernel, steps),
        grid=(first + steps,),
        in_specs=[
            pl.BlockSpec(
                (groups, 1, ROWS, LANES), lambda i: (0, jnp.minimum(i, first - 1), 0, 0)
            ),
            pl.BlockSpec(section.shape, lambda i: (0, 0)),
            pl.BlockSpec(earlier.shape, lambda i: (0, 0, 0, 0)),
            pl.BlockSpec((count, ROWS, 4 * A), late),
            pl.BlockSpec(memory_space=pl.ANY),
        ],
        out_specs=pl.BlockSpec((count, ROWS, LANES), late),
        out_shape=jax.ShapeDtypeStruct((PAIRS, ROWS, LANES), BF),
        scratch_shapes=[
            pltpu.VMEM((2 * LANES, A * SUB), BF),
            pltpu.VMEM((A, 2, A // PARTS, LANES), BF),
        ],
        compiler_params=pltpu.CompilerParams(vmem_limit_bytes=VMEM),
        cost_estimate=cost(10),
        name="forward_y",
    )(lines, section, earlier, last, after)


def inverse_kernel(steps, which, sel, spec, freq_y, square_x, table_y, table_x, *rest):
    out, mid = rest[-2:]
    step = pl.program_id(0)
    count = PAIRS // steps
    each = HALF // steps
    limit = F32(LIMIT * LIMIT)

    @pl.when(step < steps)
    def _():
        def pair(q, carry):
            pair_id = step * count + q
            offset = (2 * pair_id + sel[3 * which + 2]).astype(F32)
            row_freq = freq_y[...] + offset
            inside = row_freq * row_freq + square_x[0] <= limit
            values = jnp.where(inside, spec[q].astype(F32), 0.0).astype(BF)
            mixed = dot(table_y[q], values)
            for e in range(2):
                for part in range(2):
                    rows = slice((2 * e + part) * A, (2 * e + part + 1) * A)
                    spot = part * A * PITCH + 2 * pair_id + e
                    mid[pl.ds(spot, A, stride=PITCH), :] = mixed[rows]
            return carry

        lax.fori_loop(0, count, pair, 0, unroll=4)

    @pl.when(step >= steps)
    def _():
        def line(i, carry):
            by = (step - steps) * each + i
            rows = []
            for b in range(2):
                for part in range(2):
                    start = part * A * PITCH + (by + b * HALF) * PITCH
                    rows.append(mid[pl.ds(start, A), :].astype(BF))
            product = dot(jnp.concatenate(rows, axis=0), table_x[0, 0])
            for b in range(2):
                re = product[2 * b * A : (2 * b + 1) * A]
                im = product[(2 * b + 1) * A : (2 * b + 2) * A]
                span = slice(b * LANES, (b + 1) * LANES)
                out[i, :A, span] = (re[:, :LANES] - im[:, LANES:]).astype(BF)
                out[i, A:, span] = (re[:, LANES:] + im[:, :LANES]).astype(BF)
            return carry

        lax.fori_loop(0, each, line, 0, unroll=4)


def inverse(which, sel, spec, freq_y, square_x, table_y, table_x, after):
    steps = 2
    count = PAIRS // steps
    each = HALF // steps

    def early(i, s):
        return jnp.minimum(i, steps - 1)

    return pl.pallas_call(
        functools.partial(inverse_kernel, steps, which),
        grid_spec=pltpu.PrefetchScalarGridSpec(
            num_scalar_prefetch=1,
            grid=(2 * steps,),
            in_specs=[
                pl.BlockSpec((count, ROWS, LANES), lambda i, s: (early(i, s), 0, 0)),
                pl.BlockSpec((ROWS, LANES), lambda i, s: (0, 0)),
                pl.BlockSpec((1, 1, LANES), lambda i, s: (which, 0, 0)),
                pl.BlockSpec((count, 4 * A, ROWS), lambda i, s: (early(i, s), 0, 0)),
                pl.BlockSpec((1, 1) + table_x.shape[2:], lambda i, s: (s[3 * which], s[3 * which + 1], 0, 0)),
            ]
            + [pl.BlockSpec(memory_space=pl.ANY)] * len(after),
            out_specs=pl.BlockSpec(
                (each, 2 * A, 2 * LANES), lambda i, s: (jnp.maximum(i - steps, 0), 0, 0)
            ),
            scratch_shapes=[pltpu.VMEM((2 * A * PITCH, LANES), F32)],
        ),
        out_shape=jax.ShapeDtypeStruct((HALF, 2 * A, 2 * LANES), BF),
        compiler_params=pltpu.CompilerParams(vmem_limit_bytes=VMEM),
        cost_estimate=cost(8.5),
        name="inverse",
    )(sel, spec, freq_y, square_x, table_y, table_x, *after)


def collect_kernel(near, added, *refs):
    sheets, weights, out = refs[:near], refs[near], refs[-1]
    tiles = weights.shape[1] // 4
    fields = out.shape[0]
    lane = lax.broadcasted_iota(jnp.int32, (tiles, LANES), 1)
    lower = lane < A

    def line(i, carry):
        stacked = sheets[0][i]
        if near > 1:
            stacked = jnp.concatenate([sheet[i] for sheet in sheets], axis=0)
        sums = dot(weights[0], stacked)
        for part in range(2):
            even = sums[2 * part * tiles : (2 * part + 1) * tiles]
            odd = sums[(2 * part + 1) * tiles : (2 * part + 2) * tiles]
            keep = jnp.where(lower, even[:, :LANES], odd[:, LANES:])
            move = jnp.where(lower, even[:, LANES:], odd[:, :LANES])
            total = keep + pltpu.roll(move, A, 1)
            total = total.reshape(fields, tiles // fields, LANES)
            for a in range(added):
                total = total + refs[near + 1 + a][:, part, i].astype(F32)
            out[:, part, i] = total.astype(BF)
        return carry

    lax.fori_loop(0, out.shape[2], line, 0, unroll=2)


def collect(which, sheets, weights, fields, part, added, after):
    near = len(sheets)
    tiles = weights.shape[1] // 4
    group = tiles // fields
    lines = HALF // PARTS
    steps = 2
    each = lines // steps
    sheet_spec = pl.BlockSpec((each, 2 * A, 2 * LANES), lambda i: (part * steps + i, 0, 0))
    block = pl.BlockSpec((fields, 2, each, group, LANES), lambda i: (0, 0, i, 0, 0))
    return pl.pallas_call(
        functools.partial(collect_kernel, near, len(added)),
        grid=(steps,),
        in_specs=[sheet_spec] * near
        + [pl.BlockSpec((1,) + weights.shape[1:], lambda i: (which, 0, 0))]
        + [block] * len(added)
        + [pl.BlockSpec(memory_space=pl.ANY)] * len(after),
        out_specs=block,
        out_shape=jax.ShapeDtypeStruct((fields, 2, lines, group, LANES), BF),
        compiler_params=pltpu.CompilerParams(vmem_limit_bytes=VMEM),
        cost_estimate=cost(5),
        name="collect",
    )(*sheets, weights, *added, *after)


def crop_kernel(rows, cols, odd, mine, pot, after, out, held, sems):
    slots = out.shape[0]

    def copy(i):
        return pltpu.make_async_copy(
            pot.at[
                pl.ds(pl.multiple_of(rows[i] * A, A), A),
                pl.ds(pl.multiple_of(cols[i] * LANES, LANES), LANES),
            ],
            held.at[i],
            sems.at[i],
        )

    def begin(i, carry):
        copy(i).start()
        return carry

    def finish(i, carry):
        copy(i).wait()
        block = held[i].astype(F32)
        block = jnp.where(odd[i] == 1, pltpu.roll(block, A, 1), block)
        lane = lax.broadcasted_iota(jnp.int32, (HALF, LANES), 1)
        packed = jnp.where(lane < A, block[:HALF], pltpu.roll(block[HALF:], A, 1))
        out[i] = jnp.where(mine[i] == 1, packed, 0.0).astype(BF)
        return carry

    lax.fori_loop(0, slots, begin, 0)
    lax.fori_loop(0, slots, finish, 0)


def crop(rows, cols, odd, mine, pot, after):
    slots = rows.shape[0]
    return pl.pallas_call(
        crop_kernel,
        in_specs=[pl.BlockSpec(memory_space=pltpu.SMEM)] * 4
        + [pl.BlockSpec(memory_space=pl.ANY)] * 2,
        out_specs=pl.BlockSpec(memory_space=pltpu.VMEM),
        out_shape=jax.ShapeDtypeStruct((slots, HALF, LANES), BF),
        scratch_shapes=[pltpu.VMEM((slots, A, LANES), BF), pltpu.SemaphoreType.DMA((slots,))],
        compiler_params=pltpu.CompilerParams(vmem_limit_bytes=VMEM),
        cost_estimate=cost(7),
        name="crop",
    )(rows, cols, odd, mine, pot, after)


def detect_kernel(alpha, counts, fields, pot, plane, across, down, bins, out, lines):
    beams, slots = fields.shape[0], fields.shape[1]
    for s in range(slots):
        waves = []
        for j in range(beams):
            re, im = fields[j, s, 0].astype(F32), fields[j, s, 1].astype(F32)
            cos, sin = plane[j, 0], plane[j, 1]
            waves.append((re * cos - im * sin, re * sin + im * cos))
        turned, level = sine_cosine(pot[s].astype(F32))
        for g in range(G):
            real = jnp.zeros((HALF, LANES), F32)
            imag = jnp.zeros((HALF, LANES), F32)
            for j in range(beams):
                cos, sin = alpha[0, j, s * G + g], alpha[1, j, s * G + g]
                re, im = waves[j]
                real = real + cos * re - sin * im
                imag = imag + cos * im + sin * re
            lines[2 * (s * G + g)] = (real * level - imag * turned).astype(BF)
            lines[2 * (s * G + g) + 1] = (real * turned + imag * level).astype(BF)
    total = slots * G
    first = dot(lines[...].reshape(2 * total * HALF, LANES), across[...])
    first = first.reshape(total, 2, HALF, 2 * LANES)
    real = (first[:, 0, :, :LANES] + first[:, 1, :, LANES:]).astype(BF)
    imag = (first[:, 1, :, :LANES] - first[:, 0, :, LANES:]).astype(BF)
    lane = lax.broadcasted_iota(jnp.int32, (A, LANES), 1)
    for i in range(total):
        both = jnp.concatenate([real[i], imag[i]], axis=1)
        mixed = dot(down[...], both)
        even, odd = mixed[: 2 * A], mixed[2 * A :]
        re_cos = even[:A, :LANES] + pltpu.roll(odd[:A, :LANES], A, 1)
        re_sin = even[A:, :LANES] + pltpu.roll(odd[A:, :LANES], A, 1)
        im_cos = even[:A, LANES:] + pltpu.roll(odd[:A, LANES:], A, 1)
        im_sin = even[A:, LANES:] + pltpu.roll(odd[A:, LANES:], A, 1)
        re = re_cos + im_sin
        im = im_cos - re_sin
        power = jnp.where(lane < A, re * re + im * im, 0.0)
        sums = jnp.sum(power[None] * bins[...], axis=1)
        block, slot = divmod(i // G, slots // counts.shape[0])
        active = slot < counts[block]
        out[i] = jnp.where(active, sums, 0.0)


def detect(alpha, counts, fields, pot, plane, across, down, bins):
    slots = fields.shape[1]
    smem = pl.BlockSpec(memory_space=pltpu.SMEM)
    vmem = pl.BlockSpec(memory_space=pltpu.VMEM)
    return pl.pallas_call(
        detect_kernel,
        in_specs=[smem, smem] + [vmem] * 6,
        out_specs=vmem,
        out_shape=jax.ShapeDtypeStruct((slots * G, NDET, LANES), F32),
        scratch_shapes=[pltpu.VMEM((2 * slots * G, HALF, LANES), BF)],
        compiler_params=pltpu.CompilerParams(vmem_limit_bytes=VMEM),
        name="detect",
    )(alpha, counts, fields, pot, plane, across, down, bins)


def detect_tables(beam_total):
    n = np.arange(A)
    table = turn(n[:, None] * n[None, :], A) / A
    cos, sin = table.real, table.imag
    zero = np.zeros((A, A))
    across = np.block([[cos, zero, sin, zero], [zero, cos, zero, sin]])
    rows = np.concatenate([cos, sin], axis=0)
    down = np.concatenate([rows[:, :HALF], rows[:, HALF:]], axis=0)
    signed = np.where(n < A // 2, n, n - A)
    radius = signed[:, None] ** 2 + signed[None, :] ** 2
    width = A // (2 * NDET)
    bins = np.zeros((NDET, A, LANES))
    for d in range(NDET):
        member = (radius >= (width * d) ** 2) & (radius < (width * (d + 1)) ** 2)
        bins[d, :, :A] = member * (A * A / (beam_total * member.sum()))
    return low(across), low(down), bins.astype(np.float32)


def coefficients(tile_ids, beam_rows, shifts):
    across = N // A
    offsets = jnp.arange(G, dtype=jnp.int32)
    spot_y = (tile_ids // across)[:, None] * A + A // 2 + offsets[None, :]
    spot_x = (tile_ids % across)[:, None] * A + A // 2 + 2 * offsets[None, :]
    wave_y = jnp.remainder(F * beam_rows[:, 0], N)[:, None, None]
    wave_x = jnp.remainder(F * beam_rows[:, 1], N)[:, None, None]
    windings = (wave_y * spot_y[None] % N + wave_x * spot_x[None] % N) % N
    phases = shifts[:, None, None] + 2.0 * math.pi / N * windings.astype(F32)
    return jnp.stack([jnp.cos(phases), -jnp.sin(phases)])


def tile_weights(tile_ids, beam_row, k1_pairs):
    across = N // A
    ty = tile_ids // across - beam_row[0]
    tx = tile_ids % across - beam_row[1]
    k1y = jnp.arange(A, dtype=jnp.int32)
    k1x = k1_pairs[:, None] + jnp.arange(2, dtype=jnp.int32)[None, :]
    winding = (
        k1y[None, None, None, :] * ty[None, :, None, None]
        + (k1x.T[:, None, :] * tx[None, :, None])[..., None]
    )
    angle = 2.0 * math.pi / A * (winding % A).astype(F32)
    cos, sin = jnp.cos(angle), jnp.sin(angle)
    upper = jnp.stack([cos, -sin], axis=3)
    under = jnp.stack([sin, cos], axis=3)
    both = jnp.stack([upper, under]).astype(BF)
    return both.reshape(4 * tile_ids.shape[0], k1_pairs.shape[0] * 2 * A)


def plane_waves(beam_index):
    by = jnp.arange(HALF, dtype=jnp.int32)[:, None] + HALF * (jnp.arange(LANES) // A)[None, :]
    bx = jnp.broadcast_to((jnp.arange(LANES, dtype=jnp.int32) % A)[None, :], by.shape)
    row_y = beam_index[:, 0][:, None, None]
    row_x = beam_index[:, 1][:, None, None]
    winding = (row_y * by[None] + row_x * bx[None] + HALF * (row_y + row_x)) % A
    angle = 2.0 * math.pi / A * winding.astype(F32)
    return jnp.stack([jnp.cos(angle), jnp.sin(angle)], axis=1)


def shards(pot_first, pot_second, beam_index, aberration, tile_table, tile_count):
    field_count = lax.axis_size("beam")
    hold_count = lax.axis_size("slab")
    field_pos = lax.axis_index("beam")
    hold_pos = lax.axis_index("slab")
    band_rows = pot_first.shape[0]
    band_tiles = band_rows // A
    width_k = A // field_count
    sheets = width_k // 2
    across = N // A
    beam_total = beam_index.shape[0]
    share = hold_pos % sheets

    section_x = np.stack(
        [
            section_forward(
                np.array(
                    [width_k * p + 2 * t + ks for p in range(field_count) for ks in range(2)]
                )
            )
            for t in range(sheets)
        ]
    )
    last_x = np.stack(
        [
            np.stack(
                [
                    last_forward_x([width_k * p + 2 * t, width_k * p + 2 * t + 1])
                    for p in range(field_count)
                ]
            )
            for t in range(sheets)
        ]
    )
    section_y = section_forward(np.arange(A))
    last_y = np.stack([last_forward_y([2 * q, 2 * q + 1]) for q in range(PAIRS)])
    inverse_y = np.stack([first_inverse_y([2 * q, 2 * q + 1]) for q in range(PAIRS)])
    inverse_x = np.stack(
        [
            np.stack(
                [
                    first_inverse_x([width_k * p + 2 * t, width_k * p + 2 * t + 1])
                    for t in range(sheets)
                ]
            )
            for p in range(field_count)
        ]
    )

    blocks_dev = tile_table.shape[0] // (field_count * hold_count)
    slot_count = tile_table.shape[1]
    own_slots = blocks_dev * slot_count
    table = tile_table.reshape(field_count, hold_count, own_slots)

    def trade(value, axis):
        return lax.all_to_all(value, axis, split_axis=0, concat_axis=0, tiled=True)

    sel = share.reshape(1).astype(jnp.int32)
    received = []
    for part in range(PARTS):
        lines = trade(forward_x(sel, pot_first, section_x, last_x, field_count, part), "beam")
        if lines.shape[3] != LANES:
            ratio = LANES // lines.shape[3]
            lines = lines.reshape((field_count // ratio, ratio) + lines.shape[1:])
            lines = lines.transpose(0, 2, 3, 1, 4).reshape(-1, HIGH // PARTS, ROWS, LANES)
        received.append(lines)
    earlier = forward_y_first(received[0], section_y)

    ids = lax.dynamic_index_in_dim(table, hold_pos, 1, keepdims=False).reshape(-1)
    tile_y, tile_x = ids // across, ids % across
    mine = (tile_y // band_tiles == field_pos).astype(jnp.int32)
    rows = jnp.clip(tile_y - field_pos * band_tiles, 0, band_tiles - 1)
    crops = crop(rows, tile_x // 2, tile_x % 2, mine, pot_second, earlier)
    spec = forward_y(received[1], section_y, earlier, last_y, crops)
    crops = trade(crops.reshape(field_count, own_slots, HALF, LANES), "beam")

    near = min(sheets, 2)
    far = sheets // near
    pair_ids = share ^ jnp.arange(near, dtype=jnp.int32)
    k1_pairs = field_pos * width_k + 2 * pair_ids
    rows_of = beam_index[hold_pos ^ (near * jnp.arange(far, dtype=jnp.int32))]
    weights = jnp.stack(
        [tile_weights(tile_table.reshape(-1), rows_of[f], k1_pairs) for f in range(far)]
    )
    row = np.arange(ROWS)
    base = (row // (2 * K2_COUNT)) + A * (K2_LOW + row % K2_COUNT)
    base = np.where(row < 4 * K2_COUNT, base, 0)
    freq_y = np.broadcast_to(base[:, None], (ROWS, LANES)).astype(np.float32)
    lane = np.arange(LANES)
    base = np.where(lane < 2 * K2_COUNT, lane // K2_COUNT + A * (K2_LOW + lane % K2_COUNT), N)
    freq_x = (k1_pairs[None, :] + F * rows_of[:, 1:]).reshape(far * near, 1, 1)
    freq_x = freq_x + base.astype(np.int32)
    square_x = (freq_x * freq_x).astype(F32)
    scalars = jnp.stack(
        jnp.broadcast_arrays(field_pos, pair_ids[None, :], F * rows_of[:, :1]), axis=-1
    )
    scalars = scalars.astype(jnp.int32).reshape(-1)

    shards_x = [spec]
    for x in range(1, near):
        shards_x.append(lax.ppermute(spec, "slab", [(i, i ^ x) for i in range(hold_count)]))
    passed = [[] for _ in range(PARTS)]
    last_wave = []
    for f in reversed(range(far)):
        waves = []
        for x in range(near):
            waves.append(
                inverse(
                    f * near + x,
                    scalars,
                    shards_x[x],
                    freq_y,
                    square_x,
                    inverse_y,
                    inverse_x,
                    last_wave,
                )
            )
            last_wave = waves[-1:]
        for part in range(PARTS):
            after = [crops] if f == 0 and part == 0 else []
            partial = collect(f, waves, weights, field_count, part, passed[part] * (f == 0), after)
            if f:
                swap = [(i, i ^ (f * near)) for i in range(hold_count)]
                passed[part].append(lax.ppermute(partial, "slab", swap))
                last_wave = [partial]
            else:
                passed[part] = partial
    halves = []
    for part in range(PARTS):
        total = jnp.sum(trade(passed[part], "beam").astype(F32), axis=0).astype(BF)
        halves.append(total.transpose(2, 0, 1, 3))
    tiles = trade(jnp.concatenate(halves, axis=2), "slab")
    fields = tiles.reshape(hold_count, own_slots, 2, HALF, LANES)
    crop_total = jnp.sum(crops.astype(F32), axis=0).astype(BF)

    own = lax.dynamic_index_in_dim(
        lax.dynamic_index_in_dim(table, field_pos, 0, keepdims=False), hold_pos, 0, keepdims=False
    )
    alpha = coefficients(own, beam_index, aberration).reshape(2, beam_total, own_slots * G)
    first_block = (field_pos * hold_count + hold_pos) * blocks_dev
    counts = lax.dynamic_slice_in_dim(tile_count, first_block, blocks_dev, 0)
    bins = detect_tables(beam_total)
    sums = detect(alpha, counts, fields, crop_total, plane_waves(beam_index), *bins)
    return jnp.sum(sums, axis=2).reshape(blocks_dev, slot_count, G, NDET)


def solution(mesh):
    return jax.shard_map(
        shards,
        mesh=mesh,
        in_specs=(P("beam", None), P("beam", None), P(), P(), P(), P()),
        out_specs=P(("beam", "slab"), None, None, None),
        check_vma=False,
    )
```

```python
import functools
import math

import jax
import jax.numpy as jnp
import ml_dtypes
import numpy as np
from jax import lax
from jax.experimental import pallas as pl
from jax.experimental.pallas import tpu as pltpu
from jax.sharding import PartitionSpec as P

A = 64
N = 4096
F = 64
G = 3
NDET = 16
QMAX = 3
LIMIT = N // 3
K2_LOW = -(LIMIT // A + 1 + QMAX)
K2_COUNT = 2 * (LIMIT // A + 1 + QMAX)
PART = 104
ROWS = 2 * PART
LANES = 128
SUB = 16
HIGH = A // SUB
HALF = A // 2
PAIRS = A // 2
PARTS = 2
VMEM = 60 * 1024 * 1024
PITCH = A + 1
BF = jnp.bfloat16
F32 = jnp.float32


def low(values):
    return np.asarray(values, dtype=np.float32).astype(ml_dtypes.bfloat16)


def turn(numerator, period):
    return np.exp(2j * np.pi * (numerator % period) / period)


def digits_k2():
    return K2_LOW + np.arange(K2_COUNT)


def spread(table):
    both = np.stack([table.real, table.imag])
    eye = np.eye(SUB)
    out = both[:, :, None, :, None] * eye[None, None, :, None, :]
    return low(out.reshape(2 * table.shape[0] * SUB, table.shape[1] * SUB))


def real_rows(table):
    return np.block([[table.real, -table.imag], [table.imag, table.real]])


def section_forward(k1):
    n1 = np.arange(A)
    return spread(np.conj(turn(k1[:, None] * n1[None, :], A)) / A)


def last_forward_x(k1_pair):
    n2 = np.arange(A)
    out = np.zeros((2, PART, 2, 2, A))
    for ks, k1 in enumerate(k1_pair):
        freq = k1 + A * digits_k2()
        table = np.conj(turn(freq[:, None] * n2[None, :], N)) / A
        block = real_rows(table).reshape(2, K2_COUNT, 2, A)
        out[:, ks * K2_COUNT : (ks + 1) * K2_COUNT, ks] = block
    return low(out.reshape(ROWS, 4 * A))


def last_forward_y(k1_pair):
    n2 = np.arange(A)
    out = np.zeros((ROWS, 2, 2 * A))
    for e, k1 in enumerate(k1_pair):
        freq = k1 + A * digits_k2()
        table = np.conj(turn(freq[:, None] * n2[None, :], N)) / A
        out[e * 2 * K2_COUNT : (e + 1) * 2 * K2_COUNT, e] = real_rows(table)
    return low(out.reshape(ROWS, 4 * A))


def first_inverse(k1):
    n2 = np.arange(A)
    freq = k1 + A * digits_k2()
    return turn(n2[:, None] * freq[None, :], N) * np.conj(turn(freq * freq, 2 * N))[None, :]


def first_inverse_y(k1_pair):
    out = np.zeros((2, 2 * A, ROWS))
    for e, k1 in enumerate(k1_pair):
        out[e, :, e * 2 * K2_COUNT : (e + 1) * 2 * K2_COUNT] = real_rows(first_inverse(k1))
    return low(out.reshape(4 * A, ROWS))


def first_inverse_x(k1_pair):
    out = np.zeros((LANES, 2, 2, A))
    for ks, k1 in enumerate(k1_pair):
        table = first_inverse(k1).T
        out[ks * K2_COUNT : (ks + 1) * K2_COUNT, 0, ks] = table.real
        out[ks * K2_COUNT : (ks + 1) * K2_COUNT, 1, ks] = table.imag
    return low(out.reshape(LANES, 4 * A))


def sine_cosine(x):
    u = x * x
    s = F32(SIN_FIT[-1])
    for c in SIN_FIT[-2::-1]:
        s = s * u + F32(c)
    q = F32(COS_FIT[-1])
    for c in COS_FIT[-2::-1]:
        q = q * u + F32(c)
    return s * x, q


def fit(function, degree):
    top = 3.1421**2
    nodes = 0.5 * top * (1 - np.cos(np.pi * (np.arange(64) + 0.5) / 64))
    cheb = np.polynomial.chebyshev.Chebyshev.fit(
        nodes, function(np.sqrt(nodes)), degree, domain=[0, top]
    )
    return [float(c) for c in cheb.convert(kind=np.polynomial.Polynomial).coef]


SIN_FIT = fit(lambda x: np.sinc(x / np.pi), 5)
COS_FIT = fit(np.cos, 5)


def dot(a, b):
    return jnp.dot(a, b, preferred_element_type=F32)


def cost(micros):
    return pl.CostEstimate(flops=int(micros * 1.1e9), bytes_accessed=0, transcendentals=0)


def forward_x_kernel(sel, pot, section, last, out, cos_ref, sin_ref, twisted):
    fields = out.shape[0]
    lanes = out.shape[3]
    half = section.shape[1] // 2

    def chunk(t, carry):
        block = pot[:, 0, :, pl.ds(pl.multiple_of(t * LANES, LANES), LANES)]
        values = block.reshape(lanes, LANES).T.astype(F32)
        sine, cosine = sine_cosine(values)
        cos_ref[pl.ds(2 * t, 2)] = cosine.astype(BF).reshape(2, A, lanes)
        sin_ref[pl.ds(2 * t, 2)] = sine.astype(BF).reshape(2, A, lanes)
        return carry

    lax.fori_loop(0, N // LANES, chunk, 0, unroll=4)
    table = section[0]
    for m in range(HIGH):
        span = slice(m * SUB, (m + 1) * SUB)
        part_cos = cos_ref[:, span, :].reshape(A * SUB, lanes)
        part_sin = sin_ref[:, span, :].reshape(A * SUB, lanes)
        if lanes % LANES == 0:
            both = dot(table, jnp.concatenate([part_cos, part_sin], axis=1))
            of_cos, of_sin = both[:, :lanes], both[:, lanes:]
        else:
            of_cos, of_sin = dot(table, part_cos), dot(table, part_sin)
        real = of_cos[:half] - of_sin[half:]
        imag = of_cos[half:] + of_sin[:half]
        twisted[:, m * SUB : (m + 1) * SUB, :] = real.astype(BF).reshape(2 * fields, SUB, lanes)
        twisted[:, A + m * SUB : A + (m + 1) * SUB, :] = imag.astype(BF).reshape(
            2 * fields, SUB, lanes
        )
    for d in range(fields):
        lines = twisted[2 * d : 2 * d + 2].reshape(4 * A, lanes)
        out[d, 0] = dot(last[0, d], lines).astype(BF)


def forward_x(sel, pot, section, last, fields, part):
    groups = pot.shape[0] // A
    lanes = groups * SUB
    steps = HIGH // PARTS
    return pl.pallas_call(
        forward_x_kernel,
        grid_spec=pltpu.PrefetchScalarGridSpec(
            num_scalar_prefetch=1,
            grid=(steps,),
            in_specs=[
                pl.BlockSpec((groups, 1, SUB, N), lambda i, s: (0, part * steps + i, 0, 0)),
                pl.BlockSpec((1,) + section.shape[1:], lambda i, s: (s[0], 0, 0)),
                pl.BlockSpec((1,) + last.shape[1:], lambda i, s: (s[0], 0, 0, 0)),
            ],
            out_specs=pl.BlockSpec((fields, 1, ROWS, lanes), lambda i, s: (0, i, 0, 0)),
            scratch_shapes=[
                pltpu.VMEM((A, A, lanes), BF),
                pltpu.VMEM((A, A, lanes), BF),
                pltpu.VMEM((2 * fields, 2 * A, lanes), BF),
            ],
        ),
        out_shape=jax.ShapeDtypeStruct((fields, steps, ROWS, lanes), BF),
        compiler_params=pltpu.CompilerParams(vmem_limit_bytes=VMEM),
        cost_estimate=cost(9),
        name="forward_x",
    )(sel, pot.reshape(groups, HIGH, SUB, N), section, last)


def section_step(lines, section, gathered, twisted, start):
    chunk_rows = 16 * SUB
    for g in range(lines.shape[0]):
        block = lines[g, 0].astype(F32)
        zeros = jnp.zeros((LANES - PART, LANES), F32)
        both = jnp.concatenate([block[:PART], zeros, block[PART:], zeros], axis=0)
        gathered[:, g * LANES : (g + 1) * LANES] = both.astype(BF)
    values = gathered[...]
    for c in range(A // 16):
        rows = slice(c * chunk_rows, (c + 1) * chunk_rows)
        turned = slice(A * SUB + c * chunk_rows, A * SUB + (c + 1) * chunk_rows)
        dims = (((1,), (1,)), ((), ()))
        by_cos = lax.dot_general(section[rows, :], values, dims, preferred_element_type=F32)
        by_sin = lax.dot_general(section[turned, :], values, dims, preferred_element_type=F32)
        real = by_cos[:, :LANES] - by_sin[:, LANES:]
        imag = by_cos[:, LANES:] + by_sin[:, :LANES]
        spot = slice(c * 16, (c + 1) * 16)
        twisted[spot, 0, pl.ds(start, SUB), :] = real.astype(BF).reshape(16, SUB, LANES)
        twisted[spot, 1, pl.ds(start, SUB), :] = imag.astype(BF).reshape(16, SUB, LANES)


def forward_y_first_kernel(lines, section, twisted, gathered):
    start = pl.multiple_of(pl.program_id(0) * SUB, SUB)
    section_step(lines, section, gathered, twisted, start)


def forward_y_first(lines, section):
    groups, steps = lines.shape[:2]
    return pl.pallas_call(
        forward_y_first_kernel,
        grid=(steps,),
        in_specs=[
            pl.BlockSpec((groups, 1, ROWS, LANES), lambda i: (0, i, 0, 0)),
            pl.BlockSpec(section.shape, lambda i: (0, 0)),
        ],
        out_specs=pl.BlockSpec((A, 2, A // PARTS, LANES), lambda i: (0, 0, 0, 0)),
        out_shape=jax.ShapeDtypeStruct((A, 2, A // PARTS, LANES), BF),
        scratch_shapes=[pltpu.VMEM((2 * LANES, A * SUB), BF)],
        compiler_params=pltpu.CompilerParams(vmem_limit_bytes=VMEM),
        cost_estimate=cost(7),
        name="forward_y_first",
    )(lines, section)


def forward_y_kernel(steps, lines, section, earlier, last, after, out, gathered, twisted):
    step = pl.program_id(0)
    first = HIGH // PARTS

    @pl.when(step < first)
    def _():
        start = pl.multiple_of(step * SUB, SUB)
        section_step(lines, section, gathered, twisted, start)

    @pl.when(step >= first)
    def _():
        count = PAIRS // steps
        base = (step - first) * count
        for q in range(count):
            rows = []
            for e in range(2):
                for part in range(2):
                    rows.append(earlier[2 * (base + q) + e, part])
                    rows.append(twisted[2 * (base + q) + e, part])
            out[q] = dot(last[q], jnp.concatenate(rows, axis=0)).astype(BF)


def forward_y(lines, section, earlier, last, after):
    groups, first = lines.shape[:2]
    steps = 2
    count = PAIRS // steps

    def late(i):
        return (jnp.maximum(i - first, 0), 0, 0)

    return pl.pallas_call(
        functools.partial(forward_y_kernel, steps),
        grid=(first + steps,),
        in_specs=[
            pl.BlockSpec(
                (groups, 1, ROWS, LANES), lambda i: (0, jnp.minimum(i, first - 1), 0, 0)
            ),
            pl.BlockSpec(section.shape, lambda i: (0, 0)),
            pl.BlockSpec(earlier.shape, lambda i: (0, 0, 0, 0)),
            pl.BlockSpec((count, ROWS, 4 * A), late),
            pl.BlockSpec(memory_space=pl.ANY),
        ],
        out_specs=pl.BlockSpec((count, ROWS, LANES), late),
        out_shape=jax.ShapeDtypeStruct((PAIRS, ROWS, LANES), BF),
        scratch_shapes=[
            pltpu.VMEM((2 * LANES, A * SUB), BF),
            pltpu.VMEM((A, 2, A // PARTS, LANES), BF),
        ],
        compiler_params=pltpu.CompilerParams(vmem_limit_bytes=VMEM),
        cost_estimate=cost(10),
        name="forward_y",
    )(lines, section, earlier, last, after)


def order_kernel(value, after, out):
    pass


def order(value, after):
    return pl.pallas_call(
        order_kernel,
        in_specs=[pl.BlockSpec(memory_space=pl.ANY)] * 2,
        out_specs=pl.BlockSpec(memory_space=pl.ANY),
        out_shape=jax.ShapeDtypeStruct(value.shape, value.dtype),
        input_output_aliases={0: 0},
        name="order",
    )(value, after)


def inverse_kernel(steps, which, sel, spec, freq_y, square_x, table_y, table_x, *rest):
    out, mid = rest[-2:]
    step = pl.program_id(0)
    count = PAIRS // steps
    each = HALF // steps
    limit = F32(LIMIT * LIMIT)

    @pl.when(step < steps)
    def _():
        def pair(q, carry):
            pair_id = step * count + q
            offset = (2 * pair_id + sel[3 * which + 2]).astype(F32)
            row_freq = freq_y[...] + offset
            inside = row_freq * row_freq + square_x[0] <= limit
            values = jnp.where(inside, spec[q].astype(F32), 0.0).astype(BF)
            mixed = dot(table_y[q], values)
            for e in range(2):
                for part in range(2):
                    rows = slice((2 * e + part) * A, (2 * e + part + 1) * A)
                    spot = part * A * PITCH + 2 * pair_id + e
                    mid[pl.ds(spot, A, stride=PITCH), :] = mixed[rows]
            return carry

        lax.fori_loop(0, count, pair, 0, unroll=4)

    @pl.when(step >= steps)
    def _():
        def line(i, carry):
            by = (step - steps) * each + i
            rows = []
            for b in range(2):
                for part in range(2):
                    start = part * A * PITCH + (by + b * HALF) * PITCH
                    rows.append(mid[pl.ds(start, A), :].astype(BF))
            product = dot(jnp.concatenate(rows, axis=0), table_x[0, 0])
            for b in range(2):
                re = product[2 * b * A : (2 * b + 1) * A]
                im = product[(2 * b + 1) * A : (2 * b + 2) * A]
                span = slice(b * LANES, (b + 1) * LANES)
                out[i, :A, span] = (re[:, :LANES] - im[:, LANES:]).astype(BF)
                out[i, A:, span] = (re[:, LANES:] + im[:, :LANES]).astype(BF)
            return carry

        lax.fori_loop(0, each, line, 0, unroll=4)


def inverse(which, sel, spec, freq_y, square_x, table_y, table_x, after):
    steps = 2
    count = PAIRS // steps
    each = HALF // steps

    def early(i, s):
        return jnp.minimum(i, steps - 1)

    return pl.pallas_call(
        functools.partial(inverse_kernel, steps, which),
        grid_spec=pltpu.PrefetchScalarGridSpec(
            num_scalar_prefetch=1,
            grid=(2 * steps,),
            in_specs=[
                pl.BlockSpec((count, ROWS, LANES), lambda i, s: (early(i, s), 0, 0)),
                pl.BlockSpec((ROWS, LANES), lambda i, s: (0, 0)),
                pl.BlockSpec((1, 1, LANES), lambda i, s: (which, 0, 0)),
                pl.BlockSpec((count, 4 * A, ROWS), lambda i, s: (early(i, s), 0, 0)),
                pl.BlockSpec((1, 1) + table_x.shape[2:], lambda i, s: (s[3 * which], s[3 * which + 1], 0, 0)),
            ]
            + [pl.BlockSpec(memory_space=pl.ANY)] * len(after),
            out_specs=pl.BlockSpec(
                (each, 2 * A, 2 * LANES), lambda i, s: (jnp.maximum(i - steps, 0), 0, 0)
            ),
            scratch_shapes=[pltpu.VMEM((2 * A * PITCH, LANES), F32)],
        ),
        out_shape=jax.ShapeDtypeStruct((HALF, 2 * A, 2 * LANES), BF),
        compiler_params=pltpu.CompilerParams(vmem_limit_bytes=VMEM),
        cost_estimate=cost(3),
        name="inverse",
    )(sel, spec, freq_y, square_x, table_y, table_x, *after)


def collect_kernel(near, added, *refs):
    sheets, weights = refs[:near], refs[near]
    out, held = refs[-2:]
    devices, _, slots, lines, _ = out.shape
    tiles = devices * slots
    pitch = lines + 1
    lane = lax.broadcasted_iota(jnp.int32, (tiles, LANES), 1)
    lower = lane < A

    def line(i, carry):
        stacked = sheets[0][i]
        if near > 1:
            stacked = jnp.concatenate([sheet[i] for sheet in sheets], axis=0)
        sums = dot(weights[0], stacked)
        for part in range(2):
            even = sums[2 * part * tiles : (2 * part + 1) * tiles]
            odd = sums[(2 * part + 1) * tiles : (2 * part + 2) * tiles]
            keep = jnp.where(lower, even[:, :LANES], odd[:, LANES:])
            move = jnp.where(lower, even[:, LANES:], odd[:, :LANES])
            total = keep + pltpu.roll(move, A, 1)
            held[pl.ds(part * tiles * pitch + i, tiles, stride=pitch), :] = total
        return carry

    lax.fori_loop(0, lines, line, 0, unroll=4)

    def device(d, carry):
        for part in range(2):
            for slot in range(slots):
                start = (part * tiles + d * slots + slot) * pitch
                total = held[pl.ds(start, lines), :]
                for a in range(added):
                    total = total + refs[near + 1 + a][d, part, slot].astype(F32)
                out[d, part, slot] = total.astype(BF)
        return carry

    lax.fori_loop(0, devices, device, 0, unroll=4)


def collect(which, sheets, weights, devices, part, added):
    near = len(sheets)
    tiles = weights.shape[1] // 4
    lines = HALF // PARTS
    shape = (devices, 2, tiles // devices, lines, LANES)
    sheet_spec = pl.BlockSpec((lines, 2 * A, 2 * LANES), lambda i: (part, 0, 0))
    block = pl.BlockSpec(shape, lambda i: (0, 0, 0, 0, 0))
    return pl.pallas_call(
        functools.partial(collect_kernel, near, len(added)),
        grid=(1,),
        in_specs=[sheet_spec] * near
        + [pl.BlockSpec((1,) + weights.shape[1:], lambda i: (which, 0, 0))]
        + [block] * len(added),
        out_specs=block,
        out_shape=jax.ShapeDtypeStruct(shape, BF),
        scratch_shapes=[pltpu.VMEM((2 * tiles * (lines + 1), LANES), F32)],
        compiler_params=pltpu.CompilerParams(vmem_limit_bytes=VMEM),
        cost_estimate=cost(1.5),
        name="collect",
    )(*sheets, weights, *added)


def crop_kernel(rows, cols, odd, mine, pot, after, out, held, sems):
    slots = out.shape[0]

    def copy(i):
        return pltpu.make_async_copy(
            pot.at[
                pl.ds(pl.multiple_of(rows[i] * A, A), A),
                pl.ds(pl.multiple_of(cols[i] * LANES, LANES), LANES),
            ],
            held.at[i],
            sems.at[i],
        )

    def begin(i, carry):
        copy(i).start()
        return carry

    def finish(i, carry):
        copy(i).wait()
        block = held[i].astype(F32)
        block = jnp.where(odd[i] == 1, pltpu.roll(block, A, 1), block)
        lane = lax.broadcasted_iota(jnp.int32, (HALF, LANES), 1)
        packed = jnp.where(lane < A, block[:HALF], pltpu.roll(block[HALF:], A, 1))
        out[i] = jnp.where(mine[i] == 1, packed, 0.0).astype(BF)
        return carry

    lax.fori_loop(0, slots, begin, 0)
    lax.fori_loop(0, slots, finish, 0)


def crop(rows, cols, odd, mine, pot, after):
    slots = rows.shape[0]
    return pl.pallas_call(
        crop_kernel,
        in_specs=[pl.BlockSpec(memory_space=pltpu.SMEM)] * 4
        + [pl.BlockSpec(memory_space=pl.ANY)] * 2,
        out_specs=pl.BlockSpec(memory_space=pltpu.VMEM),
        out_shape=jax.ShapeDtypeStruct((slots, HALF, LANES), BF),
        scratch_shapes=[pltpu.VMEM((slots, A, LANES), BF), pltpu.SemaphoreType.DMA((slots,))],
        compiler_params=pltpu.CompilerParams(vmem_limit_bytes=VMEM),
        cost_estimate=cost(7),
        name="crop",
    )(rows, cols, odd, mine, pot, after)


def detect_kernel(parts, alpha, counts, *refs):
    fields = refs[:parts]
    pot, plane, across, down, bins, out, lines, held = refs[parts:]
    beams, _, slots = fields[0].shape[:3]
    for s in range(slots):
        waves = []
        for j in range(beams):
            re, im = (
                jnp.concatenate([half[j, part, s] for half in fields], axis=0).astype(F32)
                for part in range(2)
            )
            cos, sin = plane[j, 0], plane[j, 1]
            waves.append((re * cos - im * sin, re * sin + im * cos))
        turned, level = sine_cosine(pot[s].astype(F32))
        for g in range(G):
            real = jnp.zeros((HALF, LANES), F32)
            imag = jnp.zeros((HALF, LANES), F32)
            for j in range(beams):
                cos, sin = alpha[0, j, s * G + g], alpha[1, j, s * G + g]
                re, im = waves[j]
                real = real + cos * re - sin * im
                imag = imag + cos * im + sin * re
            lines[2 * (s * G + g)] = (real * level - imag * turned).astype(BF)
            lines[2 * (s * G + g) + 1] = (real * turned + imag * level).astype(BF)
    total = slots * G
    first = dot(lines[...].reshape(2 * total * HALF, LANES), across[...])
    first = first.reshape(total, 2, HALF, 2 * LANES)
    real = (first[:, 0, :, :LANES] + first[:, 1, :, LANES:]).astype(BF)
    imag = (first[:, 1, :, :LANES] - first[:, 0, :, LANES:]).astype(BF)
    lane = lax.broadcasted_iota(jnp.int32, (A, LANES), 1)
    for i in range(total):
        both = jnp.concatenate([real[i], imag[i]], axis=1)
        mixed = dot(down[...], both)
        even, odd = mixed[: 2 * A], mixed[2 * A :]
        re_cos = even[:A, :LANES] + pltpu.roll(odd[:A, :LANES], A, 1)
        re_sin = even[A:, :LANES] + pltpu.roll(odd[A:, :LANES], A, 1)
        im_cos = even[:A, LANES:] + pltpu.roll(odd[:A, LANES:], A, 1)
        im_sin = even[A:, LANES:] + pltpu.roll(odd[A:, LANES:], A, 1)
        re = re_cos + im_sin
        im = im_cos - re_sin
        power = jnp.where(lane < A, re * re + im * im, 0.0)
        sums = jnp.sum(power[None] * bins[...], axis=1)
        block, slot = divmod(i // G, slots // counts.shape[0])
        active = slot < counts[block]
        held[i * NDET : (i + 1) * NDET, :] = jnp.where(active, sums, 0.0)
    out[...] = jnp.sum(held[...].T, axis=0, keepdims=True)


def detect(alpha, counts, fields, pot, plane, across, down, bins):
    slots = fields[0].shape[2]
    rows = -(-slots * G * NDET // LANES) * LANES
    smem = pl.BlockSpec(memory_space=pltpu.SMEM)
    vmem = pl.BlockSpec(memory_space=pltpu.VMEM)
    return pl.pallas_call(
        functools.partial(detect_kernel, len(fields)),
        in_specs=[smem, smem] + [vmem] * (5 + len(fields)),
        out_specs=vmem,
        out_shape=jax.ShapeDtypeStruct((1, rows), F32),
        scratch_shapes=[
            pltpu.VMEM((2 * slots * G, HALF, LANES), BF),
            pltpu.VMEM((rows, LANES), F32),
        ],
        compiler_params=pltpu.CompilerParams(vmem_limit_bytes=VMEM),
        name="detect",
    )(alpha, counts, *fields, pot, plane, across, down, bins)


def detect_tables(beam_total):
    n = np.arange(A)
    table = turn(n[:, None] * n[None, :], A) / A
    cos, sin = table.real, table.imag
    zero = np.zeros((A, A))
    across = np.block([[cos, zero, sin, zero], [zero, cos, zero, sin]])
    rows = np.concatenate([cos, sin], axis=0)
    down = np.concatenate([rows[:, :HALF], rows[:, HALF:]], axis=0)
    signed = np.where(n < A // 2, n, n - A)
    radius = signed[:, None] ** 2 + signed[None, :] ** 2
    width = A // (2 * NDET)
    bins = np.zeros((NDET, A, LANES))
    for d in range(NDET):
        member = (radius >= (width * d) ** 2) & (radius < (width * (d + 1)) ** 2)
        bins[d, :, :A] = member * (A * A / (beam_total * member.sum()))
    return low(across), low(down), bins.astype(np.float32)


def coefficients(tile_ids, beam_rows, shifts):
    across = N // A
    offsets = jnp.arange(G, dtype=jnp.int32)
    spot_y = (tile_ids // across)[:, None] * A + A // 2 + offsets[None, :]
    spot_x = (tile_ids % across)[:, None] * A + A // 2 + 2 * offsets[None, :]
    wave_y = jnp.remainder(F * beam_rows[:, 0], N)[:, None, None]
    wave_x = jnp.remainder(F * beam_rows[:, 1], N)[:, None, None]
    windings = (wave_y * spot_y[None] % N + wave_x * spot_x[None] % N) % N
    phases = shifts[:, None, None] + 2.0 * math.pi / N * windings.astype(F32)
    return jnp.stack([jnp.cos(phases), -jnp.sin(phases)])


def tile_weights(tile_ids, beam_row, k1_pairs):
    across = N // A
    ty = tile_ids // across - beam_row[0]
    tx = tile_ids % across - beam_row[1]
    k1y = jnp.arange(A, dtype=jnp.int32)
    k1x = k1_pairs[:, None] + jnp.arange(2, dtype=jnp.int32)[None, :]
    winding = (
        k1y[None, None, None, :] * ty[None, :, None, None]
        + (k1x.T[:, None, :] * tx[None, :, None])[..., None]
    )
    angle = 2.0 * math.pi / A * (winding % A).astype(F32)
    cos, sin = jnp.cos(angle), jnp.sin(angle)
    upper = jnp.stack([cos, -sin], axis=3)
    under = jnp.stack([sin, cos], axis=3)
    both = jnp.stack([upper, under]).astype(BF)
    return both.reshape(4 * tile_ids.shape[0], k1_pairs.shape[0] * 2 * A)


def plane_waves(beam_index):
    by = jnp.arange(HALF, dtype=jnp.int32)[:, None] + HALF * (jnp.arange(LANES) // A)[None, :]
    bx = jnp.broadcast_to((jnp.arange(LANES, dtype=jnp.int32) % A)[None, :], by.shape)
    row_y = beam_index[:, 0][:, None, None]
    row_x = beam_index[:, 1][:, None, None]
    winding = (row_y * by[None] + row_x * bx[None] + HALF * (row_y + row_x)) % A
    angle = 2.0 * math.pi / A * winding.astype(F32)
    return jnp.stack([jnp.cos(angle), jnp.sin(angle)], axis=1)


def shards(pot_first, pot_second, beam_index, aberration, tile_table, tile_count):
    field_count = lax.axis_size("beam")
    hold_count = lax.axis_size("slab")
    field_pos = lax.axis_index("beam")
    hold_pos = lax.axis_index("slab")
    band_rows = pot_first.shape[0]
    band_tiles = band_rows // A
    width_k = A // field_count
    sheets = width_k // 2
    across = N // A
    beam_total = beam_index.shape[0]
    share = hold_pos % sheets

    section_x = np.stack(
        [
            section_forward(
                np.array(
                    [width_k * p + 2 * t + ks for p in range(field_count) for ks in range(2)]
                )
            )
            for t in range(sheets)
        ]
    )
    last_x = np.stack(
        [
            np.stack(
                [
                    last_forward_x([width_k * p + 2 * t, width_k * p + 2 * t + 1])
                    for p in range(field_count)
                ]
            )
            for t in range(sheets)
        ]
    )
    section_y = section_forward(np.arange(A))
    last_y = np.stack([last_forward_y([2 * q, 2 * q + 1]) for q in range(PAIRS)])
    inverse_y = np.stack([first_inverse_y([2 * q, 2 * q + 1]) for q in range(PAIRS)])
    inverse_x = np.stack(
        [
            np.stack(
                [
                    first_inverse_x([width_k * p + 2 * t, width_k * p + 2 * t + 1])
                    for t in range(sheets)
                ]
            )
            for p in range(field_count)
        ]
    )

    blocks_dev = tile_table.shape[0] // (field_count * hold_count)
    slot_count = tile_table.shape[1]
    own_slots = blocks_dev * slot_count
    table = tile_table.reshape(field_count, hold_count, own_slots)

    def trade(value, axis):
        return lax.all_to_all(value, axis, split_axis=0, concat_axis=0, tiled=True)

    sel = share.reshape(1).astype(jnp.int32)
    received = []
    for part in range(PARTS):
        lines = trade(forward_x(sel, pot_first, section_x, last_x, field_count, part), "beam")
        if lines.shape[3] != LANES:
            ratio = LANES // lines.shape[3]
            lines = lines.reshape((field_count // ratio, ratio) + lines.shape[1:])
            lines = lines.transpose(0, 2, 3, 1, 4).reshape(-1, HIGH // PARTS, ROWS, LANES)
        received.append(lines)
    earlier = forward_y_first(received[0], section_y)

    ids = lax.dynamic_index_in_dim(table, hold_pos, 1, keepdims=False).reshape(-1)
    tile_y, tile_x = ids // across, ids % across
    mine = (tile_y // band_tiles == field_pos).astype(jnp.int32)
    rows = jnp.clip(tile_y - field_pos * band_tiles, 0, band_tiles - 1)
    crops = crop(rows, tile_x // 2, tile_x % 2, mine, pot_second, earlier)
    spec = forward_y(received[1], section_y, earlier, last_y, crops)
    crops = crops.reshape(field_count, own_slots, HALF, LANES)

    near = min(sheets, 2)
    far = sheets // near
    pair_ids = share ^ jnp.arange(near, dtype=jnp.int32)
    k1_pairs = field_pos * width_k + 2 * pair_ids
    rows_of = beam_index[hold_pos ^ (near * jnp.arange(far, dtype=jnp.int32))]
    weights = jnp.stack(
        [tile_weights(tile_table.reshape(-1), rows_of[f], k1_pairs) for f in range(far)]
    )
    row = np.arange(ROWS)
    base = (row // (2 * K2_COUNT)) + A * (K2_LOW + row % K2_COUNT)
    base = np.where(row < 4 * K2_COUNT, base, 0)
    freq_y = np.broadcast_to(base[:, None], (ROWS, LANES)).astype(np.float32)
    lane = np.arange(LANES)
    base = np.where(lane < 2 * K2_COUNT, lane // K2_COUNT + A * (K2_LOW + lane % K2_COUNT), N)
    freq_x = (k1_pairs[None, :] + F * rows_of[:, 1:]).reshape(far * near, 1, 1)
    freq_x = freq_x + base.astype(np.int32)
    square_x = (freq_x * freq_x).astype(F32)
    scalars = jnp.stack(
        jnp.broadcast_arrays(field_pos, pair_ids[None, :], F * rows_of[:, :1]), axis=-1
    )
    scalars = scalars.astype(jnp.int32).reshape(-1)

    shards_x = [spec]
    for x in range(1, near):
        shards_x.append(lax.ppermute(spec, "slab", [(i, i ^ x) for i in range(hold_count)]))
    passed = [[] for _ in range(PARTS)]
    last_wave = []
    for f in reversed(range(far)):
        waves = []
        for x in range(near):
            waves.append(
                inverse(
                    f * near + x,
                    scalars,
                    shards_x[x],
                    freq_y,
                    square_x,
                    inverse_y,
                    inverse_x,
                    last_wave,
                )
            )
            last_wave = waves[-1:]
        for part in range(PARTS):
            partial = collect(
                f, waves, weights, field_count * hold_count, part, passed[part] * (f == 0)
            )
            if f:
                swap = [(i, i ^ (f * near)) for i in range(hold_count)]
                passed[part].append(lax.ppermute(partial, "slab", swap))
                last_wave = [partial]
            else:
                passed[part] = partial
        if f:
            crops = order(crops, last_wave[0])
    crops = trade(crops, "beam")
    fields = []
    for part in range(PARTS):
        tiles = trade(passed[part], ("beam", "slab"))
        tiles = tiles.reshape((field_count, hold_count) + tiles.shape[1:]).astype(F32)
        fields.append(jnp.sum(tiles, axis=0).astype(BF))
    crop_total = jnp.sum(crops.astype(F32), axis=0).astype(BF)

    own = lax.dynamic_index_in_dim(
        lax.dynamic_index_in_dim(table, field_pos, 0, keepdims=False), hold_pos, 0, keepdims=False
    )
    alpha = coefficients(own, beam_index, aberration).reshape(2, beam_total, own_slots * G)
    first_block = (field_pos * hold_count + hold_pos) * blocks_dev
    counts = lax.dynamic_slice_in_dim(tile_count, first_block, blocks_dev, 0)
    bins = detect_tables(beam_total)
    sums = detect(alpha, counts, fields, crop_total, plane_waves(beam_index), *bins)
    return sums[0, : own_slots * G * NDET].reshape(blocks_dev, slot_count, G, NDET)


def solution(mesh):
    return jax.shard_map(
        shards,
        mesh=mesh,
        in_specs=(P("beam", None), P("beam", None), P(), P(), P(), P()),
        out_specs=P(("beam", "slab"), None, None, None),
        check_vma=False,
    )
```

```python
import functools
import math

import jax
import jax.numpy as jnp
import ml_dtypes
import numpy as np
from jax import lax
from jax.experimental import pallas as pl
from jax.experimental.pallas import tpu as pltpu
from jax.sharding import PartitionSpec as P

A = 64
N = 4096
F = 64
G = 3
NDET = 16
QMAX = 3
LIMIT = N // 3
K2_LOW = -(LIMIT // A + 1 + QMAX)
K2_COUNT = 2 * (LIMIT // A + 1 + QMAX)
PART = 104
ROWS = 2 * PART
LANES = 128
SUB = 16
HIGH = A // SUB
HALF = A // 2
PAIRS = A // 2
PARTS = 2
BLOCKS = 4
VMEM = 60 * 1024 * 1024
PITCH = A + 1
BF = jnp.bfloat16
F32 = jnp.float32


def low(values):
    return np.asarray(values, dtype=np.float32).astype(ml_dtypes.bfloat16)


def turn(numerator, period):
    return np.exp(2j * np.pi * (numerator % period) / period)


def digits_k2():
    return K2_LOW + np.arange(K2_COUNT)


def spread(table):
    both = np.stack([table.real, table.imag])
    eye = np.eye(SUB)
    out = both[:, :, None, :, None] * eye[None, None, :, None, :]
    return low(out.reshape(2 * table.shape[0] * SUB, table.shape[1] * SUB))


def real_rows(table):
    return np.block([[table.real, -table.imag], [table.imag, table.real]])


def section_forward(k1):
    n1 = np.arange(A)
    return spread(np.conj(turn(k1[:, None] * n1[None, :], A)) / A)


def last_forward_x(k1_pair):
    n2 = np.arange(A)
    out = np.zeros((2, PART, 2, 2, A))
    for ks, k1 in enumerate(k1_pair):
        freq = k1 + A * digits_k2()
        table = np.conj(turn(freq[:, None] * n2[None, :], N)) / A
        block = real_rows(table).reshape(2, K2_COUNT, 2, A)
        out[:, ks * K2_COUNT : (ks + 1) * K2_COUNT, ks] = block
    return low(out.reshape(ROWS, 4 * A))


def last_forward_y(k1_pair):
    n2 = np.arange(A)
    out = np.zeros((ROWS, 2, 2 * A))
    for e, k1 in enumerate(k1_pair):
        freq = k1 + A * digits_k2()
        table = np.conj(turn(freq[:, None] * n2[None, :], N)) / A
        out[e * PART : e * PART + 2 * K2_COUNT, e] = real_rows(table)
    return low(out.reshape(ROWS, 4 * A))


def first_inverse(k1):
    n2 = np.arange(A)
    freq = k1 + A * digits_k2()
    return turn(n2[:, None] * freq[None, :], N) * np.conj(turn(freq * freq, 2 * N))[None, :]


def first_inverse_y(k1_pair):
    out = np.zeros((2, 2 * A, PART))
    for e, k1 in enumerate(k1_pair):
        out[e, :, : 2 * K2_COUNT] = real_rows(first_inverse(k1))
    return low(out)


def first_inverse_x(k1_pair):
    out = np.zeros((LANES, 2, 2, A))
    for ks, k1 in enumerate(k1_pair):
        table = first_inverse(k1).T
        out[ks * K2_COUNT : (ks + 1) * K2_COUNT, 0, ks] = table.real
        out[ks * K2_COUNT : (ks + 1) * K2_COUNT, 1, ks] = table.imag
    return low(out.reshape(LANES, 4 * A))


def sine_cosine(x):
    u = x * x
    s = F32(SIN_FIT[-1])
    for c in SIN_FIT[-2::-1]:
        s = s * u + F32(c)
    q = F32(COS_FIT[-1])
    for c in COS_FIT[-2::-1]:
        q = q * u + F32(c)
    return s * x, q


def fit(function, degree):
    top = 3.1421**2
    nodes = 0.5 * top * (1 - np.cos(np.pi * (np.arange(64) + 0.5) / 64))
    cheb = np.polynomial.chebyshev.Chebyshev.fit(
        nodes, function(np.sqrt(nodes)), degree, domain=[0, top]
    )
    return [float(c) for c in cheb.convert(kind=np.polynomial.Polynomial).coef]


SIN_FIT = fit(lambda x: np.sinc(x / np.pi), 5)
COS_FIT = fit(np.cos, 5)


def dot(a, b):
    return jnp.dot(a, b, preferred_element_type=F32)


def cost(micros):
    return pl.CostEstimate(flops=int(micros * 1.1e9), bytes_accessed=0, transcendentals=0)


def forward_x_kernel(sel, pot, section, last, out, cos_ref, sin_ref, twisted):
    fields = out.shape[0]
    lanes = out.shape[3]
    half = section.shape[1] // 2

    def chunk(t, carry):
        block = pot[:, 0, :, pl.ds(pl.multiple_of(t * LANES, LANES), LANES)]
        values = block.reshape(lanes, LANES).T.astype(F32)
        sine, cosine = sine_cosine(values)
        cos_ref[pl.ds(2 * t, 2)] = cosine.astype(BF).reshape(2, A, lanes)
        sin_ref[pl.ds(2 * t, 2)] = sine.astype(BF).reshape(2, A, lanes)
        return carry

    lax.fori_loop(0, N // LANES, chunk, 0, unroll=4)
    table = section[0]
    for m in range(HIGH):
        span = slice(m * SUB, (m + 1) * SUB)
        part_cos = cos_ref[:, span, :].reshape(A * SUB, lanes)
        part_sin = sin_ref[:, span, :].reshape(A * SUB, lanes)
        if lanes % LANES == 0:
            both = dot(table, jnp.concatenate([part_cos, part_sin], axis=1))
            of_cos, of_sin = both[:, :lanes], both[:, lanes:]
        else:
            of_cos, of_sin = dot(table, part_cos), dot(table, part_sin)
        real = of_cos[:half] - of_sin[half:]
        imag = of_cos[half:] + of_sin[:half]
        twisted[:, m * SUB : (m + 1) * SUB, :] = real.astype(BF).reshape(2 * fields, SUB, lanes)
        twisted[:, A + m * SUB : A + (m + 1) * SUB, :] = imag.astype(BF).reshape(
            2 * fields, SUB, lanes
        )
    for d in range(fields):
        lines = twisted[2 * d : 2 * d + 2].reshape(4 * A, lanes)
        out[d, 0] = dot(last[0, d], lines).astype(BF)


def forward_x(sel, pot, section, last, fields, part):
    groups = pot.shape[0] // A
    lanes = groups * SUB
    steps = HIGH // PARTS
    return pl.pallas_call(
        forward_x_kernel,
        grid_spec=pltpu.PrefetchScalarGridSpec(
            num_scalar_prefetch=1,
            grid=(steps,),
            in_specs=[
                pl.BlockSpec((groups, 1, SUB, N), lambda i, s: (0, part * steps + i, 0, 0)),
                pl.BlockSpec((1,) + section.shape[1:], lambda i, s: (s[0], 0, 0)),
                pl.BlockSpec((1,) + last.shape[1:], lambda i, s: (s[0], 0, 0, 0)),
            ],
            out_specs=pl.BlockSpec((fields, 1, ROWS, lanes), lambda i, s: (0, i, 0, 0)),
            scratch_shapes=[
                pltpu.VMEM((A, A, lanes), BF),
                pltpu.VMEM((A, A, lanes), BF),
                pltpu.VMEM((2 * fields, 2 * A, lanes), BF),
            ],
        ),
        out_shape=jax.ShapeDtypeStruct((fields, steps, ROWS, lanes), BF),
        compiler_params=pltpu.CompilerParams(vmem_limit_bytes=VMEM),
        cost_estimate=cost(9),
        name="forward_x",
    )(sel, pot.reshape(groups, HIGH, SUB, N), section, last)


def gather_lines(lines, gathered):
    steps = lines.shape[1]
    zeros = jnp.zeros((LANES - PART, LANES), F32)
    for g in range(lines.shape[0]):
        for h in range(steps):
            block = lines[g, h].astype(F32)
            both = jnp.concatenate([block[:PART], zeros, block[PART:], zeros], axis=0)
            rows = slice(2 * h * LANES, 2 * (h + 1) * LANES)
            gathered[rows, g * LANES : (g + 1) * LANES] = both.astype(BF)


def section_step(steps, section, gathered, twisted):
    count = section.shape[1] // SUB
    dims = (((1,), (1,)), ((), ()))
    values = gathered[...]
    by_cos = lax.dot_general(section[0], values, dims, preferred_element_type=F32)
    by_sin = lax.dot_general(section[1], values, dims, preferred_element_type=F32)
    for h in range(steps):
        re = slice(2 * h * LANES, (2 * h + 1) * LANES)
        im = slice((2 * h + 1) * LANES, (2 * h + 2) * LANES)
        real = by_cos[:, re] - by_sin[:, im]
        imag = by_cos[:, im] + by_sin[:, re]
        span = slice(h * SUB, (h + 1) * SUB)
        yield span, real.astype(BF).reshape(count, SUB, LANES), imag.astype(BF).reshape(
            count, SUB, LANES
        )


def forward_y_first_kernel(lines, section, twisted, gathered):
    @pl.when(pl.program_id(0) == 0)
    def _():
        gather_lines(lines, gathered)

    for span, real, imag in section_step(lines.shape[1], section, gathered, twisted):
        twisted[:, 0, span, :] = real
        twisted[:, 1, span, :] = imag


def forward_y_first(lines, section):
    steps = lines.shape[1]
    count = A // BLOCKS
    return pl.pallas_call(
        forward_y_first_kernel,
        grid=(BLOCKS,),
        in_specs=[
            pl.BlockSpec(lines.shape, lambda i: (0, 0, 0, 0)),
            pl.BlockSpec((2, count * SUB, A * SUB), lambda i: (0, i, 0)),
        ],
        out_specs=pl.BlockSpec((count, 2, A // PARTS, LANES), lambda i: (i, 0, 0, 0)),
        out_shape=jax.ShapeDtypeStruct((A, 2, A // PARTS, LANES), BF),
        scratch_shapes=[pltpu.VMEM((2 * steps * LANES, A * SUB), BF)],
        compiler_params=pltpu.CompilerParams(vmem_limit_bytes=VMEM),
        cost_estimate=cost(6),
        name="forward_y_first",
    )(lines, section)


def forward_y_kernel(lines, section, earlier, last, *rest):
    out, gathered, twisted = rest[-3:]
    step = pl.program_id(0)

    @pl.when(step == 0)
    def _():
        gather_lines(lines, gathered)

    @pl.when(step < BLOCKS)
    def _():
        count = A // BLOCKS
        spot = pl.ds(step * count, count)
        for span, real, imag in section_step(lines.shape[1], section, gathered, twisted):
            twisted[spot, 0, span, :] = real
            twisted[spot, 1, span, :] = imag

    @pl.when(step >= BLOCKS)
    def _():
        count = out.shape[0]
        base = (step - BLOCKS) * count
        for q in range(count):
            rows = []
            for e in range(2):
                for part in range(2):
                    rows.append(earlier[2 * (base + q) + e, part])
                    rows.append(twisted[2 * (base + q) + e, part])
            out[q] = dot(last[q], jnp.concatenate(rows, axis=0)).astype(BF)


def forward_y(lines, section, earlier, last, after):
    steps = 2
    count = PAIRS // steps

    def late(i):
        return (jnp.maximum(i - BLOCKS, 0), 0, 0)

    return pl.pallas_call(
        forward_y_kernel,
        grid=(BLOCKS + steps,),
        in_specs=[
            pl.BlockSpec(lines.shape, lambda i: (0, 0, 0, 0)),
            pl.BlockSpec(
                (2, A // BLOCKS * SUB, A * SUB), lambda i: (0, jnp.minimum(i, BLOCKS - 1), 0)
            ),
            pl.BlockSpec(earlier.shape, lambda i: (0, 0, 0, 0)),
            pl.BlockSpec((count, ROWS, 4 * A), late),
        ]
        + [pl.BlockSpec(memory_space=pl.ANY)] * len(after),
        out_specs=pl.BlockSpec((count, ROWS, LANES), late),
        out_shape=jax.ShapeDtypeStruct((PAIRS, ROWS, LANES), BF),
        scratch_shapes=[
            pltpu.VMEM((2 * lines.shape[1] * LANES, A * SUB), BF),
            pltpu.VMEM((A, 2, A // PARTS, LANES), BF),
        ],
        compiler_params=pltpu.CompilerParams(vmem_limit_bytes=VMEM),
        cost_estimate=cost(8),
        name="forward_y",
    )(lines, section, earlier, last, *after)


def order_kernel(value, *rest):
    pass


def order(value, after):
    return pl.pallas_call(
        order_kernel,
        in_specs=[pl.BlockSpec(memory_space=pl.ANY)] * (1 + len(after)),
        out_specs=pl.BlockSpec(memory_space=pl.ANY),
        out_shape=jax.ShapeDtypeStruct(value.shape, value.dtype),
        input_output_aliases={0: 0},
        name="order",
    )(value, *after)


def inverse_kernel(steps, which, near, sel, *refs):
    specs = refs[:near]
    freq_y, square_x, table_y = refs[near : near + 3]
    tables_x = refs[near + 3 : 2 * near + 3]
    out, mid = refs[-2:]
    step = pl.program_id(0)
    count = PAIRS // steps
    each = HALF // steps
    limit = F32(LIMIT * LIMIT)
    whole = 2 * A * PITCH

    @pl.when(step < steps)
    def _():
        def pair(q, carry):
            pair_id = step * count + q
            offset = (2 * pair_id + sel[3 * which + 2]).astype(F32)
            row_freq = freq_y[...] + offset
            row_square = row_freq * row_freq
            values = []
            for x in range(near):
                inside = row_square + square_x[x] <= limit
                values.append(jnp.where(inside, specs[x][q].astype(F32), 0.0))
            for e in range(2):
                half = [v[e * PART : (e + 1) * PART].astype(BF) for v in values]
                half = half[0] if near == 1 else jnp.concatenate(half, axis=1)
                mixed = dot(table_y[q, e], half)
                for x in range(near):
                    for part in range(2):
                        spot = x * whole + part * A * PITCH + 2 * pair_id + e
                        mid[pl.ds(spot, A, stride=PITCH), :] = mixed[
                            part * A : (part + 1) * A, x * LANES : (x + 1) * LANES
                        ]
            return carry

        lax.fori_loop(0, count, pair, 0, unroll=4)

    @pl.when(step >= steps)
    def _():
        def line(i, carry):
            by = (step - steps) * each + i
            for x in range(near):
                rows = []
                for b in range(2):
                    for part in range(2):
                        start = x * whole + part * A * PITCH + (by + b * HALF) * PITCH
                        rows.append(mid[pl.ds(start, A), :].astype(BF))
                product = dot(jnp.concatenate(rows, axis=0), tables_x[x][0, 0])
                low_row = 2 * A * x
                for b in range(2):
                    re = product[2 * b * A : (2 * b + 1) * A]
                    im = product[(2 * b + 1) * A : (2 * b + 2) * A]
                    span = slice(b * LANES, (b + 1) * LANES)
                    real = re[:, :LANES] - im[:, LANES:]
                    imag = re[:, LANES:] + im[:, :LANES]
                    out[i, low_row : low_row + A, span] = real.astype(BF)
                    out[i, low_row + A : low_row + 2 * A, span] = imag.astype(BF)
            return carry

        lax.fori_loop(0, each, line, 0, unroll=4)


def inverse(which, sel, specs, freq_y, square_x, table_y, table_x, after):
    near = len(specs)
    steps = 2
    count = PAIRS // steps
    each = HALF // steps

    def early(i, s):
        return jnp.minimum(i, steps - 1)

    def table_spec(x):
        return pl.BlockSpec(
            (1, 1) + table_x.shape[2:],
            lambda i, s: (s[3 * (which + x)], s[3 * (which + x) + 1], 0, 0),
        )

    return pl.pallas_call(
        functools.partial(inverse_kernel, steps, which, near),
        grid_spec=pltpu.PrefetchScalarGridSpec(
            num_scalar_prefetch=1,
            grid=(2 * steps,),
            in_specs=[pl.BlockSpec((count, ROWS, LANES), lambda i, s: (early(i, s), 0, 0))] * near
            + [
                pl.BlockSpec((ROWS, LANES), lambda i, s: (0, 0)),
                pl.BlockSpec((near, 1, LANES), lambda i, s: (which // near, 0, 0)),
                pl.BlockSpec((count, 2, 2 * A, PART), lambda i, s: (early(i, s), 0, 0, 0)),
            ]
            + [table_spec(x) for x in range(near)]
            + [pl.BlockSpec(memory_space=pl.ANY)] * len(after),
            out_specs=pl.BlockSpec(
                (each, 2 * A * near, 2 * LANES), lambda i, s: (jnp.maximum(i - steps, 0), 0, 0)
            ),
            scratch_shapes=[pltpu.VMEM((near * 2 * A * PITCH, LANES), F32)],
        ),
        out_shape=jax.ShapeDtypeStruct((HALF, 2 * A * near, 2 * LANES), BF),
        compiler_params=pltpu.CompilerParams(vmem_limit_bytes=VMEM),
        cost_estimate=cost(6),
        name="inverse",
    )(sel, *specs, freq_y, square_x, table_y, *[table_x] * near, *after)


def collect_kernel(*refs):
    *sheets, weights, out, held = refs
    devices, _, slots, lines, _ = out.shape
    tiles = devices * slots
    pitch = lines + 1
    lane = lax.broadcasted_iota(jnp.int32, (tiles, LANES), 1)
    lower = lane < A

    def line(i, carry):
        stacked = sheets[0][i]
        if len(sheets) > 1:
            stacked = jnp.concatenate([sheet[i] for sheet in sheets], axis=0)
        sums = dot(weights[...], stacked)
        for part in range(2):
            even = sums[2 * part * tiles : (2 * part + 1) * tiles]
            odd = sums[(2 * part + 1) * tiles : (2 * part + 2) * tiles]
            keep = jnp.where(lower, even[:, :LANES], odd[:, LANES:])
            move = jnp.where(lower, even[:, LANES:], odd[:, :LANES])
            total = keep + pltpu.roll(move, A, 1)
            held[pl.ds(part * tiles * pitch + i, tiles, stride=pitch), :] = total
        return carry

    lax.fori_loop(0, lines, line, 0, unroll=4)

    def device(d, carry):
        for part in range(2):
            for slot in range(slots):
                start = (part * tiles + d * slots + slot) * pitch
                total = held[pl.ds(start, lines), :]
                out[d, part, slot] = total.astype(BF)
        return carry

    lax.fori_loop(0, devices, device, 0, unroll=4)


def collect(sheets, weights, devices, part):
    tiles = weights.shape[0] // 4
    lines = HALF // PARTS
    shape = (devices, 2, tiles // devices, lines, LANES)
    sheet_spec = pl.BlockSpec((lines,) + sheets[0].shape[1:], lambda i: (part, 0, 0))
    block = pl.BlockSpec(shape, lambda i: (0, 0, 0, 0, 0))
    return pl.pallas_call(
        collect_kernel,
        grid=(1,),
        in_specs=[sheet_spec] * len(sheets) + [pl.BlockSpec(weights.shape, lambda i: (0, 0))],
        out_specs=block,
        out_shape=jax.ShapeDtypeStruct(shape, BF),
        scratch_shapes=[pltpu.VMEM((2 * tiles * (lines + 1), LANES), F32)],
        compiler_params=pltpu.CompilerParams(vmem_limit_bytes=VMEM),
        cost_estimate=cost(1.5),
        name="collect",
    )(*sheets, weights)


def crop_kernel(rows, cols, odd, mine, pot, after, out, held, sems):
    slots = out.shape[0]

    def copy(i):
        return pltpu.make_async_copy(
            pot.at[
                pl.ds(pl.multiple_of(rows[i] * A, A), A),
                pl.ds(pl.multiple_of(cols[i] * LANES, LANES), LANES),
            ],
            held.at[i],
            sems.at[i],
        )

    def begin(i, carry):
        copy(i).start()
        return carry

    def finish(i, carry):
        copy(i).wait()
        block = held[i].astype(F32)
        block = jnp.where(odd[i] == 1, pltpu.roll(block, A, 1), block)
        lane = lax.broadcasted_iota(jnp.int32, (HALF, LANES), 1)
        packed = jnp.where(lane < A, block[:HALF], pltpu.roll(block[HALF:], A, 1))
        out[i] = jnp.where(mine[i] == 1, packed, 0.0).astype(BF)
        return carry

    lax.fori_loop(0, slots, begin, 0)
    lax.fori_loop(0, slots, finish, 0)


def crop(rows, cols, odd, mine, pot, after):
    slots = rows.shape[0]
    return pl.pallas_call(
        crop_kernel,
        in_specs=[pl.BlockSpec(memory_space=pltpu.SMEM)] * 4
        + [pl.BlockSpec(memory_space=pl.ANY)] * 2,
        out_specs=pl.BlockSpec(memory_space=pltpu.VMEM),
        out_shape=jax.ShapeDtypeStruct((slots, HALF, LANES), BF),
        scratch_shapes=[pltpu.VMEM((slots, A, LANES), BF), pltpu.SemaphoreType.DMA((slots,))],
        compiler_params=pltpu.CompilerParams(vmem_limit_bytes=VMEM),
        cost_estimate=cost(7),
        name="crop",
    )(rows, cols, odd, mine, pot, after)


def detect_kernel(parts, alpha, counts, *refs):
    fields = refs[:parts]
    pot, plane, across, down, bins, out, lines, held = refs[parts:]
    beams, _, slots = fields[0].shape[:3]
    for s in range(slots):
        waves = []
        for j in range(beams):
            re, im = (
                jnp.concatenate([half[j, part, s] for half in fields], axis=0).astype(F32)
                for part in range(2)
            )
            cos, sin = plane[j, 0], plane[j, 1]
            waves.append((re * cos - im * sin, re * sin + im * cos))
        turned, level = sine_cosine(pot[s].astype(F32))
        for g in range(G):
            real = jnp.zeros((HALF, LANES), F32)
            imag = jnp.zeros((HALF, LANES), F32)
            for j in range(beams):
                cos, sin = alpha[0, j, s * G + g], alpha[1, j, s * G + g]
                re, im = waves[j]
                real = real + cos * re - sin * im
                imag = imag + cos * im + sin * re
            lines[2 * (s * G + g)] = (real * level - imag * turned).astype(BF)
            lines[2 * (s * G + g) + 1] = (real * turned + imag * level).astype(BF)
    total = slots * G
    first = dot(lines[...].reshape(2 * total * HALF, LANES), across[...])
    first = first.reshape(total, 2, HALF, 2 * LANES)
    real = (first[:, 0, :, :LANES] + first[:, 1, :, LANES:]).astype(BF)
    imag = (first[:, 1, :, :LANES] - first[:, 0, :, LANES:]).astype(BF)
    lane = lax.broadcasted_iota(jnp.int32, (A, LANES), 1)
    for i in range(total):
        both = jnp.concatenate([real[i], imag[i]], axis=1)
        mixed = dot(down[...], both)
        even, odd = mixed[: 2 * A], mixed[2 * A :]
        re_cos = even[:A, :LANES] + pltpu.roll(odd[:A, :LANES], A, 1)
        re_sin = even[A:, :LANES] + pltpu.roll(odd[A:, :LANES], A, 1)
        im_cos = even[:A, LANES:] + pltpu.roll(odd[:A, LANES:], A, 1)
        im_sin = even[A:, LANES:] + pltpu.roll(odd[A:, LANES:], A, 1)
        re = re_cos + im_sin
        im = im_cos - re_sin
        power = jnp.where(lane < A, re * re + im * im, 0.0)
        sums = jnp.sum(power[None] * bins[...], axis=1)
        block, slot = divmod(i // G, slots // counts.shape[0])
        active = slot < counts[block]
        held[i * NDET : (i + 1) * NDET, :] = jnp.where(active, sums, 0.0)
    out[...] = jnp.sum(held[...].T, axis=0, keepdims=True)


def detect(alpha, counts, fields, pot, plane, across, down, bins):
    slots = fields[0].shape[2]
    rows = -(-slots * G * NDET // LANES) * LANES
    smem = pl.BlockSpec(memory_space=pltpu.SMEM)
    vmem = pl.BlockSpec(memory_space=pltpu.VMEM)
    return pl.pallas_call(
        functools.partial(detect_kernel, len(fields)),
        in_specs=[smem, smem] + [vmem] * (5 + len(fields)),
        out_specs=vmem,
        out_shape=jax.ShapeDtypeStruct((1, rows), F32),
        scratch_shapes=[
            pltpu.VMEM((2 * slots * G, HALF, LANES), BF),
            pltpu.VMEM((rows, LANES), F32),
        ],
        compiler_params=pltpu.CompilerParams(vmem_limit_bytes=VMEM),
        name="detect",
    )(alpha, counts, *fields, pot, plane, across, down, bins)


def detect_tables(beam_total):
    n = np.arange(A)
    table = turn(n[:, None] * n[None, :], A) / A
    cos, sin = table.real, table.imag
    zero = np.zeros((A, A))
    across = np.block([[cos, zero, sin, zero], [zero, cos, zero, sin]])
    rows = np.concatenate([cos, sin], axis=0)
    down = np.concatenate([rows[:, :HALF], rows[:, HALF:]], axis=0)
    signed = np.where(n < A // 2, n, n - A)
    radius = signed[:, None] ** 2 + signed[None, :] ** 2
    width = A // (2 * NDET)
    bins = np.zeros((NDET, A, LANES))
    for d in range(NDET):
        member = (radius >= (width * d) ** 2) & (radius < (width * (d + 1)) ** 2)
        bins[d, :, :A] = member * (A * A / (beam_total * member.sum()))
    return low(across), low(down), bins.astype(np.float32)


def coefficients(tile_ids, beam_rows, shifts):
    across = N // A
    offsets = jnp.arange(G, dtype=jnp.int32)
    spot_y = (tile_ids // across)[:, None] * A + A // 2 + offsets[None, :]
    spot_x = (tile_ids % across)[:, None] * A + A // 2 + 2 * offsets[None, :]
    wave_y = jnp.remainder(F * beam_rows[:, 0], N)[:, None, None]
    wave_x = jnp.remainder(F * beam_rows[:, 1], N)[:, None, None]
    windings = (wave_y * spot_y[None] % N + wave_x * spot_x[None] % N) % N
    phases = shifts[:, None, None] + 2.0 * math.pi / N * windings.astype(F32)
    return jnp.stack([jnp.cos(phases), -jnp.sin(phases)])


def tile_weights(tile_ids, beam_row, k1_pairs):
    across = N // A
    ty = tile_ids // across - beam_row[0]
    tx = tile_ids % across - beam_row[1]
    k1y = jnp.arange(A, dtype=jnp.int32)
    k1x = k1_pairs[:, None] + jnp.arange(2, dtype=jnp.int32)[None, :]
    winding = (
        k1y[None, None, None, :] * ty[None, :, None, None]
        + (k1x.T[:, None, :] * tx[None, :, None])[..., None]
    )
    angle = 2.0 * math.pi / A * (winding % A).astype(F32)
    cos, sin = jnp.cos(angle), jnp.sin(angle)
    upper = jnp.stack([cos, -sin], axis=3)
    under = jnp.stack([sin, cos], axis=3)
    both = jnp.stack([upper, under]).astype(BF)
    return both.reshape(4 * tile_ids.shape[0], k1_pairs.shape[0] * 2 * A)


def plane_waves(beam_index):
    by = jnp.arange(HALF, dtype=jnp.int32)[:, None] + HALF * (jnp.arange(LANES) // A)[None, :]
    bx = jnp.broadcast_to((jnp.arange(LANES, dtype=jnp.int32) % A)[None, :], by.shape)
    row_y = beam_index[:, 0][:, None, None]
    row_x = beam_index[:, 1][:, None, None]
    winding = (row_y * by[None] + row_x * bx[None] + HALF * (row_y + row_x)) % A
    angle = 2.0 * math.pi / A * winding.astype(F32)
    return jnp.stack([jnp.cos(angle), jnp.sin(angle)], axis=1)


def shards(pot_first, pot_second, beam_index, aberration, tile_table, tile_count):
    field_count = lax.axis_size("beam")
    hold_count = lax.axis_size("slab")
    field_pos = lax.axis_index("beam")
    hold_pos = lax.axis_index("slab")
    band_rows = pot_first.shape[0]
    band_tiles = band_rows // A
    width_k = A // field_count
    sheets = width_k // 2
    across = N // A
    beam_total = beam_index.shape[0]
    share = hold_pos % sheets

    section_x = np.stack(
        [
            section_forward(
                np.array(
                    [width_k * p + 2 * t + ks for p in range(field_count) for ks in range(2)]
                )
            )
            for t in range(sheets)
        ]
    )
    last_x = np.stack(
        [
            np.stack(
                [
                    last_forward_x([width_k * p + 2 * t, width_k * p + 2 * t + 1])
                    for p in range(field_count)
                ]
            )
            for t in range(sheets)
        ]
    )
    section_y = section_forward(np.arange(A)).reshape(2, A * SUB, A * SUB)
    last_y = np.stack([last_forward_y([2 * q, 2 * q + 1]) for q in range(PAIRS)])
    inverse_y = np.stack([first_inverse_y([2 * q, 2 * q + 1]) for q in range(PAIRS)])
    inverse_x = np.stack(
        [
            np.stack(
                [
                    first_inverse_x([width_k * p + 2 * t, width_k * p + 2 * t + 1])
                    for t in range(sheets)
                ]
            )
            for p in range(field_count)
        ]
    )

    blocks_dev = tile_table.shape[0] // (field_count * hold_count)
    slot_count = tile_table.shape[1]
    own_slots = blocks_dev * slot_count
    table = tile_table.reshape(field_count, hold_count, own_slots)

    def trade(value, axis):
        return lax.all_to_all(value, axis, split_axis=0, concat_axis=0, tiled=True)

    near = min(sheets, 2)
    far = sheets // near

    def swap(value, x):
        return lax.ppermute(value, "slab", [(i, i ^ x) for i in range(hold_count)])

    ids = lax.dynamic_index_in_dim(table, hold_pos, 1, keepdims=False).reshape(-1)
    tile_y, tile_x = ids // across, ids % across
    mine = (tile_y // band_tiles == field_pos).astype(jnp.int32)
    rows = jnp.clip(tile_y - field_pos * band_tiles, 0, band_tiles - 1)

    beam_row = lax.dynamic_index_in_dim(beam_index, hold_pos, 0, keepdims=False)
    pair_ids = share ^ jnp.arange(sheets, dtype=jnp.int32)
    k1_pairs = field_pos * width_k + 2 * pair_ids
    weights = tile_weights(tile_table.reshape(-1), beam_row, k1_pairs)
    row = np.arange(ROWS)
    base = row // PART + A * (K2_LOW + row % PART % K2_COUNT)
    freq_y = np.broadcast_to(base[:, None], (ROWS, LANES)).astype(np.float32)
    lane = np.arange(LANES)
    base = np.where(lane < 2 * K2_COUNT, lane // K2_COUNT + A * (K2_LOW + lane % K2_COUNT), N)
    freq_x = (k1_pairs + F * beam_row[1])[:, None, None] + base.astype(np.int32)
    square_x = (freq_x * freq_x).astype(F32)
    scalars = jnp.stack(
        jnp.broadcast_arrays(field_pos, pair_ids, F * beam_row[0]), axis=-1
    )
    scalars = scalars.astype(jnp.int32).reshape(-1)

    sel = share.reshape(1).astype(jnp.int32)
    received = [[] for _ in range(far)]
    earlier = []
    for part in range(PARTS):
        lines = trade(forward_x(sel, pot_first, section_x, last_x, field_count, part), "beam")
        if lines.shape[3] != LANES:
            ratio = LANES // lines.shape[3]
            lines = lines.reshape((field_count // ratio, ratio) + lines.shape[1:])
            lines = lines.transpose(0, 2, 3, 1, 4).reshape(-1, HIGH // PARTS, ROWS, LANES)
        if part:
            crops = crop(rows, tile_x // 2, tile_x % 2, mine, pot_second, earlier[0])
            lines = order(lines, [crops, weights, square_x])
        for f in range(far):
            received[f].append(swap(lines, f * near) if f else lines)
        if part == 0:
            earlier = [forward_y_first(received[f][0], section_y) for f in range(far)]
    crops = lax.psum_scatter(
        crops.reshape(field_count, own_slots * HALF, LANES), "beam", scatter_dimension=0
    ).reshape(own_slots, HALF, LANES)

    waves = []
    ready = []
    token = []
    for f in range(far):
        spec = forward_y(received[f][1], section_y, earlier[f], last_y, token + earlier[1:])
        ready.append([spec] + [swap(spec, x) for x in range(1, near)])
        token = [spec]
    for f in range(far):
        waves.append(
            inverse(
                f * near, scalars, ready[f], freq_y, square_x, inverse_y, inverse_x, token
            )
        )
        token = waves[-1:]
    fields = []
    for part in range(PARTS):
        tiles = collect(waves, weights, field_count * hold_count, part)
        tiles = trade(tiles, ("beam", "slab"))
        tiles = tiles.reshape((field_count, hold_count) + tiles.shape[1:]).astype(F32)
        fields.append(jnp.sum(tiles, axis=0).astype(BF))

    own = lax.dynamic_index_in_dim(
        lax.dynamic_index_in_dim(table, field_pos, 0, keepdims=False), hold_pos, 0, keepdims=False
    )
    alpha = coefficients(own, beam_index, aberration).reshape(2, beam_total, own_slots * G)
    first_block = (field_pos * hold_count + hold_pos) * blocks_dev
    counts = lax.dynamic_slice_in_dim(tile_count, first_block, blocks_dev, 0)
    bins = detect_tables(beam_total)
    sums = detect(alpha, counts, fields, crops, plane_waves(beam_index), *bins)
    return sums[0, : own_slots * G * NDET].reshape(blocks_dev, slot_count, G, NDET)


def solution(mesh):
    return jax.shard_map(
        shards,
        mesh=mesh,
        in_specs=(P("beam", None), P("beam", None), P(), P(), P(), P()),
        out_specs=P(("beam", "slab"), None, None, None),
        check_vma=False,
    )
```

```python
import functools
import math

import jax
import jax.numpy as jnp
import ml_dtypes
import numpy as np
from jax import lax
from jax.experimental import pallas as pl
from jax.experimental.pallas import tpu as pltpu
from jax.sharding import PartitionSpec as P

A = 64
N = 4096
F = 64
G = 3
NDET = 16
QMAX = 3
LIMIT = N // 3
K2_LOW = -(LIMIT // A + 1 + QMAX)
K2_COUNT = 2 * (LIMIT // A + 1 + QMAX)
PART = 104
ROWS = 2 * PART
LANES = 128
SUB = 16
HIGH = A // SUB
HALF = A // 2
PAIRS = A // 2
PARTS = 2
BLOCKS = 4
VMEM = 60 * 1024 * 1024
PITCH = A + 1
BF = jnp.bfloat16
F32 = jnp.float32


def low(values):
    return np.asarray(values, dtype=np.float32).astype(ml_dtypes.bfloat16)


def turn(numerator, period):
    return np.exp(2j * np.pi * (numerator % period) / period)


def digits_k2():
    return K2_LOW + np.arange(K2_COUNT)


def spread(table):
    both = np.stack([table.real, table.imag])
    eye = np.eye(SUB)
    out = both[:, :, None, :, None] * eye[None, None, :, None, :]
    return low(out.reshape(2 * table.shape[0] * SUB, table.shape[1] * SUB))


def real_rows(table):
    return np.block([[table.real, -table.imag], [table.imag, table.real]])


def section_forward(k1):
    n1 = np.arange(A)
    return spread(np.conj(turn(k1[:, None] * n1[None, :], A)) / A)


def last_forward_x(k1_pair):
    n2 = np.arange(A)
    out = np.zeros((2, PART, 2, 2, A))
    for ks, k1 in enumerate(k1_pair):
        freq = k1 + A * digits_k2()
        table = np.conj(turn(freq[:, None] * n2[None, :], N)) / A
        block = real_rows(table).reshape(2, K2_COUNT, 2, A)
        out[:, ks * K2_COUNT : (ks + 1) * K2_COUNT, ks] = block
    return low(out.reshape(ROWS, 4 * A))


def last_forward_y(k1_pair):
    n2 = np.arange(A)
    out = np.zeros((ROWS, 2, 2 * A))
    for e, k1 in enumerate(k1_pair):
        freq = k1 + A * digits_k2()
        table = np.conj(turn(freq[:, None] * n2[None, :], N)) / A
        out[e * PART : e * PART + 2 * K2_COUNT, e] = real_rows(table)
    return low(out.reshape(ROWS, 4 * A))


def first_inverse(k1):
    n2 = np.arange(A)
    freq = k1 + A * digits_k2()
    return turn(n2[:, None] * freq[None, :], N) * np.conj(turn(freq * freq, 2 * N))[None, :]


def first_inverse_y(k1_pair):
    out = np.zeros((2, 2 * A, PART))
    for e, k1 in enumerate(k1_pair):
        out[e, :, : 2 * K2_COUNT] = real_rows(first_inverse(k1))
    return low(out)


def first_inverse_x(k1_pair):
    out = np.zeros((LANES, 2, 2, A))
    for ks, k1 in enumerate(k1_pair):
        table = first_inverse(k1).T
        out[ks * K2_COUNT : (ks + 1) * K2_COUNT, 0, ks] = table.real
        out[ks * K2_COUNT : (ks + 1) * K2_COUNT, 1, ks] = table.imag
    return low(out.reshape(LANES, 4 * A))


def sine_cosine(x):
    u = x * x
    s = F32(SIN_FIT[-1])
    for c in SIN_FIT[-2::-1]:
        s = s * u + F32(c)
    q = F32(COS_FIT[-1])
    for c in COS_FIT[-2::-1]:
        q = q * u + F32(c)
    return s * x, q


def fit(function, degree):
    top = 3.1421**2
    nodes = 0.5 * top * (1 - np.cos(np.pi * (np.arange(64) + 0.5) / 64))
    cheb = np.polynomial.chebyshev.Chebyshev.fit(
        nodes, function(np.sqrt(nodes)), degree, domain=[0, top]
    )
    return [float(c) for c in cheb.convert(kind=np.polynomial.Polynomial).coef]


SIN_FIT = fit(lambda x: np.sinc(x / np.pi), 5)
COS_FIT = fit(np.cos, 5)


def dot(a, b):
    return jnp.dot(a, b, preferred_element_type=F32)


def cost(micros):
    return pl.CostEstimate(flops=int(micros * 1.1e9), bytes_accessed=0, transcendentals=0)


def forward_x_kernel(sel, pot, section, last, out, cos_ref, sin_ref, twisted):
    fields = out.shape[0]
    lanes = out.shape[3]
    half = section.shape[1] // 2

    def chunk(t, carry):
        block = pot[:, 0, :, pl.ds(pl.multiple_of(t * LANES, LANES), LANES)]
        values = block.reshape(lanes, LANES).T.astype(F32)
        sine, cosine = sine_cosine(values)
        cos_ref[pl.ds(2 * t, 2)] = cosine.astype(BF).reshape(2, A, lanes)
        sin_ref[pl.ds(2 * t, 2)] = sine.astype(BF).reshape(2, A, lanes)
        return carry

    lax.fori_loop(0, N // LANES, chunk, 0, unroll=4)
    table = section[0]
    for m in range(HIGH):
        span = slice(m * SUB, (m + 1) * SUB)
        part_cos = cos_ref[:, span, :].reshape(A * SUB, lanes)
        part_sin = sin_ref[:, span, :].reshape(A * SUB, lanes)
        if lanes % LANES == 0:
            both = dot(table, jnp.concatenate([part_cos, part_sin], axis=1))
            of_cos, of_sin = both[:, :lanes], both[:, lanes:]
        else:
            of_cos, of_sin = dot(table, part_cos), dot(table, part_sin)
        real = of_cos[:half] - of_sin[half:]
        imag = of_cos[half:] + of_sin[:half]
        twisted[:, m * SUB : (m + 1) * SUB, :] = real.astype(BF).reshape(2 * fields, SUB, lanes)
        twisted[:, A + m * SUB : A + (m + 1) * SUB, :] = imag.astype(BF).reshape(
            2 * fields, SUB, lanes
        )
    for d in range(fields):
        lines = twisted[2 * d : 2 * d + 2].reshape(4 * A, lanes)
        out[d, 0] = dot(last[0, d], lines).astype(BF)


def forward_x(sel, pot, section, last, fields, part):
    groups = pot.shape[0] // A
    lanes = groups * SUB
    steps = HIGH // PARTS
    return pl.pallas_call(
        forward_x_kernel,
        grid_spec=pltpu.PrefetchScalarGridSpec(
            num_scalar_prefetch=1,
            grid=(steps,),
            in_specs=[
                pl.BlockSpec((groups, 1, SUB, N), lambda i, s: (0, part * steps + i, 0, 0)),
                pl.BlockSpec((1,) + section.shape[1:], lambda i, s: (s[0], 0, 0)),
                pl.BlockSpec((1,) + last.shape[1:], lambda i, s: (s[0], 0, 0, 0)),
            ],
            out_specs=pl.BlockSpec((fields, 1, ROWS, lanes), lambda i, s: (0, i, 0, 0)),
            scratch_shapes=[
                pltpu.VMEM((A, A, lanes), BF),
                pltpu.VMEM((A, A, lanes), BF),
                pltpu.VMEM((2 * fields, 2 * A, lanes), BF),
            ],
        ),
        out_shape=jax.ShapeDtypeStruct((fields, steps, ROWS, lanes), BF),
        compiler_params=pltpu.CompilerParams(vmem_limit_bytes=VMEM),
        cost_estimate=cost(9),
        name="forward_x",
    )(sel, pot.reshape(groups, HIGH, SUB, N), section, last)


def gather_lines(lines, gathered):
    steps = lines.shape[1]
    zeros = jnp.zeros((LANES - PART, LANES), F32)
    for g in range(lines.shape[0]):
        for h in range(steps):
            block = lines[g, h].astype(F32)
            both = jnp.concatenate([block[:PART], zeros, block[PART:], zeros], axis=0)
            columns = slice(2 * h * LANES, 2 * (h + 1) * LANES)
            gathered[g * LANES : (g + 1) * LANES, columns] = both.astype(BF).T


def section_step(steps, section, gathered):
    rows = section.shape[1]
    both = dot(section[...].reshape(2 * rows, section.shape[2]), gathered[...])
    for h in range(steps):
        re = slice(2 * h * LANES, (2 * h + 1) * LANES)
        im = slice((2 * h + 1) * LANES, (2 * h + 2) * LANES)
        real = both[:rows, re] - both[rows:, im]
        imag = both[:rows, im] + both[rows:, re]
        shape = (rows // SUB, SUB, LANES)
        span = slice(h * SUB, (h + 1) * SUB)
        yield span, real.astype(BF).reshape(shape), imag.astype(BF).reshape(shape)


def forward_y_first_kernel(lines, section, twisted, gathered):
    @pl.when(pl.program_id(0) == 0)
    def _():
        gather_lines(lines, gathered)

    for span, real, imag in section_step(lines.shape[1], section, gathered):
        twisted[:, 0, span, :] = real
        twisted[:, 1, span, :] = imag


def forward_y_first(lines, section):
    steps = lines.shape[1]
    count = A // BLOCKS
    return pl.pallas_call(
        forward_y_first_kernel,
        grid=(BLOCKS,),
        in_specs=[
            pl.BlockSpec(lines.shape, lambda i: (0, 0, 0, 0)),
            pl.BlockSpec((2, count * SUB, A * SUB), lambda i: (0, i, 0)),
        ],
        out_specs=pl.BlockSpec((count, 2, A // PARTS, LANES), lambda i: (i, 0, 0, 0)),
        out_shape=jax.ShapeDtypeStruct((A, 2, A // PARTS, LANES), BF),
        scratch_shapes=[pltpu.VMEM((A * SUB, 2 * steps * LANES), BF)],
        compiler_params=pltpu.CompilerParams(vmem_limit_bytes=VMEM),
        cost_estimate=cost(6),
        name="forward_y_first",
    )(lines, section)


def forward_y_kernel(lines, section, earlier, last, *rest):
    out, gathered, twisted = rest[-3:]
    step = pl.program_id(0)

    @pl.when(step == 0)
    def _():
        gather_lines(lines, gathered)

    @pl.when(step < BLOCKS)
    def _():
        count = A // BLOCKS
        spot = pl.ds(step * count, count)
        for span, real, imag in section_step(lines.shape[1], section, gathered):
            twisted[spot, 0, span, :] = real
            twisted[spot, 1, span, :] = imag

    @pl.when(step >= BLOCKS)
    def _():
        count = out.shape[0]
        base = (step - BLOCKS) * count
        for q in range(count):
            rows = []
            for e in range(2):
                for part in range(2):
                    rows.append(earlier[2 * (base + q) + e, part])
                    rows.append(twisted[2 * (base + q) + e, part])
            out[q] = dot(last[q], jnp.concatenate(rows, axis=0)).astype(BF)


def forward_y(lines, section, earlier, last, after):
    steps = 2
    count = PAIRS // steps

    def late(i):
        return (jnp.maximum(i - BLOCKS, 0), 0, 0)

    return pl.pallas_call(
        forward_y_kernel,
        grid=(BLOCKS + steps,),
        in_specs=[
            pl.BlockSpec(lines.shape, lambda i: (0, 0, 0, 0)),
            pl.BlockSpec(
                (2, A // BLOCKS * SUB, A * SUB), lambda i: (0, jnp.minimum(i, BLOCKS - 1), 0)
            ),
            pl.BlockSpec(earlier.shape, lambda i: (0, 0, 0, 0)),
            pl.BlockSpec((count, ROWS, 4 * A), late),
        ]
        + [pl.BlockSpec(memory_space=pl.ANY)] * len(after),
        out_specs=pl.BlockSpec((count, ROWS, LANES), late),
        out_shape=jax.ShapeDtypeStruct((PAIRS, ROWS, LANES), BF),
        scratch_shapes=[
            pltpu.VMEM((A * SUB, 2 * lines.shape[1] * LANES), BF),
            pltpu.VMEM((A, 2, A // PARTS, LANES), BF),
        ],
        compiler_params=pltpu.CompilerParams(vmem_limit_bytes=VMEM),
        cost_estimate=cost(8),
        name="forward_y",
    )(lines, section, earlier, last, *after)


def order_kernel(value, *rest):
    pass


def order(value, after):
    return pl.pallas_call(
        order_kernel,
        in_specs=[pl.BlockSpec(memory_space=pl.ANY)] * (1 + len(after)),
        out_specs=pl.BlockSpec(memory_space=pl.ANY),
        out_shape=jax.ShapeDtypeStruct(value.shape, value.dtype),
        input_output_aliases={0: 0},
        name="order",
    )(value, *after)


def inverse_kernel(steps, which, near, sel, *refs):
    specs = refs[:near]
    freq_y, square_x, table_y = refs[near : near + 3]
    tables_x = refs[near + 3 : 2 * near + 3]
    out, mid = refs[-2:]
    step = pl.program_id(0)
    count = PAIRS // steps
    each = HALF // steps
    limit = F32(LIMIT * LIMIT)
    whole = 2 * A * PITCH

    @pl.when(step < steps)
    def _():
        def pair(q, carry):
            pair_id = step * count + q
            offset = (2 * pair_id + sel[3 * which + 2]).astype(F32)
            row_freq = freq_y[...] + offset
            row_square = row_freq * row_freq
            values = []
            for x in range(near):
                inside = row_square + square_x[x] <= limit
                values.append(jnp.where(inside, specs[x][q].astype(F32), 0.0))
            for e in range(2):
                half = [v[e * PART : (e + 1) * PART].astype(BF) for v in values]
                half = half[0] if near == 1 else jnp.concatenate(half, axis=1)
                mixed = dot(table_y[q, e], half)
                for x in range(near):
                    for part in range(2):
                        spot = x * whole + part * A * PITCH + 2 * pair_id + e
                        mid[pl.ds(spot, A, stride=PITCH), :] = mixed[
                            part * A : (part + 1) * A, x * LANES : (x + 1) * LANES
                        ]
            return carry

        lax.fori_loop(0, count, pair, 0, unroll=4)

    @pl.when(step >= steps)
    def _():
        def line(i, carry):
            by = (step - steps) * each + i
            for x in range(near):
                rows = []
                for b in range(2):
                    for part in range(2):
                        start = x * whole + part * A * PITCH + (by + b * HALF) * PITCH
                        rows.append(mid[pl.ds(start, A), :].astype(BF))
                product = dot(jnp.concatenate(rows, axis=0), tables_x[x][0, 0])
                low_row = 2 * A * x
                for b in range(2):
                    re = product[2 * b * A : (2 * b + 1) * A]
                    im = product[(2 * b + 1) * A : (2 * b + 2) * A]
                    span = slice(b * LANES, (b + 1) * LANES)
                    real = re[:, :LANES] - im[:, LANES:]
                    imag = re[:, LANES:] + im[:, :LANES]
                    out[i, low_row : low_row + A, span] = real.astype(BF)
                    out[i, low_row + A : low_row + 2 * A, span] = imag.astype(BF)
            return carry

        lax.fori_loop(0, each, line, 0, unroll=4)


def inverse(which, sel, specs, freq_y, square_x, table_y, table_x, after):
    near = len(specs)
    steps = 2
    count = PAIRS // steps
    each = HALF // steps

    def early(i, s):
        return jnp.minimum(i, steps - 1)

    def table_spec(x):
        return pl.BlockSpec(
            (1, 1) + table_x.shape[2:],
            lambda i, s: (s[3 * (which + x)], s[3 * (which + x) + 1], 0, 0),
        )

    return pl.pallas_call(
        functools.partial(inverse_kernel, steps, which, near),
        grid_spec=pltpu.PrefetchScalarGridSpec(
            num_scalar_prefetch=1,
            grid=(2 * steps,),
            in_specs=[pl.BlockSpec((count, ROWS, LANES), lambda i, s: (early(i, s), 0, 0))] * near
            + [
                pl.BlockSpec((ROWS, LANES), lambda i, s: (0, 0)),
                pl.BlockSpec((near, 1, LANES), lambda i, s: (which // near, 0, 0)),
                pl.BlockSpec((count, 2, 2 * A, PART), lambda i, s: (early(i, s), 0, 0, 0)),
            ]
            + [table_spec(x) for x in range(near)]
            + [pl.BlockSpec(memory_space=pl.ANY)] * len(after),
            out_specs=pl.BlockSpec(
                (each, 2 * A * near, 2 * LANES), lambda i, s: (jnp.maximum(i - steps, 0), 0, 0)
            ),
            scratch_shapes=[pltpu.VMEM((near * 2 * A * PITCH, LANES), F32)],
        ),
        out_shape=jax.ShapeDtypeStruct((HALF, 2 * A * near, 2 * LANES), BF),
        compiler_params=pltpu.CompilerParams(vmem_limit_bytes=VMEM),
        cost_estimate=cost(6),
        name="inverse",
    )(sel, *specs, freq_y, square_x, table_y, *[table_x] * near, *after)


def collect_kernel(*refs):
    *sheets, weights, out, held = refs
    devices, _, slots, lines, _ = out.shape
    tiles = devices * slots
    pitch = lines + 1
    lane = lax.broadcasted_iota(jnp.int32, (tiles, LANES), 1)
    lower = lane < A

    def line(i, carry):
        stacked = sheets[0][i]
        if len(sheets) > 1:
            stacked = jnp.concatenate([sheet[i] for sheet in sheets], axis=0)
        sums = dot(weights[0], stacked)
        for part in range(2):
            even = sums[2 * part * tiles : (2 * part + 1) * tiles]
            odd = sums[(2 * part + 1) * tiles : (2 * part + 2) * tiles]
            keep = jnp.where(lower, even[:, :LANES], odd[:, LANES:])
            move = jnp.where(lower, even[:, LANES:], odd[:, :LANES])
            total = keep + pltpu.roll(move, A, 1)
            held[pl.ds(part * tiles * pitch + i, tiles, stride=pitch), :] = total
        return carry

    lax.fori_loop(0, lines, line, 0, unroll=4)

    def device(d, carry):
        for part in range(2):
            for slot in range(slots):
                start = (part * tiles + d * slots + slot) * pitch
                total = held[pl.ds(start, lines), :]
                out[d, part, slot] = total.astype(BF)
        return carry

    lax.fori_loop(0, devices, device, 0, unroll=4)


def collect(sheets, weights, devices, which):
    tiles = weights.shape[1] // 4
    lines = HALF
    shape = (devices, 2, tiles // devices, lines, LANES)
    sheet_spec = pl.BlockSpec(sheets[0].shape, lambda i: (0, 0, 0))
    block = pl.BlockSpec(shape, lambda i: (0, 0, 0, 0, 0))
    return pl.pallas_call(
        collect_kernel,
        grid=(1,),
        in_specs=[sheet_spec] * len(sheets) + [pl.BlockSpec((1,) + weights.shape[1:], lambda i: (which, 0, 0))],
        out_specs=block,
        out_shape=jax.ShapeDtypeStruct(shape, BF),
        scratch_shapes=[pltpu.VMEM((2 * tiles * (lines + 1), LANES), F32)],
        compiler_params=pltpu.CompilerParams(vmem_limit_bytes=VMEM),
        cost_estimate=cost(6),
        name="collect",
    )(*sheets, weights)


def crop_kernel(rows, cols, odd, mine, pot, after, out, held, sems):
    slots = out.shape[0]

    def copy(i):
        return pltpu.make_async_copy(
            pot.at[
                pl.ds(pl.multiple_of(rows[i] * A, A), A),
                pl.ds(pl.multiple_of(cols[i] * LANES, LANES), LANES),
            ],
            held.at[i],
            sems.at[i],
        )

    def begin(i, carry):
        copy(i).start()
        return carry

    def finish(i, carry):
        copy(i).wait()
        block = held[i].astype(F32)
        block = jnp.where(odd[i] == 1, pltpu.roll(block, A, 1), block)
        lane = lax.broadcasted_iota(jnp.int32, (HALF, LANES), 1)
        packed = jnp.where(lane < A, block[:HALF], pltpu.roll(block[HALF:], A, 1))
        out[i] = jnp.where(mine[i] == 1, packed, 0.0).astype(BF)
        return carry

    lax.fori_loop(0, slots, begin, 0)
    lax.fori_loop(0, slots, finish, 0)


def crop(rows, cols, odd, mine, pot, after):
    slots = rows.shape[0]
    return pl.pallas_call(
        crop_kernel,
        in_specs=[pl.BlockSpec(memory_space=pltpu.SMEM)] * 4
        + [pl.BlockSpec(memory_space=pl.ANY)] * 2,
        out_specs=pl.BlockSpec(memory_space=pltpu.VMEM),
        out_shape=jax.ShapeDtypeStruct((slots, HALF, LANES), BF),
        scratch_shapes=[pltpu.VMEM((slots, A, LANES), BF), pltpu.SemaphoreType.DMA((slots,))],
        compiler_params=pltpu.CompilerParams(vmem_limit_bytes=VMEM),
        cost_estimate=cost(7),
        name="crop",
    )(rows, cols, odd, mine, pot, after)


def detect_kernel(parts, alpha, counts, *refs):
    fields = refs[:parts]
    pot, plane, across, down, bins, out, lines, held = refs[parts:]
    beams, _, slots = fields[0].shape[:3]
    for s in range(slots):
        waves = []
        for j in range(beams):
            re, im = (
                jnp.concatenate([half[j, part, s] for half in fields], axis=0).astype(F32)
                for part in range(2)
            )
            cos, sin = plane[j, 0], plane[j, 1]
            waves.append((re * cos - im * sin, re * sin + im * cos))
        turned, level = sine_cosine(pot[s].astype(F32))
        for g in range(G):
            real = jnp.zeros((HALF, LANES), F32)
            imag = jnp.zeros((HALF, LANES), F32)
            for j in range(beams):
                cos, sin = alpha[0, j, s * G + g], alpha[1, j, s * G + g]
                re, im = waves[j]
                real = real + cos * re - sin * im
                imag = imag + cos * im + sin * re
            lines[2 * (s * G + g)] = (real * level - imag * turned).astype(BF)
            lines[2 * (s * G + g) + 1] = (real * turned + imag * level).astype(BF)
    total = slots * G
    first = dot(lines[...].reshape(2 * total * HALF, LANES), across[...])
    first = first.reshape(total, 2, HALF, 2 * LANES)
    real = (first[:, 0, :, :LANES] + first[:, 1, :, LANES:]).astype(BF)
    imag = (first[:, 1, :, :LANES] - first[:, 0, :, LANES:]).astype(BF)
    lane = lax.broadcasted_iota(jnp.int32, (A, LANES), 1)
    for i in range(total):
        both = jnp.concatenate([real[i], imag[i]], axis=1)
        mixed = dot(down[...], both)
        even, odd = mixed[: 2 * A], mixed[2 * A :]
        re_cos = even[:A, :LANES] + pltpu.roll(odd[:A, :LANES], A, 1)
        re_sin = even[A:, :LANES] + pltpu.roll(odd[A:, :LANES], A, 1)
        im_cos = even[:A, LANES:] + pltpu.roll(odd[:A, LANES:], A, 1)
        im_sin = even[A:, LANES:] + pltpu.roll(odd[A:, LANES:], A, 1)
        re = re_cos + im_sin
        im = im_cos - re_sin
        power = jnp.where(lane < A, re * re + im * im, 0.0)
        sums = jnp.sum(power[None] * bins[...], axis=1)
        block, slot = divmod(i // G, slots // counts.shape[0])
        active = slot < counts[block]
        held[i * NDET : (i + 1) * NDET, :] = jnp.where(active, sums, 0.0)
    out[...] = jnp.sum(held[...].T, axis=0, keepdims=True)


def detect(alpha, counts, fields, pot, plane, across, down, bins):
    slots = fields[0].shape[2]
    rows = -(-slots * G * NDET // LANES) * LANES
    smem = pl.BlockSpec(memory_space=pltpu.SMEM)
    vmem = pl.BlockSpec(memory_space=pltpu.VMEM)
    return pl.pallas_call(
        functools.partial(detect_kernel, len(fields)),
        in_specs=[smem, smem] + [vmem] * (5 + len(fields)),
        out_specs=vmem,
        out_shape=jax.ShapeDtypeStruct((1, rows), F32),
        scratch_shapes=[
            pltpu.VMEM((2 * slots * G, HALF, LANES), BF),
            pltpu.VMEM((rows, LANES), F32),
        ],
        compiler_params=pltpu.CompilerParams(vmem_limit_bytes=VMEM),
        name="detect",
    )(alpha, counts, *fields, pot, plane, across, down, bins)


def detect_tables(beam_total):
    n = np.arange(A)
    table = turn(n[:, None] * n[None, :], A) / A
    cos, sin = table.real, table.imag
    zero = np.zeros((A, A))
    across = np.block([[cos, zero, sin, zero], [zero, cos, zero, sin]])
    rows = np.concatenate([cos, sin], axis=0)
    down = np.concatenate([rows[:, :HALF], rows[:, HALF:]], axis=0)
    signed = np.where(n < A // 2, n, n - A)
    radius = signed[:, None] ** 2 + signed[None, :] ** 2
    width = A // (2 * NDET)
    bins = np.zeros((NDET, A, LANES))
    for d in range(NDET):
        member = (radius >= (width * d) ** 2) & (radius < (width * (d + 1)) ** 2)
        bins[d, :, :A] = member * (A * A / (beam_total * member.sum()))
    return low(across), low(down), bins.astype(np.float32)


def coefficients(tile_ids, beam_rows, shifts):
    across = N // A
    offsets = jnp.arange(G, dtype=jnp.int32)
    spot_y = (tile_ids // across)[:, None] * A + A // 2 + offsets[None, :]
    spot_x = (tile_ids % across)[:, None] * A + A // 2 + 2 * offsets[None, :]
    wave_y = jnp.remainder(F * beam_rows[:, 0], N)[:, None, None]
    wave_x = jnp.remainder(F * beam_rows[:, 1], N)[:, None, None]
    windings = (wave_y * spot_y[None] % N + wave_x * spot_x[None] % N) % N
    phases = shifts[:, None, None] + 2.0 * math.pi / N * windings.astype(F32)
    return jnp.stack([jnp.cos(phases), -jnp.sin(phases)])


def tile_weights(tile_ids, beam_row, k1_pairs):
    across = N // A
    ty = tile_ids // across - beam_row[0]
    tx = tile_ids % across - beam_row[1]
    k1y = jnp.arange(A, dtype=jnp.int32)
    k1x = k1_pairs[:, None] + jnp.arange(2, dtype=jnp.int32)[None, :]
    winding = (
        k1y[None, None, None, :] * ty[None, :, None, None]
        + (k1x.T[:, None, :] * tx[None, :, None])[..., None]
    )
    angle = 2.0 * math.pi / A * (winding % A).astype(F32)
    cos, sin = jnp.cos(angle), jnp.sin(angle)
    upper = jnp.stack([cos, -sin], axis=3)
    under = jnp.stack([sin, cos], axis=3)
    both = jnp.stack([upper, under]).astype(BF)
    return both.reshape(4 * tile_ids.shape[0], k1_pairs.shape[0] * 2 * A)


def plane_waves(beam_index):
    by = jnp.arange(HALF, dtype=jnp.int32)[:, None] + HALF * (jnp.arange(LANES) // A)[None, :]
    bx = jnp.broadcast_to((jnp.arange(LANES, dtype=jnp.int32) % A)[None, :], by.shape)
    row_y = beam_index[:, 0][:, None, None]
    row_x = beam_index[:, 1][:, None, None]
    winding = (row_y * by[None] + row_x * bx[None] + HALF * (row_y + row_x)) % A
    angle = 2.0 * math.pi / A * winding.astype(F32)
    return jnp.stack([jnp.cos(angle), jnp.sin(angle)], axis=1)


def shards(pot_first, pot_second, beam_index, aberration, tile_table, tile_count):
    field_count = lax.axis_size("beam")
    hold_count = lax.axis_size("slab")
    field_pos = lax.axis_index("beam")
    hold_pos = lax.axis_index("slab")
    band_rows = pot_first.shape[0]
    band_tiles = band_rows // A
    width_k = A // field_count
    sheets = width_k // 2
    across = N // A
    beam_total = beam_index.shape[0]
    share = hold_pos % sheets

    section_x = np.stack(
        [
            section_forward(
                np.array(
                    [width_k * p + 2 * t + ks for p in range(field_count) for ks in range(2)]
                )
            )
            for t in range(sheets)
        ]
    )
    last_x = np.stack(
        [
            np.stack(
                [
                    last_forward_x([width_k * p + 2 * t, width_k * p + 2 * t + 1])
                    for p in range(field_count)
                ]
            )
            for t in range(sheets)
        ]
    )
    section_y = section_forward(np.arange(A)).reshape(2, A * SUB, A * SUB)
    last_y = np.stack([last_forward_y([2 * q, 2 * q + 1]) for q in range(PAIRS)])
    inverse_y = np.stack([first_inverse_y([2 * q, 2 * q + 1]) for q in range(PAIRS)])
    inverse_x = np.stack(
        [
            np.stack(
                [
                    first_inverse_x([width_k * p + 2 * t, width_k * p + 2 * t + 1])
                    for t in range(sheets)
                ]
            )
            for p in range(field_count)
        ]
    )

    blocks_dev = tile_table.shape[0] // (field_count * hold_count)
    slot_count = tile_table.shape[1]
    own_slots = blocks_dev * slot_count
    table = tile_table.reshape(field_count, hold_count, own_slots)

    def trade(value, axis):
        return lax.all_to_all(value, axis, split_axis=0, concat_axis=0, tiled=True)

    near = min(sheets, 2)
    far = sheets // near

    def swap(value, x):
        return lax.ppermute(value, "slab", [(i, i ^ x) for i in range(hold_count)])

    ids = lax.dynamic_index_in_dim(table, hold_pos, 1, keepdims=False).reshape(-1)
    tile_y, tile_x = ids // across, ids % across
    mine = (tile_y // band_tiles == field_pos).astype(jnp.int32)
    rows = jnp.clip(tile_y - field_pos * band_tiles, 0, band_tiles - 1)

    beam_row = lax.dynamic_index_in_dim(beam_index, hold_pos, 0, keepdims=False)
    pair_ids = share ^ jnp.arange(sheets, dtype=jnp.int32)
    k1_pairs = field_pos * width_k + 2 * pair_ids
    parity = field_pos % 2
    sets = table.reshape(field_count // 2, 2, hold_count, own_slots)
    sets = [lax.dynamic_index_in_dim(sets, pos, 1, keepdims=False) for pos in (1 - parity, parity)]
    weights = jnp.stack([tile_weights(t.reshape(-1), beam_row, k1_pairs) for t in sets])
    row = np.arange(ROWS)
    base = row // PART + A * (K2_LOW + row % PART % K2_COUNT)
    freq_y = np.broadcast_to(base[:, None], (ROWS, LANES)).astype(np.float32)
    lane = np.arange(LANES)
    base = np.where(lane < 2 * K2_COUNT, lane // K2_COUNT + A * (K2_LOW + lane % K2_COUNT), N)
    freq_x = (k1_pairs + F * beam_row[1])[:, None, None] + base.astype(np.int32)
    square_x = (freq_x * freq_x).astype(F32)
    scalars = jnp.stack(
        jnp.broadcast_arrays(field_pos, pair_ids, F * beam_row[0]), axis=-1
    )
    scalars = scalars.astype(jnp.int32).reshape(-1)

    sel = share.reshape(1).astype(jnp.int32)
    received = [[] for _ in range(far)]
    earlier = []
    for part in range(PARTS):
        lines = trade(forward_x(sel, pot_first, section_x, last_x, field_count, part), "beam")
        if lines.shape[3] != LANES:
            ratio = LANES // lines.shape[3]
            lines = lines.reshape((field_count // ratio, ratio) + lines.shape[1:])
            lines = lines.transpose(0, 2, 3, 1, 4).reshape(-1, HIGH // PARTS, ROWS, LANES)
        if part:
            crops = crop(rows, tile_x // 2, tile_x % 2, mine, pot_second, earlier[0])
            lines = order(lines, [crops, weights, square_x])
        for f in range(far):
            received[f].append(swap(lines, f * near) if f else lines)
        if part == 0:
            earlier = [forward_y_first(received[f][0], section_y) for f in range(far)]
    waves = []
    ready = []
    token = []
    for f in range(far):
        spec = forward_y(received[f][1], section_y, earlier[f], last_y, token + earlier[1:])
        ready.append([spec] + [swap(spec, x) for x in range(1, near)])
        if f == 0:
            crops = order(crops.reshape(field_count, own_slots, HALF, LANES), [spec])
            crops = trade(crops, "beam")
        token = [spec]
    for f in range(far):
        waves.append(
            inverse(
                f * near, scalars, ready[f], freq_y, square_x, inverse_y, inverse_x, token
            )
        )
        token = waves[-1:] + [crops]
    owners = field_count // 2 * hold_count
    partial = collect(waves, weights, owners, 0)
    partial = lax.ppermute(partial, "beam", [(i, i ^ 1) for i in range(field_count)])
    tiles = collect(waves, weights, owners, 1)
    tiles = (tiles.astype(F32) + partial.astype(F32)).astype(BF)
    groups = [
        [b * hold_count + h for b in range(g, field_count, 2) for h in range(hold_count)]
        for g in range(2)
    ]
    tiles = lax.all_to_all(
        tiles,
        ("beam", "slab"),
        split_axis=0,
        concat_axis=0,
        axis_index_groups=groups,
        tiled=True,
    )
    tiles = tiles.reshape((field_count // 2, hold_count) + tiles.shape[1:]).astype(F32)
    fields = [jnp.sum(tiles, axis=0).astype(BF)]
    crops = jnp.sum(crops.astype(F32), axis=0).astype(BF)

    own = lax.dynamic_index_in_dim(
        lax.dynamic_index_in_dim(table, field_pos, 0, keepdims=False), hold_pos, 0, keepdims=False
    )
    alpha = coefficients(own, beam_index, aberration).reshape(2, beam_total, own_slots * G)
    first_block = (field_pos * hold_count + hold_pos) * blocks_dev
    counts = lax.dynamic_slice_in_dim(tile_count, first_block, blocks_dev, 0)
    bins = detect_tables(beam_total)
    sums = detect(alpha, counts, fields, crops, plane_waves(beam_index), *bins)
    return sums[0, : own_slots * G * NDET].reshape(blocks_dev, slot_count, G, NDET)


def solution(mesh):
    return jax.shard_map(
        shards,
        mesh=mesh,
        in_specs=(P("beam", None), P("beam", None), P(), P(), P(), P()),
        out_specs=P(("beam", "slab"), None, None, None),
        check_vma=False,
    )
```

```python
import functools
import math

import jax
import jax.numpy as jnp
import ml_dtypes
import numpy as np
from jax import lax
from jax.experimental import pallas as pl
from jax.experimental.pallas import tpu as pltpu
from jax.sharding import PartitionSpec as P

A = 64
N = 4096
F = 64
G = 3
NDET = 16
QMAX = 3
LIMIT = N // 3
K2_LOW = -(LIMIT // A + 1 + QMAX)
K2_COUNT = 2 * (LIMIT // A + 1 + QMAX)
PART = 104
ROWS = 2 * PART
LANES = 128
SUB = 16
FEW = 4
HIGH = A // SUB
HALF = A // 2
PAIRS = A // 2
PARTS = 2
VMEM = 60 * 1024 * 1024
PITCH = A + 1
PITCH_Y = A // PARTS + 1
BF = jnp.bfloat16
F32 = jnp.float32


def low(values):
    return np.asarray(values, dtype=np.float32).astype(ml_dtypes.bfloat16)


def turn(numerator, period):
    return np.exp(2j * np.pi * (numerator % period) / period)


def digits_k2():
    return K2_LOW + np.arange(K2_COUNT)


def spread(table, sub):
    both = np.stack([table.real, table.imag])
    return both[:, :, None, :, None] * np.eye(sub)[None, None, :, None, :]


def real_rows(table):
    return np.block([[table.real, -table.imag], [table.imag, table.real]])


def section_forward(k1):
    n1 = np.arange(A)
    return np.conj(turn(k1[:, None] * n1[None, :], A)) / A


def first_forward_x(k1):
    return low(spread(section_forward(k1), SUB).reshape(2 * len(k1) * SUB, A * SUB))


def first_forward_y():
    table = spread(section_forward(np.arange(A)), FEW).transpose(0, 2, 1, 3, 4)
    return low(table.reshape(2 * A * FEW, A * FEW))


def line_order(lanes):
    order = np.arange(lanes).reshape(-1, SUB // FEW, FEW).transpose(1, 0, 2).reshape(-1)
    out = np.zeros((lanes, lanes))
    out[order, np.arange(lanes)] = 1
    return low(out)


def last_forward_x(k1_pair):
    n2 = np.arange(A)
    out = np.zeros((2, PART, 2, 2, A))
    for ks, k1 in enumerate(k1_pair):
        freq = k1 + A * digits_k2()
        table = np.conj(turn(freq[:, None] * n2[None, :], N)) / A
        block = real_rows(table).reshape(2, K2_COUNT, 2, A)
        out[:, ks * K2_COUNT : (ks + 1) * K2_COUNT, ks] = block
    return low(out.reshape(ROWS, 4 * A))


def last_forward_y(k1_pair):
    n2 = np.arange(A)
    out = np.zeros((ROWS, 2, 2 * A))
    for e, k1 in enumerate(k1_pair):
        freq = k1 + A * digits_k2()
        table = np.conj(turn(freq[:, None] * n2[None, :], N)) / A
        out[e * PART : e * PART + 2 * K2_COUNT, e] = real_rows(table)
    return low(out.reshape(ROWS, 4 * A))


def first_inverse(k1):
    n2 = np.arange(A)
    freq = k1 + A * digits_k2()
    return turn(n2[:, None] * freq[None, :], N) * np.conj(turn(freq * freq, 2 * N))[None, :]


def first_inverse_y(k1_pair):
    out = np.zeros((2, 2 * A, PART))
    for e, k1 in enumerate(k1_pair):
        out[e, :, : 2 * K2_COUNT] = real_rows(first_inverse(k1))
    return low(out)


def first_inverse_x(k1_pair):
    out = np.zeros((2, LANES, 2, 2, A))
    for ks, k1 in enumerate(k1_pair):
        table = first_inverse(k1).T
        rows = slice(ks * K2_COUNT, (ks + 1) * K2_COUNT)
        out[0, rows, 0, ks] = table.real
        out[0, rows, 1, ks] = table.imag
        out[1, rows, 0, ks] = -table.imag
        out[1, rows, 1, ks] = table.real
    return low(out.reshape(2 * LANES, 4 * A))


def sine_cosine(x):
    u = x * x
    s = F32(SIN_FIT[-1])
    for c in SIN_FIT[-2::-1]:
        s = s * u + F32(c)
    q = F32(COS_FIT[-1])
    for c in COS_FIT[-2::-1]:
        q = q * u + F32(c)
    return s * x, q


def fit(function, degree):
    top = 3.1421**2
    nodes = 0.5 * top * (1 - np.cos(np.pi * (np.arange(64) + 0.5) / 64))
    cheb = np.polynomial.chebyshev.Chebyshev.fit(
        nodes, function(np.sqrt(nodes)), degree, domain=[0, top]
    )
    return [float(c) for c in cheb.convert(kind=np.polynomial.Polynomial).coef]


SIN_FIT = fit(lambda x: np.sinc(x / np.pi), 5)
COS_FIT = fit(np.cos, 5)


def dot(a, b):
    return jnp.dot(a, b, preferred_element_type=F32)


def cost(micros):
    return pl.CostEstimate(flops=int(micros * 1.1e9), bytes_accessed=0, transcendentals=0)


def forward_x_kernel(sel, pot, section, last, perm, out, cos_ref, sin_ref, twisted):
    fields = out.shape[0]
    lanes = out.shape[3]
    half = section.shape[1] // 2

    def chunk(t, carry):
        block = pot[:, 0, :, pl.ds(pl.multiple_of(t * LANES, LANES), LANES)]
        values = block.reshape(lanes, LANES).T.astype(F32)
        sine, cosine = sine_cosine(values)
        cos_ref[pl.ds(2 * t, 2)] = cosine.astype(BF).reshape(2, A, lanes)
        sin_ref[pl.ds(2 * t, 2)] = sine.astype(BF).reshape(2, A, lanes)
        return carry

    lax.fori_loop(0, N // LANES, chunk, 0, unroll=4)
    table = section[0]
    for m in range(HIGH):
        span = slice(m * SUB, (m + 1) * SUB)
        part_cos = cos_ref[:, span, :].reshape(A * SUB, lanes)
        part_sin = sin_ref[:, span, :].reshape(A * SUB, lanes)
        if lanes % LANES == 0:
            both = dot(table, jnp.concatenate([part_cos, part_sin], axis=1))
            of_cos, of_sin = both[:, :lanes], both[:, lanes:]
        else:
            of_cos, of_sin = dot(table, part_cos), dot(table, part_sin)
        real = of_cos[:half] - of_sin[half:]
        imag = of_cos[half:] + of_sin[:half]
        twisted[:, m * SUB : (m + 1) * SUB, :] = real.astype(BF).reshape(2 * fields, SUB, lanes)
        twisted[:, A + m * SUB : A + (m + 1) * SUB, :] = imag.astype(BF).reshape(
            2 * fields, SUB, lanes
        )
    for d in range(fields):
        lines = twisted[2 * d : 2 * d + 2].reshape(4 * A, lanes)
        out[d, 0] = dot(dot(last[0, d], lines).astype(BF), perm[...]).astype(BF)


def forward_x(sel, pot, section, last, fields, part):
    groups = pot.shape[0] // A
    lanes = groups * SUB
    steps = HIGH // PARTS
    return pl.pallas_call(
        forward_x_kernel,
        grid_spec=pltpu.PrefetchScalarGridSpec(
            num_scalar_prefetch=1,
            grid=(steps,),
            in_specs=[
                pl.BlockSpec((groups, 1, SUB, N), lambda i, s: (0, part * steps + i, 0, 0)),
                pl.BlockSpec((1,) + section.shape[1:], lambda i, s: (s[0], 0, 0)),
                pl.BlockSpec((1,) + last.shape[1:], lambda i, s: (s[0], 0, 0, 0)),
                pl.BlockSpec((lanes, lanes), lambda i, s: (0, 0)),
            ],
            out_specs=pl.BlockSpec((fields, 1, ROWS, lanes), lambda i, s: (0, i, 0, 0)),
            scratch_shapes=[
                pltpu.VMEM((A, A, lanes), BF),
                pltpu.VMEM((A, A, lanes), BF),
                pltpu.VMEM((2 * fields, 2 * A, lanes), BF),
            ],
        ),
        out_shape=jax.ShapeDtypeStruct((fields, steps, ROWS, lanes), BF),
        compiler_params=pltpu.CompilerParams(vmem_limit_bytes=VMEM),
        cost_estimate=cost(9),
        name="forward_x",
    )(sel, pot.reshape(groups, HIGH, SUB, N), section, last, line_order(lanes))


def first_section_y(lines, section, gathered, held):
    groups, steps = lines.shape[:2]
    span = LANES * FEW // SUB
    zeros = jnp.zeros((LANES - PART, LANES), F32)
    for g in range(groups):
        for h in range(steps):
            block = lines[g, h].astype(F32)
            both = jnp.concatenate([block[:PART], zeros, block[PART:], zeros], axis=0)
            turned = both.astype(BF).T
            columns = slice(2 * h * LANES, 2 * (h + 1) * LANES)
            for a in range(SUB // FEW):
                gathered[a, g * span : (g + 1) * span, columns] = turned[a * span : (a + 1) * span]
    half = A * FEW
    for a in range(SUB // FEW):
        both = dot(section[...], gathered[a])
        for h in range(steps):
            re = slice(2 * h * LANES, (2 * h + 1) * LANES)
            im = slice((2 * h + 1) * LANES, (2 * h + 2) * LANES)
            real = both[:half, re] - both[half:, im]
            imag = both[:half, im] + both[half:, re]
            for b in range(FEW):
                n2 = h * SUB + a * FEW + b
                rows = slice(b * A, (b + 1) * A)
                held[pl.ds(n2, A, stride=PITCH_Y), :] = real[rows]
                held[pl.ds(A * PITCH_Y + n2, A, stride=PITCH_Y), :] = imag[rows]


def first_section_scratch(lines):
    return [
        pltpu.VMEM((SUB // FEW, A * FEW, 2 * lines.shape[1] * LANES), BF),
        pltpu.VMEM(((2 * A + 1) * PITCH_Y, LANES), F32),
    ]


def forward_y_first_kernel(lines, section, twisted, gathered, held):
    first_section_y(lines, section, gathered, held)

    def digit(k, carry):
        for part in range(2):
            start = (part * A + k) * PITCH_Y
            twisted[k, part] = held[pl.ds(start, A // PARTS), :].astype(BF)
        return carry

    lax.fori_loop(0, A, digit, 0, unroll=8)


def forward_y_first(lines, section):
    return pl.pallas_call(
        forward_y_first_kernel,
        grid=(1,),
        in_specs=[
            pl.BlockSpec(lines.shape, lambda i: (0, 0, 0, 0)),
            pl.BlockSpec(section.shape, lambda i: (0, 0)),
        ],
        out_specs=pl.BlockSpec((A, 2, A // PARTS, LANES), lambda i: (0, 0, 0, 0)),
        out_shape=jax.ShapeDtypeStruct((A, 2, A // PARTS, LANES), BF),
        scratch_shapes=first_section_scratch(lines),
        compiler_params=pltpu.CompilerParams(vmem_limit_bytes=VMEM),
        cost_estimate=cost(4),
        name="forward_y_first",
    )(lines, section)


def forward_y_kernel(lines, section, earlier, last, *rest):
    out, gathered, held = rest[-3:]
    step = pl.program_id(0)

    @pl.when(step == 0)
    def _():
        first_section_y(lines, section, gathered, held)

    @pl.when(step > 0)
    def _():
        count = out.shape[0]
        base = (step - 1) * count
        for q in range(count):
            rows = []
            for e in range(2):
                for part in range(2):
                    k = 2 * (base + q) + e
                    rows.append(earlier[k, part])
                    start = (part * A + k) * PITCH_Y
                    rows.append(held[pl.ds(start, A // PARTS), :].astype(BF))
            out[q] = dot(last[q], jnp.concatenate(rows, axis=0)).astype(BF)


def forward_y(lines, section, earlier, last, after):
    steps = 2
    count = PAIRS // steps

    def late(i):
        return (jnp.maximum(i - 1, 0), 0, 0)

    return pl.pallas_call(
        forward_y_kernel,
        grid=(1 + steps,),
        in_specs=[
            pl.BlockSpec(lines.shape, lambda i: (0, 0, 0, 0)),
            pl.BlockSpec(section.shape, lambda i: (0, 0)),
            pl.BlockSpec(earlier.shape, lambda i: (0, 0, 0, 0)),
            pl.BlockSpec((count, ROWS, 4 * A), late),
        ]
        + [pl.BlockSpec(memory_space=pl.ANY)] * len(after),
        out_specs=pl.BlockSpec((count, ROWS, LANES), late),
        out_shape=jax.ShapeDtypeStruct((PAIRS, ROWS, LANES), BF),
        scratch_shapes=first_section_scratch(lines),
        compiler_params=pltpu.CompilerParams(vmem_limit_bytes=VMEM),
        cost_estimate=cost(6),
        name="forward_y",
    )(lines, section, earlier, last, *after)


def order_kernel(value, *rest):
    pass


def order(value, after):
    return pl.pallas_call(
        order_kernel,
        in_specs=[pl.BlockSpec(memory_space=pl.ANY)] * (1 + len(after)),
        out_specs=pl.BlockSpec(memory_space=pl.ANY),
        out_shape=jax.ShapeDtypeStruct(value.shape, value.dtype),
        input_output_aliases={0: 0},
        name="order",
    )(value, *after)


def inverse_kernel(steps, which, near, sel, *refs):
    specs = refs[:near]
    freq_y, square_x, table_y = refs[near : near + 3]
    tables_x = refs[near + 3 : 2 * near + 3]
    out, mid = refs[-2:]
    step = pl.program_id(0)
    count = PAIRS // steps
    each = HALF // steps
    limit = F32(LIMIT * LIMIT)
    whole = 2 * A * PITCH

    @pl.when(step < steps)
    def _():
        def pair(q, carry):
            pair_id = step * count + q
            offset = (2 * pair_id + sel[3 * which + 2]).astype(F32)
            row_freq = freq_y[...] + offset
            row_square = row_freq * row_freq
            values = []
            for x in range(near):
                inside = row_square + square_x[x] <= limit
                values.append(jnp.where(inside, specs[x][q].astype(F32), 0.0))
            for e in range(2):
                half = [v[e * PART : (e + 1) * PART].astype(BF) for v in values]
                half = half[0] if near == 1 else jnp.concatenate(half, axis=1)
                mixed = dot(table_y[q, e], half)
                for x in range(near):
                    for part in range(2):
                        spot = x * whole + part * A * PITCH + 2 * pair_id + e
                        mid[pl.ds(spot, A, stride=PITCH), :] = mixed[
                            part * A : (part + 1) * A, x * LANES : (x + 1) * LANES
                        ]
            return carry

        lax.fori_loop(0, count, pair, 0, unroll=4)

    @pl.when(step >= steps)
    def _():
        def line(i, carry):
            by = (step - steps) * each + i
            for x in range(near):
                rows = []
                for b in range(2):
                    start = x * whole + (by + b * HALF) * PITCH
                    real = mid[pl.ds(start, A), :].astype(BF)
                    imag = mid[pl.ds(start + A * PITCH, A), :].astype(BF)
                    rows.append(jnp.concatenate([real, imag], axis=1))
                product = dot(jnp.concatenate(rows, axis=0), tables_x[x][0, 0]).astype(BF)
                for b in range(2):
                    for part in range(2):
                        low_row = 2 * A * x + A * part
                        out[i, low_row : low_row + A, b * LANES : (b + 1) * LANES] = product[
                            b * A : (b + 1) * A, part * LANES : (part + 1) * LANES
                        ]
            return carry

        lax.fori_loop(0, each, line, 0, unroll=4)


def inverse(which, sel, specs, freq_y, square_x, table_y, table_x, after):
    near = len(specs)
    steps = 2
    count = PAIRS // steps
    each = HALF // steps

    def early(i, s):
        return jnp.minimum(i, steps - 1)

    def table_spec(x):
        return pl.BlockSpec(
            (1, 1) + table_x.shape[2:],
            lambda i, s: (s[3 * (which + x)], s[3 * (which + x) + 1], 0, 0),
        )

    return pl.pallas_call(
        functools.partial(inverse_kernel, steps, which, near),
        grid_spec=pltpu.PrefetchScalarGridSpec(
            num_scalar_prefetch=1,
            grid=(2 * steps,),
            in_specs=[pl.BlockSpec((count, ROWS, LANES), lambda i, s: (early(i, s), 0, 0))] * near
            + [
                pl.BlockSpec((ROWS, LANES), lambda i, s: (0, 0)),
                pl.BlockSpec((near, 1, LANES), lambda i, s: (which // near, 0, 0)),
                pl.BlockSpec((count, 2, 2 * A, PART), lambda i, s: (early(i, s), 0, 0, 0)),
            ]
            + [table_spec(x) for x in range(near)]
            + [pl.BlockSpec(memory_space=pl.ANY)] * len(after),
            out_specs=pl.BlockSpec(
                (each, 2 * A * near, 2 * LANES), lambda i, s: (jnp.maximum(i - steps, 0), 0, 0)
            ),
            scratch_shapes=[pltpu.VMEM(((near * 2 * A + 1) * PITCH, LANES), F32)],
        ),
        out_shape=jax.ShapeDtypeStruct((HALF, 2 * A * near, 2 * LANES), BF),
        compiler_params=pltpu.CompilerParams(vmem_limit_bytes=VMEM),
        cost_estimate=cost(6),
        name="inverse",
    )(sel, *specs, freq_y, square_x, table_y, *[table_x] * near, *after)


def collect_kernel(*refs):
    *sheets, weights, out, held = refs
    devices, _, slots, lines, _ = out.shape
    each = sheets[0].shape[0]
    step = pl.program_id(0)
    tiles = devices * slots
    pitch = lines + 1
    lane = lax.broadcasted_iota(jnp.int32, (tiles, LANES), 1)
    lower = lane < A

    def line(i, carry):
        stacked = sheets[0][i]
        if len(sheets) > 1:
            stacked = jnp.concatenate([sheet[i] for sheet in sheets], axis=0)
        sums = dot(weights[0], stacked)
        for part in range(2):
            even = sums[2 * part * tiles : (2 * part + 1) * tiles]
            odd = sums[(2 * part + 1) * tiles : (2 * part + 2) * tiles]
            keep = jnp.where(lower, even[:, :LANES], odd[:, LANES:])
            move = jnp.where(lower, even[:, LANES:], odd[:, :LANES])
            total = keep + pltpu.roll(move, A, 1)
            spot = part * tiles * pitch + step * each + i
            held[pl.ds(spot, tiles, stride=pitch), :] = total
        return carry

    lax.fori_loop(0, each, line, 0, unroll=4)

    def device(d, carry):
        for part in range(2):
            for slot in range(slots):
                start = (part * tiles + d * slots + slot) * pitch
                total = held[pl.ds(start, lines), :]
                out[d, part, slot] = total.astype(BF)
        return carry

    @pl.when(step == lines // each - 1)
    def _():
        lax.fori_loop(0, devices, device, 0, unroll=4)


def collect(sheets, weights, devices, which):
    tiles = weights.shape[1] // 4
    lines = HALF
    shape = (devices, 2, tiles // devices, lines, LANES)
    steps = 4
    sheet_spec = pl.BlockSpec((lines // steps,) + sheets[0].shape[1:], lambda i: (i, 0, 0))
    block = pl.BlockSpec(shape, lambda i: (0, 0, 0, 0, 0))
    return pl.pallas_call(
        collect_kernel,
        grid=(steps,),
        in_specs=[sheet_spec] * len(sheets) + [pl.BlockSpec((1,) + weights.shape[1:], lambda i: (which, 0, 0))],
        out_specs=block,
        out_shape=jax.ShapeDtypeStruct(shape, BF),
        scratch_shapes=[pltpu.VMEM(((2 * tiles + 1) * (lines + 1), LANES), F32)],
        compiler_params=pltpu.CompilerParams(vmem_limit_bytes=VMEM),
        cost_estimate=cost(6),
        name="collect",
    )(*sheets, weights)


def crop_kernel(rows, cols, odd, mine, pot, after, out, held, sems):
    slots = out.shape[0]

    def copy(i):
        return pltpu.make_async_copy(
            pot.at[
                pl.ds(pl.multiple_of(rows[i] * A, A), A),
                pl.ds(pl.multiple_of(cols[i] * LANES, LANES), LANES),
            ],
            held.at[i],
            sems.at[i],
        )

    def begin(i, carry):
        copy(i).start()
        return carry

    def finish(i, carry):
        copy(i).wait()
        block = held[i].astype(F32)
        block = jnp.where(odd[i] == 1, pltpu.roll(block, A, 1), block)
        lane = lax.broadcasted_iota(jnp.int32, (HALF, LANES), 1)
        packed = jnp.where(lane < A, block[:HALF], pltpu.roll(block[HALF:], A, 1))
        out[i] = jnp.where(mine[i] == 1, packed, 0.0).astype(BF)
        return carry

    lax.fori_loop(0, slots, begin, 0)
    lax.fori_loop(0, slots, finish, 0)


def crop(rows, cols, odd, mine, pot, after):
    slots = rows.shape[0]
    return pl.pallas_call(
        crop_kernel,
        in_specs=[pl.BlockSpec(memory_space=pltpu.SMEM)] * 4
        + [pl.BlockSpec(memory_space=pl.ANY)] * 2,
        out_specs=pl.BlockSpec(memory_space=pltpu.VMEM),
        out_shape=jax.ShapeDtypeStruct((slots, HALF, LANES), BF),
        scratch_shapes=[pltpu.VMEM((slots, A, LANES), BF), pltpu.SemaphoreType.DMA((slots,))],
        compiler_params=pltpu.CompilerParams(vmem_limit_bytes=VMEM),
        cost_estimate=cost(7),
        name="crop",
    )(rows, cols, odd, mine, pot, after)


def detect_kernel(parts, alpha, counts, *refs):
    fields = refs[:parts]
    pot, plane, across, down, bins, out, lines, held = refs[parts:]
    beams, _, slots = fields[0].shape[:3]
    for s in range(slots):
        waves = []
        for j in range(beams):
            re, im = (
                jnp.concatenate([half[j, part, s] for half in fields], axis=0).astype(F32)
                for part in range(2)
            )
            cos, sin = plane[j, 0], plane[j, 1]
            waves.append((re * cos - im * sin, re * sin + im * cos))
        turned, level = sine_cosine(pot[s].astype(F32))
        for g in range(G):
            real = jnp.zeros((HALF, LANES), F32)
            imag = jnp.zeros((HALF, LANES), F32)
            for j in range(beams):
                cos, sin = alpha[0, j, s * G + g], alpha[1, j, s * G + g]
                re, im = waves[j]
                real = real + cos * re - sin * im
                imag = imag + cos * im + sin * re
            lines[2 * (s * G + g)] = (real * level - imag * turned).astype(BF)
            lines[2 * (s * G + g) + 1] = (real * turned + imag * level).astype(BF)
    total = slots * G
    first = dot(lines[...].reshape(2 * total * HALF, LANES), across[...])
    first = first.reshape(total, 2, HALF, 2 * LANES)
    real = (first[:, 0, :, :LANES] + first[:, 1, :, LANES:]).astype(BF)
    imag = (first[:, 1, :, :LANES] - first[:, 0, :, LANES:]).astype(BF)
    lane = lax.broadcasted_iota(jnp.int32, (A, LANES), 1)
    for i in range(total):
        both = jnp.concatenate([real[i], imag[i]], axis=1)
        mixed = dot(down[...], both)
        even, odd = mixed[: 2 * A], mixed[2 * A :]
        re_cos = even[:A, :LANES] + pltpu.roll(odd[:A, :LANES], A, 1)
        re_sin = even[A:, :LANES] + pltpu.roll(odd[A:, :LANES], A, 1)
        im_cos = even[:A, LANES:] + pltpu.roll(odd[:A, LANES:], A, 1)
        im_sin = even[A:, LANES:] + pltpu.roll(odd[A:, LANES:], A, 1)
        re = re_cos + im_sin
        im = im_cos - re_sin
        power = jnp.where(lane < A, re * re + im * im, 0.0)
        sums = jnp.sum(power[None] * bins[...], axis=1)
        block, slot = divmod(i // G, slots // counts.shape[0])
        active = slot < counts[block]
        held[i * NDET : (i + 1) * NDET, :] = jnp.where(active, sums, 0.0)
    out[...] = jnp.sum(held[...].T, axis=0, keepdims=True)


def detect(alpha, counts, fields, pot, plane, across, down, bins):
    slots = fields[0].shape[2]
    rows = -(-slots * G * NDET // LANES) * LANES
    smem = pl.BlockSpec(memory_space=pltpu.SMEM)
    vmem = pl.BlockSpec(memory_space=pltpu.VMEM)
    return pl.pallas_call(
        functools.partial(detect_kernel, len(fields)),
        in_specs=[smem, smem] + [vmem] * (5 + len(fields)),
        out_specs=vmem,
        out_shape=jax.ShapeDtypeStruct((1, rows), F32),
        scratch_shapes=[
            pltpu.VMEM((2 * slots * G, HALF, LANES), BF),
            pltpu.VMEM((rows, LANES), F32),
        ],
        compiler_params=pltpu.CompilerParams(vmem_limit_bytes=VMEM),
        name="detect",
    )(alpha, counts, *fields, pot, plane, across, down, bins)


def detect_tables(beam_total):
    n = np.arange(A)
    table = turn(n[:, None] * n[None, :], A) / A
    cos, sin = table.real, table.imag
    zero = np.zeros((A, A))
    across = np.block([[cos, zero, sin, zero], [zero, cos, zero, sin]])
    rows = np.concatenate([cos, sin], axis=0)
    down = np.concatenate([rows[:, :HALF], rows[:, HALF:]], axis=0)
    signed = np.where(n < A // 2, n, n - A)
    radius = signed[:, None] ** 2 + signed[None, :] ** 2
    width = A // (2 * NDET)
    bins = np.zeros((NDET, A, LANES))
    for d in range(NDET):
        member = (radius >= (width * d) ** 2) & (radius < (width * (d + 1)) ** 2)
        bins[d, :, :A] = member * (A * A / (beam_total * member.sum()))
    return low(across), low(down), bins.astype(np.float32)


def coefficients(tile_ids, beam_rows, shifts):
    across = N // A
    offsets = jnp.arange(G, dtype=jnp.int32)
    spot_y = (tile_ids // across)[:, None] * A + A // 2 + offsets[None, :]
    spot_x = (tile_ids % across)[:, None] * A + A // 2 + 2 * offsets[None, :]
    wave_y = jnp.remainder(F * beam_rows[:, 0], N)[:, None, None]
    wave_x = jnp.remainder(F * beam_rows[:, 1], N)[:, None, None]
    windings = (wave_y * spot_y[None] % N + wave_x * spot_x[None] % N) % N
    phases = shifts[:, None, None] + 2.0 * math.pi / N * windings.astype(F32)
    return jnp.stack([jnp.cos(phases), -jnp.sin(phases)])


def tile_weights(tile_ids, beam_row, k1_pairs):
    across = N // A
    ty = tile_ids // across - beam_row[0]
    tx = tile_ids % across - beam_row[1]
    k1y = jnp.arange(A, dtype=jnp.int32)
    k1x = k1_pairs[:, None] + jnp.arange(2, dtype=jnp.int32)[None, :]
    winding = (
        k1y[None, None, None, :] * ty[None, :, None, None]
        + (k1x.T[:, None, :] * tx[None, :, None])[..., None]
    )
    angle = 2.0 * math.pi / A * (winding % A).astype(F32)
    cos, sin = jnp.cos(angle), jnp.sin(angle)
    upper = jnp.stack([cos, -sin], axis=3)
    under = jnp.stack([sin, cos], axis=3)
    both = jnp.stack([upper, under]).astype(BF)
    return both.reshape(4 * tile_ids.shape[0], k1_pairs.shape[0] * 2 * A)


def plane_waves(beam_index):
    by = jnp.arange(HALF, dtype=jnp.int32)[:, None] + HALF * (jnp.arange(LANES) // A)[None, :]
    bx = jnp.broadcast_to((jnp.arange(LANES, dtype=jnp.int32) % A)[None, :], by.shape)
    row_y = beam_index[:, 0][:, None, None]
    row_x = beam_index[:, 1][:, None, None]
    winding = (row_y * by[None] + row_x * bx[None] + HALF * (row_y + row_x)) % A
    angle = 2.0 * math.pi / A * winding.astype(F32)
    return jnp.stack([jnp.cos(angle), jnp.sin(angle)], axis=1)


def shards(pot_first, pot_second, beam_index, aberration, tile_table, tile_count):
    field_count = lax.axis_size("beam")
    hold_count = lax.axis_size("slab")
    field_pos = lax.axis_index("beam")
    hold_pos = lax.axis_index("slab")
    band_rows = pot_first.shape[0]
    band_tiles = band_rows // A
    width_k = A // field_count
    sheets = width_k // 2
    across = N // A
    beam_total = beam_index.shape[0]
    share = hold_pos % sheets

    section_x = np.stack(
        [
            first_forward_x(
                np.array(
                    [width_k * p + 2 * t + ks for p in range(field_count) for ks in range(2)]
                )
            )
            for t in range(sheets)
        ]
    )
    last_x = np.stack(
        [
            np.stack(
                [
                    last_forward_x([width_k * p + 2 * t, width_k * p + 2 * t + 1])
                    for p in range(field_count)
                ]
            )
            for t in range(sheets)
        ]
    )
    section_y = first_forward_y()
    last_y = np.stack([last_forward_y([2 * q, 2 * q + 1]) for q in range(PAIRS)])
    inverse_y = np.stack([first_inverse_y([2 * q, 2 * q + 1]) for q in range(PAIRS)])
    inverse_x = np.stack(
        [
            np.stack(
                [
                    first_inverse_x([width_k * p + 2 * t, width_k * p + 2 * t + 1])
                    for t in range(sheets)
                ]
            )
            for p in range(field_count)
        ]
    )

    blocks_dev = tile_table.shape[0] // (field_count * hold_count)
    slot_count = tile_table.shape[1]
    own_slots = blocks_dev * slot_count
    table = tile_table.reshape(field_count, hold_count, own_slots)

    def trade(value, axis):
        return lax.all_to_all(value, axis, split_axis=0, concat_axis=0, tiled=True)

    near = min(sheets, 2)
    far = sheets // near

    def swap(value, x):
        return lax.ppermute(value, "slab", [(i, i ^ x) for i in range(hold_count)])

    ids = lax.dynamic_index_in_dim(table, hold_pos, 1, keepdims=False).reshape(-1)
    tile_y, tile_x = ids // across, ids % across
    mine = (tile_y // band_tiles == field_pos).astype(jnp.int32)
    rows = jnp.clip(tile_y - field_pos * band_tiles, 0, band_tiles - 1)

    beam_row = lax.dynamic_index_in_dim(beam_index, hold_pos, 0, keepdims=False)
    pair_ids = share ^ jnp.arange(sheets, dtype=jnp.int32)
    k1_pairs = field_pos * width_k + 2 * pair_ids
    parity = field_pos % 2
    sets = table.reshape(field_count // 2, 2, hold_count, own_slots)
    sets = [lax.dynamic_index_in_dim(sets, pos, 1, keepdims=False) for pos in (1 - parity, parity)]
    weights = jnp.stack([tile_weights(t.reshape(-1), beam_row, k1_pairs) for t in sets])
    row = np.arange(ROWS)
    base = row // PART + A * (K2_LOW + row % PART % K2_COUNT)
    freq_y = np.broadcast_to(base[:, None], (ROWS, LANES)).astype(np.float32)
    lane = np.arange(LANES)
    base = np.where(lane < 2 * K2_COUNT, lane // K2_COUNT + A * (K2_LOW + lane % K2_COUNT), N)
    freq_x = (k1_pairs + F * beam_row[1])[:, None, None] + base.astype(np.int32)
    square_x = (freq_x * freq_x).astype(F32)
    scalars = jnp.stack(
        jnp.broadcast_arrays(field_pos, pair_ids, F * beam_row[0]), axis=-1
    )
    scalars = scalars.astype(jnp.int32).reshape(-1)

    sel = share.reshape(1).astype(jnp.int32)
    received = [[] for _ in range(far)]
    earlier = []
    for part in range(PARTS):
        lines = trade(forward_x(sel, pot_first, section_x, last_x, field_count, part), "beam")
        if lines.shape[3] != LANES:
            ratio = LANES // lines.shape[3]
            lines = lines.reshape(
                field_count // ratio, ratio, HIGH // PARTS, ROWS, SUB // FEW, -1
            )
            lines = lines.transpose(0, 2, 3, 4, 1, 5).reshape(-1, HIGH // PARTS, ROWS, LANES)
        if part:
            crops = crop(rows, tile_x // 2, tile_x % 2, mine, pot_second, earlier[0])
            lines = order(lines, [crops, weights, square_x])
        for f in range(far):
            received[f].append(swap(lines, f * near) if f else lines)
        if part == 0:
            earlier = [forward_y_first(received[f][0], section_y) for f in range(far)]
    waves = []
    ready = []
    token = []
    for f in range(far):
        spec = forward_y(received[f][1], section_y, earlier[f], last_y, token + earlier[1:])
        ready.append([spec] + [swap(spec, x) for x in range(1, near)])
        if f == 0:
            crops = order(crops.reshape(field_count, own_slots, HALF, LANES), [spec])
            crops = trade(crops, "beam")
        token = [spec, crops]
    for f in range(far):
        waves.append(
            inverse(
                f * near, scalars, ready[f], freq_y, square_x, inverse_y, inverse_x, token
            )
        )
        token = waves[-1:]
    owners = field_count // 2 * hold_count
    partial = collect(waves, weights, owners, 0)
    partial = lax.ppermute(partial, "beam", [(i, i ^ 1) for i in range(field_count)])
    tiles = collect(waves, weights, owners, 1)
    tiles = (tiles.astype(F32) + partial.astype(F32)).astype(BF)
    groups = [
        [b * hold_count + h for b in range(g, field_count, 2) for h in range(hold_count)]
        for g in range(2)
    ]
    tiles = lax.all_to_all(
        tiles,
        ("beam", "slab"),
        split_axis=0,
        concat_axis=0,
        axis_index_groups=groups,
        tiled=True,
    )
    tiles = tiles.reshape((field_count // 2, hold_count) + tiles.shape[1:]).astype(F32)
    fields = [jnp.sum(tiles, axis=0).astype(BF)]
    crops = jnp.sum(crops.astype(F32), axis=0).astype(BF)

    own = lax.dynamic_index_in_dim(
        lax.dynamic_index_in_dim(table, field_pos, 0, keepdims=False), hold_pos, 0, keepdims=False
    )
    alpha = coefficients(own, beam_index, aberration).reshape(2, beam_total, own_slots * G)
    first_block = (field_pos * hold_count + hold_pos) * blocks_dev
    counts = lax.dynamic_slice_in_dim(tile_count, first_block, blocks_dev, 0)
    bins = detect_tables(beam_total)
    sums = detect(alpha, counts, fields, crops, plane_waves(beam_index), *bins)
    return sums[0, : own_slots * G * NDET].reshape(blocks_dev, slot_count, G, NDET)


def solution(mesh):
    return jax.shard_map(
        shards,
        mesh=mesh,
        in_specs=(P("beam", None), P("beam", None), P(), P(), P(), P()),
        out_specs=P(("beam", "slab"), None, None, None),
        check_vma=False,
    )
```

```python
import functools
import math

import jax
import jax.numpy as jnp
import ml_dtypes
import numpy as np
from jax import lax
from jax.experimental import pallas as pl
from jax.experimental.pallas import tpu as pltpu
from jax.sharding import PartitionSpec as P

A = 64
N = 4096
F = 64
G = 3
NDET = 16
QMAX = 3
LIMIT = N // 3
K2_LOW = -(LIMIT // A + 1 + QMAX)
K2_COUNT = 2 * (LIMIT // A + 1 + QMAX)
PART = 104
ROWS = 2 * PART
LANES = 128
SUB = 16
FEW = 4
HIGH = A // SUB
HALF = A // 2
PAIRS = A // 2
PARTS = 2
VMEM = 60 * 1024 * 1024
PITCH = A + 1
PITCH_Y = A // PARTS + 1
BF = jnp.bfloat16
F32 = jnp.float32


def low(values):
    return np.asarray(values, dtype=np.float32).astype(ml_dtypes.bfloat16)


def turn(numerator, period):
    return np.exp(2j * np.pi * (numerator % period) / period)


def digits_k2():
    return K2_LOW + np.arange(K2_COUNT)


def spread(table, sub):
    both = np.stack([table.real, table.imag])
    return both[:, :, None, :, None] * np.eye(sub)[None, None, :, None, :]


def real_rows(table):
    return np.block([[table.real, -table.imag], [table.imag, table.real]])


def section_forward(k1):
    n1 = np.arange(A)
    return np.conj(turn(k1[:, None] * n1[None, :], A)) / A


def first_forward_x(k1):
    return low(spread(section_forward(k1), SUB).reshape(2 * len(k1) * SUB, A * SUB))


def first_forward_y():
    table = spread(section_forward(np.arange(A)), FEW).transpose(0, 2, 1, 3, 4)
    return low(table.reshape(2 * A * FEW, A * FEW))


def line_order(lanes):
    order = np.arange(lanes).reshape(-1, SUB // FEW, FEW).transpose(1, 0, 2).reshape(-1)
    out = np.zeros((lanes, lanes))
    out[order, np.arange(lanes)] = 1
    return low(out)


def last_forward_x(k1_pair):
    n2 = np.arange(A)
    out = np.zeros((2, PART, 2, 2, A))
    for ks, k1 in enumerate(k1_pair):
        freq = k1 + A * digits_k2()
        table = np.conj(turn(freq[:, None] * n2[None, :], N)) / A
        block = real_rows(table).reshape(2, K2_COUNT, 2, A)
        out[:, ks * K2_COUNT : (ks + 1) * K2_COUNT, ks] = block
    return low(out.reshape(ROWS, 4 * A))


def last_forward_y(k1_pair):
    n2 = np.arange(A)
    out = np.zeros((ROWS, 2, 2 * A))
    for e, k1 in enumerate(k1_pair):
        freq = k1 + A * digits_k2()
        table = np.conj(turn(freq[:, None] * n2[None, :], N)) / A
        out[e * PART : e * PART + 2 * K2_COUNT, e] = real_rows(table)
    return low(out.reshape(ROWS, 4 * A))


def first_inverse(k1):
    n2 = np.arange(A)
    freq = k1 + A * digits_k2()
    return turn(n2[:, None] * freq[None, :], N) * np.conj(turn(freq * freq, 2 * N))[None, :]


def first_inverse_y(k1_pair):
    out = np.zeros((2, 2 * A, PART))
    for e, k1 in enumerate(k1_pair):
        out[e, :, : 2 * K2_COUNT] = real_rows(first_inverse(k1))
    return low(out)


def first_inverse_x(k1_pair):
    out = np.zeros((2, LANES, 2, 2, A))
    for ks, k1 in enumerate(k1_pair):
        table = first_inverse(k1).T
        rows = slice(ks * K2_COUNT, (ks + 1) * K2_COUNT)
        out[0, rows, 0, ks] = table.real
        out[0, rows, 1, ks] = table.imag
        out[1, rows, 0, ks] = -table.imag
        out[1, rows, 1, ks] = table.real
    return low(out.reshape(2 * LANES, 4 * A))


def sine_cosine(x):
    u = x * x
    s = F32(SIN_FIT[-1])
    for c in SIN_FIT[-2::-1]:
        s = s * u + F32(c)
    q = F32(COS_FIT[-1])
    for c in COS_FIT[-2::-1]:
        q = q * u + F32(c)
    return s * x, q


def fit(function, degree):
    top = 3.1421**2
    nodes = 0.5 * top * (1 - np.cos(np.pi * (np.arange(64) + 0.5) / 64))
    cheb = np.polynomial.chebyshev.Chebyshev.fit(
        nodes, function(np.sqrt(nodes)), degree, domain=[0, top]
    )
    return [float(c) for c in cheb.convert(kind=np.polynomial.Polynomial).coef]


SIN_FIT = fit(lambda x: np.sinc(x / np.pi), 5)
COS_FIT = fit(np.cos, 5)


def dot(a, b):
    return jnp.dot(a, b, preferred_element_type=F32)


def cost(micros):
    return pl.CostEstimate(flops=int(micros * 1.1e9), bytes_accessed=0, transcendentals=0)


def forward_x_kernel(sel, pot, section, last, perm, out, cos_ref, sin_ref, twisted):
    fields = out.shape[0]
    lanes = out.shape[3]
    half = section.shape[1] // 2

    def chunk(t, carry):
        block = pot[:, 0, :, pl.ds(pl.multiple_of(t * LANES, LANES), LANES)]
        values = block.reshape(lanes, LANES).T.astype(F32)
        sine, cosine = sine_cosine(values)
        cos_ref[pl.ds(2 * t, 2)] = cosine.astype(BF).reshape(2, A, lanes)
        sin_ref[pl.ds(2 * t, 2)] = sine.astype(BF).reshape(2, A, lanes)
        return carry

    lax.fori_loop(0, N // LANES, chunk, 0, unroll=4)
    table = section[0]
    for m in range(HIGH):
        span = slice(m * SUB, (m + 1) * SUB)
        part_cos = cos_ref[:, span, :].reshape(A * SUB, lanes)
        part_sin = sin_ref[:, span, :].reshape(A * SUB, lanes)
        if lanes % LANES == 0:
            both = dot(table, jnp.concatenate([part_cos, part_sin], axis=1))
            of_cos, of_sin = both[:, :lanes], both[:, lanes:]
        else:
            of_cos, of_sin = dot(table, part_cos), dot(table, part_sin)
        real = of_cos[:half] - of_sin[half:]
        imag = of_cos[half:] + of_sin[:half]
        twisted[:, m * SUB : (m + 1) * SUB, :] = real.astype(BF).reshape(2 * fields, SUB, lanes)
        twisted[:, A + m * SUB : A + (m + 1) * SUB, :] = imag.astype(BF).reshape(
            2 * fields, SUB, lanes
        )
    for d in range(fields):
        lines = twisted[2 * d : 2 * d + 2].reshape(4 * A, lanes)
        out[d, 0] = dot(dot(last[0, d], lines).astype(BF), perm[...]).astype(BF)


def forward_x(sel, pot, section, last, fields, part):
    groups = pot.shape[0] // A
    lanes = groups * SUB
    steps = HIGH // PARTS
    return pl.pallas_call(
        forward_x_kernel,
        grid_spec=pltpu.PrefetchScalarGridSpec(
            num_scalar_prefetch=1,
            grid=(steps,),
            in_specs=[
                pl.BlockSpec((groups, 1, SUB, N), lambda i, s: (0, part * steps + i, 0, 0)),
                pl.BlockSpec((1,) + section.shape[1:], lambda i, s: (s[0], 0, 0)),
                pl.BlockSpec((1,) + last.shape[1:], lambda i, s: (s[0], 0, 0, 0)),
                pl.BlockSpec((lanes, lanes), lambda i, s: (0, 0)),
            ],
            out_specs=pl.BlockSpec((fields, 1, ROWS, lanes), lambda i, s: (0, i, 0, 0)),
            scratch_shapes=[
                pltpu.VMEM((A, A, lanes), BF),
                pltpu.VMEM((A, A, lanes), BF),
                pltpu.VMEM((2 * fields, 2 * A, lanes), BF),
            ],
        ),
        out_shape=jax.ShapeDtypeStruct((fields, steps, ROWS, lanes), BF),
        compiler_params=pltpu.CompilerParams(vmem_limit_bytes=VMEM),
        cost_estimate=cost(9),
        name="forward_x",
    )(sel, pot.reshape(groups, HIGH, SUB, N), section, last, line_order(lanes))


def first_section_y(lines, section, gathered, held):
    groups, steps = lines.shape[:2]
    span = LANES * FEW // SUB
    zeros = jnp.zeros((LANES - PART, LANES), F32)
    for g in range(groups):
        for h in range(steps):
            block = lines[g, h].astype(F32)
            both = jnp.concatenate([block[:PART], zeros, block[PART:], zeros], axis=0)
            turned = both.astype(BF).T
            columns = slice(2 * h * LANES, 2 * (h + 1) * LANES)
            for a in range(SUB // FEW):
                gathered[a, g * span : (g + 1) * span, columns] = turned[a * span : (a + 1) * span]
    half = A * FEW
    for a in range(SUB // FEW):
        both = dot(section[...], gathered[a])
        for h in range(steps):
            re = slice(2 * h * LANES, (2 * h + 1) * LANES)
            im = slice((2 * h + 1) * LANES, (2 * h + 2) * LANES)
            real = both[:half, re] - both[half:, im]
            imag = both[:half, im] + both[half:, re]
            for b in range(FEW):
                n2 = h * SUB + a * FEW + b
                rows = slice(b * A, (b + 1) * A)
                held[pl.ds(n2, A, stride=PITCH_Y), :] = real[rows]
                held[pl.ds(A * PITCH_Y + n2, A, stride=PITCH_Y), :] = imag[rows]


def first_section_scratch(lines):
    return [
        pltpu.VMEM((SUB // FEW, A * FEW, 2 * lines.shape[1] * LANES), BF),
        pltpu.VMEM(((2 * A + 1) * PITCH_Y, LANES), F32),
    ]


def forward_y_first_kernel(lines, section, twisted, gathered, held):
    first_section_y(lines, section, gathered, held)

    def digit(k, carry):
        for part in range(2):
            start = (part * A + k) * PITCH_Y
            twisted[k, part] = held[pl.ds(start, A // PARTS), :].astype(BF)
        return carry

    lax.fori_loop(0, A, digit, 0, unroll=8)


def forward_y_first(lines, section):
    return pl.pallas_call(
        forward_y_first_kernel,
        grid=(1,),
        in_specs=[
            pl.BlockSpec(lines.shape, lambda i: (0, 0, 0, 0)),
            pl.BlockSpec(section.shape, lambda i: (0, 0)),
        ],
        out_specs=pl.BlockSpec((A, 2, A // PARTS, LANES), lambda i: (0, 0, 0, 0)),
        out_shape=jax.ShapeDtypeStruct((A, 2, A // PARTS, LANES), BF),
        scratch_shapes=first_section_scratch(lines),
        compiler_params=pltpu.CompilerParams(vmem_limit_bytes=VMEM),
        cost_estimate=cost(4),
        name="forward_y_first",
    )(lines, section)


def forward_y_kernel(lines, section, earlier, last, *rest):
    out, gathered, held = rest[-3:]
    step = pl.program_id(0)

    @pl.when(step == 0)
    def _():
        first_section_y(lines, section, gathered, held)

    @pl.when(step > 0)
    def _():
        count = out.shape[0]
        base = (step - 1) * count
        for q in range(count):
            rows = []
            for e in range(2):
                for part in range(2):
                    k = 2 * (base + q) + e
                    rows.append(earlier[k, part])
                    start = (part * A + k) * PITCH_Y
                    rows.append(held[pl.ds(start, A // PARTS), :].astype(BF))
            out[q] = dot(last[q], jnp.concatenate(rows, axis=0)).astype(BF)


def forward_y(lines, section, earlier, last, after):
    steps = 2
    count = PAIRS // steps

    def late(i):
        return (jnp.maximum(i - 1, 0), 0, 0)

    return pl.pallas_call(
        forward_y_kernel,
        grid=(1 + steps,),
        in_specs=[
            pl.BlockSpec(lines.shape, lambda i: (0, 0, 0, 0)),
            pl.BlockSpec(section.shape, lambda i: (0, 0)),
            pl.BlockSpec(earlier.shape, lambda i: (0, 0, 0, 0)),
            pl.BlockSpec((count, ROWS, 4 * A), late),
        ]
        + [pl.BlockSpec(memory_space=pl.ANY)] * len(after),
        out_specs=pl.BlockSpec((count, ROWS, LANES), late),
        out_shape=jax.ShapeDtypeStruct((PAIRS, ROWS, LANES), BF),
        scratch_shapes=first_section_scratch(lines),
        compiler_params=pltpu.CompilerParams(vmem_limit_bytes=VMEM),
        cost_estimate=cost(6),
        name="forward_y",
    )(lines, section, earlier, last, *after)


def order_kernel(value, *rest):
    pass


def order(value, after):
    return pl.pallas_call(
        order_kernel,
        in_specs=[pl.BlockSpec(memory_space=pl.ANY)] * (1 + len(after)),
        out_specs=pl.BlockSpec(memory_space=pl.ANY),
        out_shape=jax.ShapeDtypeStruct(value.shape, value.dtype),
        input_output_aliases={0: 0},
        name="order",
    )(value, *after)


def inverse_kernel(steps, which, near, sel, *refs):
    specs = refs[:near]
    freq_y, square_x, table_y = refs[near : near + 3]
    tables_x = refs[near + 3 : 2 * near + 3]
    out, mid = refs[-2:]
    step = pl.program_id(0)
    count = PAIRS // steps
    each = HALF // steps
    limit = F32(LIMIT * LIMIT)
    whole = 2 * A * PITCH

    @pl.when(step < steps)
    def _():
        def pair(q, carry):
            pair_id = step * count + q
            offset = (2 * pair_id + sel[3 * which + 2]).astype(F32)
            row_freq = freq_y[...] + offset
            row_square = row_freq * row_freq
            values = []
            for x in range(near):
                inside = row_square + square_x[x] <= limit
                values.append(jnp.where(inside, specs[x][q].astype(F32), 0.0))
            for e in range(2):
                half = [v[e * PART : (e + 1) * PART].astype(BF) for v in values]
                half = half[0] if near == 1 else jnp.concatenate(half, axis=1)
                mixed = dot(table_y[q, e], half)
                for x in range(near):
                    for part in range(2):
                        spot = x * whole + part * A * PITCH + 2 * pair_id + e
                        mid[pl.ds(spot, A, stride=PITCH), :] = mixed[
                            part * A : (part + 1) * A, x * LANES : (x + 1) * LANES
                        ]
            return carry

        lax.fori_loop(0, count, pair, 0, unroll=4)

    @pl.when(step >= steps)
    def _():
        def line(i, carry):
            by = (step - steps) * each + i
            for x in range(near):
                rows = []
                for b in range(2):
                    start = x * whole + (by + b * HALF) * PITCH
                    real = mid[pl.ds(start, A), :].astype(BF)
                    imag = mid[pl.ds(start + A * PITCH, A), :].astype(BF)
                    rows.append(jnp.concatenate([real, imag], axis=1))
                product = dot(jnp.concatenate(rows, axis=0), tables_x[x][0, 0]).astype(BF)
                for b in range(2):
                    for part in range(2):
                        low_row = 2 * A * x + A * part
                        out[i, low_row : low_row + A, b * LANES : (b + 1) * LANES] = product[
                            b * A : (b + 1) * A, part * LANES : (part + 1) * LANES
                        ]
            return carry

        lax.fori_loop(0, each, line, 0, unroll=4)


def inverse(which, sel, specs, freq_y, square_x, table_y, table_x, after):
    near = len(specs)
    steps = 2
    count = PAIRS // steps
    each = HALF // steps

    def early(i, s):
        return jnp.minimum(i, steps - 1)

    def table_spec(x):
        return pl.BlockSpec(
            (1, 1) + table_x.shape[2:],
            lambda i, s: (s[3 * (which + x)], s[3 * (which + x) + 1], 0, 0),
        )

    return pl.pallas_call(
        functools.partial(inverse_kernel, steps, which, near),
        grid_spec=pltpu.PrefetchScalarGridSpec(
            num_scalar_prefetch=1,
            grid=(2 * steps,),
            in_specs=[pl.BlockSpec((count, ROWS, LANES), lambda i, s: (early(i, s), 0, 0))] * near
            + [
                pl.BlockSpec((ROWS, LANES), lambda i, s: (0, 0)),
                pl.BlockSpec((near, 1, LANES), lambda i, s: (which // near, 0, 0)),
                pl.BlockSpec((count, 2, 2 * A, PART), lambda i, s: (early(i, s), 0, 0, 0)),
            ]
            + [table_spec(x) for x in range(near)]
            + [pl.BlockSpec(memory_space=pl.ANY)] * len(after),
            out_specs=pl.BlockSpec(
                (each, 2 * A * near, 2 * LANES), lambda i, s: (jnp.maximum(i - steps, 0), 0, 0)
            ),
            scratch_shapes=[pltpu.VMEM(((near * 2 * A + 1) * PITCH, LANES), F32)],
        ),
        out_shape=jax.ShapeDtypeStruct((HALF, 2 * A * near, 2 * LANES), BF),
        compiler_params=pltpu.CompilerParams(vmem_limit_bytes=VMEM),
        cost_estimate=cost(6),
        name="inverse",
    )(sel, *specs, freq_y, square_x, table_y, *[table_x] * near, *after)


def collect_kernel(count, *refs):
    sheets, weights = refs[:count], refs[count]
    out, held = refs[-2:]
    devices, _, slots, lines, _ = out.shape
    each = sheets[0].shape[0]
    step = pl.program_id(0)
    tiles = devices * slots
    pitch = lines + 1
    lane = lax.broadcasted_iota(jnp.int32, (tiles, LANES), 1)
    lower = lane < A

    def line(i, carry):
        stacked = sheets[0][i]
        if len(sheets) > 1:
            stacked = jnp.concatenate([sheet[i] for sheet in sheets], axis=0)
        sums = dot(weights[0], stacked)
        for part in range(2):
            even = sums[2 * part * tiles : (2 * part + 1) * tiles]
            odd = sums[(2 * part + 1) * tiles : (2 * part + 2) * tiles]
            keep = jnp.where(lower, even[:, :LANES], odd[:, LANES:])
            move = jnp.where(lower, even[:, LANES:], odd[:, :LANES])
            total = keep + pltpu.roll(move, A, 1)
            spot = part * tiles * pitch + step * each + i
            held[pl.ds(spot, tiles, stride=pitch), :] = total
        return carry

    lax.fori_loop(0, each, line, 0, unroll=4)

    def device(d, carry):
        for part in range(2):
            for slot in range(slots):
                start = (part * tiles + d * slots + slot) * pitch
                total = held[pl.ds(start, lines), :]
                out[d, part, slot] = total.astype(BF)
        return carry

    @pl.when(step == lines // each - 1)
    def _():
        lax.fori_loop(0, devices, device, 0, unroll=4)


def collect(sheets, weights, devices, which, part, after):
    tiles = weights.shape[1] // 4
    lines = HALF // PARTS
    shape = (devices, 2, tiles // devices, lines, LANES)
    steps = 4
    sheet_spec = pl.BlockSpec(
        (lines // steps,) + sheets[0].shape[1:], lambda i: (part * steps + i, 0, 0)
    )
    block = pl.BlockSpec(shape, lambda i: (0, 0, 0, 0, 0))
    return pl.pallas_call(
        functools.partial(collect_kernel, len(sheets)),
        grid=(steps,),
        in_specs=[sheet_spec] * len(sheets) + [pl.BlockSpec((1,) + weights.shape[1:], lambda i: (which, 0, 0))]
        + [pl.BlockSpec(memory_space=pl.ANY)] * len(after),
        out_specs=block,
        out_shape=jax.ShapeDtypeStruct(shape, BF),
        scratch_shapes=[pltpu.VMEM(((2 * tiles + 1) * (lines + 1), LANES), F32)],
        compiler_params=pltpu.CompilerParams(vmem_limit_bytes=VMEM),
        cost_estimate=cost(0.05),
        name="collect",
    )(*sheets, weights, *after)


def crop_kernel(rows, cols, odd, mine, pot, after, out, held, sems):
    slots = out.shape[0]

    def copy(i):
        return pltpu.make_async_copy(
            pot.at[
                pl.ds(pl.multiple_of(rows[i] * A, A), A),
                pl.ds(pl.multiple_of(cols[i] * LANES, LANES), LANES),
            ],
            held.at[i],
            sems.at[i],
        )

    def begin(i, carry):
        copy(i).start()
        return carry

    def finish(i, carry):
        copy(i).wait()
        block = held[i].astype(F32)
        block = jnp.where(odd[i] == 1, pltpu.roll(block, A, 1), block)
        lane = lax.broadcasted_iota(jnp.int32, (HALF, LANES), 1)
        packed = jnp.where(lane < A, block[:HALF], pltpu.roll(block[HALF:], A, 1))
        out[i] = jnp.where(mine[i] == 1, packed, 0.0).astype(BF)
        return carry

    lax.fori_loop(0, slots, begin, 0)
    lax.fori_loop(0, slots, finish, 0)


def crop(rows, cols, odd, mine, pot, after):
    slots = rows.shape[0]
    return pl.pallas_call(
        crop_kernel,
        in_specs=[pl.BlockSpec(memory_space=pltpu.SMEM)] * 4
        + [pl.BlockSpec(memory_space=pl.ANY)] * 2,
        out_specs=pl.BlockSpec(memory_space=pltpu.VMEM),
        out_shape=jax.ShapeDtypeStruct((slots, HALF, LANES), BF),
        scratch_shapes=[pltpu.VMEM((slots, A, LANES), BF), pltpu.SemaphoreType.DMA((slots,))],
        compiler_params=pltpu.CompilerParams(vmem_limit_bytes=VMEM),
        cost_estimate=cost(7),
        name="crop",
    )(rows, cols, odd, mine, pot, after)


def detect_kernel(parts, alpha, counts, *refs):
    fields = refs[:parts]
    pot, plane, across, down, bins, out, lines, held = refs[parts:]
    beams, _, slots = fields[0].shape[:3]
    for s in range(slots):
        waves = []
        for j in range(beams):
            re, im = (
                jnp.concatenate([half[j, part, s] for half in fields], axis=0).astype(F32)
                for part in range(2)
            )
            cos, sin = plane[j, 0], plane[j, 1]
            waves.append((re * cos - im * sin, re * sin + im * cos))
        turned, level = sine_cosine(pot[s].astype(F32))
        for g in range(G):
            real = jnp.zeros((HALF, LANES), F32)
            imag = jnp.zeros((HALF, LANES), F32)
            for j in range(beams):
                cos, sin = alpha[0, j, s * G + g], alpha[1, j, s * G + g]
                re, im = waves[j]
                real = real + cos * re - sin * im
                imag = imag + cos * im + sin * re
            lines[2 * (s * G + g)] = (real * level - imag * turned).astype(BF)
            lines[2 * (s * G + g) + 1] = (real * turned + imag * level).astype(BF)
    total = slots * G
    first = dot(lines[...].reshape(2 * total * HALF, LANES), across[...])
    first = first.reshape(total, 2, HALF, 2 * LANES)
    real = (first[:, 0, :, :LANES] + first[:, 1, :, LANES:]).astype(BF)
    imag = (first[:, 1, :, :LANES] - first[:, 0, :, LANES:]).astype(BF)
    lane = lax.broadcasted_iota(jnp.int32, (A, LANES), 1)
    for i in range(total):
        both = jnp.concatenate([real[i], imag[i]], axis=1)
        mixed = dot(down[...], both)
        even, odd = mixed[: 2 * A], mixed[2 * A :]
        re_cos = even[:A, :LANES] + pltpu.roll(odd[:A, :LANES], A, 1)
        re_sin = even[A:, :LANES] + pltpu.roll(odd[A:, :LANES], A, 1)
        im_cos = even[:A, LANES:] + pltpu.roll(odd[:A, LANES:], A, 1)
        im_sin = even[A:, LANES:] + pltpu.roll(odd[A:, LANES:], A, 1)
        re = re_cos + im_sin
        im = im_cos - re_sin
        power = jnp.where(lane < A, re * re + im * im, 0.0)
        sums = jnp.sum(power[None] * bins[...], axis=1)
        block, slot = divmod(i // G, slots // counts.shape[0])
        active = slot < counts[block]
        held[i * NDET : (i + 1) * NDET, :] = jnp.where(active, sums, 0.0)
    out[...] = jnp.sum(held[...].T, axis=0, keepdims=True)


def detect(alpha, counts, fields, pot, plane, across, down, bins):
    slots = fields[0].shape[2]
    rows = -(-slots * G * NDET // LANES) * LANES
    smem = pl.BlockSpec(memory_space=pltpu.SMEM)
    vmem = pl.BlockSpec(memory_space=pltpu.VMEM)
    return pl.pallas_call(
        functools.partial(detect_kernel, len(fields)),
        in_specs=[smem, smem] + [vmem] * (5 + len(fields)),
        out_specs=vmem,
        out_shape=jax.ShapeDtypeStruct((1, rows), F32),
        scratch_shapes=[
            pltpu.VMEM((2 * slots * G, HALF, LANES), BF),
            pltpu.VMEM((rows, LANES), F32),
        ],
        compiler_params=pltpu.CompilerParams(vmem_limit_bytes=VMEM),
        name="detect",
    )(alpha, counts, *fields, pot, plane, across, down, bins)


def detect_tables(beam_total):
    n = np.arange(A)
    table = turn(n[:, None] * n[None, :], A) / A
    cos, sin = table.real, table.imag
    zero = np.zeros((A, A))
    across = np.block([[cos, zero, sin, zero], [zero, cos, zero, sin]])
    rows = np.concatenate([cos, sin], axis=0)
    down = np.concatenate([rows[:, :HALF], rows[:, HALF:]], axis=0)
    signed = np.where(n < A // 2, n, n - A)
    radius = signed[:, None] ** 2 + signed[None, :] ** 2
    width = A // (2 * NDET)
    bins = np.zeros((NDET, A, LANES))
    for d in range(NDET):
        member = (radius >= (width * d) ** 2) & (radius < (width * (d + 1)) ** 2)
        bins[d, :, :A] = member * (A * A / (beam_total * member.sum()))
    return low(across), low(down), bins.astype(np.float32)


def coefficients(tile_ids, beam_rows, shifts):
    across = N // A
    offsets = jnp.arange(G, dtype=jnp.int32)
    spot_y = (tile_ids // across)[:, None] * A + A // 2 + offsets[None, :]
    spot_x = (tile_ids % across)[:, None] * A + A // 2 + 2 * offsets[None, :]
    wave_y = jnp.remainder(F * beam_rows[:, 0], N)[:, None, None]
    wave_x = jnp.remainder(F * beam_rows[:, 1], N)[:, None, None]
    windings = (wave_y * spot_y[None] % N + wave_x * spot_x[None] % N) % N
    phases = shifts[:, None, None] + 2.0 * math.pi / N * windings.astype(F32)
    return jnp.stack([jnp.cos(phases), -jnp.sin(phases)])


def tile_weights(tile_ids, beam_row, k1_pairs):
    across = N // A
    ty = tile_ids // across - beam_row[0]
    tx = tile_ids % across - beam_row[1]
    k1y = jnp.arange(A, dtype=jnp.int32)
    k1x = k1_pairs[:, None] + jnp.arange(2, dtype=jnp.int32)[None, :]
    winding = (
        k1y[None, None, None, :] * ty[None, :, None, None]
        + (k1x.T[:, None, :] * tx[None, :, None])[..., None]
    )
    angle = 2.0 * math.pi / A * (winding % A).astype(F32)
    cos, sin = jnp.cos(angle), jnp.sin(angle)
    upper = jnp.stack([cos, -sin], axis=3)
    under = jnp.stack([sin, cos], axis=3)
    both = jnp.stack([upper, under]).astype(BF)
    return both.reshape(4 * tile_ids.shape[0], k1_pairs.shape[0] * 2 * A)


def plane_waves(beam_index):
    by = jnp.arange(HALF, dtype=jnp.int32)[:, None] + HALF * (jnp.arange(LANES) // A)[None, :]
    bx = jnp.broadcast_to((jnp.arange(LANES, dtype=jnp.int32) % A)[None, :], by.shape)
    row_y = beam_index[:, 0][:, None, None]
    row_x = beam_index[:, 1][:, None, None]
    winding = (row_y * by[None] + row_x * bx[None] + HALF * (row_y + row_x)) % A
    angle = 2.0 * math.pi / A * winding.astype(F32)
    return jnp.stack([jnp.cos(angle), jnp.sin(angle)], axis=1)


def shards(pot_first, pot_second, beam_index, aberration, tile_table, tile_count):
    field_count = lax.axis_size("beam")
    hold_count = lax.axis_size("slab")
    field_pos = lax.axis_index("beam")
    hold_pos = lax.axis_index("slab")
    band_rows = pot_first.shape[0]
    band_tiles = band_rows // A
    width_k = A // field_count
    sheets = width_k // 2
    across = N // A
    beam_total = beam_index.shape[0]
    share = hold_pos % sheets

    section_x = np.stack(
        [
            first_forward_x(
                np.array(
                    [width_k * p + 2 * t + ks for p in range(field_count) for ks in range(2)]
                )
            )
            for t in range(sheets)
        ]
    )
    last_x = np.stack(
        [
            np.stack(
                [
                    last_forward_x([width_k * p + 2 * t, width_k * p + 2 * t + 1])
                    for p in range(field_count)
                ]
            )
            for t in range(sheets)
        ]
    )
    section_y = first_forward_y()
    last_y = np.stack([last_forward_y([2 * q, 2 * q + 1]) for q in range(PAIRS)])
    inverse_y = np.stack([first_inverse_y([2 * q, 2 * q + 1]) for q in range(PAIRS)])
    inverse_x = np.stack(
        [
            np.stack(
                [
                    first_inverse_x([width_k * p + 2 * t, width_k * p + 2 * t + 1])
                    for t in range(sheets)
                ]
            )
            for p in range(field_count)
        ]
    )

    blocks_dev = tile_table.shape[0] // (field_count * hold_count)
    slot_count = tile_table.shape[1]
    own_slots = blocks_dev * slot_count
    table = tile_table.reshape(field_count, hold_count, own_slots)

    def trade(value, axis):
        return lax.all_to_all(value, axis, split_axis=0, concat_axis=0, tiled=True)

    near = min(sheets, 2)
    far = sheets // near

    def swap(value, x):
        return lax.ppermute(value, "slab", [(i, i ^ x) for i in range(hold_count)])

    ids = lax.dynamic_index_in_dim(table, hold_pos, 1, keepdims=False).reshape(-1)
    tile_y, tile_x = ids // across, ids % across
    mine = (tile_y // band_tiles == field_pos).astype(jnp.int32)
    rows = jnp.clip(tile_y - field_pos * band_tiles, 0, band_tiles - 1)

    beam_row = lax.dynamic_index_in_dim(beam_index, hold_pos, 0, keepdims=False)
    pair_ids = share ^ jnp.arange(sheets, dtype=jnp.int32)
    k1_pairs = field_pos * width_k + 2 * pair_ids
    parity = field_pos % 2
    sets = table.reshape(field_count // 2, 2, hold_count, own_slots)
    sets = [lax.dynamic_index_in_dim(sets, pos, 1, keepdims=False) for pos in (1 - parity, parity)]
    weights = jnp.stack([tile_weights(t.reshape(-1), beam_row, k1_pairs) for t in sets])
    row = np.arange(ROWS)
    base = row // PART + A * (K2_LOW + row % PART % K2_COUNT)
    freq_y = np.broadcast_to(base[:, None], (ROWS, LANES)).astype(np.float32)
    lane = np.arange(LANES)
    base = np.where(lane < 2 * K2_COUNT, lane // K2_COUNT + A * (K2_LOW + lane % K2_COUNT), N)
    freq_x = (k1_pairs + F * beam_row[1])[:, None, None] + base.astype(np.int32)
    square_x = (freq_x * freq_x).astype(F32)
    scalars = jnp.stack(
        jnp.broadcast_arrays(field_pos, pair_ids, F * beam_row[0]), axis=-1
    )
    scalars = scalars.astype(jnp.int32).reshape(-1)

    sel = share.reshape(1).astype(jnp.int32)
    received = [[] for _ in range(far)]
    earlier = []
    for part in range(PARTS):
        lines = trade(forward_x(sel, pot_first, section_x, last_x, field_count, part), "beam")
        if lines.shape[3] != LANES:
            ratio = LANES // lines.shape[3]
            lines = lines.reshape(
                field_count // ratio, ratio, HIGH // PARTS, ROWS, SUB // FEW, -1
            )
            lines = lines.transpose(0, 2, 3, 4, 1, 5).reshape(-1, HIGH // PARTS, ROWS, LANES)
        if part:
            crops = crop(rows, tile_x // 2, tile_x % 2, mine, pot_second, earlier[0])
            lines = order(lines, [crops, weights, square_x])
        for f in range(far):
            received[f].append(swap(lines, f * near) if f else lines)
        if part == 0:
            earlier = [forward_y_first(received[f][0], section_y) for f in range(far)]
    crops = order(crops.reshape(field_count, own_slots, HALF, LANES), received[0][1:])
    crops = trade(crops, "beam")

    waves = []
    ready = []
    token = []
    for f in range(far):
        spec = forward_y(received[f][1], section_y, earlier[f], last_y, token + earlier[1:])
        ready.append([spec] + [swap(spec, x) for x in range(1, near)])
        token = [spec, crops]
    for f in range(far):
        waves.append(
            inverse(
                f * near, scalars, ready[f], freq_y, square_x, inverse_y, inverse_x, token
            )
        )
        token = waves[-1:]
    owners = field_count // 2 * hold_count
    groups = [
        [b * hold_count + h for b in range(g, field_count, 2) for h in range(hold_count)]
        for g in range(2)
    ]
    token = []
    partial = []
    for which in range(2):
        for part in range(PARTS):
            partial.append(collect(waves, weights, owners, which, part, token))
            token = partial[-1:]
    fields = []
    for part in range(PARTS):
        passed = lax.ppermute(partial[part], "beam", [(i, i ^ 1) for i in range(field_count)])
        tiles = (partial[PARTS + part].astype(F32) + passed.astype(F32)).astype(BF)
        tiles = lax.all_to_all(
            tiles,
            ("beam", "slab"),
            split_axis=0,
            concat_axis=0,
            axis_index_groups=groups,
            tiled=True,
        )
        tiles = tiles.reshape((field_count // 2, hold_count) + tiles.shape[1:]).astype(F32)
        fields.append(jnp.sum(tiles, axis=0).astype(BF))
    crops = jnp.sum(crops.astype(F32), axis=0).astype(BF)

    own = lax.dynamic_index_in_dim(
        lax.dynamic_index_in_dim(table, field_pos, 0, keepdims=False), hold_pos, 0, keepdims=False
    )
    alpha = coefficients(own, beam_index, aberration).reshape(2, beam_total, own_slots * G)
    first_block = (field_pos * hold_count + hold_pos) * blocks_dev
    counts = lax.dynamic_slice_in_dim(tile_count, first_block, blocks_dev, 0)
    bins = detect_tables(beam_total)
    sums = detect(alpha, counts, fields, crops, plane_waves(beam_index), *bins)
    return sums[0, : own_slots * G * NDET].reshape(blocks_dev, slot_count, G, NDET)


def solution(mesh):
    return jax.shard_map(
        shards,
        mesh=mesh,
        in_specs=(P("beam", None), P("beam", None), P(), P(), P(), P()),
        out_specs=P(("beam", "slab"), None, None, None),
        check_vma=False,
    )
```

```python
import functools
import math

import jax
import jax.numpy as jnp
import ml_dtypes
import numpy as np
from jax import lax
from jax.experimental import pallas as pl
from jax.experimental.pallas import tpu as pltpu
from jax.sharding import PartitionSpec as P

A = 64
N = 4096
F = 64
G = 3
NDET = 16
QMAX = 3
LIMIT = N // 3
K2_LOW = -(LIMIT // A + 1 + QMAX)
K2_COUNT = 2 * (LIMIT // A + 1 + QMAX)
PART = 104
ROWS = 2 * PART
LANES = 128
SUB = 16
FEW = 4
HIGH = A // SUB
HALF = A // 2
PAIRS = A // 2
PARTS = 2
VMEM = 60 * 1024 * 1024
PITCH = A + 1
PITCH_Y = A // PARTS + 1
BF = jnp.bfloat16
F32 = jnp.float32


def low(values):
    return np.asarray(values, dtype=np.float32).astype(ml_dtypes.bfloat16)


def turn(numerator, period):
    return np.exp(2j * np.pi * (numerator % period) / period)


def digits_k2():
    return K2_LOW + np.arange(K2_COUNT)


def spread(table, sub):
    both = np.stack([table.real, table.imag])
    return both[:, :, None, :, None] * np.eye(sub)[None, None, :, None, :]


def real_rows(table):
    return np.block([[table.real, -table.imag], [table.imag, table.real]])


def section_forward(k1):
    n1 = np.arange(A)
    return np.conj(turn(k1[:, None] * n1[None, :], A)) / A


def first_forward_x(k1):
    return low(spread(section_forward(k1), SUB).reshape(2 * len(k1) * SUB, A * SUB))


def first_forward_y():
    table = spread(section_forward(np.arange(A)), FEW).transpose(0, 2, 1, 3, 4)
    return low(table.reshape(2 * A * FEW, A * FEW))


def line_order(lanes):
    order = np.arange(lanes).reshape(-1, SUB // FEW, FEW).transpose(1, 0, 2).reshape(-1)
    out = np.zeros((lanes, lanes))
    out[order, np.arange(lanes)] = 1
    return low(out)


def last_forward_x(k1_pair):
    n2 = np.arange(A)
    out = np.zeros((2, PART, 2, 2, A))
    for ks, k1 in enumerate(k1_pair):
        freq = k1 + A * digits_k2()
        table = np.conj(turn(freq[:, None] * n2[None, :], N)) / A
        block = real_rows(table).reshape(2, K2_COUNT, 2, A)
        out[:, ks * K2_COUNT : (ks + 1) * K2_COUNT, ks] = block
    return low(out.reshape(ROWS, 4 * A))


def last_forward_y(k1_pair):
    n2 = np.arange(A)
    out = np.zeros((ROWS, 2, 2 * A))
    for e, k1 in enumerate(k1_pair):
        freq = k1 + A * digits_k2()
        table = np.conj(turn(freq[:, None] * n2[None, :], N)) / A
        out[e * PART : e * PART + 2 * K2_COUNT, e] = real_rows(table)
    return low(out.reshape(ROWS, 4 * A))


def first_inverse(k1):
    n2 = np.arange(A)
    freq = k1 + A * digits_k2()
    return turn(n2[:, None] * freq[None, :], N) * np.conj(turn(freq * freq, 2 * N))[None, :]


def first_inverse_y(k1_pair):
    out = np.zeros((2, 2 * A, PART))
    for e, k1 in enumerate(k1_pair):
        out[e, :, : 2 * K2_COUNT] = real_rows(first_inverse(k1))
    return low(out)


def first_inverse_x(k1_pair):
    out = np.zeros((2, LANES, 2, 2, A))
    for ks, k1 in enumerate(k1_pair):
        table = first_inverse(k1).T
        rows = slice(ks * K2_COUNT, (ks + 1) * K2_COUNT)
        out[0, rows, 0, ks] = table.real
        out[0, rows, 1, ks] = table.imag
        out[1, rows, 0, ks] = -table.imag
        out[1, rows, 1, ks] = table.real
    return low(out.reshape(2 * LANES, 4 * A))


def sine_cosine(x):
    u = x * x
    s = F32(SIN_FIT[-1])
    for c in SIN_FIT[-2::-1]:
        s = s * u + F32(c)
    q = F32(COS_FIT[-1])
    for c in COS_FIT[-2::-1]:
        q = q * u + F32(c)
    return s * x, q


def fit(function, degree):
    top = 3.1421**2
    nodes = 0.5 * top * (1 - np.cos(np.pi * (np.arange(64) + 0.5) / 64))
    cheb = np.polynomial.chebyshev.Chebyshev.fit(
        nodes, function(np.sqrt(nodes)), degree, domain=[0, top]
    )
    return [float(c) for c in cheb.convert(kind=np.polynomial.Polynomial).coef]


SIN_FIT = fit(lambda x: np.sinc(x / np.pi), 5)
COS_FIT = fit(np.cos, 5)


def dot(a, b):
    return jnp.dot(a, b, preferred_element_type=F32)


def cost(micros):
    return pl.CostEstimate(flops=int(micros * 1.1e9), bytes_accessed=0, transcendentals=0)


def forward_x_kernel(sel, pot, section, last, perm, out, cos_ref, sin_ref, twisted):
    fields = out.shape[0]
    lanes = out.shape[3]
    half = section.shape[1] // 2

    def chunk(t, carry):
        block = pot[:, 0, :, pl.ds(pl.multiple_of(t * LANES, LANES), LANES)]
        values = block.reshape(lanes, LANES).T.astype(F32)
        sine, cosine = sine_cosine(values)
        cos_ref[pl.ds(2 * t, 2)] = cosine.astype(BF).reshape(2, A, lanes)
        sin_ref[pl.ds(2 * t, 2)] = sine.astype(BF).reshape(2, A, lanes)
        return carry

    lax.fori_loop(0, N // LANES, chunk, 0, unroll=4)
    table = section[0]
    for m in range(HIGH):
        span = slice(m * SUB, (m + 1) * SUB)
        part_cos = cos_ref[:, span, :].reshape(A * SUB, lanes)
        part_sin = sin_ref[:, span, :].reshape(A * SUB, lanes)
        if lanes % LANES == 0:
            both = dot(table, jnp.concatenate([part_cos, part_sin], axis=1))
            of_cos, of_sin = both[:, :lanes], both[:, lanes:]
        else:
            of_cos, of_sin = dot(table, part_cos), dot(table, part_sin)
        real = of_cos[:half] - of_sin[half:]
        imag = of_cos[half:] + of_sin[:half]
        twisted[:, m * SUB : (m + 1) * SUB, :] = real.astype(BF).reshape(2 * fields, SUB, lanes)
        twisted[:, A + m * SUB : A + (m + 1) * SUB, :] = imag.astype(BF).reshape(
            2 * fields, SUB, lanes
        )
    for d in range(fields):
        lines = twisted[2 * d : 2 * d + 2].reshape(4 * A, lanes)
        out[d, 0] = dot(dot(last[0, d], lines).astype(BF), perm[...]).astype(BF)


def forward_x(sel, pot, section, last, fields, part):
    groups = pot.shape[0] // A
    lanes = groups * SUB
    steps = HIGH // PARTS
    return pl.pallas_call(
        forward_x_kernel,
        grid_spec=pltpu.PrefetchScalarGridSpec(
            num_scalar_prefetch=1,
            grid=(steps,),
            in_specs=[
                pl.BlockSpec((groups, 1, SUB, N), lambda i, s: (0, part * steps + i, 0, 0)),
                pl.BlockSpec((1,) + section.shape[1:], lambda i, s: (s[0], 0, 0)),
                pl.BlockSpec((1,) + last.shape[1:], lambda i, s: (s[0], 0, 0, 0)),
                pl.BlockSpec((lanes, lanes), lambda i, s: (0, 0)),
            ],
            out_specs=pl.BlockSpec((fields, 1, ROWS, lanes), lambda i, s: (0, i, 0, 0)),
            scratch_shapes=[
                pltpu.VMEM((A, A, lanes), BF),
                pltpu.VMEM((A, A, lanes), BF),
                pltpu.VMEM((2 * fields, 2 * A, lanes), BF),
            ],
        ),
        out_shape=jax.ShapeDtypeStruct((fields, steps, ROWS, lanes), BF),
        compiler_params=pltpu.CompilerParams(vmem_limit_bytes=VMEM),
        cost_estimate=cost(9),
        name="forward_x",
    )(sel, pot.reshape(groups, HIGH, SUB, N), section, last, line_order(lanes))


def first_section_y(lines, section, gathered, held):
    groups, steps = lines.shape[:2]
    span = LANES * FEW // SUB
    zeros = jnp.zeros((LANES - PART, LANES), F32)
    for g in range(groups):
        for h in range(steps):
            block = lines[g, h].astype(F32)
            both = jnp.concatenate([block[:PART], zeros, block[PART:], zeros], axis=0)
            turned = both.astype(BF).T
            columns = slice(2 * h * LANES, 2 * (h + 1) * LANES)
            for a in range(SUB // FEW):
                gathered[a, g * span : (g + 1) * span, columns] = turned[a * span : (a + 1) * span]
    half = A * FEW
    for a in range(SUB // FEW):
        both = dot(section[...], gathered[a])
        for h in range(steps):
            re = slice(2 * h * LANES, (2 * h + 1) * LANES)
            im = slice((2 * h + 1) * LANES, (2 * h + 2) * LANES)
            real = both[:half, re] - both[half:, im]
            imag = both[:half, im] + both[half:, re]
            for b in range(FEW):
                n2 = h * SUB + a * FEW + b
                rows = slice(b * A, (b + 1) * A)
                held[pl.ds(n2, A, stride=PITCH_Y), :] = real[rows]
                held[pl.ds(A * PITCH_Y + n2, A, stride=PITCH_Y), :] = imag[rows]


def first_section_scratch(lines):
    return [
        pltpu.VMEM((SUB // FEW, A * FEW, 2 * lines.shape[1] * LANES), BF),
        pltpu.VMEM(((2 * A + 1) * PITCH_Y, LANES), F32),
    ]


def forward_y_first_kernel(lines, section, twisted, gathered, held):
    first_section_y(lines, section, gathered, held)

    def digit(k, carry):
        for part in range(2):
            start = (part * A + k) * PITCH_Y
            twisted[k, part] = held[pl.ds(start, A // PARTS), :].astype(BF)
        return carry

    lax.fori_loop(0, A, digit, 0, unroll=8)


def forward_y_first(lines, section):
    return pl.pallas_call(
        forward_y_first_kernel,
        grid=(1,),
        in_specs=[
            pl.BlockSpec(lines.shape, lambda i: (0, 0, 0, 0)),
            pl.BlockSpec(section.shape, lambda i: (0, 0)),
        ],
        out_specs=pl.BlockSpec((A, 2, A // PARTS, LANES), lambda i: (0, 0, 0, 0)),
        out_shape=jax.ShapeDtypeStruct((A, 2, A // PARTS, LANES), BF),
        scratch_shapes=first_section_scratch(lines),
        compiler_params=pltpu.CompilerParams(vmem_limit_bytes=VMEM),
        cost_estimate=cost(4),
        name="forward_y_first",
    )(lines, section)


def forward_y_kernel(lines, section, earlier, last, *rest):
    out, gathered, held = rest[-3:]
    step = pl.program_id(0)

    @pl.when(step == 0)
    def _():
        first_section_y(lines, section, gathered, held)

    @pl.when(step > 0)
    def _():
        count = out.shape[0]
        base = (step - 1) * count
        for q in range(count):
            rows = []
            for e in range(2):
                for part in range(2):
                    k = 2 * (base + q) + e
                    rows.append(earlier[k, part])
                    start = (part * A + k) * PITCH_Y
                    rows.append(held[pl.ds(start, A // PARTS), :].astype(BF))
            out[q] = dot(last[q], jnp.concatenate(rows, axis=0)).astype(BF)


def forward_y(lines, section, earlier, last, after):
    steps = 2
    count = PAIRS // steps

    def late(i):
        return (jnp.maximum(i - 1, 0), 0, 0)

    return pl.pallas_call(
        forward_y_kernel,
        grid=(1 + steps,),
        in_specs=[
            pl.BlockSpec(lines.shape, lambda i: (0, 0, 0, 0)),
            pl.BlockSpec(section.shape, lambda i: (0, 0)),
            pl.BlockSpec(earlier.shape, lambda i: (0, 0, 0, 0)),
            pl.BlockSpec((count, ROWS, 4 * A), late),
        ]
        + [pl.BlockSpec(memory_space=pl.ANY)] * len(after),
        out_specs=pl.BlockSpec((count, ROWS, LANES), late),
        out_shape=jax.ShapeDtypeStruct((PAIRS, ROWS, LANES), BF),
        scratch_shapes=first_section_scratch(lines),
        compiler_params=pltpu.CompilerParams(vmem_limit_bytes=VMEM),
        cost_estimate=cost(6),
        name="forward_y",
    )(lines, section, earlier, last, *after)


def order_kernel(value, *rest):
    pass


def order(value, after):
    return pl.pallas_call(
        order_kernel,
        in_specs=[pl.BlockSpec(memory_space=pl.ANY)] * (1 + len(after)),
        out_specs=pl.BlockSpec(memory_space=pl.ANY),
        out_shape=jax.ShapeDtypeStruct(value.shape, value.dtype),
        input_output_aliases={0: 0},
        name="order",
    )(value, *after)


def inverse_kernel(steps, which, near, sel, *refs):
    specs = refs[:near]
    freq_y, square_x, table_y = refs[near : near + 3]
    tables_x = refs[near + 3 : 2 * near + 3]
    out, mid = refs[-2:]
    step = pl.program_id(0)
    count = PAIRS // steps
    each = HALF // steps
    limit = F32(LIMIT * LIMIT)
    whole = 2 * A * PITCH

    @pl.when(step < steps)
    def _():
        def pair(q, carry):
            pair_id = step * count + q
            offset = (2 * pair_id + sel[3 * which + 2]).astype(F32)
            row_freq = freq_y[...] + offset
            row_square = row_freq * row_freq
            values = []
            for x in range(near):
                inside = row_square + square_x[x] <= limit
                values.append(jnp.where(inside, specs[x][q].astype(F32), 0.0))
            for e in range(2):
                half = [v[e * PART : (e + 1) * PART].astype(BF) for v in values]
                half = half[0] if near == 1 else jnp.concatenate(half, axis=1)
                mixed = dot(table_y[q, e], half)
                for x in range(near):
                    for part in range(2):
                        spot = x * whole + part * A * PITCH + 2 * pair_id + e
                        mid[pl.ds(spot, A, stride=PITCH), :] = mixed[
                            part * A : (part + 1) * A, x * LANES : (x + 1) * LANES
                        ]
            return carry

        lax.fori_loop(0, count, pair, 0, unroll=4)

    @pl.when(step >= steps)
    def _():
        def line(i, carry):
            by = (step - steps) * each + i
            for x in range(near):
                rows = []
                for b in range(2):
                    start = x * whole + (by + b * HALF) * PITCH
                    real = mid[pl.ds(start, A), :].astype(BF)
                    imag = mid[pl.ds(start + A * PITCH, A), :].astype(BF)
                    rows.append(jnp.concatenate([real, imag], axis=1))
                product = dot(jnp.concatenate(rows, axis=0), tables_x[x][0, 0]).astype(BF)
                for b in range(2):
                    for part in range(2):
                        low_row = 2 * A * x + A * part
                        out[i, low_row : low_row + A, b * LANES : (b + 1) * LANES] = product[
                            b * A : (b + 1) * A, part * LANES : (part + 1) * LANES
                        ]
            return carry

        lax.fori_loop(0, each, line, 0, unroll=4)


def inverse(which, sel, specs, freq_y, square_x, table_y, table_x, after):
    near = len(specs)
    steps = 2
    count = PAIRS // steps
    each = HALF // steps

    def early(i, s):
        return jnp.minimum(i, steps - 1)

    def table_spec(x):
        return pl.BlockSpec(
            (1, 1) + table_x.shape[2:],
            lambda i, s: (s[3 * (which + x)], s[3 * (which + x) + 1], 0, 0),
        )

    return pl.pallas_call(
        functools.partial(inverse_kernel, steps, which, near),
        grid_spec=pltpu.PrefetchScalarGridSpec(
            num_scalar_prefetch=1,
            grid=(2 * steps,),
            in_specs=[pl.BlockSpec((count, ROWS, LANES), lambda i, s: (early(i, s), 0, 0))] * near
            + [
                pl.BlockSpec((ROWS, LANES), lambda i, s: (0, 0)),
                pl.BlockSpec((near, 1, LANES), lambda i, s: (which // near, 0, 0)),
                pl.BlockSpec((count, 2, 2 * A, PART), lambda i, s: (early(i, s), 0, 0, 0)),
            ]
            + [table_spec(x) for x in range(near)]
            + [pl.BlockSpec(memory_space=pl.ANY)] * len(after),
            out_specs=pl.BlockSpec(
                (each, 2 * A * near, 2 * LANES), lambda i, s: (jnp.maximum(i - steps, 0), 0, 0)
            ),
            scratch_shapes=[pltpu.VMEM(((near * 2 * A + 1) * PITCH, LANES), F32)],
        ),
        out_shape=jax.ShapeDtypeStruct((HALF, 2 * A * near, 2 * LANES), BF),
        compiler_params=pltpu.CompilerParams(vmem_limit_bytes=VMEM),
        cost_estimate=cost(6),
        name="inverse",
    )(sel, *specs, freq_y, square_x, table_y, *[table_x] * near, *after)


def collect_kernel(count, *refs):
    sheets, weights = refs[:count], refs[count]
    out, held = refs[-2:]
    devices, _, slots, lines, _ = out.shape
    each = sheets[0].shape[0]
    step = pl.program_id(0)
    tiles = devices * slots
    pitch = lines + 1
    lane = lax.broadcasted_iota(jnp.int32, (tiles, LANES), 1)
    lower = lane < A

    def line(i, carry):
        stacked = sheets[0][i]
        if len(sheets) > 1:
            stacked = jnp.concatenate([sheet[i] for sheet in sheets], axis=0)
        sums = dot(weights[0], stacked)
        for part in range(2):
            even = sums[2 * part * tiles : (2 * part + 1) * tiles]
            odd = sums[(2 * part + 1) * tiles : (2 * part + 2) * tiles]
            keep = jnp.where(lower, even[:, :LANES], odd[:, LANES:])
            move = jnp.where(lower, even[:, LANES:], odd[:, :LANES])
            total = keep + pltpu.roll(move, A, 1)
            spot = part * tiles * pitch + step * each + i
            held[pl.ds(spot, tiles, stride=pitch), :] = total
        return carry

    lax.fori_loop(0, each, line, 0, unroll=4)

    def device(d, carry):
        for part in range(2):
            for slot in range(slots):
                start = (part * tiles + d * slots + slot) * pitch
                total = held[pl.ds(start, lines), :]
                out[d, part, slot] = total.astype(BF)
        return carry

    @pl.when(step == lines // each - 1)
    def _():
        lax.fori_loop(0, devices, device, 0, unroll=4)


def collect(sheets, weights, devices, which, part, after):
    tiles = weights.shape[1] // 4
    lines = HALF // PARTS
    shape = (devices, 2, tiles // devices, lines, LANES)
    steps = 2
    sheet_spec = pl.BlockSpec(
        (lines // steps,) + sheets[0].shape[1:], lambda i: (part * steps + i, 0, 0)
    )
    block = pl.BlockSpec(shape, lambda i: (0, 0, 0, 0, 0))
    return pl.pallas_call(
        functools.partial(collect_kernel, len(sheets)),
        grid=(steps,),
        in_specs=[sheet_spec] * len(sheets) + [pl.BlockSpec((1,) + weights.shape[1:], lambda i: (which, 0, 0))]
        + [pl.BlockSpec(memory_space=pl.ANY)] * len(after),
        out_specs=block,
        out_shape=jax.ShapeDtypeStruct(shape, BF),
        scratch_shapes=[pltpu.VMEM(((2 * tiles + 1) * (lines + 1), LANES), F32)],
        compiler_params=pltpu.CompilerParams(vmem_limit_bytes=VMEM),
        cost_estimate=cost(0.05),
        name="collect",
    )(*sheets, weights, *after)


def crop_kernel(rows, cols, odd, mine, pot, after, out, held, sems):
    slots = out.shape[0]

    def copy(i):
        return pltpu.make_async_copy(
            pot.at[
                pl.ds(pl.multiple_of(rows[i] * A, A), A),
                pl.ds(pl.multiple_of(cols[i] * LANES, LANES), LANES),
            ],
            held.at[i],
            sems.at[i],
        )

    def begin(i, carry):
        copy(i).start()
        return carry

    def finish(i, carry):
        copy(i).wait()
        block = held[i].astype(F32)
        block = jnp.where(odd[i] == 1, pltpu.roll(block, A, 1), block)
        lane = lax.broadcasted_iota(jnp.int32, (HALF, LANES), 1)
        packed = jnp.where(lane < A, block[:HALF], pltpu.roll(block[HALF:], A, 1))
        out[i] = jnp.where(mine[i] == 1, packed, 0.0).astype(BF)
        return carry

    lax.fori_loop(0, slots, begin, 0)
    lax.fori_loop(0, slots, finish, 0)


def crop(rows, cols, odd, mine, pot, after):
    slots = rows.shape[0]
    return pl.pallas_call(
        crop_kernel,
        in_specs=[pl.BlockSpec(memory_space=pltpu.SMEM)] * 4
        + [pl.BlockSpec(memory_space=pl.ANY)] * 2,
        out_specs=pl.BlockSpec(memory_space=pltpu.VMEM),
        out_shape=jax.ShapeDtypeStruct((slots, HALF, LANES), BF),
        scratch_shapes=[pltpu.VMEM((slots, A, LANES), BF), pltpu.SemaphoreType.DMA((slots,))],
        compiler_params=pltpu.CompilerParams(vmem_limit_bytes=VMEM),
        cost_estimate=cost(7),
        name="crop",
    )(rows, cols, odd, mine, pot, after)


def detect_kernel(parts, alpha, counts, *refs):
    fields = refs[:parts]
    pot, plane, across, down, bins, out, lines, held = refs[parts:]
    beams, _, slots = fields[0].shape[:3]
    for s in range(slots):
        waves = []
        for j in range(beams):
            re, im = (
                jnp.concatenate([half[j, part, s] for half in fields], axis=0).astype(F32)
                for part in range(2)
            )
            cos, sin = plane[j, 0], plane[j, 1]
            waves.append((re * cos - im * sin, re * sin + im * cos))
        turned, level = sine_cosine(pot[s].astype(F32))
        for g in range(G):
            real = jnp.zeros((HALF, LANES), F32)
            imag = jnp.zeros((HALF, LANES), F32)
            for j in range(beams):
                cos, sin = alpha[0, j, s * G + g], alpha[1, j, s * G + g]
                re, im = waves[j]
                real = real + cos * re - sin * im
                imag = imag + cos * im + sin * re
            lines[2 * (s * G + g)] = (real * level - imag * turned).astype(BF)
            lines[2 * (s * G + g) + 1] = (real * turned + imag * level).astype(BF)
    total = slots * G
    first = dot(lines[...].reshape(2 * total * HALF, LANES), across[...])
    first = first.reshape(total, 2, HALF, 2 * LANES)
    real = (first[:, 0, :, :LANES] + first[:, 1, :, LANES:]).astype(BF)
    imag = (first[:, 1, :, :LANES] - first[:, 0, :, LANES:]).astype(BF)
    lane = lax.broadcasted_iota(jnp.int32, (A, LANES), 1)
    for i in range(total):
        both = jnp.concatenate([real[i], imag[i]], axis=1)
        mixed = dot(down[...], both)
        even, odd = mixed[: 2 * A], mixed[2 * A :]
        re_cos = even[:A, :LANES] + pltpu.roll(odd[:A, :LANES], A, 1)
        re_sin = even[A:, :LANES] + pltpu.roll(odd[A:, :LANES], A, 1)
        im_cos = even[:A, LANES:] + pltpu.roll(odd[:A, LANES:], A, 1)
        im_sin = even[A:, LANES:] + pltpu.roll(odd[A:, LANES:], A, 1)
        re = re_cos + im_sin
        im = im_cos - re_sin
        power = jnp.where(lane < A, re * re + im * im, 0.0)
        sums = jnp.sum(power[None] * bins[...], axis=1)
        block, slot = divmod(i // G, slots // counts.shape[0])
        active = slot < counts[block]
        held[i * NDET : (i + 1) * NDET, :] = jnp.where(active, sums, 0.0)
    out[...] = jnp.sum(held[...].T, axis=0, keepdims=True)


def detect(alpha, counts, fields, pot, plane, across, down, bins):
    slots = fields[0].shape[2]
    rows = -(-slots * G * NDET // LANES) * LANES
    smem = pl.BlockSpec(memory_space=pltpu.SMEM)
    vmem = pl.BlockSpec(memory_space=pltpu.VMEM)
    return pl.pallas_call(
        functools.partial(detect_kernel, len(fields)),
        in_specs=[smem, smem] + [vmem] * (5 + len(fields)),
        out_specs=vmem,
        out_shape=jax.ShapeDtypeStruct((1, rows), F32),
        scratch_shapes=[
            pltpu.VMEM((2 * slots * G, HALF, LANES), BF),
            pltpu.VMEM((rows, LANES), F32),
        ],
        compiler_params=pltpu.CompilerParams(vmem_limit_bytes=VMEM),
        name="detect",
    )(alpha, counts, *fields, pot, plane, across, down, bins)


def detect_tables(beam_total):
    n = np.arange(A)
    table = turn(n[:, None] * n[None, :], A) / A
    cos, sin = table.real, table.imag
    zero = np.zeros((A, A))
    across = np.block([[cos, zero, sin, zero], [zero, cos, zero, sin]])
    rows = np.concatenate([cos, sin], axis=0)
    down = np.concatenate([rows[:, :HALF], rows[:, HALF:]], axis=0)
    signed = np.where(n < A // 2, n, n - A)
    radius = signed[:, None] ** 2 + signed[None, :] ** 2
    width = A // (2 * NDET)
    bins = np.zeros((NDET, A, LANES))
    for d in range(NDET):
        member = (radius >= (width * d) ** 2) & (radius < (width * (d + 1)) ** 2)
        bins[d, :, :A] = member * (A * A / (beam_total * member.sum()))
    return low(across), low(down), bins.astype(np.float32)


def coefficients(tile_ids, beam_rows, shifts):
    across = N // A
    offsets = jnp.arange(G, dtype=jnp.int32)
    spot_y = (tile_ids // across)[:, None] * A + A // 2 + offsets[None, :]
    spot_x = (tile_ids % across)[:, None] * A + A // 2 + 2 * offsets[None, :]
    wave_y = jnp.remainder(F * beam_rows[:, 0], N)[:, None, None]
    wave_x = jnp.remainder(F * beam_rows[:, 1], N)[:, None, None]
    windings = (wave_y * spot_y[None] % N + wave_x * spot_x[None] % N) % N
    phases = shifts[:, None, None] + 2.0 * math.pi / N * windings.astype(F32)
    return jnp.stack([jnp.cos(phases), -jnp.sin(phases)])


def tile_weights(tile_ids, beam_row, k1_pairs):
    across = N // A
    ty = tile_ids // across - beam_row[0]
    tx = tile_ids % across - beam_row[1]
    k1y = jnp.arange(A, dtype=jnp.int32)
    k1x = k1_pairs[:, None] + jnp.arange(2, dtype=jnp.int32)[None, :]
    winding = (
        k1y[None, None, None, :] * ty[None, :, None, None]
        + (k1x.T[:, None, :] * tx[None, :, None])[..., None]
    )
    angle = 2.0 * math.pi / A * (winding % A).astype(F32)
    cos, sin = jnp.cos(angle), jnp.sin(angle)
    upper = jnp.stack([cos, -sin], axis=3)
    under = jnp.stack([sin, cos], axis=3)
    both = jnp.stack([upper, under]).astype(BF)
    return both.reshape(4 * tile_ids.shape[0], k1_pairs.shape[0] * 2 * A)


def plane_waves(beam_index):
    by = jnp.arange(HALF, dtype=jnp.int32)[:, None] + HALF * (jnp.arange(LANES) // A)[None, :]
    bx = jnp.broadcast_to((jnp.arange(LANES, dtype=jnp.int32) % A)[None, :], by.shape)
    row_y = beam_index[:, 0][:, None, None]
    row_x = beam_index[:, 1][:, None, None]
    winding = (row_y * by[None] + row_x * bx[None] + HALF * (row_y + row_x)) % A
    angle = 2.0 * math.pi / A * winding.astype(F32)
    return jnp.stack([jnp.cos(angle), jnp.sin(angle)], axis=1)


def shards(pot_first, pot_second, beam_index, aberration, tile_table, tile_count):
    field_count = lax.axis_size("beam")
    hold_count = lax.axis_size("slab")
    field_pos = lax.axis_index("beam")
    hold_pos = lax.axis_index("slab")
    band_rows = pot_first.shape[0]
    band_tiles = band_rows // A
    width_k = A // field_count
    sheets = width_k // 2
    across = N // A
    beam_total = beam_index.shape[0]
    share = hold_pos % sheets

    section_x = np.stack(
        [
            first_forward_x(
                np.array(
                    [width_k * p + 2 * t + ks for p in range(field_count) for ks in range(2)]
                )
            )
            for t in range(sheets)
        ]
    )
    last_x = np.stack(
        [
            np.stack(
                [
                    last_forward_x([width_k * p + 2 * t, width_k * p + 2 * t + 1])
                    for p in range(field_count)
                ]
            )
            for t in range(sheets)
        ]
    )
    section_y = first_forward_y()
    last_y = np.stack([last_forward_y([2 * q, 2 * q + 1]) for q in range(PAIRS)])
    inverse_y = np.stack([first_inverse_y([2 * q, 2 * q + 1]) for q in range(PAIRS)])
    inverse_x = np.stack(
        [
            np.stack(
                [
                    first_inverse_x([width_k * p + 2 * t, width_k * p + 2 * t + 1])
                    for t in range(sheets)
                ]
            )
            for p in range(field_count)
        ]
    )

    blocks_dev = tile_table.shape[0] // (field_count * hold_count)
    slot_count = tile_table.shape[1]
    own_slots = blocks_dev * slot_count
    table = tile_table.reshape(field_count, hold_count, own_slots)

    def trade(value, axis):
        return lax.all_to_all(value, axis, split_axis=0, concat_axis=0, tiled=True)

    near = min(sheets, 2)
    far = sheets // near

    def swap(value, x):
        return lax.ppermute(value, "slab", [(i, i ^ x) for i in range(hold_count)])

    ids = lax.dynamic_index_in_dim(table, hold_pos, 1, keepdims=False).reshape(-1)
    tile_y, tile_x = ids // across, ids % across
    mine = (tile_y // band_tiles == field_pos).astype(jnp.int32)
    rows = jnp.clip(tile_y - field_pos * band_tiles, 0, band_tiles - 1)

    beam_row = lax.dynamic_index_in_dim(beam_index, hold_pos, 0, keepdims=False)
    pair_ids = share ^ jnp.arange(sheets, dtype=jnp.int32)
    k1_pairs = field_pos * width_k + 2 * pair_ids
    near_bit, far_bit = (jnp.stack([1 - v, v]) for v in (field_pos % 2, field_pos // 2 % 2))
    corners = table.reshape(field_count // 4, 2, 2, hold_count, own_slots)
    corners = corners.transpose(2, 1, 0, 3, 4)[near_bit][:, far_bit]
    sets = [corners[0], corners[1], corners[:, 0], corners[:, 1]]
    weights = jnp.stack([tile_weights(t.reshape(-1), beam_row, k1_pairs) for t in sets])
    row = np.arange(ROWS)
    base = row // PART + A * (K2_LOW + row % PART % K2_COUNT)
    freq_y = np.broadcast_to(base[:, None], (ROWS, LANES)).astype(np.float32)
    lane = np.arange(LANES)
    base = np.where(lane < 2 * K2_COUNT, lane // K2_COUNT + A * (K2_LOW + lane % K2_COUNT), N)
    freq_x = (k1_pairs + F * beam_row[1])[:, None, None] + base.astype(np.int32)
    square_x = (freq_x * freq_x).astype(F32)
    scalars = jnp.stack(
        jnp.broadcast_arrays(field_pos, pair_ids, F * beam_row[0]), axis=-1
    )
    scalars = scalars.astype(jnp.int32).reshape(-1)

    sel = share.reshape(1).astype(jnp.int32)
    received = [[] for _ in range(far)]
    earlier = []
    for part in range(PARTS):
        lines = trade(forward_x(sel, pot_first, section_x, last_x, field_count, part), "beam")
        if lines.shape[3] != LANES:
            ratio = LANES // lines.shape[3]
            lines = lines.reshape(
                field_count // ratio, ratio, HIGH // PARTS, ROWS, SUB // FEW, -1
            )
            lines = lines.transpose(0, 2, 3, 4, 1, 5).reshape(-1, HIGH // PARTS, ROWS, LANES)
        if part:
            crops = crop(rows, tile_x // 2, tile_x % 2, mine, pot_second, earlier[0])
            lines = order(lines, [crops, weights, square_x])
        for f in range(far):
            received[f].append(swap(lines, f * near) if f else lines)
        if part == 0:
            earlier = [forward_y_first(received[f][0], section_y) for f in range(far)]
    crops = order(crops.reshape(field_count, own_slots, HALF, LANES), received[0][1:])
    crops = trade(crops, "beam")

    waves = []
    ready = []
    token = []
    for f in range(far):
        spec = forward_y(received[f][1], section_y, earlier[f], last_y, token + earlier[1:])
        ready.append([spec] + [swap(spec, x) for x in range(1, near)])
        token = [spec, crops]
    for f in range(far):
        waves.append(
            inverse(
                f * near, scalars, ready[f], freq_y, square_x, inverse_y, inverse_x, token
            )
        )
        token = waves[-1:]
    owners = field_count // 2 * hold_count
    token = []
    partial = []
    for which in range(2):
        for part in range(PARTS):
            index = 2 * part + which
            partial.append(collect(waves, weights, owners, index, part, token))
            token = partial[-1:]

    def hop(value, bit):
        pairs = [(i, i ^ (1 << bit)) for i in range(field_count)]
        return lax.ppermute(value, "beam", pairs).astype(F32)

    totals = []
    arrived = [hop(partial[part], part) for part in range(PARTS)]
    for part in range(PARTS):
        own = partial[PARTS + part].astype(F32) + arrived[part]
        rest = own[: owners // 2].astype(BF)
        totals.append(own[owners // 2 :] + hop(rest, 1 - part))
    tiles = jnp.concatenate(totals, axis=3).astype(BF)
    groups = [
        [b * hold_count + h for b in range(g, field_count, 4) for h in range(hold_count)]
        for g in range(4)
    ]
    tiles = lax.all_to_all(
        tiles,
        ("beam", "slab"),
        split_axis=0,
        concat_axis=0,
        axis_index_groups=groups,
        tiled=True,
    )
    tiles = tiles.reshape((field_count // 4, hold_count) + tiles.shape[1:]).astype(F32)
    fields = [jnp.sum(tiles, axis=0).astype(BF)]
    crops = jnp.sum(crops.astype(F32), axis=0).astype(BF)

    own = lax.dynamic_index_in_dim(
        lax.dynamic_index_in_dim(table, field_pos, 0, keepdims=False), hold_pos, 0, keepdims=False
    )
    alpha = coefficients(own, beam_index, aberration).reshape(2, beam_total, own_slots * G)
    first_block = (field_pos * hold_count + hold_pos) * blocks_dev
    counts = lax.dynamic_slice_in_dim(tile_count, first_block, blocks_dev, 0)
    bins = detect_tables(beam_total)
    sums = detect(alpha, counts, fields, crops, plane_waves(beam_index), *bins)
    return sums[0, : own_slots * G * NDET].reshape(blocks_dev, slot_count, G, NDET)


def solution(mesh):
    return jax.shard_map(
        shards,
        mesh=mesh,
        in_specs=(P("beam", None), P("beam", None), P(), P(), P(), P()),
        out_specs=P(("beam", "slab"), None, None, None),
        check_vma=False,
    )
```

```python
import functools
import math

import jax
import jax.numpy as jnp
import ml_dtypes
import numpy as np
from jax import lax
from jax.experimental import pallas as pl
from jax.experimental.pallas import tpu as pltpu
from jax.sharding import PartitionSpec as P

A = 64
N = 4096
F = 64
G = 3
NDET = 16
QMAX = 3
LIMIT = N // 3
K2_LOW = -(LIMIT // A + 1 + QMAX)
K2_COUNT = 2 * (LIMIT // A + 1 + QMAX)
PART = 104
ROWS = 2 * PART
LANES = 128
SUB = 16
FEW = 4
HIGH = A // SUB
HALF = A // 2
PAIRS = A // 2
PARTS = 2
VMEM = 60 * 1024 * 1024
PITCH = A + 1
PITCH_Y = A // PARTS + 1
BF = jnp.bfloat16
F32 = jnp.float32


def low(values):
    return np.asarray(values, dtype=np.float32).astype(ml_dtypes.bfloat16)


def turn(numerator, period):
    return np.exp(2j * np.pi * (numerator % period) / period)


def digits_k2():
    return K2_LOW + np.arange(K2_COUNT)


def spread(table, sub):
    both = np.stack([table.real, table.imag])
    return both[:, :, None, :, None] * np.eye(sub)[None, None, :, None, :]


def real_rows(table):
    return np.block([[table.real, -table.imag], [table.imag, table.real]])


def section_forward(k1):
    n1 = np.arange(A)
    return np.conj(turn(k1[:, None] * n1[None, :], A)) / A


def first_forward_x(k1):
    return low(spread(section_forward(k1), SUB).reshape(2 * len(k1) * SUB, A * SUB))


def first_forward_y():
    table = spread(section_forward(np.arange(A)), FEW).transpose(0, 2, 1, 3, 4)
    return low(table.reshape(2 * A * FEW, A * FEW))


def line_order(lanes):
    order = np.arange(lanes).reshape(-1, SUB // FEW, FEW).transpose(1, 0, 2).reshape(-1)
    out = np.zeros((lanes, lanes))
    out[order, np.arange(lanes)] = 1
    return low(out)


def last_forward_x(k1_pair):
    n2 = np.arange(A)
    out = np.zeros((2, PART, 2, 2, A))
    for ks, k1 in enumerate(k1_pair):
        freq = k1 + A * digits_k2()
        table = np.conj(turn(freq[:, None] * n2[None, :], N)) / A
        block = real_rows(table).reshape(2, K2_COUNT, 2, A)
        out[:, ks * K2_COUNT : (ks + 1) * K2_COUNT, ks] = block
    return low(out.reshape(ROWS, 4 * A))


def last_forward_y(k1_pair):
    n2 = np.arange(A)
    out = np.zeros((ROWS, 2, 2 * A))
    for e, k1 in enumerate(k1_pair):
        freq = k1 + A * digits_k2()
        table = np.conj(turn(freq[:, None] * n2[None, :], N)) / A
        out[e * PART : e * PART + 2 * K2_COUNT, e] = real_rows(table)
    return low(out.reshape(ROWS, 4 * A))


def first_inverse(k1):
    n2 = np.arange(A)
    freq = k1 + A * digits_k2()
    return turn(n2[:, None] * freq[None, :], N) * np.conj(turn(freq * freq, 2 * N))[None, :]


def first_inverse_y(k1_pair):
    out = np.zeros((2, 2 * A, PART))
    for e, k1 in enumerate(k1_pair):
        out[e, :, : 2 * K2_COUNT] = real_rows(first_inverse(k1))
    return low(out)


def first_inverse_x(k1_pair):
    out = np.zeros((2, LANES, 2, 2, A))
    for ks, k1 in enumerate(k1_pair):
        table = first_inverse(k1).T
        rows = slice(ks * K2_COUNT, (ks + 1) * K2_COUNT)
        out[0, rows, 0, ks] = table.real
        out[0, rows, 1, ks] = table.imag
        out[1, rows, 0, ks] = -table.imag
        out[1, rows, 1, ks] = table.real
    return low(out.reshape(2 * LANES, 4 * A))


def cosine(u):
    q = F32(COS_FIT[-1])
    for c in COS_FIT[-2::-1]:
        q = q * u + F32(c)
    return q


def sine_cosine(x):
    u = x * x
    s = F32(SIN_FIT[-1])
    for c in SIN_FIT[-2::-1]:
        s = s * u + F32(c)
    return s * x, cosine(u)


def fit(function, degree):
    top = 3.1421**2
    nodes = 0.5 * top * (1 - np.cos(np.pi * (np.arange(64) + 0.5) / 64))
    cheb = np.polynomial.chebyshev.Chebyshev.fit(
        nodes, function(np.sqrt(nodes)), degree, domain=[0, top]
    )
    return [float(c) for c in cheb.convert(kind=np.polynomial.Polynomial).coef]


SIN_FIT = fit(lambda x: np.sinc(x / np.pi), 5)
COS_FIT = fit(np.cos, 5)


def dot(a, b):
    return jnp.dot(a, b, preferred_element_type=F32)


def cost(micros):
    return pl.CostEstimate(flops=int(micros * 1.1e9), bytes_accessed=0, transcendentals=0)


def forward_x_kernel(sel, pot, section, last, perm, out, cos_ref, sin_ref, twisted):
    fields = out.shape[0]
    lanes = out.shape[3]
    half = section.shape[1] // 2

    def chunk(t, carry):
        block = pot[:, 0, :, pl.ds(pl.multiple_of(t * LANES, LANES), LANES)]
        values = block.reshape(lanes, LANES).T.astype(F32)
        sine, cosine = sine_cosine(values)
        cos_ref[pl.ds(2 * t, 2)] = cosine.astype(BF).reshape(2, A, lanes)
        sin_ref[pl.ds(2 * t, 2)] = sine.astype(BF).reshape(2, A, lanes)
        return carry

    lax.fori_loop(0, N // LANES, chunk, 0, unroll=4)
    table = section[0]
    for m in range(HIGH):
        span = slice(m * SUB, (m + 1) * SUB)
        part_cos = cos_ref[:, span, :].reshape(A * SUB, lanes)
        part_sin = sin_ref[:, span, :].reshape(A * SUB, lanes)
        if lanes % LANES == 0:
            both = dot(table, jnp.concatenate([part_cos, part_sin], axis=1))
            of_cos, of_sin = both[:, :lanes], both[:, lanes:]
        else:
            of_cos, of_sin = dot(table, part_cos), dot(table, part_sin)
        real = of_cos[:half] - of_sin[half:]
        imag = of_cos[half:] + of_sin[:half]
        twisted[:, m * SUB : (m + 1) * SUB, :] = real.astype(BF).reshape(2 * fields, SUB, lanes)
        twisted[:, A + m * SUB : A + (m + 1) * SUB, :] = imag.astype(BF).reshape(
            2 * fields, SUB, lanes
        )
    for d in range(fields):
        lines = twisted[2 * d : 2 * d + 2].reshape(4 * A, lanes)
        out[d, 0] = dot(dot(last[0, d], lines).astype(BF), perm[...]).astype(BF)


def forward_x(sel, pot, section, last, fields, part):
    groups = pot.shape[0] // A
    lanes = groups * SUB
    steps = HIGH // PARTS
    return pl.pallas_call(
        forward_x_kernel,
        grid_spec=pltpu.PrefetchScalarGridSpec(
            num_scalar_prefetch=1,
            grid=(steps,),
            in_specs=[
                pl.BlockSpec((groups, 1, SUB, N), lambda i, s: (0, part * steps + i, 0, 0)),
                pl.BlockSpec((1,) + section.shape[1:], lambda i, s: (s[0], 0, 0)),
                pl.BlockSpec((1,) + last.shape[1:], lambda i, s: (s[0], 0, 0, 0)),
                pl.BlockSpec((lanes, lanes), lambda i, s: (0, 0)),
            ],
            out_specs=pl.BlockSpec((fields, 1, ROWS, lanes), lambda i, s: (0, i, 0, 0)),
            scratch_shapes=[
                pltpu.VMEM((A, A, lanes), BF),
                pltpu.VMEM((A, A, lanes), BF),
                pltpu.VMEM((2 * fields, 2 * A, lanes), BF),
            ],
        ),
        out_shape=jax.ShapeDtypeStruct((fields, steps, ROWS, lanes), BF),
        compiler_params=pltpu.CompilerParams(vmem_limit_bytes=VMEM),
        cost_estimate=cost(9),
        name="forward_x",
    )(sel, pot.reshape(groups, HIGH, SUB, N), section, last, line_order(lanes))


def first_section_y(lines, section, gathered, held):
    groups, steps = lines.shape[:2]
    span = LANES * FEW // SUB
    zeros = jnp.zeros((LANES - PART, LANES), F32)
    for g in range(groups):
        for h in range(steps):
            block = lines[g, h].astype(F32)
            both = jnp.concatenate([block[:PART], zeros, block[PART:], zeros], axis=0)
            turned = both.astype(BF).T
            columns = slice(2 * h * LANES, 2 * (h + 1) * LANES)
            for a in range(SUB // FEW):
                gathered[a, g * span : (g + 1) * span, columns] = turned[a * span : (a + 1) * span]
    half = A * FEW
    for a in range(SUB // FEW):
        both = dot(section[...], gathered[a])
        for h in range(steps):
            re = slice(2 * h * LANES, (2 * h + 1) * LANES)
            im = slice((2 * h + 1) * LANES, (2 * h + 2) * LANES)
            real = both[:half, re] - both[half:, im]
            imag = both[:half, im] + both[half:, re]
            for b in range(FEW):
                n2 = h * SUB + a * FEW + b
                rows = slice(b * A, (b + 1) * A)
                held[pl.ds(n2, A, stride=PITCH_Y), :] = real[rows]
                held[pl.ds(A * PITCH_Y + n2, A, stride=PITCH_Y), :] = imag[rows]


def first_section_scratch(lines):
    return [
        pltpu.VMEM((SUB // FEW, A * FEW, 2 * lines.shape[1] * LANES), BF),
        pltpu.VMEM(((2 * A + 1) * PITCH_Y, LANES), F32),
    ]


def forward_y_first_kernel(lines, section, twisted, gathered, held):
    first_section_y(lines, section, gathered, held)

    def digit(k, carry):
        for part in range(2):
            start = (part * A + k) * PITCH_Y
            twisted[k, part] = held[pl.ds(start, A // PARTS), :].astype(BF)
        return carry

    lax.fori_loop(0, A, digit, 0, unroll=8)


def forward_y_first(lines, section):
    return pl.pallas_call(
        forward_y_first_kernel,
        grid=(1,),
        in_specs=[
            pl.BlockSpec(lines.shape, lambda i: (0, 0, 0, 0)),
            pl.BlockSpec(section.shape, lambda i: (0, 0)),
        ],
        out_specs=pl.BlockSpec((A, 2, A // PARTS, LANES), lambda i: (0, 0, 0, 0)),
        out_shape=jax.ShapeDtypeStruct((A, 2, A // PARTS, LANES), BF),
        scratch_shapes=first_section_scratch(lines),
        compiler_params=pltpu.CompilerParams(vmem_limit_bytes=VMEM),
        cost_estimate=cost(4),
        name="forward_y_first",
    )(lines, section)


def forward_y_kernel(lines, section, earlier, last, *rest):
    out, gathered, held = rest[-3:]
    step = pl.program_id(0)

    @pl.when(step == 0)
    def _():
        first_section_y(lines, section, gathered, held)

    @pl.when(step > 0)
    def _():
        count = out.shape[0]
        base = (step - 1) * count
        for q in range(count):
            rows = []
            for e in range(2):
                for part in range(2):
                    k = 2 * (base + q) + e
                    rows.append(earlier[k, part])
                    start = (part * A + k) * PITCH_Y
                    rows.append(held[pl.ds(start, A // PARTS), :].astype(BF))
            out[q] = dot(last[q], jnp.concatenate(rows, axis=0)).astype(BF)


def forward_y(lines, section, earlier, last, after):
    steps = 2
    count = PAIRS // steps

    def late(i):
        return (jnp.maximum(i - 1, 0), 0, 0)

    return pl.pallas_call(
        forward_y_kernel,
        grid=(1 + steps,),
        in_specs=[
            pl.BlockSpec(lines.shape, lambda i: (0, 0, 0, 0)),
            pl.BlockSpec(section.shape, lambda i: (0, 0)),
            pl.BlockSpec(earlier.shape, lambda i: (0, 0, 0, 0)),
            pl.BlockSpec((count, ROWS, 4 * A), late),
        ]
        + [pl.BlockSpec(memory_space=pl.ANY)] * len(after),
        out_specs=pl.BlockSpec((count, ROWS, LANES), late),
        out_shape=jax.ShapeDtypeStruct((PAIRS, ROWS, LANES), BF),
        scratch_shapes=first_section_scratch(lines),
        compiler_params=pltpu.CompilerParams(vmem_limit_bytes=VMEM),
        cost_estimate=cost(6),
        name="forward_y",
    )(lines, section, earlier, last, *after)


def order_kernel(value, *rest):
    pass


def order(value, after):
    return pl.pallas_call(
        order_kernel,
        in_specs=[pl.BlockSpec(memory_space=pl.ANY)] * (1 + len(after)),
        out_specs=pl.BlockSpec(memory_space=pl.ANY),
        out_shape=jax.ShapeDtypeStruct(value.shape, value.dtype),
        input_output_aliases={0: 0},
        name="order",
    )(value, *after)


def inverse_kernel(steps, which, near, sel, *refs):
    specs = refs[:near]
    freq_y, square_x, table_y = refs[near : near + 3]
    tables_x = refs[near + 3 : 2 * near + 3]
    out, mid = refs[-2:]
    step = pl.program_id(0)
    count = PAIRS // steps
    each = HALF // steps
    limit = F32(LIMIT * LIMIT)
    whole = 2 * A * PITCH

    @pl.when(step < steps)
    def _():
        def pair(q, carry):
            pair_id = step * count + q
            offset = (2 * pair_id + sel[3 * which + 2]).astype(F32)
            row_freq = freq_y[...] + offset
            row_square = row_freq * row_freq
            values = []
            for x in range(near):
                inside = row_square + square_x[x] <= limit
                values.append(jnp.where(inside, specs[x][q].astype(F32), 0.0))
            for e in range(2):
                half = [v[e * PART : (e + 1) * PART].astype(BF) for v in values]
                half = half[0] if near == 1 else jnp.concatenate(half, axis=1)
                mixed = dot(table_y[q, e], half)
                for x in range(near):
                    for part in range(2):
                        spot = x * whole + part * A * PITCH + 2 * pair_id + e
                        mid[pl.ds(spot, A, stride=PITCH), :] = mixed[
                            part * A : (part + 1) * A, x * LANES : (x + 1) * LANES
                        ]
            return carry

        lax.fori_loop(0, count, pair, 0, unroll=4)

    @pl.when(step >= steps)
    def _():
        def line(i, carry):
            by = (step - steps) * each + i
            for x in range(near):
                rows = []
                for b in range(2):
                    start = x * whole + (by + b * HALF) * PITCH
                    real = mid[pl.ds(start, A), :].astype(BF)
                    imag = mid[pl.ds(start + A * PITCH, A), :].astype(BF)
                    rows.append(jnp.concatenate([real, imag], axis=1))
                product = dot(jnp.concatenate(rows, axis=0), tables_x[x][0, 0]).astype(BF)
                for b in range(2):
                    for part in range(2):
                        low_row = 2 * A * x + A * part
                        out[i, low_row : low_row + A, b * LANES : (b + 1) * LANES] = product[
                            b * A : (b + 1) * A, part * LANES : (part + 1) * LANES
                        ]
            return carry

        lax.fori_loop(0, each, line, 0, unroll=4)


def inverse(which, sel, specs, freq_y, square_x, table_y, table_x, after):
    near = len(specs)
    steps = 2
    count = PAIRS // steps
    each = HALF // steps

    def early(i, s):
        return jnp.minimum(i, steps - 1)

    def table_spec(x):
        return pl.BlockSpec(
            (1, 1) + table_x.shape[2:],
            lambda i, s: (s[3 * (which + x)], s[3 * (which + x) + 1], 0, 0),
        )

    return pl.pallas_call(
        functools.partial(inverse_kernel, steps, which, near),
        grid_spec=pltpu.PrefetchScalarGridSpec(
            num_scalar_prefetch=1,
            grid=(2 * steps,),
            in_specs=[pl.BlockSpec((count, ROWS, LANES), lambda i, s: (early(i, s), 0, 0))] * near
            + [
                pl.BlockSpec((ROWS, LANES), lambda i, s: (0, 0)),
                pl.BlockSpec((near, 1, LANES), lambda i, s: (which // near, 0, 0)),
                pl.BlockSpec((count, 2, 2 * A, PART), lambda i, s: (early(i, s), 0, 0, 0)),
            ]
            + [table_spec(x) for x in range(near)]
            + [pl.BlockSpec(memory_space=pl.ANY)] * len(after),
            out_specs=pl.BlockSpec(
                (each, 2 * A * near, 2 * LANES), lambda i, s: (jnp.maximum(i - steps, 0), 0, 0)
            ),
            scratch_shapes=[pltpu.VMEM(((near * 2 * A + 1) * PITCH, LANES), F32)],
        ),
        out_shape=jax.ShapeDtypeStruct((HALF, 2 * A * near, 2 * LANES), BF),
        compiler_params=pltpu.CompilerParams(vmem_limit_bytes=VMEM),
        cost_estimate=cost(6),
        name="inverse",
    )(sel, *specs, freq_y, square_x, table_y, *[table_x] * near, *after)


def collect_kernel(count, k1_pairs, *refs):
    sheets, places = refs[:count], refs[count]
    outs = refs[-2 - PARTS : -2]
    weights, held = refs[-2:]
    devices, _, slots, lines, _ = outs[0].shape
    each = sheets[0].shape[0]
    steps = lines // each
    step = pl.program_id(0) % steps
    part_id = pl.program_id(0) // steps
    tiles = devices * slots
    pitch = lines + 1
    lane = lax.broadcasted_iota(jnp.int32, (tiles, LANES), 1)
    lower = lane < A

    @pl.when(step == 0)
    def _():
        quarter = A // 4
        base = places[0, 0, 0] * (lane % A) + quarter * (lane // A)
        for x in range(weights.shape[1] // LANES):
            for ks in range(2):
                winding = base + places[0, 0, 1] * (k1_pairs[x] + ks)
                for part in range(2):
                    angle = ((winding - quarter * part) & (A - 1)) - A // 2
                    angle = angle.astype(F32) * F32(2.0 * math.pi / A)
                    rows = slice((2 * part + ks) * tiles, (2 * part + ks + 1) * tiles)
                    weights[rows, x * LANES : (x + 1) * LANES] = (-cosine(angle * angle)).astype(BF)

    def line(i, carry):
        stacked = sheets[0][i]
        if len(sheets) > 1:
            stacked = jnp.concatenate([sheet[i] for sheet in sheets], axis=0)
        sums = dot(weights[...], stacked)
        for part in range(2):
            even = sums[2 * part * tiles : (2 * part + 1) * tiles]
            odd = sums[(2 * part + 1) * tiles : (2 * part + 2) * tiles]
            keep = jnp.where(lower, even[:, :LANES], odd[:, LANES:])
            move = jnp.where(lower, even[:, LANES:], odd[:, :LANES])
            total = keep + pltpu.roll(move, A, 1)
            spot = part * tiles * pitch + step * each + i
            held[pl.ds(spot, tiles, stride=pitch), :] = total
        return carry

    lax.fori_loop(0, each, line, 0, unroll=4)

    for p, out in enumerate(outs):

        def device(d, carry, out=out):
            for part in range(2):
                for slot in range(slots):
                    start = (part * tiles + d * slots + slot) * pitch
                    out[d, part, slot] = held[pl.ds(start, lines), :].astype(BF)
            return carry

        @pl.when((step == steps - 1) & (part_id == p))
        def _(device=device):
            lax.fori_loop(0, devices, device, 0, unroll=4)


def collect(sheets, k1_pairs, places, devices, which, after):
    tiles = places.shape[3]
    lines = HALF // PARTS
    steps = 2
    shape = (devices, 2, tiles // devices, lines, LANES)
    depth = sum(sheet.shape[1] for sheet in sheets)
    sheet_spec = pl.BlockSpec((lines // steps,) + sheets[0].shape[1:], lambda i, s: (i, 0, 0))
    block = pl.BlockSpec(shape, lambda i, s: (0, 0, 0, 0, 0))
    return pl.pallas_call(
        functools.partial(collect_kernel, len(sheets)),
        grid_spec=pltpu.PrefetchScalarGridSpec(
            num_scalar_prefetch=1,
            grid=(PARTS * steps,),
            in_specs=[sheet_spec] * len(sheets)
            + [
                pl.BlockSpec(
                    (1, 1) + places.shape[2:], lambda i, s: (which, i // steps, 0, 0, 0)
                )
            ]
            + [pl.BlockSpec(memory_space=pl.ANY)] * len(after),
            out_specs=[block] * PARTS,
            scratch_shapes=[
                pltpu.VMEM((4 * tiles, depth), BF),
                pltpu.VMEM(((2 * tiles + 1) * (lines + 1), LANES), F32),
            ],
        ),
        out_shape=[jax.ShapeDtypeStruct(shape, BF)] * PARTS,
        compiler_params=pltpu.CompilerParams(vmem_limit_bytes=VMEM),
        cost_estimate=cost(0.05),
        name="collect",
    )(k1_pairs, *sheets, places, *after)


def crop_kernel(rows, cols, odd, mine, pot, after, out, held, sems):
    slots = out.shape[0]

    def copy(i):
        return pltpu.make_async_copy(
            pot.at[
                pl.ds(pl.multiple_of(rows[i] * A, A), A),
                pl.ds(pl.multiple_of(cols[i] * LANES, LANES), LANES),
            ],
            held.at[i],
            sems.at[i],
        )

    def begin(i, carry):
        copy(i).start()
        return carry

    def finish(i, carry):
        copy(i).wait()
        block = held[i].astype(F32)
        block = jnp.where(odd[i] == 1, pltpu.roll(block, A, 1), block)
        lane = lax.broadcasted_iota(jnp.int32, (HALF, LANES), 1)
        packed = jnp.where(lane < A, block[:HALF], pltpu.roll(block[HALF:], A, 1))
        out[i] = jnp.where(mine[i] == 1, packed, 0.0).astype(BF)
        return carry

    lax.fori_loop(0, slots, begin, 0)
    lax.fori_loop(0, slots, finish, 0)


def crop(rows, cols, odd, mine, pot, after):
    slots = rows.shape[0]
    return pl.pallas_call(
        crop_kernel,
        in_specs=[pl.BlockSpec(memory_space=pltpu.SMEM)] * 4
        + [pl.BlockSpec(memory_space=pl.ANY)] * 2,
        out_specs=pl.BlockSpec(memory_space=pltpu.VMEM),
        out_shape=jax.ShapeDtypeStruct((slots, HALF, LANES), BF),
        scratch_shapes=[pltpu.VMEM((slots, A, LANES), BF), pltpu.SemaphoreType.DMA((slots,))],
        compiler_params=pltpu.CompilerParams(vmem_limit_bytes=VMEM),
        cost_estimate=cost(7),
        name="crop",
    )(rows, cols, odd, mine, pot, after)


def detect_kernel(parts, alpha, counts, *refs):
    fields = refs[:parts]
    pot, plane, across, down, bins, out, lines, held = refs[parts:]
    beams, _, slots = fields[0].shape[:3]
    for s in range(slots):
        waves = []
        for j in range(beams):
            re, im = (
                jnp.concatenate([half[j, part, s] for half in fields], axis=0).astype(F32)
                for part in range(2)
            )
            cos, sin = plane[j, 0], plane[j, 1]
            waves.append((re * cos - im * sin, re * sin + im * cos))
        turned, level = sine_cosine(pot[s].astype(F32))
        for g in range(G):
            real = jnp.zeros((HALF, LANES), F32)
            imag = jnp.zeros((HALF, LANES), F32)
            for j in range(beams):
                cos, sin = alpha[0, j, s * G + g], alpha[1, j, s * G + g]
                re, im = waves[j]
                real = real + cos * re - sin * im
                imag = imag + cos * im + sin * re
            lines[2 * (s * G + g)] = (real * level - imag * turned).astype(BF)
            lines[2 * (s * G + g) + 1] = (real * turned + imag * level).astype(BF)
    total = slots * G
    first = dot(lines[...].reshape(2 * total * HALF, LANES), across[...])
    first = first.reshape(total, 2, HALF, 2 * LANES)
    real = (first[:, 0, :, :LANES] + first[:, 1, :, LANES:]).astype(BF)
    imag = (first[:, 1, :, :LANES] - first[:, 0, :, LANES:]).astype(BF)
    lane = lax.broadcasted_iota(jnp.int32, (A, LANES), 1)
    for i in range(total):
        both = jnp.concatenate([real[i], imag[i]], axis=1)
        mixed = dot(down[...], both)
        even, odd = mixed[: 2 * A], mixed[2 * A :]
        re_cos = even[:A, :LANES] + pltpu.roll(odd[:A, :LANES], A, 1)
        re_sin = even[A:, :LANES] + pltpu.roll(odd[A:, :LANES], A, 1)
        im_cos = even[:A, LANES:] + pltpu.roll(odd[:A, LANES:], A, 1)
        im_sin = even[A:, LANES:] + pltpu.roll(odd[A:, LANES:], A, 1)
        re = re_cos + im_sin
        im = im_cos - re_sin
        power = jnp.where(lane < A, re * re + im * im, 0.0)
        sums = jnp.sum(power[None] * bins[...], axis=1)
        block, slot = divmod(i // G, slots // counts.shape[0])
        active = slot < counts[block]
        held[i * NDET : (i + 1) * NDET, :] = jnp.where(active, sums, 0.0)
    out[...] = jnp.sum(held[...].T, axis=0, keepdims=True)


def detect(alpha, counts, fields, pot, plane, across, down, bins):
    slots = fields[0].shape[2]
    rows = -(-slots * G * NDET // LANES) * LANES
    smem = pl.BlockSpec(memory_space=pltpu.SMEM)
    vmem = pl.BlockSpec(memory_space=pltpu.VMEM)
    return pl.pallas_call(
        functools.partial(detect_kernel, len(fields)),
        in_specs=[smem, smem] + [vmem] * (5 + len(fields)),
        out_specs=vmem,
        out_shape=jax.ShapeDtypeStruct((1, rows), F32),
        scratch_shapes=[
            pltpu.VMEM((2 * slots * G, HALF, LANES), BF),
            pltpu.VMEM((rows, LANES), F32),
        ],
        compiler_params=pltpu.CompilerParams(vmem_limit_bytes=VMEM),
        name="detect",
    )(alpha, counts, *fields, pot, plane, across, down, bins)


def detect_tables(beam_total):
    n = np.arange(A)
    table = turn(n[:, None] * n[None, :], A) / A
    cos, sin = table.real, table.imag
    zero = np.zeros((A, A))
    across = np.block([[cos, zero, sin, zero], [zero, cos, zero, sin]])
    rows = np.concatenate([cos, sin], axis=0)
    down = np.concatenate([rows[:, :HALF], rows[:, HALF:]], axis=0)
    signed = np.where(n < A // 2, n, n - A)
    radius = signed[:, None] ** 2 + signed[None, :] ** 2
    width = A // (2 * NDET)
    bins = np.zeros((NDET, A, LANES))
    for d in range(NDET):
        member = (radius >= (width * d) ** 2) & (radius < (width * (d + 1)) ** 2)
        bins[d, :, :A] = member * (A * A / (beam_total * member.sum()))
    return low(across), low(down), bins.astype(np.float32)


def coefficients(tile_ids, beam_rows, shifts):
    across = N // A
    offsets = jnp.arange(G, dtype=jnp.int32)
    spot_y = (tile_ids // across)[:, None] * A + A // 2 + offsets[None, :]
    spot_x = (tile_ids % across)[:, None] * A + A // 2 + 2 * offsets[None, :]
    wave_y = jnp.remainder(F * beam_rows[:, 0], N)[:, None, None]
    wave_x = jnp.remainder(F * beam_rows[:, 1], N)[:, None, None]
    windings = (wave_y * spot_y[None] % N + wave_x * spot_x[None] % N) % N
    phases = shifts[:, None, None] + 2.0 * math.pi / N * windings.astype(F32)
    return jnp.stack([jnp.cos(phases), -jnp.sin(phases)])


def plane_waves(beam_index):
    by = jnp.arange(HALF, dtype=jnp.int32)[:, None] + HALF * (jnp.arange(LANES) // A)[None, :]
    bx = jnp.broadcast_to((jnp.arange(LANES, dtype=jnp.int32) % A)[None, :], by.shape)
    row_y = beam_index[:, 0][:, None, None]
    row_x = beam_index[:, 1][:, None, None]
    winding = (row_y * by[None] + row_x * bx[None] + HALF * (row_y + row_x)) % A
    angle = 2.0 * math.pi / A * winding.astype(F32)
    return jnp.stack([jnp.cos(angle), jnp.sin(angle)], axis=1)


def shards(pot_first, pot_second, beam_index, aberration, tile_table, tile_count):
    field_count = lax.axis_size("beam")
    hold_count = lax.axis_size("slab")
    field_pos = lax.axis_index("beam")
    hold_pos = lax.axis_index("slab")
    band_rows = pot_first.shape[0]
    band_tiles = band_rows // A
    width_k = A // field_count
    sheets = width_k // 2
    across = N // A
    beam_total = beam_index.shape[0]
    share = hold_pos % sheets

    section_x = np.stack(
        [
            first_forward_x(
                np.array(
                    [width_k * p + 2 * t + ks for p in range(field_count) for ks in range(2)]
                )
            )
            for t in range(sheets)
        ]
    )
    last_x = np.stack(
        [
            np.stack(
                [
                    last_forward_x([width_k * p + 2 * t, width_k * p + 2 * t + 1])
                    for p in range(field_count)
                ]
            )
            for t in range(sheets)
        ]
    )
    section_y = first_forward_y()
    last_y = np.stack([last_forward_y([2 * q, 2 * q + 1]) for q in range(PAIRS)])
    inverse_y = np.stack([first_inverse_y([2 * q, 2 * q + 1]) for q in range(PAIRS)])
    inverse_x = np.stack(
        [
            np.stack(
                [
                    first_inverse_x([width_k * p + 2 * t, width_k * p + 2 * t + 1])
                    for t in range(sheets)
                ]
            )
            for p in range(field_count)
        ]
    )

    blocks_dev = tile_table.shape[0] // (field_count * hold_count)
    slot_count = tile_table.shape[1]
    own_slots = blocks_dev * slot_count
    table = tile_table.reshape(field_count, hold_count, own_slots)

    def trade(value, axis):
        return lax.all_to_all(value, axis, split_axis=0, concat_axis=0, tiled=True)

    near = min(sheets, 2)
    far = sheets // near

    def swap(value, x):
        return lax.ppermute(value, "slab", [(i, i ^ x) for i in range(hold_count)])

    ids = lax.dynamic_index_in_dim(table, hold_pos, 1, keepdims=False).reshape(-1)
    tile_y, tile_x = ids // across, ids % across
    mine = (tile_y // band_tiles == field_pos).astype(jnp.int32)
    rows = jnp.clip(tile_y - field_pos * band_tiles, 0, band_tiles - 1)

    beam_row = lax.dynamic_index_in_dim(beam_index, hold_pos, 0, keepdims=False)
    pair_ids = share ^ jnp.arange(sheets, dtype=jnp.int32)
    k1_pairs = field_pos * width_k + 2 * pair_ids
    near_bit, far_bit = (jnp.stack([1 - v, v]) for v in (field_pos % 2, field_pos // 2 % 2))
    corners = table.reshape(field_count // 4, 2, 2, hold_count, own_slots)
    corners = corners.transpose(2, 1, 0, 3, 4)[near_bit][:, far_bit]
    sets = jnp.stack([corners, corners.transpose(1, 0, 2, 3, 4)], axis=1)
    sets = sets.reshape(2, PARTS, -1)
    places = jnp.stack([sets // across - beam_row[0], sets % across - beam_row[1]], axis=2)
    places = jnp.broadcast_to(places[..., None], places.shape + (LANES,))
    row = np.arange(ROWS)
    base = row // PART + A * (K2_LOW + row % PART % K2_COUNT)
    freq_y = np.broadcast_to(base[:, None], (ROWS, LANES)).astype(np.float32)
    lane = np.arange(LANES)
    base = np.where(lane < 2 * K2_COUNT, lane // K2_COUNT + A * (K2_LOW + lane % K2_COUNT), N)
    freq_x = (k1_pairs + F * beam_row[1])[:, None, None] + base.astype(np.int32)
    square_x = (freq_x * freq_x).astype(F32)
    scalars = jnp.stack(
        jnp.broadcast_arrays(field_pos, pair_ids, F * beam_row[0]), axis=-1
    )
    scalars = scalars.astype(jnp.int32).reshape(-1)

    sel = share.reshape(1).astype(jnp.int32)
    received = [[] for _ in range(far)]
    earlier = []
    for part in range(PARTS):
        lines = trade(forward_x(sel, pot_first, section_x, last_x, field_count, part), "beam")
        if lines.shape[3] != LANES:
            ratio = LANES // lines.shape[3]
            lines = lines.reshape(
                field_count // ratio, ratio, HIGH // PARTS, ROWS, SUB // FEW, -1
            )
            lines = lines.transpose(0, 2, 3, 4, 1, 5).reshape(-1, HIGH // PARTS, ROWS, LANES)
        if part:
            crops = crop(rows, tile_x // 2, tile_x % 2, mine, pot_second, earlier[0])
            lines = order(lines, [crops, square_x] + [r[0] for r in received[1:]])
        for f in range(far):
            received[f].append(swap(lines, f * near) if f else lines)
        if part == 0:
            earlier = [forward_y_first(received[f][0], section_y) for f in range(far)]
    waves = []
    token = []
    for f in range(far):
        spec = forward_y(received[f][1], section_y, earlier[f], last_y, token)
        ready = [spec] + [swap(spec, x) for x in range(1, near)]
        if f == 0:
            token = [spec]
        waves.append(
            inverse(
                f * near, scalars, ready, freq_y, square_x, inverse_y, inverse_x, token + earlier[1:]
            )
        )
        token = waves[-1:]
    crops = order(crops.reshape(field_count, own_slots, HALF, LANES), [spec])
    crops = trade(crops, "beam")
    owners = field_count // 2 * hold_count
    other = collect(waves, k1_pairs, places, owners, 0, [crops])
    partial = other + collect(waves, k1_pairs, places, owners, 1, other[:1])

    def hop(value, bit):
        pairs = [(i, i ^ (1 << bit)) for i in range(field_count)]
        return lax.ppermute(value, "beam", pairs).astype(F32)

    totals = []
    arrived = [hop(partial[part], part) for part in range(PARTS)]
    for part in range(PARTS):
        own = partial[PARTS + part].astype(F32) + arrived[part]
        rest = own[: owners // 2].astype(BF)
        totals.append(own[owners // 2 :] + hop(rest, 1 - part))
    tiles = jnp.concatenate(totals, axis=3).astype(BF)
    groups = [
        [b * hold_count + h for b in range(g, field_count, 4) for h in range(hold_count)]
        for g in range(4)
    ]
    tiles = lax.all_to_all(
        tiles,
        ("beam", "slab"),
        split_axis=0,
        concat_axis=0,
        axis_index_groups=groups,
        tiled=True,
    )
    tiles = tiles.reshape((field_count // 4, hold_count) + tiles.shape[1:]).astype(F32)
    fields = [jnp.sum(tiles, axis=0).astype(BF)]
    crops = jnp.sum(crops.astype(F32), axis=0).astype(BF)

    own = lax.dynamic_index_in_dim(
        lax.dynamic_index_in_dim(table, field_pos, 0, keepdims=False), hold_pos, 0, keepdims=False
    )
    alpha = coefficients(own, beam_index, aberration).reshape(2, beam_total, own_slots * G)
    first_block = (field_pos * hold_count + hold_pos) * blocks_dev
    counts = lax.dynamic_slice_in_dim(tile_count, first_block, blocks_dev, 0)
    bins = detect_tables(beam_total)
    sums = detect(alpha, counts, fields, crops, plane_waves(beam_index), *bins)
    return sums[0, : own_slots * G * NDET].reshape(blocks_dev, slot_count, G, NDET)


def solution(mesh):
    return jax.shard_map(
        shards,
        mesh=mesh,
        in_specs=(P("beam", None), P("beam", None), P(), P(), P(), P()),
        out_specs=P(("beam", "slab"), None, None, None),
        check_vma=False,
    )
```

```python
import functools
import math

import jax
import jax.numpy as jnp
import ml_dtypes
import numpy as np
from jax import lax
from jax.experimental import pallas as pl
from jax.experimental.pallas import tpu as pltpu
from jax.sharding import PartitionSpec as P

A = 64
N = 4096
F = 64
G = 3
NDET = 16
QMAX = 3
LIMIT = N // 3
K2_LOW = -(LIMIT // A + 1 + QMAX)
K2_COUNT = 2 * (LIMIT // A + 1 + QMAX)
PART = 104
ROWS = 2 * PART
LANES = 128
SUB = 16
FEW = 4
HIGH = A // SUB
HALF = A // 2
PAIRS = A // 2
PARTS = 2
VMEM = 60 * 1024 * 1024
PITCH = A + 1
PITCH_Y = A // PARTS + 1
SMALL = pl.CostEstimate(flops=1 << 20, bytes_accessed=0, transcendentals=0)
BF = jnp.bfloat16
F32 = jnp.float32


def low(values):
    return np.asarray(values, dtype=np.float32).astype(ml_dtypes.bfloat16)


def turn(numerator, period):
    return np.exp(2j * np.pi * (numerator % period) / period)


def digits_k2():
    return K2_LOW + np.arange(K2_COUNT)


def spread(table, sub):
    both = np.stack([table.real, table.imag])
    return both[:, :, None, :, None] * np.eye(sub)[None, None, :, None, :]


def real_rows(table):
    return np.block([[table.real, -table.imag], [table.imag, table.real]])


def section_forward(k1):
    n1 = np.arange(A)
    return np.conj(turn(k1[:, None] * n1[None, :], A)) / A


def first_forward_x(k1):
    return low(spread(section_forward(k1), SUB).reshape(2 * len(k1) * SUB, A * SUB))


def first_forward_y():
    table = spread(section_forward(np.arange(A)), FEW).transpose(0, 2, 1, 3, 4)
    return low(table.reshape(2 * A * FEW, A * FEW))


def line_order(lanes):
    order = np.arange(lanes).reshape(-1, SUB // FEW, FEW).transpose(1, 0, 2).reshape(-1)
    out = np.zeros((lanes, lanes))
    out[order, np.arange(lanes)] = 1
    return low(out)


def last_forward_x(k1_pair):
    n2 = np.arange(A)
    out = np.zeros((2, PART, 2, 2, A))
    for ks, k1 in enumerate(k1_pair):
        freq = k1 + A * digits_k2()
        table = np.conj(turn(freq[:, None] * n2[None, :], N)) / A
        block = real_rows(table).reshape(2, K2_COUNT, 2, A)
        out[:, ks * K2_COUNT : (ks + 1) * K2_COUNT, ks] = block
    return low(out.reshape(ROWS, 4 * A))


def last_forward_y(k1_pair):
    n2 = np.arange(A)
    out = np.zeros((ROWS, 2, 2 * A))
    for e, k1 in enumerate(k1_pair):
        freq = k1 + A * digits_k2()
        table = np.conj(turn(freq[:, None] * n2[None, :], N)) / A
        out[e * PART : e * PART + 2 * K2_COUNT, e] = real_rows(table)
    return low(out.reshape(ROWS, 4 * A))


def first_inverse(k1):
    n2 = np.arange(A)
    freq = k1 + A * digits_k2()
    return turn(n2[:, None] * freq[None, :], N) * np.conj(turn(freq * freq, 2 * N))[None, :]


def first_inverse_y(k1_pair):
    out = np.zeros((2, 2 * A, PART))
    for e, k1 in enumerate(k1_pair):
        out[e, :, : 2 * K2_COUNT] = real_rows(first_inverse(k1))
    return low(out)


def first_inverse_x(k1_pair):
    out = np.zeros((2, LANES, 2, 2, A))
    for ks, k1 in enumerate(k1_pair):
        table = first_inverse(k1).T
        rows = slice(ks * K2_COUNT, (ks + 1) * K2_COUNT)
        out[0, rows, 0, ks] = table.real
        out[0, rows, 1, ks] = table.imag
        out[1, rows, 0, ks] = -table.imag
        out[1, rows, 1, ks] = table.real
    return low(out.reshape(2 * LANES, 4 * A))


def cosine(u):
    q = F32(COS_FIT[-1])
    for c in COS_FIT[-2::-1]:
        q = q * u + F32(c)
    return q


def sine_cosine(x):
    u = x * x
    s = F32(SIN_FIT[-1])
    for c in SIN_FIT[-2::-1]:
        s = s * u + F32(c)
    return s * x, cosine(u)


def fit(function, degree):
    top = 3.1421**2
    nodes = 0.5 * top * (1 - np.cos(np.pi * (np.arange(64) + 0.5) / 64))
    cheb = np.polynomial.chebyshev.Chebyshev.fit(
        nodes, function(np.sqrt(nodes)), degree, domain=[0, top]
    )
    return [float(c) for c in cheb.convert(kind=np.polynomial.Polynomial).coef]


SIN_FIT = fit(lambda x: np.sinc(x / np.pi), 5)
COS_FIT = fit(np.cos, 5)


def dot(a, b):
    return jnp.dot(a, b, preferred_element_type=F32)


def forward_x_kernel(sel, pot, section, last, perm, out, cos_ref, sin_ref, twisted):
    fields = out.shape[0]
    lanes = out.shape[3]
    half = section.shape[1] // 2

    def chunk(t, carry):
        block = pot[:, 0, :, pl.ds(pl.multiple_of(t * LANES, LANES), LANES)]
        values = block.reshape(lanes, LANES).T.astype(F32)
        sine, cosine = sine_cosine(values)
        cos_ref[pl.ds(2 * t, 2)] = cosine.astype(BF).reshape(2, A, lanes)
        sin_ref[pl.ds(2 * t, 2)] = sine.astype(BF).reshape(2, A, lanes)
        return carry

    lax.fori_loop(0, N // LANES, chunk, 0, unroll=4)
    table = section[0]
    for m in range(HIGH):
        span = slice(m * SUB, (m + 1) * SUB)
        part_cos = cos_ref[:, span, :].reshape(A * SUB, lanes)
        part_sin = sin_ref[:, span, :].reshape(A * SUB, lanes)
        if lanes % LANES == 0:
            both = dot(table, jnp.concatenate([part_cos, part_sin], axis=1))
            of_cos, of_sin = both[:, :lanes], both[:, lanes:]
        else:
            of_cos, of_sin = dot(table, part_cos), dot(table, part_sin)
        real = of_cos[:half] - of_sin[half:]
        imag = of_cos[half:] + of_sin[:half]
        twisted[:, m * SUB : (m + 1) * SUB, :] = real.astype(BF).reshape(2 * fields, SUB, lanes)
        twisted[:, A + m * SUB : A + (m + 1) * SUB, :] = imag.astype(BF).reshape(
            2 * fields, SUB, lanes
        )
    for d in range(fields):
        lines = twisted[2 * d : 2 * d + 2].reshape(4 * A, lanes)
        out[d, 0] = dot(dot(last[0, d], lines).astype(BF), perm[...]).astype(BF)


def forward_x(sel, pot, section, last, fields, part):
    groups = pot.shape[0] // A
    lanes = groups * SUB
    steps = HIGH // PARTS
    return pl.pallas_call(
        forward_x_kernel,
        grid_spec=pltpu.PrefetchScalarGridSpec(
            num_scalar_prefetch=1,
            grid=(steps,),
            in_specs=[
                pl.BlockSpec((groups, 1, SUB, N), lambda i, s: (0, part * steps + i, 0, 0)),
                pl.BlockSpec((1,) + section.shape[1:], lambda i, s: (s[0], 0, 0)),
                pl.BlockSpec((1,) + last.shape[1:], lambda i, s: (s[0], 0, 0, 0)),
                pl.BlockSpec((lanes, lanes), lambda i, s: (0, 0)),
            ],
            out_specs=pl.BlockSpec((fields, 1, ROWS, lanes), lambda i, s: (0, i, 0, 0)),
            scratch_shapes=[
                pltpu.VMEM((A, A, lanes), BF),
                pltpu.VMEM((A, A, lanes), BF),
                pltpu.VMEM((2 * fields, 2 * A, lanes), BF),
            ],
        ),
        out_shape=jax.ShapeDtypeStruct((fields, steps, ROWS, lanes), BF),
        compiler_params=pltpu.CompilerParams(vmem_limit_bytes=VMEM),
        cost_estimate=SMALL,
        name="forward_x",
    )(sel, pot.reshape(groups, HIGH, SUB, N), section, last, line_order(lanes))


def first_section_y(lines, section, gathered, held):
    groups, steps = lines.shape[:2]
    span = LANES * FEW // SUB
    zeros = jnp.zeros((LANES - PART, LANES), F32)
    for g in range(groups):
        for h in range(steps):
            block = lines[g, h].astype(F32)
            both = jnp.concatenate([block[:PART], zeros, block[PART:], zeros], axis=0)
            turned = both.astype(BF).T
            columns = slice(2 * h * LANES, 2 * (h + 1) * LANES)
            for a in range(SUB // FEW):
                gathered[a, g * span : (g + 1) * span, columns] = turned[a * span : (a + 1) * span]
    half = A * FEW
    for a in range(SUB // FEW):
        both = dot(section[...], gathered[a])
        for h in range(steps):
            re = slice(2 * h * LANES, (2 * h + 1) * LANES)
            im = slice((2 * h + 1) * LANES, (2 * h + 2) * LANES)
            real = both[:half, re] - both[half:, im]
            imag = both[:half, im] + both[half:, re]
            for b in range(FEW):
                n2 = h * SUB + a * FEW + b
                rows = slice(b * A, (b + 1) * A)
                held[pl.ds(n2, A, stride=PITCH_Y), :] = real[rows]
                held[pl.ds(A * PITCH_Y + n2, A, stride=PITCH_Y), :] = imag[rows]


def first_section_scratch(lines):
    return [
        pltpu.VMEM((SUB // FEW, A * FEW, 2 * lines.shape[1] * LANES), BF),
        pltpu.VMEM(((2 * A + 1) * PITCH_Y, LANES), F32),
    ]


def forward_y_first_kernel(lines, section, twisted, gathered, held):
    first_section_y(lines, section, gathered, held)

    def digit(k, carry):
        for part in range(2):
            start = (part * A + k) * PITCH_Y
            twisted[k, part] = held[pl.ds(start, A // PARTS), :].astype(BF)
        return carry

    lax.fori_loop(0, A, digit, 0, unroll=8)


def forward_y_first(lines, section):
    return pl.pallas_call(
        forward_y_first_kernel,
        grid=(1,),
        in_specs=[
            pl.BlockSpec(lines.shape, lambda i: (0, 0, 0, 0)),
            pl.BlockSpec(section.shape, lambda i: (0, 0)),
        ],
        out_specs=pl.BlockSpec((A, 2, A // PARTS, LANES), lambda i: (0, 0, 0, 0)),
        out_shape=jax.ShapeDtypeStruct((A, 2, A // PARTS, LANES), BF),
        scratch_shapes=first_section_scratch(lines),
        compiler_params=pltpu.CompilerParams(vmem_limit_bytes=VMEM),
        cost_estimate=SMALL,
        name="forward_y_first",
    )(lines, section)


def forward_y_kernel(lines, section, earlier, last, *rest):
    out, gathered, held = rest[-3:]
    step = pl.program_id(0)

    @pl.when(step == 0)
    def _():
        first_section_y(lines, section, gathered, held)

    @pl.when(step > 0)
    def _():
        count = out.shape[0]
        base = (step - 1) * count
        for q in range(count):
            rows = []
            for e in range(2):
                for part in range(2):
                    k = 2 * (base + q) + e
                    rows.append(earlier[k, part])
                    start = (part * A + k) * PITCH_Y
                    rows.append(held[pl.ds(start, A // PARTS), :].astype(BF))
            out[q] = dot(last[q], jnp.concatenate(rows, axis=0)).astype(BF)


def forward_y(lines, section, earlier, last, after):
    steps = 2
    count = PAIRS // steps

    def late(i):
        return (jnp.maximum(i - 1, 0), 0, 0)

    return pl.pallas_call(
        forward_y_kernel,
        grid=(1 + steps,),
        in_specs=[
            pl.BlockSpec(lines.shape, lambda i: (0, 0, 0, 0)),
            pl.BlockSpec(section.shape, lambda i: (0, 0)),
            pl.BlockSpec(earlier.shape, lambda i: (0, 0, 0, 0)),
            pl.BlockSpec((count, ROWS, 4 * A), late),
        ]
        + [pl.BlockSpec(memory_space=pl.ANY)] * len(after),
        out_specs=pl.BlockSpec((count, ROWS, LANES), late),
        out_shape=jax.ShapeDtypeStruct((PAIRS, ROWS, LANES), BF),
        scratch_shapes=first_section_scratch(lines),
        compiler_params=pltpu.CompilerParams(vmem_limit_bytes=VMEM),
        cost_estimate=SMALL,
        name="forward_y",
    )(lines, section, earlier, last, *after)


def order_kernel(value, *rest):
    pass


def order(value, after):
    return pl.pallas_call(
        order_kernel,
        in_specs=[pl.BlockSpec(memory_space=pl.ANY)] * (1 + len(after)),
        out_specs=pl.BlockSpec(memory_space=pl.ANY),
        out_shape=jax.ShapeDtypeStruct(value.shape, value.dtype),
        input_output_aliases={0: 0},
        name="order",
    )(value, *after)


def inverse_kernel(steps, which, near, sel, *refs):
    specs = refs[:near]
    freq_y, square_x, table_y = refs[near : near + 3]
    tables_x = refs[near + 3 : 2 * near + 3]
    out, mid = refs[-2:]
    step = pl.program_id(0)
    count = PAIRS // steps
    each = HALF // steps
    limit = F32(LIMIT * LIMIT)
    whole = 2 * A * PITCH

    @pl.when(step < steps)
    def _():
        def pair(q, carry):
            pair_id = step * count + q
            offset = (2 * pair_id + sel[3 * which + 2]).astype(F32)
            row_freq = freq_y[...] + offset
            row_square = row_freq * row_freq
            values = []
            for x in range(near):
                inside = row_square + square_x[x] <= limit
                values.append(jnp.where(inside, specs[x][q].astype(F32), 0.0))
            for e in range(2):
                half = [v[e * PART : (e + 1) * PART].astype(BF) for v in values]
                half = half[0] if near == 1 else jnp.concatenate(half, axis=1)
                mixed = dot(table_y[q, e], half)
                for x in range(near):
                    for part in range(2):
                        spot = x * whole + part * A * PITCH + 2 * pair_id + e
                        mid[pl.ds(spot, A, stride=PITCH), :] = mixed[
                            part * A : (part + 1) * A, x * LANES : (x + 1) * LANES
                        ]
            return carry

        lax.fori_loop(0, count, pair, 0, unroll=4)

    @pl.when(step >= steps)
    def _():
        def line(i, carry):
            by = (step - steps) * each + i
            for x in range(near):
                rows = []
                for b in range(2):
                    start = x * whole + (by + b * HALF) * PITCH
                    real = mid[pl.ds(start, A), :].astype(BF)
                    imag = mid[pl.ds(start + A * PITCH, A), :].astype(BF)
                    rows.append(jnp.concatenate([real, imag], axis=1))
                product = dot(jnp.concatenate(rows, axis=0), tables_x[x][0, 0]).astype(BF)
                for b in range(2):
                    for part in range(2):
                        low_row = 2 * A * x + A * part
                        out[i, low_row : low_row + A, b * LANES : (b + 1) * LANES] = product[
                            b * A : (b + 1) * A, part * LANES : (part + 1) * LANES
                        ]
            return carry

        lax.fori_loop(0, each, line, 0, unroll=4)


def inverse(which, sel, specs, freq_y, square_x, table_y, table_x, after):
    near = len(specs)
    steps = 2
    count = PAIRS // steps
    each = HALF // steps

    def early(i, s):
        return jnp.minimum(i, steps - 1)

    def table_spec(x):
        return pl.BlockSpec(
            (1, 1) + table_x.shape[2:],
            lambda i, s: (s[3 * (which + x)], s[3 * (which + x) + 1], 0, 0),
        )

    return pl.pallas_call(
        functools.partial(inverse_kernel, steps, which, near),
        grid_spec=pltpu.PrefetchScalarGridSpec(
            num_scalar_prefetch=1,
            grid=(2 * steps,),
            in_specs=[pl.BlockSpec((count, ROWS, LANES), lambda i, s: (early(i, s), 0, 0))] * near
            + [
                pl.BlockSpec((ROWS, LANES), lambda i, s: (0, 0)),
                pl.BlockSpec((near, 1, LANES), lambda i, s: (which // near, 0, 0)),
                pl.BlockSpec((count, 2, 2 * A, PART), lambda i, s: (early(i, s), 0, 0, 0)),
            ]
            + [table_spec(x) for x in range(near)]
            + [pl.BlockSpec(memory_space=pl.ANY)] * len(after),
            out_specs=pl.BlockSpec(
                (each, 2 * A * near, 2 * LANES), lambda i, s: (jnp.maximum(i - steps, 0), 0, 0)
            ),
            scratch_shapes=[pltpu.VMEM(((near * 2 * A + 1) * PITCH, LANES), F32)],
        ),
        out_shape=jax.ShapeDtypeStruct((HALF, 2 * A * near, 2 * LANES), BF),
        compiler_params=pltpu.CompilerParams(vmem_limit_bytes=VMEM),
        cost_estimate=SMALL,
        name="inverse",
    )(sel, *specs, freq_y, square_x, table_y, *[table_x] * near, *after)


def collect_kernel(count, k1_pairs, *refs):
    sheets, places = refs[:count], refs[count]
    outs = refs[-2 - PARTS : -2]
    weights, held = refs[-2:]
    devices, _, slots, lines, _ = outs[0].shape
    each = sheets[0].shape[0]
    steps = lines // each
    step = pl.program_id(0) % steps
    part_id = pl.program_id(0) // steps
    tiles = devices * slots
    pitch = lines + 1
    lane = lax.broadcasted_iota(jnp.int32, (tiles, LANES), 1)
    lower = lane < A

    @pl.when(step == 0)
    def _():
        quarter = A // 4
        base = places[0, 0, 0] * (lane % A) + quarter * (lane // A)
        for x in range(weights.shape[1] // LANES):
            for ks in range(2):
                winding = base + places[0, 0, 1] * (k1_pairs[x] + ks)
                for part in range(2):
                    angle = ((winding - quarter * part) & (A - 1)) - A // 2
                    angle = angle.astype(F32) * F32(2.0 * math.pi / A)
                    rows = slice((2 * part + ks) * tiles, (2 * part + ks + 1) * tiles)
                    weights[rows, x * LANES : (x + 1) * LANES] = (-cosine(angle * angle)).astype(BF)

    def line(i, carry):
        stacked = sheets[0][i]
        if len(sheets) > 1:
            stacked = jnp.concatenate([sheet[i] for sheet in sheets], axis=0)
        sums = dot(weights[...], stacked)
        for part in range(2):
            even = sums[2 * part * tiles : (2 * part + 1) * tiles]
            odd = sums[(2 * part + 1) * tiles : (2 * part + 2) * tiles]
            keep = jnp.where(lower, even[:, :LANES], odd[:, LANES:])
            move = jnp.where(lower, even[:, LANES:], odd[:, :LANES])
            total = keep + pltpu.roll(move, A, 1)
            spot = part * tiles * pitch + step * each + i
            held[pl.ds(spot, tiles, stride=pitch), :] = total
        return carry

    lax.fori_loop(0, each, line, 0, unroll=4)

    for p, out in enumerate(outs):

        def device(d, carry, out=out):
            for part in range(2):
                for slot in range(slots):
                    start = (part * tiles + d * slots + slot) * pitch
                    out[d, part, slot] = held[pl.ds(start, lines), :].astype(BF)
            return carry

        @pl.when((step == steps - 1) & (part_id == p))
        def _(device=device):
            lax.fori_loop(0, devices, device, 0, unroll=4)


def collect(sheets, k1_pairs, places, devices, which, after):
    tiles = places.shape[3]
    lines = HALF // PARTS
    steps = 2
    shape = (devices, 2, tiles // devices, lines, LANES)
    depth = sum(sheet.shape[1] for sheet in sheets)
    sheet_spec = pl.BlockSpec((lines // steps,) + sheets[0].shape[1:], lambda i, s: (i, 0, 0))
    block = pl.BlockSpec(shape, lambda i, s: (0, 0, 0, 0, 0))
    return pl.pallas_call(
        functools.partial(collect_kernel, len(sheets)),
        grid_spec=pltpu.PrefetchScalarGridSpec(
            num_scalar_prefetch=1,
            grid=(PARTS * steps,),
            in_specs=[sheet_spec] * len(sheets)
            + [
                pl.BlockSpec(
                    (1, 1) + places.shape[2:], lambda i, s: (which, i // steps, 0, 0, 0)
                )
            ]
            + [pl.BlockSpec(memory_space=pl.ANY)] * len(after),
            out_specs=[block] * PARTS,
            scratch_shapes=[
                pltpu.VMEM((4 * tiles, depth), BF),
                pltpu.VMEM(((2 * tiles + 1) * (lines + 1), LANES), F32),
            ],
        ),
        out_shape=[jax.ShapeDtypeStruct(shape, BF)] * PARTS,
        compiler_params=pltpu.CompilerParams(vmem_limit_bytes=VMEM),
        cost_estimate=SMALL,
        name="collect",
    )(k1_pairs, *sheets, places, *after)


def crop_kernel(rows, cols, odd, mine, pot, after, out, held, sems):
    slots = out.shape[0]

    def copy(i):
        return pltpu.make_async_copy(
            pot.at[
                pl.ds(pl.multiple_of(rows[i] * A, A), A),
                pl.ds(pl.multiple_of(cols[i] * LANES, LANES), LANES),
            ],
            held.at[i],
            sems.at[i],
        )

    def begin(i, carry):
        copy(i).start()
        return carry

    def finish(i, carry):
        copy(i).wait()
        block = held[i].astype(F32)
        block = jnp.where(odd[i] == 1, pltpu.roll(block, A, 1), block)
        lane = lax.broadcasted_iota(jnp.int32, (HALF, LANES), 1)
        packed = jnp.where(lane < A, block[:HALF], pltpu.roll(block[HALF:], A, 1))
        out[i] = jnp.where(mine[i] == 1, packed, 0.0).astype(BF)
        return carry

    lax.fori_loop(0, slots, begin, 0)
    lax.fori_loop(0, slots, finish, 0)


def crop(rows, cols, odd, mine, pot, after):
    slots = rows.shape[0]
    return pl.pallas_call(
        crop_kernel,
        in_specs=[pl.BlockSpec(memory_space=pltpu.SMEM)] * 4
        + [pl.BlockSpec(memory_space=pl.ANY)] * 2,
        out_specs=pl.BlockSpec(memory_space=pltpu.VMEM),
        out_shape=jax.ShapeDtypeStruct((slots, HALF, LANES), BF),
        scratch_shapes=[pltpu.VMEM((slots, A, LANES), BF), pltpu.SemaphoreType.DMA((slots,))],
        compiler_params=pltpu.CompilerParams(vmem_limit_bytes=VMEM),
        cost_estimate=SMALL,
        name="crop",
    )(rows, cols, odd, mine, pot, after)


def detect_kernel(parts, alpha, counts, *refs):
    fields = refs[:parts]
    pot, plane, across, down, bins, out, lines, held = refs[parts:]
    beams, _, slots = fields[0].shape[:3]
    for s in range(slots):
        waves = []
        for j in range(beams):
            re, im = (
                jnp.concatenate([half[j, part, s] for half in fields], axis=0).astype(F32)
                for part in range(2)
            )
            cos, sin = plane[j, 0], plane[j, 1]
            waves.append((re * cos - im * sin, re * sin + im * cos))
        turned, level = sine_cosine(pot[s].astype(F32))
        for g in range(G):
            real = jnp.zeros((HALF, LANES), F32)
            imag = jnp.zeros((HALF, LANES), F32)
            for j in range(beams):
                cos, sin = alpha[0, j, s * G + g], alpha[1, j, s * G + g]
                re, im = waves[j]
                real = real + cos * re - sin * im
                imag = imag + cos * im + sin * re
            lines[2 * (s * G + g)] = (real * level - imag * turned).astype(BF)
            lines[2 * (s * G + g) + 1] = (real * turned + imag * level).astype(BF)
    total = slots * G
    first = dot(lines[...].reshape(2 * total * HALF, LANES), across[...])
    first = first.reshape(total, 2, HALF, 2 * LANES)
    real = (first[:, 0, :, :LANES] + first[:, 1, :, LANES:]).astype(BF)
    imag = (first[:, 1, :, :LANES] - first[:, 0, :, LANES:]).astype(BF)
    lane = lax.broadcasted_iota(jnp.int32, (A, LANES), 1)
    for i in range(total):
        both = jnp.concatenate([real[i], imag[i]], axis=1)
        mixed = dot(down[...], both)
        even, odd = mixed[: 2 * A], mixed[2 * A :]
        re_cos = even[:A, :LANES] + pltpu.roll(odd[:A, :LANES], A, 1)
        re_sin = even[A:, :LANES] + pltpu.roll(odd[A:, :LANES], A, 1)
        im_cos = even[:A, LANES:] + pltpu.roll(odd[:A, LANES:], A, 1)
        im_sin = even[A:, LANES:] + pltpu.roll(odd[A:, LANES:], A, 1)
        re = re_cos + im_sin
        im = im_cos - re_sin
        power = jnp.where(lane < A, re * re + im * im, 0.0)
        sums = jnp.sum(power[None] * bins[...], axis=1)
        block, slot = divmod(i // G, slots // counts.shape[0])
        active = slot < counts[block]
        held[i * NDET : (i + 1) * NDET, :] = jnp.where(active, sums, 0.0)
    out[...] = jnp.sum(held[...].T, axis=0, keepdims=True)


def detect(alpha, counts, fields, pot, plane, across, down, bins):
    slots = fields[0].shape[2]
    rows = -(-slots * G * NDET // LANES) * LANES
    smem = pl.BlockSpec(memory_space=pltpu.SMEM)
    vmem = pl.BlockSpec(memory_space=pltpu.VMEM)
    return pl.pallas_call(
        functools.partial(detect_kernel, len(fields)),
        in_specs=[smem, smem] + [vmem] * (5 + len(fields)),
        out_specs=vmem,
        out_shape=jax.ShapeDtypeStruct((1, rows), F32),
        scratch_shapes=[
            pltpu.VMEM((2 * slots * G, HALF, LANES), BF),
            pltpu.VMEM((rows, LANES), F32),
        ],
        compiler_params=pltpu.CompilerParams(vmem_limit_bytes=VMEM),
        name="detect",
    )(alpha, counts, *fields, pot, plane, across, down, bins)


def detect_tables(beam_total):
    n = np.arange(A)
    table = turn(n[:, None] * n[None, :], A) / A
    cos, sin = table.real, table.imag
    zero = np.zeros((A, A))
    across = np.block([[cos, zero, sin, zero], [zero, cos, zero, sin]])
    rows = np.concatenate([cos, sin], axis=0)
    down = np.concatenate([rows[:, :HALF], rows[:, HALF:]], axis=0)
    signed = np.where(n < A // 2, n, n - A)
    radius = signed[:, None] ** 2 + signed[None, :] ** 2
    width = A // (2 * NDET)
    bins = np.zeros((NDET, A, LANES))
    for d in range(NDET):
        member = (radius >= (width * d) ** 2) & (radius < (width * (d + 1)) ** 2)
        bins[d, :, :A] = member * (A * A / (beam_total * member.sum()))
    return low(across), low(down), bins.astype(np.float32)


def coefficients(tile_ids, beam_rows, shifts):
    across = N // A
    offsets = jnp.arange(G, dtype=jnp.int32)
    spot_y = (tile_ids // across)[:, None] * A + A // 2 + offsets[None, :]
    spot_x = (tile_ids % across)[:, None] * A + A // 2 + 2 * offsets[None, :]
    wave_y = jnp.remainder(F * beam_rows[:, 0], N)[:, None, None]
    wave_x = jnp.remainder(F * beam_rows[:, 1], N)[:, None, None]
    windings = (wave_y * spot_y[None] % N + wave_x * spot_x[None] % N) % N
    phases = shifts[:, None, None] + 2.0 * math.pi / N * windings.astype(F32)
    return jnp.stack([jnp.cos(phases), -jnp.sin(phases)])


def plane_waves(beam_index):
    by = jnp.arange(HALF, dtype=jnp.int32)[:, None] + HALF * (jnp.arange(LANES) // A)[None, :]
    bx = jnp.broadcast_to((jnp.arange(LANES, dtype=jnp.int32) % A)[None, :], by.shape)
    row_y = beam_index[:, 0][:, None, None]
    row_x = beam_index[:, 1][:, None, None]
    winding = (row_y * by[None] + row_x * bx[None] + HALF * (row_y + row_x)) % A
    angle = 2.0 * math.pi / A * winding.astype(F32)
    return jnp.stack([jnp.cos(angle), jnp.sin(angle)], axis=1)


def shards(pot_first, pot_second, beam_index, aberration, tile_table, tile_count):
    field_count = lax.axis_size("beam")
    hold_count = lax.axis_size("slab")
    field_pos = lax.axis_index("beam")
    hold_pos = lax.axis_index("slab")
    band_rows = pot_first.shape[0]
    band_tiles = band_rows // A
    width_k = A // field_count
    sheets = width_k // 2
    across = N // A
    beam_total = beam_index.shape[0]
    share = hold_pos % sheets

    section_x = np.stack(
        [
            first_forward_x(
                np.array(
                    [width_k * p + 2 * t + ks for p in range(field_count) for ks in range(2)]
                )
            )
            for t in range(sheets)
        ]
    )
    last_x = np.stack(
        [
            np.stack(
                [
                    last_forward_x([width_k * p + 2 * t, width_k * p + 2 * t + 1])
                    for p in range(field_count)
                ]
            )
            for t in range(sheets)
        ]
    )
    section_y = first_forward_y()
    last_y = np.stack([last_forward_y([2 * q, 2 * q + 1]) for q in range(PAIRS)])
    inverse_y = np.stack([first_inverse_y([2 * q, 2 * q + 1]) for q in range(PAIRS)])
    inverse_x = np.stack(
        [
            np.stack(
                [
                    first_inverse_x([width_k * p + 2 * t, width_k * p + 2 * t + 1])
                    for t in range(sheets)
                ]
            )
            for p in range(field_count)
        ]
    )

    blocks_dev = tile_table.shape[0] // (field_count * hold_count)
    slot_count = tile_table.shape[1]
    own_slots = blocks_dev * slot_count
    table = tile_table.reshape(field_count, hold_count, own_slots)

    def trade(value, axis):
        return lax.all_to_all(value, axis, split_axis=0, concat_axis=0, tiled=True)

    near = min(sheets, 2)
    far = sheets // near

    def swap(value, x):
        return lax.ppermute(value, "slab", [(i, i ^ x) for i in range(hold_count)])

    ids = lax.dynamic_index_in_dim(table, hold_pos, 1, keepdims=False).reshape(-1)
    tile_y, tile_x = ids // across, ids % across
    mine = (tile_y // band_tiles == field_pos).astype(jnp.int32)
    rows = jnp.clip(tile_y - field_pos * band_tiles, 0, band_tiles - 1)

    beam_row = lax.dynamic_index_in_dim(beam_index, hold_pos, 0, keepdims=False)
    pair_ids = share ^ jnp.arange(sheets, dtype=jnp.int32)
    k1_pairs = field_pos * width_k + 2 * pair_ids
    near_bit, far_bit = (jnp.stack([1 - v, v]) for v in (field_pos % 2, field_pos // 2 % 2))
    corners = table.reshape(field_count // 4, 2, 2, hold_count, own_slots)
    corners = corners.transpose(2, 1, 0, 3, 4)[near_bit][:, far_bit]
    sets = jnp.stack([corners, corners.transpose(1, 0, 2, 3, 4)], axis=1)
    sets = sets.reshape(2, PARTS, -1)
    places = jnp.stack([sets // across - beam_row[0], sets % across - beam_row[1]], axis=2)
    places = jnp.broadcast_to(places[..., None], places.shape + (LANES,))
    row = np.arange(ROWS)
    base = row // PART + A * (K2_LOW + row % PART % K2_COUNT)
    freq_y = np.broadcast_to(base[:, None], (ROWS, LANES)).astype(np.float32)
    lane = np.arange(LANES)
    base = np.where(lane < 2 * K2_COUNT, lane // K2_COUNT + A * (K2_LOW + lane % K2_COUNT), N)
    freq_x = (k1_pairs + F * beam_row[1])[:, None, None] + base.astype(np.int32)
    square_x = (freq_x * freq_x).astype(F32)
    scalars = jnp.stack(
        jnp.broadcast_arrays(field_pos, pair_ids, F * beam_row[0]), axis=-1
    )
    scalars = scalars.astype(jnp.int32).reshape(-1)

    sel = share.reshape(1).astype(jnp.int32)
    received = [[] for _ in range(far)]
    earlier = []
    for part in range(PARTS):
        lines = trade(forward_x(sel, pot_first, section_x, last_x, field_count, part), "beam")
        if lines.shape[3] != LANES:
            ratio = LANES // lines.shape[3]
            lines = lines.reshape(
                field_count // ratio, ratio, HIGH // PARTS, ROWS, SUB // FEW, -1
            )
            lines = lines.transpose(0, 2, 3, 4, 1, 5).reshape(-1, HIGH // PARTS, ROWS, LANES)
        if part:
            crops = crop(rows, tile_x // 2, tile_x % 2, mine, pot_second, earlier[0])
            lines = order(lines, [crops, square_x, places] + [r[0] for r in received[1:]])
        for f in range(far):
            received[f].append(swap(lines, f * near) if f else lines)
        if part == 0:
            earlier = [forward_y_first(received[f][0], section_y) for f in range(far)]
    waves = []
    for f in range(far):
        spec = forward_y(received[f][1], section_y, earlier[f], last_y, [])
        ready = [spec] + [swap(spec, x) for x in range(1, near)]
        waves.append(
            inverse(
                f * near, scalars, ready, freq_y, square_x, inverse_y, inverse_x, waves[-1:]
            )
        )
    crops = order(crops.reshape(field_count, own_slots, HALF, LANES), [spec])
    crops = trade(crops, "beam")
    owners = field_count // 2 * hold_count
    other = collect(waves, k1_pairs, places, owners, 0, [crops])
    partial = other + collect(waves, k1_pairs, places, owners, 1, other[:1])

    def hop(value, bit):
        pairs = [(i, i ^ (1 << bit)) for i in range(field_count)]
        return lax.ppermute(value, "beam", pairs).astype(F32)

    totals = []
    arrived = [hop(partial[part], part) for part in range(PARTS)]
    for part in range(PARTS):
        own = partial[PARTS + part].astype(F32) + arrived[part]
        rest = own[: owners // 2].astype(BF)
        totals.append(own[owners // 2 :] + hop(rest, 1 - part))
    tiles = jnp.concatenate(totals, axis=3).astype(BF)
    groups = [
        [b * hold_count + h for b in range(g, field_count, 4) for h in range(hold_count)]
        for g in range(4)
    ]
    tiles = lax.all_to_all(
        tiles,
        ("beam", "slab"),
        split_axis=0,
        concat_axis=0,
        axis_index_groups=groups,
        tiled=True,
    )
    tiles = tiles.reshape((field_count // 4, hold_count) + tiles.shape[1:]).astype(F32)
    fields = [jnp.sum(tiles, axis=0).astype(BF)]
    crops = jnp.sum(crops.astype(F32), axis=0).astype(BF)

    own = lax.dynamic_index_in_dim(
        lax.dynamic_index_in_dim(table, field_pos, 0, keepdims=False), hold_pos, 0, keepdims=False
    )
    alpha = coefficients(own, beam_index, aberration).reshape(2, beam_total, own_slots * G)
    first_block = (field_pos * hold_count + hold_pos) * blocks_dev
    counts = lax.dynamic_slice_in_dim(tile_count, first_block, blocks_dev, 0)
    bins = detect_tables(beam_total)
    sums = detect(alpha, counts, fields, crops, plane_waves(beam_index), *bins)
    return sums[0, : own_slots * G * NDET].reshape(blocks_dev, slot_count, G, NDET)


def solution(mesh):
    return jax.shard_map(
        shards,
        mesh=mesh,
        in_specs=(P("beam", None), P("beam", None), P(), P(), P(), P()),
        out_specs=P(("beam", "slab"), None, None, None),
        check_vma=False,
    )
```

```python
import functools
import math

import jax
import jax.numpy as jnp
import ml_dtypes
import numpy as np
from jax import lax
from jax.experimental import pallas as pl
from jax.experimental.pallas import tpu as pltpu
from jax.sharding import PartitionSpec as P

A = 64
N = 4096
F = 64
G = 3
NDET = 16
QMAX = 3
LIMIT = N // 3
K2_LOW = -(LIMIT // A + 1 + QMAX)
K2_COUNT = 2 * (LIMIT // A + 1 + QMAX)
PART = 104
ROWS = 2 * PART
LANES = 128
SUB = 16
FEW = 4
HIGH = A // SUB
HALF = A // 2
PAIRS = A // 2
PARTS = 2
VMEM = 60 * 1024 * 1024
PITCH = A + 1
PITCH_Y = A // PARTS + 1
SMALL = pl.CostEstimate(flops=1 << 20, bytes_accessed=0, transcendentals=0)
BF = jnp.bfloat16
F32 = jnp.float32


def low(values):
    return np.asarray(values, dtype=np.float32).astype(ml_dtypes.bfloat16)


def turn(numerator, period):
    return np.exp(2j * np.pi * (numerator % period) / period)


def digits_k2():
    return K2_LOW + np.arange(K2_COUNT)


def spread(table, sub):
    both = np.stack([table.real, table.imag])
    return both[:, :, None, :, None] * np.eye(sub)[None, None, :, None, :]


def real_rows(table):
    return np.block([[table.real, -table.imag], [table.imag, table.real]])


def section_forward(k1):
    n1 = np.arange(A)
    return np.conj(turn(k1[:, None] * n1[None, :], A)) / A


def first_forward_x(k1):
    return low(spread(section_forward(k1), SUB).reshape(2 * len(k1) * SUB, A * SUB))


def first_forward_y():
    table = spread(section_forward(np.arange(A)), FEW).transpose(0, 2, 1, 3, 4)
    return low(table.reshape(2 * A * FEW, A * FEW))


def line_order(lanes):
    order = np.arange(lanes).reshape(-1, SUB // FEW, FEW).transpose(1, 0, 2).reshape(-1)
    out = np.zeros((lanes, lanes))
    out[order, np.arange(lanes)] = 1
    return low(out)


def last_forward_x(k1_pair):
    n2 = np.arange(A)
    out = np.zeros((2, PART, 2, 2, A))
    for ks, k1 in enumerate(k1_pair):
        freq = k1 + A * digits_k2()
        table = np.conj(turn(freq[:, None] * n2[None, :], N)) / A
        block = real_rows(table).reshape(2, K2_COUNT, 2, A)
        out[:, ks * K2_COUNT : (ks + 1) * K2_COUNT, ks] = block
    return low(out.reshape(ROWS, 4 * A))


def last_forward_y(k1_pair):
    n2 = np.arange(A)
    out = np.zeros((ROWS, 2, 2 * A))
    for e, k1 in enumerate(k1_pair):
        freq = k1 + A * digits_k2()
        table = np.conj(turn(freq[:, None] * n2[None, :], N)) / A
        out[e * PART : e * PART + 2 * K2_COUNT, e] = real_rows(table)
    return low(out.reshape(ROWS, 4 * A))


def first_inverse(k1):
    n2 = np.arange(A)
    freq = k1 + A * digits_k2()
    return turn(n2[:, None] * freq[None, :], N) * np.conj(turn(freq * freq, 2 * N))[None, :]


def first_inverse_y(k1_pair):
    out = np.zeros((2, 2 * A, PART))
    for e, k1 in enumerate(k1_pair):
        out[e, :, : 2 * K2_COUNT] = real_rows(first_inverse(k1))
    return low(out)


def first_inverse_x(k1_pair):
    out = np.zeros((2, LANES, 2, 2, A))
    for ks, k1 in enumerate(k1_pair):
        table = first_inverse(k1).T
        rows = slice(ks * K2_COUNT, (ks + 1) * K2_COUNT)
        out[0, rows, 0, ks] = table.real
        out[0, rows, 1, ks] = table.imag
        out[1, rows, 0, ks] = -table.imag
        out[1, rows, 1, ks] = table.real
    return low(out.reshape(2 * LANES, 4 * A))


def cosine(u):
    q = F32(COS_FIT[-1])
    for c in COS_FIT[-2::-1]:
        q = q * u + F32(c)
    return q


def sine_cosine(x):
    u = x * x
    s = F32(SIN_FIT[-1])
    for c in SIN_FIT[-2::-1]:
        s = s * u + F32(c)
    return s * x, cosine(u)


def fit(function, degree):
    top = 3.1421**2
    nodes = 0.5 * top * (1 - np.cos(np.pi * (np.arange(64) + 0.5) / 64))
    cheb = np.polynomial.chebyshev.Chebyshev.fit(
        nodes, function(np.sqrt(nodes)), degree, domain=[0, top]
    )
    return [float(c) for c in cheb.convert(kind=np.polynomial.Polynomial).coef]


SIN_FIT = fit(lambda x: np.sinc(x / np.pi), 5)
COS_FIT = fit(np.cos, 5)


def dot(a, b):
    return jnp.dot(a, b, preferred_element_type=F32)


def forward_x_kernel(sel, pot, section, last, perm, out, cos_ref, sin_ref, twisted):
    fields = out.shape[0]
    lanes = out.shape[3]
    half = section.shape[1] // 2

    def chunk(t, carry):
        block = pot[:, 0, :, pl.ds(pl.multiple_of(t * LANES, LANES), LANES)]
        values = block.reshape(lanes, LANES).T.astype(F32)
        sine, cosine = sine_cosine(values)
        cos_ref[pl.ds(2 * t, 2)] = cosine.astype(BF).reshape(2, A, lanes)
        sin_ref[pl.ds(2 * t, 2)] = sine.astype(BF).reshape(2, A, lanes)
        return carry

    lax.fori_loop(0, N // LANES, chunk, 0, unroll=4)
    table = section[0]
    for m in range(HIGH):
        span = slice(m * SUB, (m + 1) * SUB)
        part_cos = cos_ref[:, span, :].reshape(A * SUB, lanes)
        part_sin = sin_ref[:, span, :].reshape(A * SUB, lanes)
        if lanes % LANES == 0:
            both = dot(table, jnp.concatenate([part_cos, part_sin], axis=1))
            of_cos, of_sin = both[:, :lanes], both[:, lanes:]
        else:
            of_cos, of_sin = dot(table, part_cos), dot(table, part_sin)
        real = of_cos[:half] - of_sin[half:]
        imag = of_cos[half:] + of_sin[:half]
        twisted[:, m * SUB : (m + 1) * SUB, :] = real.astype(BF).reshape(2 * fields, SUB, lanes)
        twisted[:, A + m * SUB : A + (m + 1) * SUB, :] = imag.astype(BF).reshape(
            2 * fields, SUB, lanes
        )
    for d in range(fields):
        lines = twisted[2 * d : 2 * d + 2].reshape(4 * A, lanes)
        out[d, 0] = dot(dot(last[0, d], lines).astype(BF), perm[...]).astype(BF)


def forward_x(sel, pot, section, last, fields, part):
    groups = pot.shape[0] // A
    lanes = groups * SUB
    steps = HIGH // PARTS
    return pl.pallas_call(
        forward_x_kernel,
        grid_spec=pltpu.PrefetchScalarGridSpec(
            num_scalar_prefetch=1,
            grid=(steps,),
            in_specs=[
                pl.BlockSpec((groups, 1, SUB, N), lambda i, s: (0, part * steps + i, 0, 0)),
                pl.BlockSpec((1,) + section.shape[1:], lambda i, s: (s[0], 0, 0)),
                pl.BlockSpec((1,) + last.shape[1:], lambda i, s: (s[0], 0, 0, 0)),
                pl.BlockSpec((lanes, lanes), lambda i, s: (0, 0)),
            ],
            out_specs=pl.BlockSpec((fields, 1, ROWS, lanes), lambda i, s: (0, i, 0, 0)),
            scratch_shapes=[
                pltpu.VMEM((A, A, lanes), BF),
                pltpu.VMEM((A, A, lanes), BF),
                pltpu.VMEM((2 * fields, 2 * A, lanes), BF),
            ],
        ),
        out_shape=jax.ShapeDtypeStruct((fields, steps, ROWS, lanes), BF),
        compiler_params=pltpu.CompilerParams(vmem_limit_bytes=VMEM),
        cost_estimate=SMALL,
        name="forward_x",
    )(sel, pot.reshape(groups, HIGH, SUB, N), section, last, line_order(lanes))


def first_section_y(lines, section, gathered, held):
    groups, steps = lines.shape[:2]
    span = LANES * FEW // SUB
    zeros = jnp.zeros((LANES - PART, LANES), F32)
    for g in range(groups):
        for h in range(steps):
            block = lines[g, h].astype(F32)
            both = jnp.concatenate([block[:PART], zeros, block[PART:], zeros], axis=0)
            turned = both.astype(BF).T
            columns = slice(2 * h * LANES, 2 * (h + 1) * LANES)
            for a in range(SUB // FEW):
                gathered[a, g * span : (g + 1) * span, columns] = turned[a * span : (a + 1) * span]
    half = A * FEW
    for a in range(SUB // FEW):
        both = dot(section[...], gathered[a])
        for h in range(steps):
            re = slice(2 * h * LANES, (2 * h + 1) * LANES)
            im = slice((2 * h + 1) * LANES, (2 * h + 2) * LANES)
            real = both[:half, re] - both[half:, im]
            imag = both[:half, im] + both[half:, re]
            for b in range(FEW):
                n2 = h * SUB + a * FEW + b
                rows = slice(b * A, (b + 1) * A)
                held[pl.ds(n2, A, stride=PITCH_Y), :] = real[rows]
                held[pl.ds(A * PITCH_Y + n2, A, stride=PITCH_Y), :] = imag[rows]


def first_section_scratch(lines):
    return [
        pltpu.VMEM((SUB // FEW, A * FEW, 2 * lines.shape[1] * LANES), BF),
        pltpu.VMEM(((2 * A + 1) * PITCH_Y, LANES), F32),
    ]


def forward_y_first_kernel(lines, section, twisted, gathered, held):
    first_section_y(lines, section, gathered, held)

    def digit(k, carry):
        for part in range(2):
            start = (part * A + k) * PITCH_Y
            twisted[k, part] = held[pl.ds(start, A // PARTS), :].astype(BF)
        return carry

    lax.fori_loop(0, A, digit, 0, unroll=8)


def forward_y_first(lines, section):
    return pl.pallas_call(
        forward_y_first_kernel,
        grid=(1,),
        in_specs=[
            pl.BlockSpec(lines.shape, lambda i: (0, 0, 0, 0)),
            pl.BlockSpec(section.shape, lambda i: (0, 0)),
        ],
        out_specs=pl.BlockSpec((A, 2, A // PARTS, LANES), lambda i: (0, 0, 0, 0)),
        out_shape=jax.ShapeDtypeStruct((A, 2, A // PARTS, LANES), BF),
        scratch_shapes=first_section_scratch(lines),
        compiler_params=pltpu.CompilerParams(vmem_limit_bytes=VMEM),
        cost_estimate=SMALL,
        name="forward_y_first",
    )(lines, section)


def forward_y_kernel(lines, section, earlier, last, *rest):
    out, gathered, held = rest[-3:]
    step = pl.program_id(0)

    @pl.when(step == 0)
    def _():
        first_section_y(lines, section, gathered, held)

    @pl.when(step > 0)
    def _():
        count = out.shape[0]
        base = (step - 1) * count
        for q in range(count):
            rows = []
            for e in range(2):
                for part in range(2):
                    k = 2 * (base + q) + e
                    rows.append(earlier[k, part])
                    start = (part * A + k) * PITCH_Y
                    rows.append(held[pl.ds(start, A // PARTS), :].astype(BF))
            out[q] = dot(last[q], jnp.concatenate(rows, axis=0)).astype(BF)


def forward_y(lines, section, earlier, last, after):
    steps = 2
    count = PAIRS // steps

    def late(i):
        return (jnp.maximum(i - 1, 0), 0, 0)

    return pl.pallas_call(
        forward_y_kernel,
        grid=(1 + steps,),
        in_specs=[
            pl.BlockSpec(lines.shape, lambda i: (0, 0, 0, 0)),
            pl.BlockSpec(section.shape, lambda i: (0, 0)),
            pl.BlockSpec(earlier.shape, lambda i: (0, 0, 0, 0)),
            pl.BlockSpec((count, ROWS, 4 * A), late),
        ]
        + [pl.BlockSpec(memory_space=pl.ANY)] * len(after),
        out_specs=pl.BlockSpec((count, ROWS, LANES), late),
        out_shape=jax.ShapeDtypeStruct((PAIRS, ROWS, LANES), BF),
        scratch_shapes=first_section_scratch(lines),
        compiler_params=pltpu.CompilerParams(vmem_limit_bytes=VMEM),
        cost_estimate=SMALL,
        name="forward_y",
    )(lines, section, earlier, last, *after)


def order_kernel(value, *rest):
    pass


def order(value, after):
    return pl.pallas_call(
        order_kernel,
        in_specs=[pl.BlockSpec(memory_space=pl.ANY)] * (1 + len(after)),
        out_specs=pl.BlockSpec(memory_space=pl.ANY),
        out_shape=jax.ShapeDtypeStruct(value.shape, value.dtype),
        input_output_aliases={0: 0},
        name="order",
    )(value, *after)


def inverse_kernel(steps, which, near, sel, *refs):
    specs = refs[:near]
    freq_y, square_x, table_y = refs[near : near + 3]
    tables_x = refs[near + 3 : 2 * near + 3]
    out, mid = refs[-2:]
    step = pl.program_id(0)
    count = PAIRS // steps
    each = HALF // steps
    limit = F32(LIMIT * LIMIT)
    whole = 2 * A * PITCH

    @pl.when(step < steps)
    def _():
        def pair(q, carry):
            pair_id = step * count + q
            offset = (2 * pair_id + sel[3 * which + 2]).astype(F32)
            row_freq = freq_y[...] + offset
            row_square = row_freq * row_freq
            values = []
            for x in range(near):
                inside = row_square + square_x[x] <= limit
                values.append(jnp.where(inside, specs[x][q].astype(F32), 0.0))
            for e in range(2):
                half = [v[e * PART : (e + 1) * PART].astype(BF) for v in values]
                half = half[0] if near == 1 else jnp.concatenate(half, axis=1)
                mixed = dot(table_y[q, e], half)
                for x in range(near):
                    for part in range(2):
                        spot = x * whole + part * A * PITCH + 2 * pair_id + e
                        mid[pl.ds(spot, A, stride=PITCH), :] = mixed[
                            part * A : (part + 1) * A, x * LANES : (x + 1) * LANES
                        ]
            return carry

        lax.fori_loop(0, count, pair, 0, unroll=8)

    @pl.when(step >= steps)
    def _():
        def line(i, carry):
            by = (step - steps) * each + i
            for x in range(near):
                rows = []
                for b in range(2):
                    start = x * whole + (by + b * HALF) * PITCH
                    real = mid[pl.ds(start, A), :].astype(BF)
                    imag = mid[pl.ds(start + A * PITCH, A), :].astype(BF)
                    rows.append(jnp.concatenate([real, imag], axis=1))
                product = dot(jnp.concatenate(rows, axis=0), tables_x[x][0, 0]).astype(BF)
                for b in range(2):
                    for part in range(2):
                        low_row = 2 * A * x + A * part
                        out[i, low_row : low_row + A, b * LANES : (b + 1) * LANES] = product[
                            b * A : (b + 1) * A, part * LANES : (part + 1) * LANES
                        ]
            return carry

        lax.fori_loop(0, each, line, 0, unroll=8)


def inverse(which, sel, specs, freq_y, square_x, table_y, table_x, after):
    near = len(specs)
    steps = 2
    count = PAIRS // steps
    each = HALF // steps

    def early(i, s):
        return jnp.minimum(i, steps - 1)

    def table_spec(x):
        return pl.BlockSpec(
            (1, 1) + table_x.shape[2:],
            lambda i, s: (s[3 * (which + x)], s[3 * (which + x) + 1], 0, 0),
        )

    return pl.pallas_call(
        functools.partial(inverse_kernel, steps, which, near),
        grid_spec=pltpu.PrefetchScalarGridSpec(
            num_scalar_prefetch=1,
            grid=(2 * steps,),
            in_specs=[pl.BlockSpec((count, ROWS, LANES), lambda i, s: (early(i, s), 0, 0))] * near
            + [
                pl.BlockSpec((ROWS, LANES), lambda i, s: (0, 0)),
                pl.BlockSpec((near, 1, LANES), lambda i, s: (which // near, 0, 0)),
                pl.BlockSpec((count, 2, 2 * A, PART), lambda i, s: (early(i, s), 0, 0, 0)),
            ]
            + [table_spec(x) for x in range(near)]
            + [pl.BlockSpec(memory_space=pl.ANY)] * len(after),
            out_specs=pl.BlockSpec(
                (each, 2 * A * near, 2 * LANES), lambda i, s: (jnp.maximum(i - steps, 0), 0, 0)
            ),
            scratch_shapes=[pltpu.VMEM(((near * 2 * A + 1) * PITCH, LANES), F32)],
        ),
        out_shape=jax.ShapeDtypeStruct((HALF, 2 * A * near, 2 * LANES), BF),
        compiler_params=pltpu.CompilerParams(vmem_limit_bytes=VMEM),
        cost_estimate=SMALL,
        name="inverse",
    )(sel, *specs, freq_y, square_x, table_y, *[table_x] * near, *after)


def collect_kernel(count, k1_pairs, *refs):
    sheets, places = refs[:count], refs[count]
    outs = refs[-2 - PARTS : -2]
    weights, held = refs[-2:]
    devices, _, slots, lines, _ = outs[0].shape
    each = sheets[0].shape[0]
    steps = lines // each
    step = pl.program_id(0) % steps
    part_id = pl.program_id(0) // steps
    tiles = devices * slots
    pitch = lines + 1
    lane = lax.broadcasted_iota(jnp.int32, (tiles, LANES), 1)
    lower = lane < A

    @pl.when(step == 0)
    def _():
        quarter = A // 4
        base = places[0, 0, 0] * (lane % A) + quarter * (lane // A)
        for x in range(weights.shape[1] // LANES):
            for ks in range(2):
                winding = base + places[0, 0, 1] * (k1_pairs[x] + ks)
                for part in range(2):
                    angle = ((winding - quarter * part) & (A - 1)) - A // 2
                    angle = angle.astype(F32) * F32(2.0 * math.pi / A)
                    rows = slice((2 * part + ks) * tiles, (2 * part + ks + 1) * tiles)
                    weights[rows, x * LANES : (x + 1) * LANES] = (-cosine(angle * angle)).astype(BF)

    def line(i, carry):
        stacked = sheets[0][i]
        if len(sheets) > 1:
            stacked = jnp.concatenate([sheet[i] for sheet in sheets], axis=0)
        sums = dot(weights[...], stacked)
        for part in range(2):
            even = sums[2 * part * tiles : (2 * part + 1) * tiles]
            odd = sums[(2 * part + 1) * tiles : (2 * part + 2) * tiles]
            keep = jnp.where(lower, even[:, :LANES], odd[:, LANES:])
            move = jnp.where(lower, even[:, LANES:], odd[:, :LANES])
            total = keep + pltpu.roll(move, A, 1)
            spot = part * tiles * pitch + step * each + i
            held[pl.ds(spot, tiles, stride=pitch), :] = total
        return carry

    lax.fori_loop(0, each, line, 0, unroll=8)

    for p, out in enumerate(outs):

        def device(d, carry, out=out):
            for part in range(2):
                for slot in range(slots):
                    start = (part * tiles + d * slots + slot) * pitch
                    out[d, part, slot] = held[pl.ds(start, lines), :].astype(BF)
            return carry

        @pl.when((step == steps - 1) & (part_id == p))
        def _(device=device):
            lax.fori_loop(0, devices, device, 0, unroll=4)


def collect(sheets, k1_pairs, places, devices, which, after):
    tiles = places.shape[3]
    lines = HALF // PARTS
    steps = 2
    shape = (devices, 2, tiles // devices, lines, LANES)
    depth = sum(sheet.shape[1] for sheet in sheets)
    sheet_spec = pl.BlockSpec((lines // steps,) + sheets[0].shape[1:], lambda i, s: (i, 0, 0))
    block = pl.BlockSpec(shape, lambda i, s: (0, 0, 0, 0, 0))
    return pl.pallas_call(
        functools.partial(collect_kernel, len(sheets)),
        grid_spec=pltpu.PrefetchScalarGridSpec(
            num_scalar_prefetch=1,
            grid=(PARTS * steps,),
            in_specs=[sheet_spec] * len(sheets)
            + [
                pl.BlockSpec(
                    (1, 1) + places.shape[2:], lambda i, s: (which, i // steps, 0, 0, 0)
                )
            ]
            + [pl.BlockSpec(memory_space=pl.ANY)] * len(after),
            out_specs=[block] * PARTS,
            scratch_shapes=[
                pltpu.VMEM((4 * tiles, depth), BF),
                pltpu.VMEM(((2 * tiles + 1) * (lines + 1), LANES), F32),
            ],
        ),
        out_shape=[jax.ShapeDtypeStruct(shape, BF)] * PARTS,
        compiler_params=pltpu.CompilerParams(vmem_limit_bytes=VMEM),
        cost_estimate=SMALL,
        name="collect",
    )(k1_pairs, *sheets, places, *after)


def crop_kernel(rows, cols, odd, mine, pot, after, out, held, sems):
    slots = out.shape[0]

    def copy(i):
        return pltpu.make_async_copy(
            pot.at[
                pl.ds(pl.multiple_of(rows[i] * A, A), A),
                pl.ds(pl.multiple_of(cols[i] * LANES, LANES), LANES),
            ],
            held.at[i],
            sems.at[i],
        )

    def begin(i, carry):
        copy(i).start()
        return carry

    def finish(i, carry):
        copy(i).wait()
        block = held[i].astype(F32)
        block = jnp.where(odd[i] == 1, pltpu.roll(block, A, 1), block)
        lane = lax.broadcasted_iota(jnp.int32, (HALF, LANES), 1)
        packed = jnp.where(lane < A, block[:HALF], pltpu.roll(block[HALF:], A, 1))
        out[i] = jnp.where(mine[i] == 1, packed, 0.0).astype(BF)
        return carry

    lax.fori_loop(0, slots, begin, 0)
    lax.fori_loop(0, slots, finish, 0)


def crop(rows, cols, odd, mine, pot, after):
    slots = rows.shape[0]
    return pl.pallas_call(
        crop_kernel,
        in_specs=[pl.BlockSpec(memory_space=pltpu.SMEM)] * 4
        + [pl.BlockSpec(memory_space=pl.ANY)] * 2,
        out_specs=pl.BlockSpec(memory_space=pltpu.VMEM),
        out_shape=jax.ShapeDtypeStruct((slots, HALF, LANES), BF),
        scratch_shapes=[pltpu.VMEM((slots, A, LANES), BF), pltpu.SemaphoreType.DMA((slots,))],
        compiler_params=pltpu.CompilerParams(vmem_limit_bytes=VMEM),
        cost_estimate=SMALL,
        name="crop",
    )(rows, cols, odd, mine, pot, after)


def detect_kernel(parts, alpha, counts, *refs):
    fields = refs[:parts]
    pot, plane, across, down, bins, out, lines, held = refs[parts:]
    beams, _, slots = fields[0].shape[:3]
    for s in range(slots):
        waves = []
        for j in range(beams):
            re, im = (
                jnp.concatenate([half[j, part, s] for half in fields], axis=0).astype(F32)
                for part in range(2)
            )
            cos, sin = plane[j, 0], plane[j, 1]
            waves.append((re * cos - im * sin, re * sin + im * cos))
        turned, level = sine_cosine(pot[s].astype(F32))
        for g in range(G):
            real = jnp.zeros((HALF, LANES), F32)
            imag = jnp.zeros((HALF, LANES), F32)
            for j in range(beams):
                cos, sin = alpha[0, j, s * G + g], alpha[1, j, s * G + g]
                re, im = waves[j]
                real = real + cos * re - sin * im
                imag = imag + cos * im + sin * re
            lines[2 * (s * G + g)] = (real * level - imag * turned).astype(BF)
            lines[2 * (s * G + g) + 1] = (real * turned + imag * level).astype(BF)
    total = slots * G
    first = dot(lines[...].reshape(2 * total * HALF, LANES), across[...])
    first = first.reshape(total, 2, HALF, 2 * LANES)
    real = (first[:, 0, :, :LANES] + first[:, 1, :, LANES:]).astype(BF)
    imag = (first[:, 1, :, :LANES] - first[:, 0, :, LANES:]).astype(BF)
    lane = lax.broadcasted_iota(jnp.int32, (A, LANES), 1)
    for i in range(total):
        both = jnp.concatenate([real[i], imag[i]], axis=1)
        mixed = dot(down[...], both)
        even, odd = mixed[: 2 * A], mixed[2 * A :]
        re_cos = even[:A, :LANES] + pltpu.roll(odd[:A, :LANES], A, 1)
        re_sin = even[A:, :LANES] + pltpu.roll(odd[A:, :LANES], A, 1)
        im_cos = even[:A, LANES:] + pltpu.roll(odd[:A, LANES:], A, 1)
        im_sin = even[A:, LANES:] + pltpu.roll(odd[A:, LANES:], A, 1)
        re = re_cos + im_sin
        im = im_cos - re_sin
        power = jnp.where(lane < A, re * re + im * im, 0.0)
        sums = jnp.sum(power[None] * bins[...], axis=1)
        block, slot = divmod(i // G, slots // counts.shape[0])
        active = slot < counts[block]
        held[i * NDET : (i + 1) * NDET, :] = jnp.where(active, sums, 0.0)
    out[...] = jnp.sum(held[...].T, axis=0, keepdims=True)


def detect(alpha, counts, fields, pot, plane, across, down, bins):
    slots = fields[0].shape[2]
    rows = -(-slots * G * NDET // LANES) * LANES
    smem = pl.BlockSpec(memory_space=pltpu.SMEM)
    vmem = pl.BlockSpec(memory_space=pltpu.VMEM)
    return pl.pallas_call(
        functools.partial(detect_kernel, len(fields)),
        in_specs=[smem, smem] + [vmem] * (5 + len(fields)),
        out_specs=vmem,
        out_shape=jax.ShapeDtypeStruct((1, rows), F32),
        scratch_shapes=[
            pltpu.VMEM((2 * slots * G, HALF, LANES), BF),
            pltpu.VMEM((rows, LANES), F32),
        ],
        compiler_params=pltpu.CompilerParams(vmem_limit_bytes=VMEM),
        name="detect",
    )(alpha, counts, *fields, pot, plane, across, down, bins)


def detect_tables(beam_total):
    n = np.arange(A)
    table = turn(n[:, None] * n[None, :], A) / A
    cos, sin = table.real, table.imag
    zero = np.zeros((A, A))
    across = np.block([[cos, zero, sin, zero], [zero, cos, zero, sin]])
    rows = np.concatenate([cos, sin], axis=0)
    down = np.concatenate([rows[:, :HALF], rows[:, HALF:]], axis=0)
    signed = np.where(n < A // 2, n, n - A)
    radius = signed[:, None] ** 2 + signed[None, :] ** 2
    width = A // (2 * NDET)
    bins = np.zeros((NDET, A, LANES))
    for d in range(NDET):
        member = (radius >= (width * d) ** 2) & (radius < (width * (d + 1)) ** 2)
        bins[d, :, :A] = member * (A * A / (beam_total * member.sum()))
    return low(across), low(down), bins.astype(np.float32)


def coefficients(tile_ids, beam_rows, shifts):
    across = N // A
    offsets = jnp.arange(G, dtype=jnp.int32)
    spot_y = (tile_ids // across)[:, None] * A + A // 2 + offsets[None, :]
    spot_x = (tile_ids % across)[:, None] * A + A // 2 + 2 * offsets[None, :]
    wave_y = jnp.remainder(F * beam_rows[:, 0], N)[:, None, None]
    wave_x = jnp.remainder(F * beam_rows[:, 1], N)[:, None, None]
    windings = (wave_y * spot_y[None] % N + wave_x * spot_x[None] % N) % N
    phases = shifts[:, None, None] + 2.0 * math.pi / N * windings.astype(F32)
    return jnp.stack([jnp.cos(phases), -jnp.sin(phases)])


def plane_waves(beam_index):
    by = jnp.arange(HALF, dtype=jnp.int32)[:, None] + HALF * (jnp.arange(LANES) // A)[None, :]
    bx = jnp.broadcast_to((jnp.arange(LANES, dtype=jnp.int32) % A)[None, :], by.shape)
    row_y = beam_index[:, 0][:, None, None]
    row_x = beam_index[:, 1][:, None, None]
    winding = (row_y * by[None] + row_x * bx[None] + HALF * (row_y + row_x)) % A
    angle = 2.0 * math.pi / A * winding.astype(F32)
    return jnp.stack([jnp.cos(angle), jnp.sin(angle)], axis=1)


def shards(pot_first, pot_second, beam_index, aberration, tile_table, tile_count):
    field_count = lax.axis_size("beam")
    hold_count = lax.axis_size("slab")
    field_pos = lax.axis_index("beam")
    hold_pos = lax.axis_index("slab")
    band_rows = pot_first.shape[0]
    band_tiles = band_rows // A
    width_k = A // field_count
    sheets = width_k // 2
    across = N // A
    beam_total = beam_index.shape[0]
    share = hold_pos % sheets

    section_x = np.stack(
        [
            first_forward_x(
                np.array(
                    [width_k * p + 2 * t + ks for p in range(field_count) for ks in range(2)]
                )
            )
            for t in range(sheets)
        ]
    )
    last_x = np.stack(
        [
            np.stack(
                [
                    last_forward_x([width_k * p + 2 * t, width_k * p + 2 * t + 1])
                    for p in range(field_count)
                ]
            )
            for t in range(sheets)
        ]
    )
    section_y = first_forward_y()
    last_y = np.stack([last_forward_y([2 * q, 2 * q + 1]) for q in range(PAIRS)])
    inverse_y = np.stack([first_inverse_y([2 * q, 2 * q + 1]) for q in range(PAIRS)])
    inverse_x = np.stack(
        [
            np.stack(
                [
                    first_inverse_x([width_k * p + 2 * t, width_k * p + 2 * t + 1])
                    for t in range(sheets)
                ]
            )
            for p in range(field_count)
        ]
    )

    blocks_dev = tile_table.shape[0] // (field_count * hold_count)
    slot_count = tile_table.shape[1]
    own_slots = blocks_dev * slot_count
    table = tile_table.reshape(field_count, hold_count, own_slots)

    def trade(value, axis):
        return lax.all_to_all(value, axis, split_axis=0, concat_axis=0, tiled=True)

    near = min(sheets, 2)
    far = sheets // near

    def swap(value, x):
        return lax.ppermute(value, "slab", [(i, i ^ x) for i in range(hold_count)])

    ids = lax.dynamic_index_in_dim(table, hold_pos, 1, keepdims=False).reshape(-1)
    tile_y, tile_x = ids // across, ids % across
    mine = (tile_y // band_tiles == field_pos).astype(jnp.int32)
    rows = jnp.clip(tile_y - field_pos * band_tiles, 0, band_tiles - 1)

    beam_row = lax.dynamic_index_in_dim(beam_index, hold_pos, 0, keepdims=False)
    pair_ids = share ^ jnp.arange(sheets, dtype=jnp.int32)
    k1_pairs = field_pos * width_k + 2 * pair_ids
    near_bit, far_bit = (jnp.stack([1 - v, v]) for v in (field_pos % 2, field_pos // 2 % 2))
    corners = table.reshape(field_count // 4, 2, 2, hold_count, own_slots)
    corners = corners.transpose(2, 1, 0, 3, 4)[near_bit][:, far_bit]
    sets = jnp.stack([corners, corners.transpose(1, 0, 2, 3, 4)], axis=1)
    sets = sets.reshape(2, PARTS, -1)
    places = jnp.stack([sets // across - beam_row[0], sets % across - beam_row[1]], axis=2)
    places = jnp.broadcast_to(places[..., None], places.shape + (LANES,))
    row = np.arange(ROWS)
    base = row // PART + A * (K2_LOW + row % PART % K2_COUNT)
    freq_y = np.broadcast_to(base[:, None], (ROWS, LANES)).astype(np.float32)
    lane = np.arange(LANES)
    base = np.where(lane < 2 * K2_COUNT, lane // K2_COUNT + A * (K2_LOW + lane % K2_COUNT), N)
    freq_x = (k1_pairs + F * beam_row[1])[:, None, None] + base.astype(np.int32)
    square_x = (freq_x * freq_x).astype(F32)
    scalars = jnp.stack(
        jnp.broadcast_arrays(field_pos, pair_ids, F * beam_row[0]), axis=-1
    )
    scalars = scalars.astype(jnp.int32).reshape(-1)

    sel = share.reshape(1).astype(jnp.int32)
    received = [[] for _ in range(far)]
    earlier = []
    for part in range(PARTS):
        lines = trade(forward_x(sel, pot_first, section_x, last_x, field_count, part), "beam")
        if lines.shape[3] != LANES:
            ratio = LANES // lines.shape[3]
            lines = lines.reshape(
                field_count // ratio, ratio, HIGH // PARTS, ROWS, SUB // FEW, -1
            )
            lines = lines.transpose(0, 2, 3, 4, 1, 5).reshape(-1, HIGH // PARTS, ROWS, LANES)
        if part:
            crops = crop(rows, tile_x // 2, tile_x % 2, mine, pot_second, earlier[0])
            lines = order(lines, [crops, square_x, places, scalars] + [r[0] for r in received[1:]])
        for f in range(far):
            received[f].append(swap(lines, f * near) if f else lines)
        if part == 0:
            earlier = [forward_y_first(received[f][0], section_y) for f in range(far)]
    waves = []
    for f in range(far):
        spec = forward_y(received[f][1], section_y, earlier[f], last_y, [])
        ready = [spec] + [swap(spec, x) for x in range(1, near)]
        if f == 0:
            crops = order(crops.reshape(field_count, own_slots, HALF, LANES), [spec])
            crops = trade(crops, "beam")
        waves.append(
            inverse(
                f * near, scalars, ready, freq_y, square_x, inverse_y, inverse_x, waves[-1:]
            )
        )
    owners = field_count // 2 * hold_count
    other = collect(waves, k1_pairs, places, owners, 0, [crops])
    partial = other + collect(waves, k1_pairs, places, owners, 1, other[:1])

    def hop(value, bit):
        pairs = [(i, i ^ (1 << bit)) for i in range(field_count)]
        return lax.ppermute(value, "beam", pairs).astype(F32)

    totals = []
    arrived = [hop(partial[part], part) for part in range(PARTS)]
    for part in range(PARTS):
        own = partial[PARTS + part].astype(F32) + arrived[part]
        rest = own[: owners // 2].astype(BF)
        totals.append(own[owners // 2 :] + hop(rest, 1 - part))
    tiles = jnp.concatenate(totals, axis=3).astype(BF)
    groups = [
        [b * hold_count + h for b in range(g, field_count, 4) for h in range(hold_count)]
        for g in range(4)
    ]
    tiles = lax.all_to_all(
        tiles,
        ("beam", "slab"),
        split_axis=0,
        concat_axis=0,
        axis_index_groups=groups,
        tiled=True,
    )
    tiles = tiles.reshape((field_count // 4, hold_count) + tiles.shape[1:]).astype(F32)
    fields = [jnp.sum(tiles, axis=0).astype(BF)]
    crops = jnp.sum(crops.astype(F32), axis=0).astype(BF)

    own = lax.dynamic_index_in_dim(
        lax.dynamic_index_in_dim(table, field_pos, 0, keepdims=False), hold_pos, 0, keepdims=False
    )
    alpha = coefficients(own, beam_index, aberration).reshape(2, beam_total, own_slots * G)
    first_block = (field_pos * hold_count + hold_pos) * blocks_dev
    counts = lax.dynamic_slice_in_dim(tile_count, first_block, blocks_dev, 0)
    bins = detect_tables(beam_total)
    sums = detect(alpha, counts, fields, crops, plane_waves(beam_index), *bins)
    return sums[0, : own_slots * G * NDET].reshape(blocks_dev, slot_count, G, NDET)


def solution(mesh):
    return jax.shard_map(
        shards,
        mesh=mesh,
        in_specs=(P("beam", None), P("beam", None), P(), P(), P(), P()),
        out_specs=P(("beam", "slab"), None, None, None),
        check_vma=False,
    )
```

```python
import functools
import math

import jax
import jax.numpy as jnp
import ml_dtypes
import numpy as np
from jax import lax
from jax.experimental import pallas as pl
from jax.experimental.pallas import tpu as pltpu
from jax.sharding import PartitionSpec as P

A = 64
N = 4096
F = 64
G = 3
NDET = 16
QMAX = 3
LIMIT = N // 3
K2_LOW = -(LIMIT // A + 1 + QMAX)
K2_COUNT = 2 * (LIMIT // A + 1 + QMAX)
PART = 104
ROWS = 2 * PART
LANES = 128
SUB = 16
FEW = 4
HIGH = A // SUB
HALF = A // 2
PAIRS = A // 2
PARTS = 2
VMEM = 60 * 1024 * 1024
PITCH = A + 1
PITCH_Y = A // PARTS + 1
SMALL = pl.CostEstimate(flops=1 << 20, bytes_accessed=0, transcendentals=0)
BF = jnp.bfloat16
F32 = jnp.float32


def low(values):
    return np.asarray(values, dtype=np.float32).astype(ml_dtypes.bfloat16)


def turn(numerator, period):
    return np.exp(2j * np.pi * (numerator % period) / period)


def digits_k2():
    return K2_LOW + np.arange(K2_COUNT)


def spread(table, sub):
    both = np.stack([table.real, table.imag])
    return both[:, :, None, :, None] * np.eye(sub)[None, None, :, None, :]


def real_rows(table):
    return np.block([[table.real, -table.imag], [table.imag, table.real]])


def section_forward(k1):
    n1 = np.arange(A)
    return np.conj(turn(k1[:, None] * n1[None, :], A)) / A


def first_forward_x(k1):
    return low(spread(section_forward(k1), SUB).reshape(2 * len(k1) * SUB, A * SUB))


def first_forward_y():
    table = spread(section_forward(np.arange(A)), FEW).transpose(0, 2, 1, 3, 4)
    return low(table.reshape(2 * A * FEW, A * FEW))


def line_order(lanes):
    order = np.arange(lanes).reshape(-1, SUB // FEW, FEW).transpose(1, 0, 2).reshape(-1)
    out = np.zeros((lanes, lanes))
    out[order, np.arange(lanes)] = 1
    return low(out)


def last_forward_x(k1_pair):
    n2 = np.arange(A)
    out = np.zeros((2, PART, 2, 2, A))
    for ks, k1 in enumerate(k1_pair):
        freq = k1 + A * digits_k2()
        table = np.conj(turn(freq[:, None] * n2[None, :], N)) / A
        block = real_rows(table).reshape(2, K2_COUNT, 2, A)
        out[:, ks * K2_COUNT : (ks + 1) * K2_COUNT, ks] = block
    return low(out.reshape(ROWS, 4 * A))


def last_forward_y(k1_pair):
    n2 = np.arange(A)
    out = np.zeros((ROWS, 2, 2 * A))
    for e, k1 in enumerate(k1_pair):
        freq = k1 + A * digits_k2()
        table = np.conj(turn(freq[:, None] * n2[None, :], N)) / A
        out[e * PART : e * PART + 2 * K2_COUNT, e] = real_rows(table)
    return low(out.reshape(ROWS, 4 * A))


def first_inverse(k1):
    n2 = np.arange(A)
    freq = k1 + A * digits_k2()
    return turn(n2[:, None] * freq[None, :], N) * np.conj(turn(freq * freq, 2 * N))[None, :]


def first_inverse_y(k1_pair):
    out = np.zeros((2, 2 * A, PART))
    for e, k1 in enumerate(k1_pair):
        out[e, :, : 2 * K2_COUNT] = real_rows(first_inverse(k1))
    return low(out)


def first_inverse_x(k1_pair):
    out = np.zeros((2, LANES, 2, 2, A))
    for ks, k1 in enumerate(k1_pair):
        table = first_inverse(k1).T
        rows = slice(ks * K2_COUNT, (ks + 1) * K2_COUNT)
        out[0, rows, 0, ks] = table.real
        out[0, rows, 1, ks] = table.imag
        out[1, rows, 0, ks] = -table.imag
        out[1, rows, 1, ks] = table.real
    return low(out.reshape(2 * LANES, 4 * A))


def cosine(u):
    q = F32(COS_FIT[-1])
    for c in COS_FIT[-2::-1]:
        q = q * u + F32(c)
    return q


def sine_cosine(x):
    u = x * x
    s = F32(SIN_FIT[-1])
    for c in SIN_FIT[-2::-1]:
        s = s * u + F32(c)
    return s * x, cosine(u)


def fit(function, degree):
    top = 3.1421**2
    nodes = 0.5 * top * (1 - np.cos(np.pi * (np.arange(64) + 0.5) / 64))
    cheb = np.polynomial.chebyshev.Chebyshev.fit(
        nodes, function(np.sqrt(nodes)), degree, domain=[0, top]
    )
    return [float(c) for c in cheb.convert(kind=np.polynomial.Polynomial).coef]


SIN_FIT = fit(lambda x: np.sinc(x / np.pi), 5)
COS_FIT = fit(np.cos, 5)


def dot(a, b):
    return jnp.dot(a, b, preferred_element_type=F32)


def forward_x_kernel(sel, pot, section, last, perm, out, *scratch):
    fields, steps, _, lanes = out.shape
    waves, twisted = scratch[: 2 * steps], scratch[2 * steps :]
    half = section.shape[1] // 2
    chunks = N // LANES

    def fill(h, t):
        cos_ref, sin_ref = waves[2 * h], waves[2 * h + 1]
        block = pot[:, h, :, pl.ds(pl.multiple_of(t * LANES, LANES), LANES)]
        values = block.reshape(lanes, LANES).T.astype(F32)
        sine, cosine = sine_cosine(values)
        cos_ref[pl.ds(2 * t, 2)] = cosine.astype(BF).reshape(2, A, lanes)
        sin_ref[pl.ds(2 * t, 2)] = sine.astype(BF).reshape(2, A, lanes)

    def multiply(h, m):
        cos_ref, sin_ref = waves[2 * h], waves[2 * h + 1]
        start = pl.multiple_of(m * SUB, SUB)
        part_cos = cos_ref[:, pl.ds(start, SUB), :].reshape(A * SUB, lanes)
        part_sin = sin_ref[:, pl.ds(start, SUB), :].reshape(A * SUB, lanes)
        table = section[0]
        if lanes % LANES == 0:
            both = dot(table, jnp.concatenate([part_cos, part_sin], axis=1))
            of_cos, of_sin = both[:, :lanes], both[:, lanes:]
        else:
            of_cos, of_sin = dot(table, part_cos), dot(table, part_sin)
        real = of_cos[:half] - of_sin[half:]
        imag = of_cos[half:] + of_sin[:half]
        shape = (2 * fields, SUB, lanes)
        twisted[h][:, pl.ds(start, SUB), :] = real.astype(BF).reshape(shape)
        twisted[h][:, pl.ds(A + start, SUB), :] = imag.astype(BF).reshape(shape)

    def first(t, carry):
        fill(0, t)
        return carry

    lax.fori_loop(0, chunks, first, 0, unroll=4)
    for h in range(steps):

        def both(m, carry, h=h):
            multiply(h, m)
            if h + 1 < steps:
                for c in range(chunks // HIGH):
                    fill(h + 1, m * (chunks // HIGH) + c)
            return carry

        lax.fori_loop(0, HIGH, both, 0)
        for d in range(fields):
            lines = twisted[h][2 * d : 2 * d + 2].reshape(4 * A, lanes)
            out[d, h] = dot(dot(last[0, d], lines).astype(BF), perm[...]).astype(BF)


def forward_x(sel, pot, section, last, fields, part):
    groups = pot.shape[0] // A
    lanes = groups * SUB
    steps = HIGH // PARTS
    shape = (fields, steps, ROWS, lanes)
    return pl.pallas_call(
        forward_x_kernel,
        grid_spec=pltpu.PrefetchScalarGridSpec(
            num_scalar_prefetch=1,
            grid=(1,),
            in_specs=[
                pl.BlockSpec((groups, steps, SUB, N), lambda i, s: (0, part, 0, 0)),
                pl.BlockSpec((1,) + section.shape[1:], lambda i, s: (s[0], 0, 0)),
                pl.BlockSpec((1,) + last.shape[1:], lambda i, s: (s[0], 0, 0, 0)),
                pl.BlockSpec((lanes, lanes), lambda i, s: (0, 0)),
            ],
            out_specs=pl.BlockSpec(shape, lambda i, s: (0, 0, 0, 0)),
            scratch_shapes=[pltpu.VMEM((A, A, lanes), BF)] * (2 * steps)
            + [pltpu.VMEM((2 * fields, 2 * A, lanes), BF)] * steps,
        ),
        out_shape=jax.ShapeDtypeStruct(shape, BF),
        compiler_params=pltpu.CompilerParams(vmem_limit_bytes=VMEM),
        cost_estimate=SMALL,
        name="forward_x",
    )(sel, pot.reshape(groups, HIGH, SUB, N), section, last, line_order(lanes))


def first_section_y(lines, section, gathered, held):
    groups, steps = lines.shape[:2]
    span = LANES * FEW // SUB
    zeros = jnp.zeros((LANES - PART, LANES), F32)
    for g in range(groups):
        for h in range(steps):
            block = lines[g, h].astype(F32)
            both = jnp.concatenate([block[:PART], zeros, block[PART:], zeros], axis=0)
            turned = both.astype(BF).T
            columns = slice(2 * h * LANES, 2 * (h + 1) * LANES)
            for a in range(SUB // FEW):
                gathered[a, g * span : (g + 1) * span, columns] = turned[a * span : (a + 1) * span]
    half = A * FEW
    for a in range(SUB // FEW):
        both = dot(section[...], gathered[a])
        for h in range(steps):
            re = slice(2 * h * LANES, (2 * h + 1) * LANES)
            im = slice((2 * h + 1) * LANES, (2 * h + 2) * LANES)
            real = both[:half, re] - both[half:, im]
            imag = both[:half, im] + both[half:, re]
            for b in range(FEW):
                n2 = h * SUB + a * FEW + b
                rows = slice(b * A, (b + 1) * A)
                held[pl.ds(n2, A, stride=PITCH_Y), :] = real[rows]
                held[pl.ds(A * PITCH_Y + n2, A, stride=PITCH_Y), :] = imag[rows]


def first_section_scratch(lines):
    return [
        pltpu.VMEM((SUB // FEW, A * FEW, 2 * lines.shape[1] * LANES), BF),
        pltpu.VMEM(((2 * A + 1) * PITCH_Y, LANES), F32),
    ]


def forward_y_first_kernel(lines, section, twisted, gathered, held):
    first_section_y(lines, section, gathered, held)

    def digit(k, carry):
        for part in range(2):
            start = (part * A + k) * PITCH_Y
            twisted[k, part] = held[pl.ds(start, A // PARTS), :].astype(BF)
        return carry

    lax.fori_loop(0, A, digit, 0, unroll=8)


def forward_y_first(lines, section):
    return pl.pallas_call(
        forward_y_first_kernel,
        grid=(1,),
        in_specs=[
            pl.BlockSpec(lines.shape, lambda i: (0, 0, 0, 0)),
            pl.BlockSpec(section.shape, lambda i: (0, 0)),
        ],
        out_specs=pl.BlockSpec((A, 2, A // PARTS, LANES), lambda i: (0, 0, 0, 0)),
        out_shape=jax.ShapeDtypeStruct((A, 2, A // PARTS, LANES), BF),
        scratch_shapes=first_section_scratch(lines),
        compiler_params=pltpu.CompilerParams(vmem_limit_bytes=VMEM),
        cost_estimate=SMALL,
        name="forward_y_first",
    )(lines, section)


def forward_y_kernel(lines, section, earlier, last, *rest):
    out, gathered, held = rest[-3:]
    step = pl.program_id(0)

    @pl.when(step == 0)
    def _():
        first_section_y(lines, section, gathered, held)

    @pl.when(step > 0)
    def _():
        count = out.shape[0]
        base = (step - 1) * count
        for q in range(count):
            rows = []
            for e in range(2):
                for part in range(2):
                    k = 2 * (base + q) + e
                    rows.append(earlier[k, part])
                    start = (part * A + k) * PITCH_Y
                    rows.append(held[pl.ds(start, A // PARTS), :].astype(BF))
            out[q] = dot(last[q], jnp.concatenate(rows, axis=0)).astype(BF)


def forward_y(lines, section, earlier, last, after):
    steps = 2
    count = PAIRS // steps

    def late(i):
        return (jnp.maximum(i - 1, 0), 0, 0)

    return pl.pallas_call(
        forward_y_kernel,
        grid=(1 + steps,),
        in_specs=[
            pl.BlockSpec(lines.shape, lambda i: (0, 0, 0, 0)),
            pl.BlockSpec(section.shape, lambda i: (0, 0)),
            pl.BlockSpec(earlier.shape, lambda i: (0, 0, 0, 0)),
            pl.BlockSpec((count, ROWS, 4 * A), late),
        ]
        + [pl.BlockSpec(memory_space=pl.ANY)] * len(after),
        out_specs=pl.BlockSpec((count, ROWS, LANES), late),
        out_shape=jax.ShapeDtypeStruct((PAIRS, ROWS, LANES), BF),
        scratch_shapes=first_section_scratch(lines),
        compiler_params=pltpu.CompilerParams(vmem_limit_bytes=VMEM),
        cost_estimate=SMALL,
        name="forward_y",
    )(lines, section, earlier, last, *after)


def order_kernel(value, *rest):
    pass


def order(value, after):
    return pl.pallas_call(
        order_kernel,
        in_specs=[pl.BlockSpec(memory_space=pl.ANY)] * (1 + len(after)),
        out_specs=pl.BlockSpec(memory_space=pl.ANY),
        out_shape=jax.ShapeDtypeStruct(value.shape, value.dtype),
        input_output_aliases={0: 0},
        name="order",
    )(value, *after)


def inverse_kernel(steps, which, near, sel, *refs):
    specs = refs[:near]
    freq_y, square_x, table_y = refs[near : near + 3]
    tables_x = refs[near + 3 : 2 * near + 3]
    out, mid = refs[-2:]
    step = pl.program_id(0)
    count = PAIRS // steps
    each = HALF // steps
    limit = F32(LIMIT * LIMIT)
    whole = 2 * A * PITCH

    @pl.when(step < steps)
    def _():
        def pair(q, carry):
            pair_id = step * count + q
            offset = (2 * pair_id + sel[3 * which + 2]).astype(F32)
            row_freq = freq_y[...] + offset
            row_square = row_freq * row_freq
            values = []
            for x in range(near):
                inside = row_square + square_x[x] <= limit
                values.append(jnp.where(inside, specs[x][q].astype(F32), 0.0))
            for e in range(2):
                half = [v[e * PART : (e + 1) * PART].astype(BF) for v in values]
                half = half[0] if near == 1 else jnp.concatenate(half, axis=1)
                mixed = dot(table_y[q, e], half)
                for x in range(near):
                    for part in range(2):
                        spot = x * whole + part * A * PITCH + 2 * pair_id + e
                        mid[pl.ds(spot, A, stride=PITCH), :] = mixed[
                            part * A : (part + 1) * A, x * LANES : (x + 1) * LANES
                        ]
            return carry

        lax.fori_loop(0, count, pair, 0, unroll=8)

    @pl.when(step >= steps)
    def _():
        def line(i, carry):
            by = (step - steps) * each + i
            for x in range(near):
                rows = []
                for b in range(2):
                    start = x * whole + (by + b * HALF) * PITCH
                    real = mid[pl.ds(start, A), :].astype(BF)
                    imag = mid[pl.ds(start + A * PITCH, A), :].astype(BF)
                    rows.append(jnp.concatenate([real, imag], axis=1))
                product = dot(jnp.concatenate(rows, axis=0), tables_x[x][0, 0]).astype(BF)
                for b in range(2):
                    for part in range(2):
                        low_row = 2 * A * x + A * part
                        out[i, low_row : low_row + A, b * LANES : (b + 1) * LANES] = product[
                            b * A : (b + 1) * A, part * LANES : (part + 1) * LANES
                        ]
            return carry

        lax.fori_loop(0, each, line, 0, unroll=8)


def inverse(which, sel, specs, freq_y, square_x, table_y, table_x, after):
    near = len(specs)
    steps = 2
    count = PAIRS // steps
    each = HALF // steps

    def early(i, s):
        return jnp.minimum(i, steps - 1)

    def table_spec(x):
        return pl.BlockSpec(
            (1, 1) + table_x.shape[2:],
            lambda i, s: (s[3 * (which + x)], s[3 * (which + x) + 1], 0, 0),
        )

    return pl.pallas_call(
        functools.partial(inverse_kernel, steps, which, near),
        grid_spec=pltpu.PrefetchScalarGridSpec(
            num_scalar_prefetch=1,
            grid=(2 * steps,),
            in_specs=[pl.BlockSpec((count, ROWS, LANES), lambda i, s: (early(i, s), 0, 0))] * near
            + [
                pl.BlockSpec((ROWS, LANES), lambda i, s: (0, 0)),
                pl.BlockSpec((near, 1, LANES), lambda i, s: (which // near, 0, 0)),
                pl.BlockSpec((count, 2, 2 * A, PART), lambda i, s: (early(i, s), 0, 0, 0)),
            ]
            + [table_spec(x) for x in range(near)]
            + [pl.BlockSpec(memory_space=pl.ANY)] * len(after),
            out_specs=pl.BlockSpec(
                (each, 2 * A * near, 2 * LANES), lambda i, s: (jnp.maximum(i - steps, 0), 0, 0)
            ),
            scratch_shapes=[pltpu.VMEM(((near * 2 * A + 1) * PITCH, LANES), F32)],
        ),
        out_shape=jax.ShapeDtypeStruct((HALF, 2 * A * near, 2 * LANES), BF),
        compiler_params=pltpu.CompilerParams(vmem_limit_bytes=VMEM),
        cost_estimate=SMALL,
        name="inverse",
    )(sel, *specs, freq_y, square_x, table_y, *[table_x] * near, *after)


def collect_kernel(count, k1_pairs, *refs):
    sheets, places = refs[:count], refs[count]
    outs = refs[-2 - PARTS : -2]
    weights, held = refs[-2:]
    devices, _, slots, lines, _ = outs[0].shape
    each = sheets[0].shape[0]
    steps = lines // each
    step = pl.program_id(0) % steps
    part_id = pl.program_id(0) // steps
    tiles = devices * slots
    pitch = lines + 1
    lane = lax.broadcasted_iota(jnp.int32, (tiles, LANES), 1)
    lower = lane < A

    @pl.when(step == 0)
    def _():
        quarter = A // 4
        base = places[0, 0, 0] * (lane % A) + quarter * (lane // A)
        for x in range(weights.shape[1] // LANES):
            for ks in range(2):
                winding = base + places[0, 0, 1] * (k1_pairs[x] + ks)
                for part in range(2):
                    angle = ((winding - quarter * part) & (A - 1)) - A // 2
                    angle = angle.astype(F32) * F32(2.0 * math.pi / A)
                    rows = slice((2 * part + ks) * tiles, (2 * part + ks + 1) * tiles)
                    weights[rows, x * LANES : (x + 1) * LANES] = (-cosine(angle * angle)).astype(BF)

    def line(i, carry):
        stacked = sheets[0][i]
        if len(sheets) > 1:
            stacked = jnp.concatenate([sheet[i] for sheet in sheets], axis=0)
        sums = dot(weights[...], stacked)
        for part in range(2):
            even = sums[2 * part * tiles : (2 * part + 1) * tiles]
            odd = sums[(2 * part + 1) * tiles : (2 * part + 2) * tiles]
            keep = jnp.where(lower, even[:, :LANES], odd[:, LANES:])
            move = jnp.where(lower, even[:, LANES:], odd[:, :LANES])
            total = keep + pltpu.roll(move, A, 1)
            spot = part * tiles * pitch + step * each + i
            held[pl.ds(spot, tiles, stride=pitch), :] = total
        return carry

    lax.fori_loop(0, each, line, 0, unroll=8)

    for p, out in enumerate(outs):

        def device(d, carry, out=out):
            for part in range(2):
                for slot in range(slots):
                    start = (part * tiles + d * slots + slot) * pitch
                    out[d, part, slot] = held[pl.ds(start, lines), :].astype(BF)
            return carry

        @pl.when((step == steps - 1) & (part_id == p))
        def _(device=device):
            lax.fori_loop(0, devices, device, 0, unroll=4)


def collect(sheets, k1_pairs, places, devices, which, after):
    tiles = places.shape[3]
    lines = HALF // PARTS
    steps = 2
    shape = (devices, 2, tiles // devices, lines, LANES)
    depth = sum(sheet.shape[1] for sheet in sheets)
    sheet_spec = pl.BlockSpec((lines // steps,) + sheets[0].shape[1:], lambda i, s: (i, 0, 0))
    block = pl.BlockSpec(shape, lambda i, s: (0, 0, 0, 0, 0))
    return pl.pallas_call(
        functools.partial(collect_kernel, len(sheets)),
        grid_spec=pltpu.PrefetchScalarGridSpec(
            num_scalar_prefetch=1,
            grid=(PARTS * steps,),
            in_specs=[sheet_spec] * len(sheets)
            + [
                pl.BlockSpec(
                    (1, 1) + places.shape[2:], lambda i, s: (which, i // steps, 0, 0, 0)
                )
            ]
            + [pl.BlockSpec(memory_space=pl.ANY)] * len(after),
            out_specs=[block] * PARTS,
            scratch_shapes=[
                pltpu.VMEM((4 * tiles, depth), BF),
                pltpu.VMEM(((2 * tiles + 1) * (lines + 1), LANES), F32),
            ],
        ),
        out_shape=[jax.ShapeDtypeStruct(shape, BF)] * PARTS,
        compiler_params=pltpu.CompilerParams(vmem_limit_bytes=VMEM),
        cost_estimate=SMALL,
        name="collect",
    )(k1_pairs, *sheets, places, *after)


def crop_kernel(rows, cols, odd, mine, pot, after, out, held, sems):
    slots = out.shape[0]

    def copy(i):
        return pltpu.make_async_copy(
            pot.at[
                pl.ds(pl.multiple_of(rows[i] * A, A), A),
                pl.ds(pl.multiple_of(cols[i] * LANES, LANES), LANES),
            ],
            held.at[i],
            sems.at[i],
        )

    def begin(i, carry):
        copy(i).start()
        return carry

    def finish(i, carry):
        copy(i).wait()
        block = held[i].astype(F32)
        block = jnp.where(odd[i] == 1, pltpu.roll(block, A, 1), block)
        lane = lax.broadcasted_iota(jnp.int32, (HALF, LANES), 1)
        packed = jnp.where(lane < A, block[:HALF], pltpu.roll(block[HALF:], A, 1))
        out[i] = jnp.where(mine[i] == 1, packed, 0.0).astype(BF)
        return carry

    lax.fori_loop(0, slots, begin, 0)
    lax.fori_loop(0, slots, finish, 0)


def crop(rows, cols, odd, mine, pot, after):
    slots = rows.shape[0]
    return pl.pallas_call(
        crop_kernel,
        in_specs=[pl.BlockSpec(memory_space=pltpu.SMEM)] * 4
        + [pl.BlockSpec(memory_space=pl.ANY)] * 2,
        out_specs=pl.BlockSpec(memory_space=pltpu.VMEM),
        out_shape=jax.ShapeDtypeStruct((slots, HALF, LANES), BF),
        scratch_shapes=[pltpu.VMEM((slots, A, LANES), BF), pltpu.SemaphoreType.DMA((slots,))],
        compiler_params=pltpu.CompilerParams(vmem_limit_bytes=VMEM),
        cost_estimate=SMALL,
        name="crop",
    )(rows, cols, odd, mine, pot, after)


def detect_kernel(parts, alpha, counts, *refs):
    fields = refs[:parts]
    pot, plane, across, down, bins, out, lines, held = refs[parts:]
    beams, _, slots = fields[0].shape[:3]
    for s in range(slots):
        waves = []
        for j in range(beams):
            re, im = (
                jnp.concatenate([half[j, part, s] for half in fields], axis=0).astype(F32)
                for part in range(2)
            )
            cos, sin = plane[j, 0], plane[j, 1]
            waves.append((re * cos - im * sin, re * sin + im * cos))
        turned, level = sine_cosine(pot[s].astype(F32))
        for g in range(G):
            real = jnp.zeros((HALF, LANES), F32)
            imag = jnp.zeros((HALF, LANES), F32)
            for j in range(beams):
                cos, sin = alpha[0, j, s * G + g], alpha[1, j, s * G + g]
                re, im = waves[j]
                real = real + cos * re - sin * im
                imag = imag + cos * im + sin * re
            lines[2 * (s * G + g)] = (real * level - imag * turned).astype(BF)
            lines[2 * (s * G + g) + 1] = (real * turned + imag * level).astype(BF)
    total = slots * G
    first = dot(lines[...].reshape(2 * total * HALF, LANES), across[...])
    first = first.reshape(total, 2, HALF, 2 * LANES)
    real = (first[:, 0, :, :LANES] + first[:, 1, :, LANES:]).astype(BF)
    imag = (first[:, 1, :, :LANES] - first[:, 0, :, LANES:]).astype(BF)
    lane = lax.broadcasted_iota(jnp.int32, (A, LANES), 1)
    for i in range(total):
        both = jnp.concatenate([real[i], imag[i]], axis=1)
        mixed = dot(down[...], both)
        even, odd = mixed[: 2 * A], mixed[2 * A :]
        re_cos = even[:A, :LANES] + pltpu.roll(odd[:A, :LANES], A, 1)
        re_sin = even[A:, :LANES] + pltpu.roll(odd[A:, :LANES], A, 1)
        im_cos = even[:A, LANES:] + pltpu.roll(odd[:A, LANES:], A, 1)
        im_sin = even[A:, LANES:] + pltpu.roll(odd[A:, LANES:], A, 1)
        re = re_cos + im_sin
        im = im_cos - re_sin
        power = jnp.where(lane < A, re * re + im * im, 0.0)
        sums = jnp.sum(power[None] * bins[...], axis=1)
        block, slot = divmod(i // G, slots // counts.shape[0])
        active = slot < counts[block]
        held[i * NDET : (i + 1) * NDET, :] = jnp.where(active, sums, 0.0)
    out[...] = jnp.sum(held[...].T, axis=0, keepdims=True)


def detect(alpha, counts, fields, pot, plane, across, down, bins):
    slots = fields[0].shape[2]
    rows = -(-slots * G * NDET // LANES) * LANES
    smem = pl.BlockSpec(memory_space=pltpu.SMEM)
    vmem = pl.BlockSpec(memory_space=pltpu.VMEM)
    return pl.pallas_call(
        functools.partial(detect_kernel, len(fields)),
        in_specs=[smem, smem] + [vmem] * (5 + len(fields)),
        out_specs=vmem,
        out_shape=jax.ShapeDtypeStruct((1, rows), F32),
        scratch_shapes=[
            pltpu.VMEM((2 * slots * G, HALF, LANES), BF),
            pltpu.VMEM((rows, LANES), F32),
        ],
        compiler_params=pltpu.CompilerParams(vmem_limit_bytes=VMEM),
        name="detect",
    )(alpha, counts, *fields, pot, plane, across, down, bins)


def detect_tables(beam_total):
    n = np.arange(A)
    table = turn(n[:, None] * n[None, :], A) / A
    cos, sin = table.real, table.imag
    zero = np.zeros((A, A))
    across = np.block([[cos, zero, sin, zero], [zero, cos, zero, sin]])
    rows = np.concatenate([cos, sin], axis=0)
    down = np.concatenate([rows[:, :HALF], rows[:, HALF:]], axis=0)
    signed = np.where(n < A // 2, n, n - A)
    radius = signed[:, None] ** 2 + signed[None, :] ** 2
    width = A // (2 * NDET)
    bins = np.zeros((NDET, A, LANES))
    for d in range(NDET):
        member = (radius >= (width * d) ** 2) & (radius < (width * (d + 1)) ** 2)
        bins[d, :, :A] = member * (A * A / (beam_total * member.sum()))
    return low(across), low(down), bins.astype(np.float32)


def coefficients(tile_ids, beam_rows, shifts):
    across = N // A
    offsets = jnp.arange(G, dtype=jnp.int32)
    spot_y = (tile_ids // across)[:, None] * A + A // 2 + offsets[None, :]
    spot_x = (tile_ids % across)[:, None] * A + A // 2 + 2 * offsets[None, :]
    wave_y = jnp.remainder(F * beam_rows[:, 0], N)[:, None, None]
    wave_x = jnp.remainder(F * beam_rows[:, 1], N)[:, None, None]
    windings = (wave_y * spot_y[None] % N + wave_x * spot_x[None] % N) % N
    phases = shifts[:, None, None] + 2.0 * math.pi / N * windings.astype(F32)
    return jnp.stack([jnp.cos(phases), -jnp.sin(phases)])


def plane_waves(beam_index):
    by = jnp.arange(HALF, dtype=jnp.int32)[:, None] + HALF * (jnp.arange(LANES) // A)[None, :]
    bx = jnp.broadcast_to((jnp.arange(LANES, dtype=jnp.int32) % A)[None, :], by.shape)
    row_y = beam_index[:, 0][:, None, None]
    row_x = beam_index[:, 1][:, None, None]
    winding = (row_y * by[None] + row_x * bx[None] + HALF * (row_y + row_x)) % A
    angle = 2.0 * math.pi / A * winding.astype(F32)
    return jnp.stack([jnp.cos(angle), jnp.sin(angle)], axis=1)


def shards(pot_first, pot_second, beam_index, aberration, tile_table, tile_count):
    field_count = lax.axis_size("beam")
    hold_count = lax.axis_size("slab")
    field_pos = lax.axis_index("beam")
    hold_pos = lax.axis_index("slab")
    band_rows = pot_first.shape[0]
    band_tiles = band_rows // A
    width_k = A // field_count
    sheets = width_k // 2
    across = N // A
    beam_total = beam_index.shape[0]
    share = hold_pos % sheets

    section_x = np.stack(
        [
            first_forward_x(
                np.array(
                    [width_k * p + 2 * t + ks for p in range(field_count) for ks in range(2)]
                )
            )
            for t in range(sheets)
        ]
    )
    last_x = np.stack(
        [
            np.stack(
                [
                    last_forward_x([width_k * p + 2 * t, width_k * p + 2 * t + 1])
                    for p in range(field_count)
                ]
            )
            for t in range(sheets)
        ]
    )
    section_y = first_forward_y()
    last_y = np.stack([last_forward_y([2 * q, 2 * q + 1]) for q in range(PAIRS)])
    inverse_y = np.stack([first_inverse_y([2 * q, 2 * q + 1]) for q in range(PAIRS)])
    inverse_x = np.stack(
        [
            np.stack(
                [
                    first_inverse_x([width_k * p + 2 * t, width_k * p + 2 * t + 1])
                    for t in range(sheets)
                ]
            )
            for p in range(field_count)
        ]
    )

    blocks_dev = tile_table.shape[0] // (field_count * hold_count)
    slot_count = tile_table.shape[1]
    own_slots = blocks_dev * slot_count
    table = tile_table.reshape(field_count, hold_count, own_slots)

    def trade(value, axis):
        return lax.all_to_all(value, axis, split_axis=0, concat_axis=0, tiled=True)

    near = min(sheets, 2)
    far = sheets // near

    def swap(value, x):
        return lax.ppermute(value, "slab", [(i, i ^ x) for i in range(hold_count)])

    ids = lax.dynamic_index_in_dim(table, hold_pos, 1, keepdims=False).reshape(-1)
    tile_y, tile_x = ids // across, ids % across
    mine = (tile_y // band_tiles == field_pos).astype(jnp.int32)
    rows = jnp.clip(tile_y - field_pos * band_tiles, 0, band_tiles - 1)

    beam_row = lax.dynamic_index_in_dim(beam_index, hold_pos, 0, keepdims=False)
    pair_ids = share ^ jnp.arange(sheets, dtype=jnp.int32)
    k1_pairs = field_pos * width_k + 2 * pair_ids
    near_bit, far_bit = (jnp.stack([1 - v, v]) for v in (field_pos % 2, field_pos // 2 % 2))
    corners = table.reshape(field_count // 4, 2, 2, hold_count, own_slots)
    corners = corners.transpose(2, 1, 0, 3, 4)[near_bit][:, far_bit]
    sets = jnp.stack([corners, corners.transpose(1, 0, 2, 3, 4)], axis=1)
    sets = sets.reshape(2, PARTS, -1)
    places = jnp.stack([sets // across - beam_row[0], sets % across - beam_row[1]], axis=2)
    places = jnp.broadcast_to(places[..., None], places.shape + (LANES,))
    row = np.arange(ROWS)
    base = row // PART + A * (K2_LOW + row % PART % K2_COUNT)
    freq_y = np.broadcast_to(base[:, None], (ROWS, LANES)).astype(np.float32)
    lane = np.arange(LANES)
    base = np.where(lane < 2 * K2_COUNT, lane // K2_COUNT + A * (K2_LOW + lane % K2_COUNT), N)
    freq_x = (k1_pairs + F * beam_row[1])[:, None, None] + base.astype(np.int32)
    square_x = (freq_x * freq_x).astype(F32)
    scalars = jnp.stack(
        jnp.broadcast_arrays(field_pos, pair_ids, F * beam_row[0]), axis=-1
    )
    scalars = scalars.astype(jnp.int32).reshape(-1)

    sel = share.reshape(1).astype(jnp.int32)
    received = [[] for _ in range(far)]
    earlier = []
    for part in range(PARTS):
        lines = trade(forward_x(sel, pot_first, section_x, last_x, field_count, part), "beam")
        if lines.shape[3] != LANES:
            ratio = LANES // lines.shape[3]
            lines = lines.reshape(
                field_count // ratio, ratio, HIGH // PARTS, ROWS, SUB // FEW, -1
            )
            lines = lines.transpose(0, 2, 3, 4, 1, 5).reshape(-1, HIGH // PARTS, ROWS, LANES)
        if part:
            crops = crop(rows, tile_x // 2, tile_x % 2, mine, pot_second, earlier[0])
            lines = order(lines, [crops, square_x, places, scalars] + [r[0] for r in received[1:]])
        for f in range(far):
            received[f].append(swap(lines, f * near) if f else lines)
        if part == 0:
            earlier = [forward_y_first(received[f][0], section_y) for f in range(far)]
    waves = []
    for f in range(far):
        spec = forward_y(received[f][1], section_y, earlier[f], last_y, [crops] if f else [])
        ready = [spec] + [swap(spec, x) for x in range(1, near)]
        if f == 0:
            crops = order(crops.reshape(field_count, own_slots, HALF, LANES), [spec])
            crops = trade(crops, "beam")
        waves.append(
            inverse(
                f * near, scalars, ready, freq_y, square_x, inverse_y, inverse_x, waves[-1:]
            )
        )
    owners = field_count // 2 * hold_count
    other = collect(waves, k1_pairs, places, owners, 0, [crops])
    partial = other + collect(waves, k1_pairs, places, owners, 1, other[:1])

    def hop(value, bit):
        pairs = [(i, i ^ (1 << bit)) for i in range(field_count)]
        return lax.ppermute(value, "beam", pairs).astype(F32)

    totals = []
    arrived = [hop(partial[part], part) for part in range(PARTS)]
    for part in range(PARTS):
        own = partial[PARTS + part].astype(F32) + arrived[part]
        rest = own[: owners // 2].astype(BF)
        totals.append(own[owners // 2 :] + hop(rest, 1 - part))
    tiles = jnp.concatenate(totals, axis=3).astype(BF)
    groups = [
        [b * hold_count + h for b in range(g, field_count, 4) for h in range(hold_count)]
        for g in range(4)
    ]
    tiles = lax.all_to_all(
        tiles,
        ("beam", "slab"),
        split_axis=0,
        concat_axis=0,
        axis_index_groups=groups,
        tiled=True,
    )
    tiles = tiles.reshape((field_count // 4, hold_count) + tiles.shape[1:]).astype(F32)
    fields = [jnp.sum(tiles, axis=0).astype(BF)]
    crops = jnp.sum(crops.astype(F32), axis=0).astype(BF)

    own = lax.dynamic_index_in_dim(
        lax.dynamic_index_in_dim(table, field_pos, 0, keepdims=False), hold_pos, 0, keepdims=False
    )
    alpha = coefficients(own, beam_index, aberration).reshape(2, beam_total, own_slots * G)
    first_block = (field_pos * hold_count + hold_pos) * blocks_dev
    counts = lax.dynamic_slice_in_dim(tile_count, first_block, blocks_dev, 0)
    bins = detect_tables(beam_total)
    sums = detect(alpha, counts, fields, crops, plane_waves(beam_index), *bins)
    return sums[0, : own_slots * G * NDET].reshape(blocks_dev, slot_count, G, NDET)


def solution(mesh):
    return jax.shard_map(
        shards,
        mesh=mesh,
        in_specs=(P("beam", None), P("beam", None), P(), P(), P(), P()),
        out_specs=P(("beam", "slab"), None, None, None),
        check_vma=False,
    )
```

```python
import functools
import math

import jax
import jax.numpy as jnp
import ml_dtypes
import numpy as np
from jax import lax
from jax.experimental import pallas as pl
from jax.experimental.pallas import tpu as pltpu
from jax.sharding import PartitionSpec as P

A = 64
N = 4096
F = 64
G = 3
NDET = 16
QMAX = 3
LIMIT = N // 3
K2_LOW = -(LIMIT // A + 1 + QMAX)
K2_COUNT = 2 * (LIMIT // A + 1 + QMAX)
PART = 104
ROWS = 2 * PART
LANES = 128
SUB = 16
FEW = 4
HIGH = A // SUB
HALF = A // 2
PAIRS = A // 2
PARTS = 2
VMEM = 60 * 1024 * 1024
PITCH = A + 1
PITCH_Y = A // PARTS + 1
SMALL = pl.CostEstimate(flops=1 << 20, bytes_accessed=0, transcendentals=0)
BF = jnp.bfloat16
F32 = jnp.float32


def low(values):
    return np.asarray(values, dtype=np.float32).astype(ml_dtypes.bfloat16)


def turn(numerator, period):
    return np.exp(2j * np.pi * (numerator % period) / period)


def digits_k2():
    return K2_LOW + np.arange(K2_COUNT)


def spread(table, sub):
    both = np.stack([table.real, table.imag])
    return both[:, :, None, :, None] * np.eye(sub)[None, None, :, None, :]


def real_rows(table):
    return np.block([[table.real, -table.imag], [table.imag, table.real]])


def section_forward(k1):
    n1 = np.arange(A)
    return np.conj(turn(k1[:, None] * n1[None, :], A)) / A


def first_forward_x(k1):
    return low(spread(section_forward(k1), SUB).reshape(2 * len(k1) * SUB, A * SUB))


def first_forward_y():
    table = spread(section_forward(np.arange(A)), FEW).transpose(0, 2, 1, 3, 4)
    return low(table.reshape(2 * A * FEW, A * FEW))


def line_order(lanes):
    order = np.arange(lanes).reshape(-1, SUB // FEW, FEW).transpose(1, 0, 2).reshape(-1)
    out = np.zeros((lanes, lanes))
    out[order, np.arange(lanes)] = 1
    return low(out)


def last_forward_x(k1_pair):
    n2 = np.arange(A)
    out = np.zeros((2, PART, 2, 2, A))
    for ks, k1 in enumerate(k1_pair):
        freq = k1 + A * digits_k2()
        table = np.conj(turn(freq[:, None] * n2[None, :], N)) / A
        block = real_rows(table).reshape(2, K2_COUNT, 2, A)
        out[:, ks * K2_COUNT : (ks + 1) * K2_COUNT, ks] = block
    return low(out.reshape(ROWS, 4 * A))


def last_forward_y(k1_pair):
    n2 = np.arange(A)
    out = np.zeros((ROWS, 2, 2 * A))
    for e, k1 in enumerate(k1_pair):
        freq = k1 + A * digits_k2()
        table = np.conj(turn(freq[:, None] * n2[None, :], N)) / A
        out[e * PART : e * PART + 2 * K2_COUNT, e] = real_rows(table)
    return low(out.reshape(ROWS, 4 * A))


def first_inverse(k1):
    n2 = np.arange(A)
    freq = k1 + A * digits_k2()
    return turn(n2[:, None] * freq[None, :], N) * np.conj(turn(freq * freq, 2 * N))[None, :]


def first_inverse_y(k1_pair):
    out = np.zeros((2, 2 * A, PART))
    for e, k1 in enumerate(k1_pair):
        out[e, :, : 2 * K2_COUNT] = real_rows(first_inverse(k1))
    return low(out)


def first_inverse_x(k1_pair):
    out = np.zeros((2, LANES, 2, 2, A))
    for ks, k1 in enumerate(k1_pair):
        table = first_inverse(k1).T
        rows = slice(ks * K2_COUNT, (ks + 1) * K2_COUNT)
        out[0, rows, 0, ks] = table.real
        out[0, rows, 1, ks] = table.imag
        out[1, rows, 0, ks] = -table.imag
        out[1, rows, 1, ks] = table.real
    return low(out.reshape(2 * LANES, 4 * A))


def cosine(u):
    q = F32(COS_FIT[-1])
    for c in COS_FIT[-2::-1]:
        q = q * u + F32(c)
    return q


def sine_cosine(x):
    u = x * x
    s = F32(SIN_FIT[-1])
    for c in SIN_FIT[-2::-1]:
        s = s * u + F32(c)
    return s * x, cosine(u)


def fit(function, degree):
    top = 3.1421**2
    nodes = 0.5 * top * (1 - np.cos(np.pi * (np.arange(64) + 0.5) / 64))
    cheb = np.polynomial.chebyshev.Chebyshev.fit(
        nodes, function(np.sqrt(nodes)), degree, domain=[0, top]
    )
    return [float(c) for c in cheb.convert(kind=np.polynomial.Polynomial).coef]


SIN_FIT = fit(lambda x: np.sinc(x / np.pi), 5)
COS_FIT = fit(np.cos, 5)


def dot(a, b):
    return jnp.dot(a, b, preferred_element_type=F32)


def forward_x_kernel(sel, pot, section, last, perm, out, cos_ref, sin_ref, twisted):
    fields = out.shape[0]
    lanes = out.shape[3]
    half = section.shape[1] // 2

    def chunk(t, carry):
        block = pot[:, 0, :, pl.ds(pl.multiple_of(t * LANES, LANES), LANES)]
        values = block.reshape(lanes, LANES).T.astype(F32)
        sine, cosine = sine_cosine(values)
        cos_ref[pl.ds(2 * t, 2)] = cosine.astype(BF).reshape(2, A, lanes)
        sin_ref[pl.ds(2 * t, 2)] = sine.astype(BF).reshape(2, A, lanes)
        return carry

    lax.fori_loop(0, N // LANES, chunk, 0, unroll=8)
    table = section[0]
    for m in range(HIGH):
        span = slice(m * SUB, (m + 1) * SUB)
        part_cos = cos_ref[:, span, :].reshape(A * SUB, lanes)
        part_sin = sin_ref[:, span, :].reshape(A * SUB, lanes)
        if lanes % LANES == 0:
            both = dot(table, jnp.concatenate([part_cos, part_sin], axis=1))
            of_cos, of_sin = both[:, :lanes], both[:, lanes:]
        else:
            of_cos, of_sin = dot(table, part_cos), dot(table, part_sin)
        real = of_cos[:half] - of_sin[half:]
        imag = of_cos[half:] + of_sin[:half]
        twisted[:, m * SUB : (m + 1) * SUB, :] = real.astype(BF).reshape(2 * fields, SUB, lanes)
        twisted[:, A + m * SUB : A + (m + 1) * SUB, :] = imag.astype(BF).reshape(
            2 * fields, SUB, lanes
        )
    for d in range(fields):
        lines = twisted[2 * d : 2 * d + 2].reshape(4 * A, lanes)
        out[d, 0] = dot(dot(last[0, d], lines).astype(BF), perm[...]).astype(BF)


def forward_x(sel, pot, section, last, fields, part):
    groups = pot.shape[0] // A
    lanes = groups * SUB
    steps = HIGH // PARTS
    return pl.pallas_call(
        forward_x_kernel,
        grid_spec=pltpu.PrefetchScalarGridSpec(
            num_scalar_prefetch=1,
            grid=(steps,),
            in_specs=[
                pl.BlockSpec((groups, 1, SUB, N), lambda i, s: (0, part * steps + i, 0, 0)),
                pl.BlockSpec((1,) + section.shape[1:], lambda i, s: (s[0], 0, 0)),
                pl.BlockSpec((1,) + last.shape[1:], lambda i, s: (s[0], 0, 0, 0)),
                pl.BlockSpec((lanes, lanes), lambda i, s: (0, 0)),
            ],
            out_specs=pl.BlockSpec((fields, 1, ROWS, lanes), lambda i, s: (0, i, 0, 0)),
            scratch_shapes=[
                pltpu.VMEM((A, A, lanes), BF),
                pltpu.VMEM((A, A, lanes), BF),
                pltpu.VMEM((2 * fields, 2 * A, lanes), BF),
            ],
        ),
        out_shape=jax.ShapeDtypeStruct((fields, steps, ROWS, lanes), BF),
        compiler_params=pltpu.CompilerParams(vmem_limit_bytes=VMEM),
        cost_estimate=SMALL,
        name="forward_x",
    )(sel, pot.reshape(groups, HIGH, SUB, N), section, last, line_order(lanes))


def first_section_y(lines, section, gathered, held):
    groups, steps = lines.shape[:2]
    span = LANES * FEW // SUB
    zeros = jnp.zeros((LANES - PART, LANES), F32)
    for g in range(groups):
        for h in range(steps):
            block = lines[g, h].astype(F32)
            both = jnp.concatenate([block[:PART], zeros, block[PART:], zeros], axis=0)
            turned = both.astype(BF).T
            columns = slice(2 * h * LANES, 2 * (h + 1) * LANES)
            for a in range(SUB // FEW):
                gathered[a, g * span : (g + 1) * span, columns] = turned[a * span : (a + 1) * span]
    half = A * FEW
    for a in range(SUB // FEW):
        both = dot(section[...], gathered[a])
        for h in range(steps):
            re = slice(2 * h * LANES, (2 * h + 1) * LANES)
            im = slice((2 * h + 1) * LANES, (2 * h + 2) * LANES)
            real = both[:half, re] - both[half:, im]
            imag = both[:half, im] + both[half:, re]
            for b in range(FEW):
                n2 = h * SUB + a * FEW + b
                rows = slice(b * A, (b + 1) * A)
                held[pl.ds(n2, A, stride=PITCH_Y), :] = real[rows]
                held[pl.ds(A * PITCH_Y + n2, A, stride=PITCH_Y), :] = imag[rows]


def first_section_scratch(lines):
    return [
        pltpu.VMEM((SUB // FEW, A * FEW, 2 * lines.shape[1] * LANES), BF),
        pltpu.VMEM(((2 * A + 1) * PITCH_Y, LANES), F32),
    ]


def forward_y_first_kernel(lines, section, twisted, gathered, held):
    first_section_y(lines, section, gathered, held)

    def digit(k, carry):
        for part in range(2):
            start = (part * A + k) * PITCH_Y
            twisted[k, part] = held[pl.ds(start, A // PARTS), :].astype(BF)
        return carry

    lax.fori_loop(0, A, digit, 0, unroll=8)


def forward_y_first(lines, section):
    return pl.pallas_call(
        forward_y_first_kernel,
        grid=(1,),
        in_specs=[
            pl.BlockSpec(lines.shape, lambda i: (0, 0, 0, 0)),
            pl.BlockSpec(section.shape, lambda i: (0, 0)),
        ],
        out_specs=pl.BlockSpec((A, 2, A // PARTS, LANES), lambda i: (0, 0, 0, 0)),
        out_shape=jax.ShapeDtypeStruct((A, 2, A // PARTS, LANES), BF),
        scratch_shapes=first_section_scratch(lines),
        compiler_params=pltpu.CompilerParams(vmem_limit_bytes=VMEM),
        cost_estimate=SMALL,
        name="forward_y_first",
    )(lines, section)


def forward_y_kernel(lines, section, earlier, last, *rest):
    out, gathered, held = rest[-3:]
    step = pl.program_id(0)

    @pl.when(step == 0)
    def _():
        first_section_y(lines, section, gathered, held)

    @pl.when(step > 0)
    def _():
        count = out.shape[0]
        base = (step - 1) * count
        for q in range(count):
            rows = []
            for e in range(2):
                for part in range(2):
                    k = 2 * (base + q) + e
                    rows.append(earlier[k, part])
                    start = (part * A + k) * PITCH_Y
                    rows.append(held[pl.ds(start, A // PARTS), :].astype(BF))
            out[q] = dot(last[q], jnp.concatenate(rows, axis=0)).astype(BF)


def forward_y(lines, section, earlier, last, after):
    steps = 2
    count = PAIRS // steps

    def late(i):
        return (jnp.maximum(i - 1, 0), 0, 0)

    return pl.pallas_call(
        forward_y_kernel,
        grid=(1 + steps,),
        in_specs=[
            pl.BlockSpec(lines.shape, lambda i: (0, 0, 0, 0)),
            pl.BlockSpec(section.shape, lambda i: (0, 0)),
            pl.BlockSpec(earlier.shape, lambda i: (0, 0, 0, 0)),
            pl.BlockSpec((count, ROWS, 4 * A), late),
        ]
        + [pl.BlockSpec(memory_space=pl.ANY)] * len(after),
        out_specs=pl.BlockSpec((count, ROWS, LANES), late),
        out_shape=jax.ShapeDtypeStruct((PAIRS, ROWS, LANES), BF),
        scratch_shapes=first_section_scratch(lines),
        compiler_params=pltpu.CompilerParams(vmem_limit_bytes=VMEM),
        cost_estimate=SMALL,
        name="forward_y",
    )(lines, section, earlier, last, *after)


def order_kernel(value, *rest):
    pass


def order(value, after):
    return pl.pallas_call(
        order_kernel,
        in_specs=[pl.BlockSpec(memory_space=pl.ANY)] * (1 + len(after)),
        out_specs=pl.BlockSpec(memory_space=pl.ANY),
        out_shape=jax.ShapeDtypeStruct(value.shape, value.dtype),
        input_output_aliases={0: 0},
        name="order",
    )(value, *after)


def inverse_kernel(steps, which, near, sel, *refs):
    specs = refs[:near]
    freq_y, square_x, table_y = refs[near : near + 3]
    tables_x = refs[near + 3 : 2 * near + 3]
    out, mid = refs[-2:]
    step = pl.program_id(0)
    count = PAIRS // steps
    each = HALF // steps
    limit = F32(LIMIT * LIMIT)
    whole = 2 * A * PITCH

    @pl.when(step < steps)
    def _():
        def pair(q, carry):
            pair_id = step * count + q
            offset = (2 * pair_id + sel[3 * which + 2]).astype(F32)
            row_freq = freq_y[...] + offset
            row_square = row_freq * row_freq
            values = []
            for x in range(near):
                inside = row_square + square_x[x] <= limit
                values.append(jnp.where(inside, specs[x][q].astype(F32), 0.0))
            for e in range(2):
                half = [v[e * PART : (e + 1) * PART].astype(BF) for v in values]
                half = half[0] if near == 1 else jnp.concatenate(half, axis=1)
                mixed = dot(table_y[q, e], half)
                for x in range(near):
                    for part in range(2):
                        spot = x * whole + part * A * PITCH + 2 * pair_id + e
                        mid[pl.ds(spot, A, stride=PITCH), :] = mixed[
                            part * A : (part + 1) * A, x * LANES : (x + 1) * LANES
                        ]
            return carry

        lax.fori_loop(0, count, pair, 0, unroll=8)

    @pl.when(step >= steps)
    def _():
        def line(i, carry):
            by = (step - steps) * each + i
            for x in range(near):
                rows = []
                for b in range(2):
                    start = x * whole + (by + b * HALF) * PITCH
                    real = mid[pl.ds(start, A), :].astype(BF)
                    imag = mid[pl.ds(start + A * PITCH, A), :].astype(BF)
                    rows.append(jnp.concatenate([real, imag], axis=1))
                product = dot(jnp.concatenate(rows, axis=0), tables_x[x][0, 0]).astype(BF)
                for b in range(2):
                    for part in range(2):
                        low_row = 2 * A * x + A * part
                        out[i, low_row : low_row + A, b * LANES : (b + 1) * LANES] = product[
                            b * A : (b + 1) * A, part * LANES : (part + 1) * LANES
                        ]
            return carry

        lax.fori_loop(0, each, line, 0, unroll=8)


def inverse(which, sel, specs, freq_y, square_x, table_y, table_x, after):
    near = len(specs)
    steps = 2
    count = PAIRS // steps
    each = HALF // steps

    def early(i, s):
        return jnp.minimum(i, steps - 1)

    def table_spec(x):
        return pl.BlockSpec(
            (1, 1) + table_x.shape[2:],
            lambda i, s: (s[3 * (which + x)], s[3 * (which + x) + 1], 0, 0),
        )

    return pl.pallas_call(
        functools.partial(inverse_kernel, steps, which, near),
        grid_spec=pltpu.PrefetchScalarGridSpec(
            num_scalar_prefetch=1,
            grid=(2 * steps,),
            in_specs=[pl.BlockSpec((count, ROWS, LANES), lambda i, s: (early(i, s), 0, 0))] * near
            + [
                pl.BlockSpec((ROWS, LANES), lambda i, s: (0, 0)),
                pl.BlockSpec((near, 1, LANES), lambda i, s: (which // near, 0, 0)),
                pl.BlockSpec((count, 2, 2 * A, PART), lambda i, s: (early(i, s), 0, 0, 0)),
            ]
            + [table_spec(x) for x in range(near)]
            + [pl.BlockSpec(memory_space=pl.ANY)] * len(after),
            out_specs=pl.BlockSpec(
                (each, 2 * A * near, 2 * LANES), lambda i, s: (jnp.maximum(i - steps, 0), 0, 0)
            ),
            scratch_shapes=[pltpu.VMEM(((near * 2 * A + 1) * PITCH, LANES), F32)],
        ),
        out_shape=jax.ShapeDtypeStruct((HALF, 2 * A * near, 2 * LANES), BF),
        compiler_params=pltpu.CompilerParams(vmem_limit_bytes=VMEM),
        cost_estimate=SMALL,
        name="inverse",
    )(sel, *specs, freq_y, square_x, table_y, *[table_x] * near, *after)


def collect_kernel(count, k1_pairs, *refs):
    sheets, places = refs[:count], refs[count]
    outs = refs[-2 - PARTS : -2]
    weights, held = refs[-2:]
    devices, _, slots, lines, _ = outs[0].shape
    each = sheets[0].shape[0]
    steps = lines // each
    step = pl.program_id(0) % steps
    part_id = pl.program_id(0) // steps
    tiles = devices * slots
    pitch = lines + 1
    lane = lax.broadcasted_iota(jnp.int32, (tiles, LANES), 1)
    lower = lane < A

    @pl.when(step == 0)
    def _():
        quarter = A // 4
        base = places[0, 0, 0] * (lane % A) + quarter * (lane // A)
        for x in range(weights.shape[1] // LANES):
            for ks in range(2):
                winding = base + places[0, 0, 1] * (k1_pairs[x] + ks)
                for part in range(2):
                    angle = ((winding - quarter * part) & (A - 1)) - A // 2
                    angle = angle.astype(F32) * F32(2.0 * math.pi / A)
                    rows = slice((2 * part + ks) * tiles, (2 * part + ks + 1) * tiles)
                    weights[rows, x * LANES : (x + 1) * LANES] = (-cosine(angle * angle)).astype(BF)

    def line(i, carry):
        stacked = sheets[0][i]
        if len(sheets) > 1:
            stacked = jnp.concatenate([sheet[i] for sheet in sheets], axis=0)
        sums = dot(weights[...], stacked)
        for part in range(2):
            even = sums[2 * part * tiles : (2 * part + 1) * tiles]
            odd = sums[(2 * part + 1) * tiles : (2 * part + 2) * tiles]
            keep = jnp.where(lower, even[:, :LANES], odd[:, LANES:])
            move = jnp.where(lower, even[:, LANES:], odd[:, :LANES])
            total = keep + pltpu.roll(move, A, 1)
            spot = part * tiles * pitch + step * each + i
            held[pl.ds(spot, tiles, stride=pitch), :] = total
        return carry

    lax.fori_loop(0, each, line, 0, unroll=8)

    for p, out in enumerate(outs):

        def device(d, carry, out=out):
            for part in range(2):
                for slot in range(slots):
                    start = (part * tiles + d * slots + slot) * pitch
                    out[d, part, slot] = held[pl.ds(start, lines), :].astype(BF)
            return carry

        @pl.when((step == steps - 1) & (part_id == p))
        def _(device=device):
            lax.fori_loop(0, devices, device, 0, unroll=4)


def collect(sheets, k1_pairs, places, devices, which, after):
    tiles = places.shape[3]
    lines = HALF // PARTS
    steps = 2
    shape = (devices, 2, tiles // devices, lines, LANES)
    depth = sum(sheet.shape[1] for sheet in sheets)
    sheet_spec = pl.BlockSpec((lines // steps,) + sheets[0].shape[1:], lambda i, s: (i, 0, 0))
    block = pl.BlockSpec(shape, lambda i, s: (0, 0, 0, 0, 0))
    return pl.pallas_call(
        functools.partial(collect_kernel, len(sheets)),
        grid_spec=pltpu.PrefetchScalarGridSpec(
            num_scalar_prefetch=1,
            grid=(PARTS * steps,),
            in_specs=[sheet_spec] * len(sheets)
            + [
                pl.BlockSpec(
                    (1, 1) + places.shape[2:], lambda i, s: (which, i // steps, 0, 0, 0)
                )
            ]
            + [pl.BlockSpec(memory_space=pl.ANY)] * len(after),
            out_specs=[block] * PARTS,
            scratch_shapes=[
                pltpu.VMEM((4 * tiles, depth), BF),
                pltpu.VMEM(((2 * tiles + 1) * (lines + 1), LANES), F32),
            ],
        ),
        out_shape=[jax.ShapeDtypeStruct(shape, BF)] * PARTS,
        compiler_params=pltpu.CompilerParams(vmem_limit_bytes=VMEM),
        cost_estimate=SMALL,
        name="collect",
    )(k1_pairs, *sheets, places, *after)


def crop_kernel(rows, cols, odd, mine, pot, after, out, held, sems):
    slots = out.shape[0]

    def copy(i):
        return pltpu.make_async_copy(
            pot.at[
                pl.ds(pl.multiple_of(rows[i] * A, A), A),
                pl.ds(pl.multiple_of(cols[i] * LANES, LANES), LANES),
            ],
            held.at[i],
            sems.at[i],
        )

    def begin(i, carry):
        copy(i).start()
        return carry

    def finish(i, carry):
        copy(i).wait()
        block = held[i].astype(F32)
        block = jnp.where(odd[i] == 1, pltpu.roll(block, A, 1), block)
        lane = lax.broadcasted_iota(jnp.int32, (HALF, LANES), 1)
        packed = jnp.where(lane < A, block[:HALF], pltpu.roll(block[HALF:], A, 1))
        out[i] = jnp.where(mine[i] == 1, packed, 0.0).astype(BF)
        return carry

    lax.fori_loop(0, slots, begin, 0)
    lax.fori_loop(0, slots, finish, 0)


def crop(rows, cols, odd, mine, pot, after):
    slots = rows.shape[0]
    return pl.pallas_call(
        crop_kernel,
        in_specs=[pl.BlockSpec(memory_space=pltpu.SMEM)] * 4
        + [pl.BlockSpec(memory_space=pl.ANY)] * 2,
        out_specs=pl.BlockSpec(memory_space=pltpu.VMEM),
        out_shape=jax.ShapeDtypeStruct((slots, HALF, LANES), BF),
        scratch_shapes=[pltpu.VMEM((slots, A, LANES), BF), pltpu.SemaphoreType.DMA((slots,))],
        compiler_params=pltpu.CompilerParams(vmem_limit_bytes=VMEM),
        cost_estimate=SMALL,
        name="crop",
    )(rows, cols, odd, mine, pot, after)


def detect_kernel(parts, alpha, counts, *refs):
    fields = refs[:parts]
    pot, plane, across, down, bins, out, lines, held = refs[parts:]
    beams, _, slots = fields[0].shape[:3]
    for s in range(slots):
        waves = []
        for j in range(beams):
            re, im = (
                jnp.concatenate([half[j, part, s] for half in fields], axis=0).astype(F32)
                for part in range(2)
            )
            cos, sin = plane[j, 0], plane[j, 1]
            waves.append((re * cos - im * sin, re * sin + im * cos))
        turned, level = sine_cosine(pot[s].astype(F32))
        for g in range(G):
            real = jnp.zeros((HALF, LANES), F32)
            imag = jnp.zeros((HALF, LANES), F32)
            for j in range(beams):
                cos, sin = alpha[0, j, s * G + g], alpha[1, j, s * G + g]
                re, im = waves[j]
                real = real + cos * re - sin * im
                imag = imag + cos * im + sin * re
            lines[2 * (s * G + g)] = (real * level - imag * turned).astype(BF)
            lines[2 * (s * G + g) + 1] = (real * turned + imag * level).astype(BF)
    total = slots * G
    first = dot(lines[...].reshape(2 * total * HALF, LANES), across[...])
    first = first.reshape(total, 2, HALF, 2 * LANES)
    real = (first[:, 0, :, :LANES] + first[:, 1, :, LANES:]).astype(BF)
    imag = (first[:, 1, :, :LANES] - first[:, 0, :, LANES:]).astype(BF)
    lane = lax.broadcasted_iota(jnp.int32, (A, LANES), 1)
    for i in range(total):
        both = jnp.concatenate([real[i], imag[i]], axis=1)
        mixed = dot(down[...], both)
        even, odd = mixed[: 2 * A], mixed[2 * A :]
        re_cos = even[:A, :LANES] + pltpu.roll(odd[:A, :LANES], A, 1)
        re_sin = even[A:, :LANES] + pltpu.roll(odd[A:, :LANES], A, 1)
        im_cos = even[:A, LANES:] + pltpu.roll(odd[:A, LANES:], A, 1)
        im_sin = even[A:, LANES:] + pltpu.roll(odd[A:, LANES:], A, 1)
        re = re_cos + im_sin
        im = im_cos - re_sin
        power = jnp.where(lane < A, re * re + im * im, 0.0)
        sums = jnp.sum(power[None] * bins[...], axis=1)
        block, slot = divmod(i // G, slots // counts.shape[0])
        active = slot < counts[block]
        held[i * NDET : (i + 1) * NDET, :] = jnp.where(active, sums, 0.0)
    out[...] = jnp.sum(held[...].T, axis=0, keepdims=True)


def detect(alpha, counts, fields, pot, plane, across, down, bins):
    slots = fields[0].shape[2]
    rows = -(-slots * G * NDET // LANES) * LANES
    smem = pl.BlockSpec(memory_space=pltpu.SMEM)
    vmem = pl.BlockSpec(memory_space=pltpu.VMEM)
    return pl.pallas_call(
        functools.partial(detect_kernel, len(fields)),
        in_specs=[smem, smem] + [vmem] * (5 + len(fields)),
        out_specs=vmem,
        out_shape=jax.ShapeDtypeStruct((1, rows), F32),
        scratch_shapes=[
            pltpu.VMEM((2 * slots * G, HALF, LANES), BF),
            pltpu.VMEM((rows, LANES), F32),
        ],
        compiler_params=pltpu.CompilerParams(vmem_limit_bytes=VMEM),
        name="detect",
    )(alpha, counts, *fields, pot, plane, across, down, bins)


def detect_tables(beam_total):
    n = np.arange(A)
    table = turn(n[:, None] * n[None, :], A) / A
    cos, sin = table.real, table.imag
    zero = np.zeros((A, A))
    across = np.block([[cos, zero, sin, zero], [zero, cos, zero, sin]])
    rows = np.concatenate([cos, sin], axis=0)
    down = np.concatenate([rows[:, :HALF], rows[:, HALF:]], axis=0)
    signed = np.where(n < A // 2, n, n - A)
    radius = signed[:, None] ** 2 + signed[None, :] ** 2
    width = A // (2 * NDET)
    bins = np.zeros((NDET, A, LANES))
    for d in range(NDET):
        member = (radius >= (width * d) ** 2) & (radius < (width * (d + 1)) ** 2)
        bins[d, :, :A] = member * (A * A / (beam_total * member.sum()))
    return low(across), low(down), bins.astype(np.float32)


def coefficients(tile_ids, beam_rows, shifts):
    across = N // A
    offsets = jnp.arange(G, dtype=jnp.int32)
    spot_y = (tile_ids // across)[:, None] * A + A // 2 + offsets[None, :]
    spot_x = (tile_ids % across)[:, None] * A + A // 2 + 2 * offsets[None, :]
    wave_y = jnp.remainder(F * beam_rows[:, 0], N)[:, None, None]
    wave_x = jnp.remainder(F * beam_rows[:, 1], N)[:, None, None]
    windings = (wave_y * spot_y[None] % N + wave_x * spot_x[None] % N) % N
    phases = shifts[:, None, None] + 2.0 * math.pi / N * windings.astype(F32)
    return jnp.stack([jnp.cos(phases), -jnp.sin(phases)])


def plane_waves(beam_index):
    by = jnp.arange(HALF, dtype=jnp.int32)[:, None] + HALF * (jnp.arange(LANES) // A)[None, :]
    bx = jnp.broadcast_to((jnp.arange(LANES, dtype=jnp.int32) % A)[None, :], by.shape)
    row_y = beam_index[:, 0][:, None, None]
    row_x = beam_index[:, 1][:, None, None]
    winding = (row_y * by[None] + row_x * bx[None] + HALF * (row_y + row_x)) % A
    angle = 2.0 * math.pi / A * winding.astype(F32)
    return jnp.stack([jnp.cos(angle), jnp.sin(angle)], axis=1)


def shards(pot_first, pot_second, beam_index, aberration, tile_table, tile_count):
    field_count = lax.axis_size("beam")
    hold_count = lax.axis_size("slab")
    field_pos = lax.axis_index("beam")
    hold_pos = lax.axis_index("slab")
    band_rows = pot_first.shape[0]
    band_tiles = band_rows // A
    width_k = A // field_count
    sheets = width_k // 2
    across = N // A
    beam_total = beam_index.shape[0]
    share = hold_pos % sheets

    section_x = np.stack(
        [
            first_forward_x(
                np.array(
                    [width_k * p + 2 * t + ks for p in range(field_count) for ks in range(2)]
                )
            )
            for t in range(sheets)
        ]
    )
    last_x = np.stack(
        [
            np.stack(
                [
                    last_forward_x([width_k * p + 2 * t, width_k * p + 2 * t + 1])
                    for p in range(field_count)
                ]
            )
            for t in range(sheets)
        ]
    )
    section_y = first_forward_y()
    last_y = np.stack([last_forward_y([2 * q, 2 * q + 1]) for q in range(PAIRS)])
    inverse_y = np.stack([first_inverse_y([2 * q, 2 * q + 1]) for q in range(PAIRS)])
    inverse_x = np.stack(
        [
            np.stack(
                [
                    first_inverse_x([width_k * p + 2 * t, width_k * p + 2 * t + 1])
                    for t in range(sheets)
                ]
            )
            for p in range(field_count)
        ]
    )

    blocks_dev = tile_table.shape[0] // (field_count * hold_count)
    slot_count = tile_table.shape[1]
    own_slots = blocks_dev * slot_count
    table = tile_table.reshape(field_count, hold_count, own_slots)

    def trade(value, axis):
        return lax.all_to_all(value, axis, split_axis=0, concat_axis=0, tiled=True)

    near = min(sheets, 2)
    far = sheets // near

    def swap(value, x):
        return lax.ppermute(value, "slab", [(i, i ^ x) for i in range(hold_count)])

    ids = lax.dynamic_index_in_dim(table, hold_pos, 1, keepdims=False).reshape(-1)
    tile_y, tile_x = ids // across, ids % across
    mine = (tile_y // band_tiles == field_pos).astype(jnp.int32)
    rows = jnp.clip(tile_y - field_pos * band_tiles, 0, band_tiles - 1)
    columns, odd = tile_x // 2, tile_x % 2

    beam_row = lax.dynamic_index_in_dim(beam_index, hold_pos, 0, keepdims=False)
    pair_ids = share ^ jnp.arange(sheets, dtype=jnp.int32)
    k1_pairs = field_pos * width_k + 2 * pair_ids
    near_bit, far_bit = (jnp.stack([1 - v, v]) for v in (field_pos % 2, field_pos // 2 % 2))
    corners = table.reshape(field_count // 4, 2, 2, hold_count, own_slots)
    corners = corners.transpose(2, 1, 0, 3, 4)[near_bit][:, far_bit]
    sets = jnp.stack([corners, corners.transpose(1, 0, 2, 3, 4)], axis=1)
    sets = sets.reshape(2, PARTS, -1)
    places = jnp.stack([sets // across - beam_row[0], sets % across - beam_row[1]], axis=2)
    places = jnp.broadcast_to(places[..., None], places.shape + (LANES,))
    row = np.arange(ROWS)
    base = row // PART + A * (K2_LOW + row % PART % K2_COUNT)
    freq_y = np.broadcast_to(base[:, None], (ROWS, LANES)).astype(np.float32)
    lane = np.arange(LANES)
    base = np.where(lane < 2 * K2_COUNT, lane // K2_COUNT + A * (K2_LOW + lane % K2_COUNT), N)
    freq_x = (k1_pairs + F * beam_row[1])[:, None, None] + base.astype(np.int32)
    square_x = (freq_x * freq_x).astype(F32)
    scalars = jnp.stack(
        jnp.broadcast_arrays(field_pos, pair_ids, F * beam_row[0]), axis=-1
    )
    scalars = scalars.astype(jnp.int32).reshape(-1)

    sel = share.reshape(1).astype(jnp.int32)
    received = [[] for _ in range(far)]
    earlier = []
    for part in range(PARTS):
        lines = forward_x(sel, pot_first, section_x, last_x, field_count, part)
        if part:
            lines = order(lines, [places, scalars, square_x, rows, columns, odd, mine])
        lines = trade(lines, "beam")
        if lines.shape[3] != LANES:
            ratio = LANES // lines.shape[3]
            lines = lines.reshape(
                field_count // ratio, ratio, HIGH // PARTS, ROWS, SUB // FEW, -1
            )
            lines = lines.transpose(0, 2, 3, 4, 1, 5).reshape(-1, HIGH // PARTS, ROWS, LANES)
        if part:
            crops = crop(rows, columns, odd, mine, pot_second, earlier[0])
            lines = order(lines, [crops] + [r[0] for r in received[1:]])
        for f in range(far):
            received[f].append(swap(lines, f * near) if f else lines)
        if part == 0:
            earlier = [forward_y_first(received[f][0], section_y) for f in range(far)]
    crops = order(crops.reshape(field_count, own_slots, HALF, LANES), received[0][1:])
    crops = trade(crops, "beam")
    waves = []
    for f in range(far):
        spec = forward_y(received[f][1], section_y, earlier[f], last_y, [crops] if f else [])
        ready = [spec] + [swap(spec, x) for x in range(1, near)]
        waves.append(
            inverse(
                f * near, scalars, ready, freq_y, square_x, inverse_y, inverse_x, waves[-1:]
            )
        )
    owners = field_count // 2 * hold_count
    other = collect(waves, k1_pairs, places, owners, 0, [crops])
    partial = other + collect(waves, k1_pairs, places, owners, 1, other[:1])

    def hop(value, bit):
        pairs = [(i, i ^ (1 << bit)) for i in range(field_count)]
        return lax.ppermute(value, "beam", pairs).astype(F32)

    totals = []
    arrived = [hop(partial[part], part) for part in range(PARTS)]
    for part in range(PARTS):
        own = partial[PARTS + part].astype(F32) + arrived[part]
        rest = own[: owners // 2].astype(BF)
        totals.append(own[owners // 2 :] + hop(rest, 1 - part))
    tiles = jnp.concatenate(totals, axis=3).astype(BF)
    groups = [
        [b * hold_count + h for b in range(g, field_count, 4) for h in range(hold_count)]
        for g in range(4)
    ]
    tiles = lax.all_to_all(
        tiles,
        ("beam", "slab"),
        split_axis=0,
        concat_axis=0,
        axis_index_groups=groups,
        tiled=True,
    )
    tiles = tiles.reshape((field_count // 4, hold_count) + tiles.shape[1:]).astype(F32)
    fields = [jnp.sum(tiles, axis=0).astype(BF)]
    crops = jnp.sum(crops.astype(F32), axis=0).astype(BF)

    own = lax.dynamic_index_in_dim(
        lax.dynamic_index_in_dim(table, field_pos, 0, keepdims=False), hold_pos, 0, keepdims=False
    )
    alpha = coefficients(own, beam_index, aberration).reshape(2, beam_total, own_slots * G)
    first_block = (field_pos * hold_count + hold_pos) * blocks_dev
    counts = lax.dynamic_slice_in_dim(tile_count, first_block, blocks_dev, 0)
    bins = detect_tables(beam_total)
    sums = detect(alpha, counts, fields, crops, plane_waves(beam_index), *bins)
    return sums[0, : own_slots * G * NDET].reshape(blocks_dev, slot_count, G, NDET)


def solution(mesh):
    return jax.shard_map(
        shards,
        mesh=mesh,
        in_specs=(P("beam", None), P("beam", None), P(), P(), P(), P()),
        out_specs=P(("beam", "slab"), None, None, None),
        check_vma=False,
    )
```

```python
import functools
import math

import jax
import jax.numpy as jnp
import ml_dtypes
import numpy as np
from jax import lax
from jax.experimental import pallas as pl
from jax.experimental.pallas import tpu as pltpu
from jax.sharding import PartitionSpec as P

A = 64
N = 4096
F = 64
G = 3
NDET = 16
QMAX = 3
LIMIT = N // 3
K2_LOW = -(LIMIT // A + 1 + QMAX)
K2_COUNT = 2 * (LIMIT // A + 1 + QMAX)
PART = 104
ROWS = 2 * PART
LANES = 128
SUB = 16
FEW = 4
HIGH = A // SUB
HALF = A // 2
PAIRS = A // 2
PARTS = 2
VMEM = 60 * 1024 * 1024
PITCH = A + 1
PITCH_Y = A // PARTS + 1
SMALL = pl.CostEstimate(flops=1 << 20, bytes_accessed=0, transcendentals=0)
BF = jnp.bfloat16
F32 = jnp.float32


def low(values):
    return np.asarray(values, dtype=np.float32).astype(ml_dtypes.bfloat16)


def turn(numerator, period):
    return np.exp(2j * np.pi * (numerator % period) / period)


def digits_k2():
    return K2_LOW + np.arange(K2_COUNT)


def spread(table, sub):
    both = np.stack([table.real, table.imag])
    return both[:, :, None, :, None] * np.eye(sub)[None, None, :, None, :]


def real_rows(table):
    return np.block([[table.real, -table.imag], [table.imag, table.real]])


def section_forward(k1):
    n1 = np.arange(A)
    return np.conj(turn(k1[:, None] * n1[None, :], A)) / A


def first_forward_x(k1):
    return low(spread(section_forward(k1), SUB).reshape(2 * len(k1) * SUB, A * SUB))


def first_forward_y():
    table = spread(section_forward(np.arange(A)), FEW).transpose(0, 2, 1, 3, 4)
    return low(table.reshape(2 * A * FEW, A * FEW))


def line_order(lanes):
    order = np.arange(lanes).reshape(-1, SUB // FEW, FEW).transpose(1, 0, 2).reshape(-1)
    out = np.zeros((lanes, lanes))
    out[order, np.arange(lanes)] = 1
    return low(out)


def last_forward_x(k1_pair):
    n2 = np.arange(A)
    out = np.zeros((2, PART, 2, 2, A))
    for ks, k1 in enumerate(k1_pair):
        freq = k1 + A * digits_k2()
        table = np.conj(turn(freq[:, None] * n2[None, :], N)) / A
        block = real_rows(table).reshape(2, K2_COUNT, 2, A)
        out[:, ks * K2_COUNT : (ks + 1) * K2_COUNT, ks] = block
    return low(out.reshape(ROWS, 4 * A))


def last_forward_y(k1_pair):
    n2 = np.arange(A)
    out = np.zeros((ROWS, 2, 2 * A))
    for e, k1 in enumerate(k1_pair):
        freq = k1 + A * digits_k2()
        table = np.conj(turn(freq[:, None] * n2[None, :], N)) / A
        out[e * PART : e * PART + 2 * K2_COUNT, e] = real_rows(table)
    return low(out.reshape(ROWS, 4 * A))


def first_inverse(k1):
    n2 = np.arange(A)
    freq = k1 + A * digits_k2()
    return turn(n2[:, None] * freq[None, :], N) * np.conj(turn(freq * freq, 2 * N))[None, :]


def first_inverse_y(k1_pair):
    out = np.zeros((2, 2 * A, PART))
    for e, k1 in enumerate(k1_pair):
        out[e, :, : 2 * K2_COUNT] = real_rows(first_inverse(k1))
    return low(out)


def first_inverse_x(k1_pair):
    out = np.zeros((2, LANES, 2, 2, A))
    for ks, k1 in enumerate(k1_pair):
        table = first_inverse(k1).T
        rows = slice(ks * K2_COUNT, (ks + 1) * K2_COUNT)
        out[0, rows, 0, ks] = table.real
        out[0, rows, 1, ks] = table.imag
        out[1, rows, 0, ks] = -table.imag
        out[1, rows, 1, ks] = table.real
    return low(out.reshape(2 * LANES, 4 * A))


def cosine(u):
    q = F32(COS_FIT[-1])
    for c in COS_FIT[-2::-1]:
        q = q * u + F32(c)
    return q


def sine_cosine(x):
    u = x * x
    s = F32(SIN_FIT[-1])
    for c in SIN_FIT[-2::-1]:
        s = s * u + F32(c)
    return s * x, cosine(u)


def fit(function, degree):
    top = 3.1421**2
    nodes = 0.5 * top * (1 - np.cos(np.pi * (np.arange(64) + 0.5) / 64))
    cheb = np.polynomial.chebyshev.Chebyshev.fit(
        nodes, function(np.sqrt(nodes)), degree, domain=[0, top]
    )
    return [float(c) for c in cheb.convert(kind=np.polynomial.Polynomial).coef]


SIN_FIT = fit(lambda x: np.sinc(x / np.pi), 5)
COS_FIT = fit(np.cos, 5)


def dot(a, b):
    return jnp.dot(a, b, preferred_element_type=F32)


def forward_x_kernel(sel, pot, section, last, perm, out, cos_ref, sin_ref, twisted):
    fields = out.shape[0]
    lanes = out.shape[3]
    half = section.shape[1] // 2

    def chunk(t, carry):
        block = pot[:, 0, :, pl.ds(pl.multiple_of(t * LANES, LANES), LANES)]
        values = block.reshape(lanes, LANES).T.astype(F32)
        sine, cosine = sine_cosine(values)
        cos_ref[pl.ds(2 * t, 2)] = cosine.astype(BF).reshape(2, A, lanes)
        sin_ref[pl.ds(2 * t, 2)] = sine.astype(BF).reshape(2, A, lanes)
        return carry

    lax.fori_loop(0, N // LANES, chunk, 0, unroll=8)
    table = section[0]
    for m in range(HIGH):
        span = slice(m * SUB, (m + 1) * SUB)
        part_cos = cos_ref[:, span, :].reshape(A * SUB, lanes)
        part_sin = sin_ref[:, span, :].reshape(A * SUB, lanes)
        if lanes % LANES == 0:
            both = dot(table, jnp.concatenate([part_cos, part_sin], axis=1))
            of_cos, of_sin = both[:, :lanes], both[:, lanes:]
        else:
            of_cos, of_sin = dot(table, part_cos), dot(table, part_sin)
        real = of_cos[:half] - of_sin[half:]
        imag = of_cos[half:] + of_sin[:half]
        twisted[:, m * SUB : (m + 1) * SUB, :] = real.astype(BF).reshape(2 * fields, SUB, lanes)
        twisted[:, A + m * SUB : A + (m + 1) * SUB, :] = imag.astype(BF).reshape(
            2 * fields, SUB, lanes
        )
    for d in range(fields):
        lines = twisted[2 * d : 2 * d + 2].reshape(4 * A, lanes)
        out[d, 0] = dot(dot(last[0, d], lines).astype(BF), perm[...]).astype(BF)


def forward_x(sel, pot, section, last, fields, part):
    groups = pot.shape[0] // A
    lanes = groups * SUB
    steps = HIGH // PARTS
    return pl.pallas_call(
        forward_x_kernel,
        grid_spec=pltpu.PrefetchScalarGridSpec(
            num_scalar_prefetch=1,
            grid=(steps,),
            in_specs=[
                pl.BlockSpec((groups, 1, SUB, N), lambda i, s: (0, part * steps + i, 0, 0)),
                pl.BlockSpec((1,) + section.shape[1:], lambda i, s: (s[0], 0, 0)),
                pl.BlockSpec((1,) + last.shape[1:], lambda i, s: (s[0], 0, 0, 0)),
                pl.BlockSpec((lanes, lanes), lambda i, s: (0, 0)),
            ],
            out_specs=pl.BlockSpec((fields, 1, ROWS, lanes), lambda i, s: (0, i, 0, 0)),
            scratch_shapes=[
                pltpu.VMEM((A, A, lanes), BF),
                pltpu.VMEM((A, A, lanes), BF),
                pltpu.VMEM((2 * fields, 2 * A, lanes), BF),
            ],
        ),
        out_shape=jax.ShapeDtypeStruct((fields, steps, ROWS, lanes), BF),
        compiler_params=pltpu.CompilerParams(vmem_limit_bytes=VMEM),
        cost_estimate=SMALL,
        name="forward_x",
    )(sel, pot.reshape(groups, HIGH, SUB, N), section, last, line_order(lanes))


def first_section_y(lines, section, gathered, held):
    groups, steps = lines.shape[:2]
    span = LANES * FEW // SUB
    zeros = jnp.zeros((LANES - PART, LANES), F32)
    for g in range(groups):
        for h in range(steps):
            block = lines[g, h].astype(F32)
            both = jnp.concatenate([block[:PART], zeros, block[PART:], zeros], axis=0)
            turned = both.astype(BF).T
            columns = slice(2 * h * LANES, 2 * (h + 1) * LANES)
            for a in range(SUB // FEW):
                gathered[a, g * span : (g + 1) * span, columns] = turned[a * span : (a + 1) * span]
    half = A * FEW
    for a in range(SUB // FEW):
        both = dot(section[...], gathered[a])
        for h in range(steps):
            re = slice(2 * h * LANES, (2 * h + 1) * LANES)
            im = slice((2 * h + 1) * LANES, (2 * h + 2) * LANES)
            real = both[:half, re] - both[half:, im]
            imag = both[:half, im] + both[half:, re]
            for b in range(FEW):
                n2 = h * SUB + a * FEW + b
                rows = slice(b * A, (b + 1) * A)
                held[pl.ds(n2, A, stride=PITCH_Y), :] = real[rows]
                held[pl.ds(A * PITCH_Y + n2, A, stride=PITCH_Y), :] = imag[rows]


def first_section_scratch(lines):
    return [
        pltpu.VMEM((SUB // FEW, A * FEW, 2 * lines.shape[1] * LANES), BF),
        pltpu.VMEM(((2 * A + 1) * PITCH_Y, LANES), F32),
    ]


def forward_y_first_kernel(lines, section, twisted, gathered, held):
    first_section_y(lines, section, gathered, held)

    def digit(k, carry):
        for part in range(2):
            start = (part * A + k) * PITCH_Y
            twisted[k, part] = held[pl.ds(start, A // PARTS), :].astype(BF)
        return carry

    lax.fori_loop(0, A, digit, 0, unroll=8)


def forward_y_first(lines, section):
    return pl.pallas_call(
        forward_y_first_kernel,
        grid=(1,),
        in_specs=[
            pl.BlockSpec(lines.shape, lambda i: (0, 0, 0, 0)),
            pl.BlockSpec(section.shape, lambda i: (0, 0)),
        ],
        out_specs=pl.BlockSpec((A, 2, A // PARTS, LANES), lambda i: (0, 0, 0, 0)),
        out_shape=jax.ShapeDtypeStruct((A, 2, A // PARTS, LANES), BF),
        scratch_shapes=first_section_scratch(lines),
        compiler_params=pltpu.CompilerParams(vmem_limit_bytes=VMEM),
        cost_estimate=SMALL,
        name="forward_y_first",
    )(lines, section)


def forward_y_kernel(lines, section, earlier, last, *rest):
    out, gathered, held = rest[-3:]
    step = pl.program_id(0)

    @pl.when(step == 0)
    def _():
        first_section_y(lines, section, gathered, held)

    @pl.when(step > 0)
    def _():
        count = out.shape[0]
        base = (step - 1) * count
        for q in range(count):
            rows = []
            for e in range(2):
                for part in range(2):
                    k = 2 * (base + q) + e
                    rows.append(earlier[k, part])
                    start = (part * A + k) * PITCH_Y
                    rows.append(held[pl.ds(start, A // PARTS), :].astype(BF))
            out[q] = dot(last[q], jnp.concatenate(rows, axis=0)).astype(BF)


def forward_y(lines, section, earlier, last, after):
    steps = 2
    count = PAIRS // steps

    def late(i):
        return (jnp.maximum(i - 1, 0), 0, 0)

    return pl.pallas_call(
        forward_y_kernel,
        grid=(1 + steps,),
        in_specs=[
            pl.BlockSpec(lines.shape, lambda i: (0, 0, 0, 0)),
            pl.BlockSpec(section.shape, lambda i: (0, 0)),
            pl.BlockSpec(earlier.shape, lambda i: (0, 0, 0, 0)),
            pl.BlockSpec((count, ROWS, 4 * A), late),
        ]
        + [pl.BlockSpec(memory_space=pl.ANY)] * len(after),
        out_specs=pl.BlockSpec((count, ROWS, LANES), late),
        out_shape=jax.ShapeDtypeStruct((PAIRS, ROWS, LANES), BF),
        scratch_shapes=first_section_scratch(lines),
        compiler_params=pltpu.CompilerParams(vmem_limit_bytes=VMEM),
        cost_estimate=SMALL,
        name="forward_y",
    )(lines, section, earlier, last, *after)


def order_kernel(value, *rest):
    pass


def order(value, after):
    return pl.pallas_call(
        order_kernel,
        in_specs=[pl.BlockSpec(memory_space=pl.ANY)] * (1 + len(after)),
        out_specs=pl.BlockSpec(memory_space=pl.ANY),
        out_shape=jax.ShapeDtypeStruct(value.shape, value.dtype),
        input_output_aliases={0: 0},
        name="order",
    )(value, *after)


def inverse_kernel(steps, which, near, sel, *refs):
    specs = refs[:near]
    freq_y, square_x, table_y = refs[near : near + 3]
    tables_x = refs[near + 3 : 2 * near + 3]
    out, mid = refs[-2:]
    step = pl.program_id(0)
    count = PAIRS // steps
    each = HALF // steps
    limit = F32(LIMIT * LIMIT)
    whole = 2 * A * PITCH

    @pl.when(step < steps)
    def _():
        def pair(q, carry):
            pair_id = step * count + q
            offset = (2 * pair_id + sel[3 * which + 2]).astype(F32)
            row_freq = freq_y[...] + offset
            row_square = row_freq * row_freq
            values = []
            for x in range(near):
                inside = row_square + square_x[x] <= limit
                values.append(jnp.where(inside, specs[x][q].astype(F32), 0.0))
            for e in range(2):
                half = [v[e * PART : (e + 1) * PART].astype(BF) for v in values]
                half = half[0] if near == 1 else jnp.concatenate(half, axis=1)
                mixed = dot(table_y[q, e], half)
                for x in range(near):
                    for part in range(2):
                        spot = x * whole + part * A * PITCH + 2 * pair_id + e
                        mid[pl.ds(spot, A, stride=PITCH), :] = mixed[
                            part * A : (part + 1) * A, x * LANES : (x + 1) * LANES
                        ]
            return carry

        lax.fori_loop(0, count, pair, 0, unroll=8)

    @pl.when(step >= steps)
    def _():
        def line(i, carry):
            by = (step - steps) * each + i
            for x in range(near):
                rows = []
                for b in range(2):
                    start = x * whole + (by + b * HALF) * PITCH
                    real = mid[pl.ds(start, A), :].astype(BF)
                    imag = mid[pl.ds(start + A * PITCH, A), :].astype(BF)
                    rows.append(jnp.concatenate([real, imag], axis=1))
                product = dot(jnp.concatenate(rows, axis=0), tables_x[x][0, 0]).astype(BF)
                for b in range(2):
                    for part in range(2):
                        low_row = 2 * A * x + A * part
                        out[i, low_row : low_row + A, b * LANES : (b + 1) * LANES] = product[
                            b * A : (b + 1) * A, part * LANES : (part + 1) * LANES
                        ]
            return carry

        lax.fori_loop(0, each, line, 0, unroll=8)


def inverse(which, sel, specs, freq_y, square_x, table_y, table_x, after):
    near = len(specs)
    steps = 2
    count = PAIRS // steps
    each = HALF // steps

    def early(i, s):
        return jnp.minimum(i, steps - 1)

    def table_spec(x):
        return pl.BlockSpec(
            (1, 1) + table_x.shape[2:],
            lambda i, s: (s[3 * (which + x)], s[3 * (which + x) + 1], 0, 0),
        )

    return pl.pallas_call(
        functools.partial(inverse_kernel, steps, which, near),
        grid_spec=pltpu.PrefetchScalarGridSpec(
            num_scalar_prefetch=1,
            grid=(2 * steps,),
            in_specs=[pl.BlockSpec((count, ROWS, LANES), lambda i, s: (early(i, s), 0, 0))] * near
            + [
                pl.BlockSpec((ROWS, LANES), lambda i, s: (0, 0)),
                pl.BlockSpec((near, 1, LANES), lambda i, s: (which // near, 0, 0)),
                pl.BlockSpec((count, 2, 2 * A, PART), lambda i, s: (early(i, s), 0, 0, 0)),
            ]
            + [table_spec(x) for x in range(near)]
            + [pl.BlockSpec(memory_space=pl.ANY)] * len(after),
            out_specs=pl.BlockSpec(
                (each, 2 * A * near, 2 * LANES), lambda i, s: (jnp.maximum(i - steps, 0), 0, 0)
            ),
            scratch_shapes=[pltpu.VMEM(((near * 2 * A + 1) * PITCH, LANES), F32)],
        ),
        out_shape=jax.ShapeDtypeStruct((HALF, 2 * A * near, 2 * LANES), BF),
        compiler_params=pltpu.CompilerParams(vmem_limit_bytes=VMEM),
        cost_estimate=SMALL,
        name="inverse",
    )(sel, *specs, freq_y, square_x, table_y, *[table_x] * near, *after)


def collect_kernel(count, k1_pairs, *refs):
    sheets, places = refs[:count], refs[count]
    outs = refs[-2 - PARTS : -2]
    weights, held = refs[-2:]
    devices, _, slots, lines, _ = outs[0].shape
    each = sheets[0].shape[0]
    steps = lines // each
    step = pl.program_id(0) % steps
    part_id = pl.program_id(0) // steps
    tiles = devices * slots
    pitch = lines + 1
    lane = lax.broadcasted_iota(jnp.int32, (tiles, LANES), 1)
    lower = lane < A

    @pl.when(step == 0)
    def _():
        quarter = A // 4
        base = places[0, 0, 0] * (lane % A) + quarter * (lane // A)
        for x in range(weights.shape[1] // LANES):
            for ks in range(2):
                winding = base + places[0, 0, 1] * (k1_pairs[x] + ks)
                for part in range(2):
                    angle = ((winding - quarter * part) & (A - 1)) - A // 2
                    angle = angle.astype(F32) * F32(2.0 * math.pi / A)
                    rows = slice((2 * part + ks) * tiles, (2 * part + ks + 1) * tiles)
                    weights[rows, x * LANES : (x + 1) * LANES] = (-cosine(angle * angle)).astype(BF)

    def line(i, carry):
        stacked = sheets[0][i]
        if len(sheets) > 1:
            stacked = jnp.concatenate([sheet[i] for sheet in sheets], axis=0)
        sums = dot(weights[...], stacked)
        for part in range(2):
            even = sums[2 * part * tiles : (2 * part + 1) * tiles]
            odd = sums[(2 * part + 1) * tiles : (2 * part + 2) * tiles]
            keep = jnp.where(lower, even[:, :LANES], odd[:, LANES:])
            move = jnp.where(lower, even[:, LANES:], odd[:, :LANES])
            total = keep + pltpu.roll(move, A, 1)
            spot = part * tiles * pitch + step * each + i
            held[pl.ds(spot, tiles, stride=pitch), :] = total
        return carry

    lax.fori_loop(0, each, line, 0, unroll=8)

    for p, out in enumerate(outs):

        def device(d, carry, out=out):
            for part in range(2):
                for slot in range(slots):
                    start = (part * tiles + d * slots + slot) * pitch
                    out[d, part, slot] = held[pl.ds(start, lines), :].astype(BF)
            return carry

        @pl.when((step == steps - 1) & (part_id == p))
        def _(device=device):
            lax.fori_loop(0, devices, device, 0, unroll=4)


def collect(sheets, k1_pairs, places, devices, which, after):
    tiles = places.shape[3]
    lines = HALF // PARTS
    steps = 2
    shape = (devices, 2, tiles // devices, lines, LANES)
    depth = sum(sheet.shape[1] for sheet in sheets)
    sheet_spec = pl.BlockSpec((lines // steps,) + sheets[0].shape[1:], lambda i, s: (i, 0, 0))
    block = pl.BlockSpec(shape, lambda i, s: (0, 0, 0, 0, 0))
    return pl.pallas_call(
        functools.partial(collect_kernel, len(sheets)),
        grid_spec=pltpu.PrefetchScalarGridSpec(
            num_scalar_prefetch=1,
            grid=(PARTS * steps,),
            in_specs=[sheet_spec] * len(sheets)
            + [
                pl.BlockSpec(
                    (1, 1) + places.shape[2:], lambda i, s: (which, i // steps, 0, 0, 0)
                )
            ]
            + [pl.BlockSpec(memory_space=pl.ANY)] * len(after),
            out_specs=[block] * PARTS,
            scratch_shapes=[
                pltpu.VMEM((4 * tiles, depth), BF),
                pltpu.VMEM(((2 * tiles + 1) * (lines + 1), LANES), F32),
            ],
        ),
        out_shape=[jax.ShapeDtypeStruct(shape, BF)] * PARTS,
        compiler_params=pltpu.CompilerParams(vmem_limit_bytes=VMEM),
        cost_estimate=SMALL,
        name="collect",
    )(k1_pairs, *sheets, places, *after)


def crop_kernel(rows, cols, odd, mine, pot, after, out, held, sems):
    slots = out.shape[0]

    def copy(i):
        return pltpu.make_async_copy(
            pot.at[
                pl.ds(pl.multiple_of(rows[i] * A, A), A),
                pl.ds(pl.multiple_of(cols[i] * LANES, LANES), LANES),
            ],
            held.at[i],
            sems.at[i],
        )

    def begin(i, carry):
        copy(i).start()
        return carry

    def finish(i, carry):
        copy(i).wait()
        block = held[i].astype(F32)
        block = jnp.where(odd[i] == 1, pltpu.roll(block, A, 1), block)
        lane = lax.broadcasted_iota(jnp.int32, (HALF, LANES), 1)
        packed = jnp.where(lane < A, block[:HALF], pltpu.roll(block[HALF:], A, 1))
        out[i] = jnp.where(mine[i] == 1, packed, 0.0).astype(BF)
        return carry

    lax.fori_loop(0, slots, begin, 0)
    lax.fori_loop(0, slots, finish, 0)


def crop(rows, cols, odd, mine, pot, after):
    slots = rows.shape[0]
    return pl.pallas_call(
        crop_kernel,
        in_specs=[pl.BlockSpec(memory_space=pltpu.SMEM)] * 4
        + [pl.BlockSpec(memory_space=pl.ANY)] * 2,
        out_specs=pl.BlockSpec(memory_space=pltpu.VMEM),
        out_shape=jax.ShapeDtypeStruct((slots, HALF, LANES), BF),
        scratch_shapes=[pltpu.VMEM((slots, A, LANES), BF), pltpu.SemaphoreType.DMA((slots,))],
        compiler_params=pltpu.CompilerParams(vmem_limit_bytes=VMEM),
        cost_estimate=SMALL,
        name="crop",
    )(rows, cols, odd, mine, pot, after)


def detect_kernel(parts, alpha, counts, *refs):
    fields = refs[:parts]
    pot, plane, across, down, bins, out, lines, held = refs[parts:]
    beams, _, slots = fields[0].shape[:3]
    for s in range(slots):
        waves = []
        for j in range(beams):
            re, im = (
                jnp.concatenate([half[j, part, s] for half in fields], axis=0).astype(F32)
                for part in range(2)
            )
            cos, sin = plane[j, 0], plane[j, 1]
            waves.append((re * cos - im * sin, re * sin + im * cos))
        turned, level = sine_cosine(pot[s].astype(F32))
        for g in range(G):
            real = jnp.zeros((HALF, LANES), F32)
            imag = jnp.zeros((HALF, LANES), F32)
            for j in range(beams):
                cos, sin = alpha[0, j, s * G + g], alpha[1, j, s * G + g]
                re, im = waves[j]
                real = real + cos * re - sin * im
                imag = imag + cos * im + sin * re
            lines[2 * (s * G + g)] = (real * level - imag * turned).astype(BF)
            lines[2 * (s * G + g) + 1] = (real * turned + imag * level).astype(BF)
    total = slots * G
    first = dot(lines[...].reshape(2 * total * HALF, LANES), across[...])
    first = first.reshape(total, 2, HALF, 2 * LANES)
    real = (first[:, 0, :, :LANES] + first[:, 1, :, LANES:]).astype(BF)
    imag = (first[:, 1, :, :LANES] - first[:, 0, :, LANES:]).astype(BF)
    lane = lax.broadcasted_iota(jnp.int32, (A, LANES), 1)
    for i in range(total):
        both = jnp.concatenate([real[i], imag[i]], axis=1)
        mixed = dot(down[...], both)
        even, odd = mixed[: 2 * A], mixed[2 * A :]
        re_cos = even[:A, :LANES] + pltpu.roll(odd[:A, :LANES], A, 1)
        re_sin = even[A:, :LANES] + pltpu.roll(odd[A:, :LANES], A, 1)
        im_cos = even[:A, LANES:] + pltpu.roll(odd[:A, LANES:], A, 1)
        im_sin = even[A:, LANES:] + pltpu.roll(odd[A:, LANES:], A, 1)
        re = re_cos + im_sin
        im = im_cos - re_sin
        power = jnp.where(lane < A, re * re + im * im, 0.0)
        sums = jnp.sum(power[None] * bins[...], axis=1)
        block, slot = divmod(i // G, slots // counts.shape[0])
        active = slot < counts[block]
        held[i * NDET : (i + 1) * NDET, :] = jnp.where(active, sums, 0.0)
    sums = jnp.sum(held[...].T, axis=0, keepdims=True)
    each = slots // counts.shape[0]
    for i in range(total):
        block, slot = divmod(i // G, each)
        out[block, slot, i % G : i % G + 1, :] = sums[:, i * NDET : (i + 1) * NDET]


def detect(alpha, counts, fields, pot, plane, across, down, bins):
    slots = fields[0].shape[2]
    rows = -(-slots * G * NDET // LANES) * LANES
    blocks = counts.shape[0]
    smem = pl.BlockSpec(memory_space=pltpu.SMEM)
    vmem = pl.BlockSpec(memory_space=pltpu.VMEM)
    return pl.pallas_call(
        functools.partial(detect_kernel, len(fields)),
        in_specs=[smem, smem] + [vmem] * (5 + len(fields)),
        out_specs=vmem,
        out_shape=jax.ShapeDtypeStruct((blocks, slots // blocks, G, NDET), F32),
        scratch_shapes=[
            pltpu.VMEM((2 * slots * G, HALF, LANES), BF),
            pltpu.VMEM((rows, LANES), F32),
        ],
        compiler_params=pltpu.CompilerParams(vmem_limit_bytes=VMEM),
        name="detect",
    )(alpha, counts, *fields, pot, plane, across, down, bins)


def detect_tables(beam_total):
    n = np.arange(A)
    table = turn(n[:, None] * n[None, :], A) / A
    cos, sin = table.real, table.imag
    zero = np.zeros((A, A))
    across = np.block([[cos, zero, sin, zero], [zero, cos, zero, sin]])
    rows = np.concatenate([cos, sin], axis=0)
    down = np.concatenate([rows[:, :HALF], rows[:, HALF:]], axis=0)
    signed = np.where(n < A // 2, n, n - A)
    radius = signed[:, None] ** 2 + signed[None, :] ** 2
    width = A // (2 * NDET)
    bins = np.zeros((NDET, A, LANES))
    for d in range(NDET):
        member = (radius >= (width * d) ** 2) & (radius < (width * (d + 1)) ** 2)
        bins[d, :, :A] = member * (A * A / (beam_total * member.sum()))
    return low(across), low(down), bins.astype(np.float32)


def coefficients(tile_ids, beam_rows, shifts):
    across = N // A
    offsets = jnp.arange(G, dtype=jnp.int32)
    spot_y = (tile_ids // across)[:, None] * A + A // 2 + offsets[None, :]
    spot_x = (tile_ids % across)[:, None] * A + A // 2 + 2 * offsets[None, :]
    wave_y = jnp.remainder(F * beam_rows[:, 0], N)[:, None, None]
    wave_x = jnp.remainder(F * beam_rows[:, 1], N)[:, None, None]
    windings = (wave_y * spot_y[None] % N + wave_x * spot_x[None] % N) % N
    phases = shifts[:, None, None] + 2.0 * math.pi / N * windings.astype(F32)
    return jnp.stack([jnp.cos(phases), -jnp.sin(phases)])


def plane_waves(beam_index):
    by = jnp.arange(HALF, dtype=jnp.int32)[:, None] + HALF * (jnp.arange(LANES) // A)[None, :]
    bx = jnp.broadcast_to((jnp.arange(LANES, dtype=jnp.int32) % A)[None, :], by.shape)
    row_y = beam_index[:, 0][:, None, None]
    row_x = beam_index[:, 1][:, None, None]
    winding = (row_y * by[None] + row_x * bx[None] + HALF * (row_y + row_x)) % A
    angle = 2.0 * math.pi / A * winding.astype(F32)
    return jnp.stack([jnp.cos(angle), jnp.sin(angle)], axis=1)


def shards(pot_first, pot_second, beam_index, aberration, tile_table, tile_count):
    field_count = lax.axis_size("beam")
    hold_count = lax.axis_size("slab")
    field_pos = lax.axis_index("beam")
    hold_pos = lax.axis_index("slab")
    band_rows = pot_first.shape[0]
    band_tiles = band_rows // A
    width_k = A // field_count
    sheets = width_k // 2
    across = N // A
    beam_total = beam_index.shape[0]
    share = hold_pos % sheets

    section_x = np.stack(
        [
            first_forward_x(
                np.array(
                    [width_k * p + 2 * t + ks for p in range(field_count) for ks in range(2)]
                )
            )
            for t in range(sheets)
        ]
    )
    last_x = np.stack(
        [
            np.stack(
                [
                    last_forward_x([width_k * p + 2 * t, width_k * p + 2 * t + 1])
                    for p in range(field_count)
                ]
            )
            for t in range(sheets)
        ]
    )
    section_y = first_forward_y()
    last_y = np.stack([last_forward_y([2 * q, 2 * q + 1]) for q in range(PAIRS)])
    inverse_y = np.stack([first_inverse_y([2 * q, 2 * q + 1]) for q in range(PAIRS)])
    inverse_x = np.stack(
        [
            np.stack(
                [
                    first_inverse_x([width_k * p + 2 * t, width_k * p + 2 * t + 1])
                    for t in range(sheets)
                ]
            )
            for p in range(field_count)
        ]
    )

    blocks_dev = tile_table.shape[0] // (field_count * hold_count)
    slot_count = tile_table.shape[1]
    own_slots = blocks_dev * slot_count
    table = tile_table.reshape(field_count, hold_count, own_slots)

    def trade(value, axis):
        return lax.all_to_all(value, axis, split_axis=0, concat_axis=0, tiled=True)

    near = min(sheets, 2)
    far = sheets // near

    def swap(value, x):
        return lax.ppermute(value, "slab", [(i, i ^ x) for i in range(hold_count)])

    ids = lax.dynamic_index_in_dim(table, hold_pos, 1, keepdims=False).reshape(-1)
    tile_y, tile_x = ids // across, ids % across
    mine = (tile_y // band_tiles == field_pos).astype(jnp.int32)
    rows = jnp.clip(tile_y - field_pos * band_tiles, 0, band_tiles - 1)
    columns, odd = tile_x // 2, tile_x % 2

    beam_row = lax.dynamic_index_in_dim(beam_index, hold_pos, 0, keepdims=False)
    pair_ids = share ^ jnp.arange(sheets, dtype=jnp.int32)
    k1_pairs = field_pos * width_k + 2 * pair_ids
    near_bit, far_bit = (jnp.stack([1 - v, v]) for v in (field_pos % 2, field_pos // 2 % 2))
    corners = table.reshape(field_count // 4, 2, 2, hold_count, own_slots)
    corners = corners.transpose(2, 1, 0, 3, 4)[near_bit][:, far_bit]
    sets = jnp.stack([corners, corners.transpose(1, 0, 2, 3, 4)], axis=1)
    sets = sets.reshape(2, PARTS, -1)
    places = jnp.stack([sets // across - beam_row[0], sets % across - beam_row[1]], axis=2)
    places = jnp.broadcast_to(places[..., None], places.shape + (LANES,))
    row = np.arange(ROWS)
    base = row // PART + A * (K2_LOW + row % PART % K2_COUNT)
    freq_y = np.broadcast_to(base[:, None], (ROWS, LANES)).astype(np.float32)
    lane = np.arange(LANES)
    base = np.where(lane < 2 * K2_COUNT, lane // K2_COUNT + A * (K2_LOW + lane % K2_COUNT), N)
    freq_x = (k1_pairs + F * beam_row[1])[:, None, None] + base.astype(np.int32)
    square_x = (freq_x * freq_x).astype(F32)
    scalars = jnp.stack(
        jnp.broadcast_arrays(field_pos, pair_ids, F * beam_row[0]), axis=-1
    )
    scalars = scalars.astype(jnp.int32).reshape(-1)

    sel = share.reshape(1).astype(jnp.int32)
    received = [[] for _ in range(far)]
    earlier = []
    for part in range(PARTS):
        lines = forward_x(sel, pot_first, section_x, last_x, field_count, part)
        if part:
            lines = order(lines, [places, scalars, square_x, rows, columns, odd, mine])
        lines = trade(lines, "beam")
        if lines.shape[3] != LANES:
            ratio = LANES // lines.shape[3]
            lines = lines.reshape(
                field_count // ratio, ratio, HIGH // PARTS, ROWS, SUB // FEW, -1
            )
            lines = lines.transpose(0, 2, 3, 4, 1, 5).reshape(-1, HIGH // PARTS, ROWS, LANES)
        if part:
            crops = crop(rows, columns, odd, mine, pot_second, earlier[0])
            lines = order(lines, [crops] + [r[0] for r in received[1:]])
        for f in range(far):
            received[f].append(swap(lines, f * near) if f else lines)
        if part == 0:
            earlier = [forward_y_first(received[f][0], section_y) for f in range(far)]
    crops = order(crops.reshape(field_count, own_slots, HALF, LANES), received[0][1:])
    crops = trade(crops, "beam")
    waves = []
    for f in range(far):
        spec = forward_y(received[f][1], section_y, earlier[f], last_y, [crops] if f else [])
        ready = [spec] + [swap(spec, x) for x in range(1, near)]
        waves.append(
            inverse(
                f * near, scalars, ready, freq_y, square_x, inverse_y, inverse_x, waves[-1:]
            )
        )
    owners = field_count // 2 * hold_count
    other = collect(waves, k1_pairs, places, owners, 0, [crops])
    partial = other + collect(waves, k1_pairs, places, owners, 1, other[:1])

    def hop(value, bit):
        return lax.ppermute(value, "beam", [(i, i ^ (1 << bit)) for i in range(field_count)])

    def total(arrays, span):
        return functools.reduce(jnp.add, [array[span].astype(F32) for array in arrays])

    moving, staying = slice(0, owners // 2), slice(owners // 2, owners)
    arrived = [hop(partial[part], part) for part in range(PARTS)]
    halves = [[partial[PARTS + part], arrived[part]] for part in range(PARTS)]
    passed = [hop(total(halves[part], moving).astype(BF), 1 - part) for part in range(PARTS)]
    tiles = jnp.concatenate(
        [total(halves[part], staying) + passed[part].astype(F32) for part in range(PARTS)], axis=3
    ).astype(BF)
    groups = [
        [b * hold_count + h for b in range(g, field_count, 4) for h in range(hold_count)]
        for g in range(4)
    ]
    tiles = lax.all_to_all(
        tiles,
        ("beam", "slab"),
        split_axis=0,
        concat_axis=0,
        axis_index_groups=groups,
        tiled=True,
    )
    tiles = tiles.reshape((field_count // 4, hold_count) + tiles.shape[1:]).astype(F32)
    fields = [jnp.sum(tiles, axis=0).astype(BF)]
    crops = jnp.sum(crops.astype(F32), axis=0).astype(BF)

    own = lax.dynamic_index_in_dim(
        lax.dynamic_index_in_dim(table, field_pos, 0, keepdims=False), hold_pos, 0, keepdims=False
    )
    alpha = coefficients(own, beam_index, aberration).reshape(2, beam_total, own_slots * G)
    first_block = (field_pos * hold_count + hold_pos) * blocks_dev
    counts = lax.dynamic_slice_in_dim(tile_count, first_block, blocks_dev, 0)
    bins = detect_tables(beam_total)
    return detect(alpha, counts, fields, crops, plane_waves(beam_index), *bins)


def solution(mesh):
    return jax.shard_map(
        shards,
        mesh=mesh,
        in_specs=(P("beam", None), P("beam", None), P(), P(), P(), P()),
        out_specs=P(("beam", "slab"), None, None, None),
        check_vma=False,
    )
```

```python
import functools
import math

import jax
import jax.numpy as jnp
import ml_dtypes
import numpy as np
from jax import lax
from jax.experimental import pallas as pl
from jax.experimental.pallas import tpu as pltpu
from jax.sharding import PartitionSpec as P

A = 64
N = 4096
F = 64
G = 3
NDET = 16
QMAX = 3
LIMIT = N // 3
K2_LOW = -(LIMIT // A + 1 + QMAX)
K2_COUNT = 2 * (LIMIT // A + 1 + QMAX)
PART = 104
ROWS = 2 * PART
LANES = 128
SUB = 16
FEW = 4
HIGH = A // SUB
HALF = A // 2
PAIRS = A // 2
PARTS = 2
VMEM = 60 * 1024 * 1024
PITCH = A + 1
PITCH_Y = A // PARTS + 1
SMALL = pl.CostEstimate(flops=1 << 20, bytes_accessed=0, transcendentals=0)
BF = jnp.bfloat16
F32 = jnp.float32


def low(values):
    return np.asarray(values, dtype=np.float32).astype(ml_dtypes.bfloat16)


def turn(numerator, period):
    return np.exp(2j * np.pi * (numerator % period) / period)


def digits_k2():
    return K2_LOW + np.arange(K2_COUNT)


def spread(table, sub):
    both = np.stack([table.real, table.imag])
    return both[:, :, None, :, None] * np.eye(sub)[None, None, :, None, :]


def real_rows(table):
    return np.block([[table.real, -table.imag], [table.imag, table.real]])


def section_forward(k1):
    n1 = np.arange(A)
    return np.conj(turn(k1[:, None] * n1[None, :], A)) / A


def first_forward_x(k1):
    return low(spread(section_forward(k1), SUB).reshape(2 * len(k1) * SUB, A * SUB))


def first_forward_y():
    table = spread(section_forward(np.arange(A)), FEW).transpose(0, 2, 1, 3, 4)
    return low(table.reshape(2 * A * FEW, A * FEW))


def line_order(lanes):
    order = np.arange(lanes).reshape(-1, SUB // FEW, FEW).transpose(1, 0, 2).reshape(-1)
    out = np.zeros((lanes, lanes))
    out[order, np.arange(lanes)] = 1
    return low(out)


def last_forward_x(k1_pair):
    n2 = np.arange(A)
    out = np.zeros((2, PART, 2, 2, A))
    for ks, k1 in enumerate(k1_pair):
        freq = k1 + A * digits_k2()
        table = np.conj(turn(freq[:, None] * n2[None, :], N)) / A
        block = real_rows(table).reshape(2, K2_COUNT, 2, A)
        out[:, ks * K2_COUNT : (ks + 1) * K2_COUNT, ks] = block
    return low(out.reshape(ROWS, 4 * A))


def last_forward_y(k1_pair):
    n2 = np.arange(A)
    out = np.zeros((ROWS, 2, 2 * A))
    for e, k1 in enumerate(k1_pair):
        freq = k1 + A * digits_k2()
        table = np.conj(turn(freq[:, None] * n2[None, :], N)) / A
        out[e * PART : e * PART + 2 * K2_COUNT, e] = real_rows(table)
    return low(out.reshape(ROWS, 4 * A))


def first_inverse(k1):
    n2 = np.arange(A)
    freq = k1 + A * digits_k2()
    return turn(n2[:, None] * freq[None, :], N) * np.conj(turn(freq * freq, 2 * N))[None, :]


def first_inverse_y(k1_pair):
    out = np.zeros((2, 2 * A, PART))
    for e, k1 in enumerate(k1_pair):
        out[e, :, : 2 * K2_COUNT] = real_rows(first_inverse(k1))
    return low(out)


def first_inverse_x(k1_pair):
    out = np.zeros((2, LANES, 2, 2, A))
    for ks, k1 in enumerate(k1_pair):
        table = first_inverse(k1).T
        rows = slice(ks * K2_COUNT, (ks + 1) * K2_COUNT)
        out[0, rows, 0, ks] = table.real
        out[0, rows, 1, ks] = table.imag
        out[1, rows, 0, ks] = -table.imag
        out[1, rows, 1, ks] = table.real
    return low(out.reshape(2 * LANES, 4 * A))


def cosine(u):
    q = F32(COS_FIT[-1])
    for c in COS_FIT[-2::-1]:
        q = q * u + F32(c)
    return q


def sine_cosine(x):
    u = x * x
    s = F32(SIN_FIT[-1])
    for c in SIN_FIT[-2::-1]:
        s = s * u + F32(c)
    return s * x, cosine(u)


def fit(function, degree):
    top = 3.1421**2
    nodes = 0.5 * top * (1 - np.cos(np.pi * (np.arange(64) + 0.5) / 64))
    cheb = np.polynomial.chebyshev.Chebyshev.fit(
        nodes, function(np.sqrt(nodes)), degree, domain=[0, top]
    )
    return [float(c) for c in cheb.convert(kind=np.polynomial.Polynomial).coef]


SIN_FIT = fit(lambda x: np.sinc(x / np.pi), 5)
COS_FIT = fit(np.cos, 5)


def dot(a, b):
    return jnp.dot(a, b, preferred_element_type=F32)


def forward_x_kernel(sel, pot, section, last, perm, out, cos_ref, sin_ref, twisted):
    fields = out.shape[0]
    lanes = out.shape[3]
    half = section.shape[1] // 2

    def chunk(t, carry):
        block = pot[:, 0, :, pl.ds(pl.multiple_of(t * LANES, LANES), LANES)]
        values = block.reshape(lanes, LANES).T.astype(F32)
        sine, cosine = sine_cosine(values)
        cos_ref[pl.ds(2 * t, 2)] = cosine.astype(BF).reshape(2, A, lanes)
        sin_ref[pl.ds(2 * t, 2)] = sine.astype(BF).reshape(2, A, lanes)
        return carry

    lax.fori_loop(0, N // LANES, chunk, 0, unroll=16)
    table = section[0]
    for m in range(HIGH):
        span = slice(m * SUB, (m + 1) * SUB)
        part_cos = cos_ref[:, span, :].reshape(A * SUB, lanes)
        part_sin = sin_ref[:, span, :].reshape(A * SUB, lanes)
        if lanes % LANES == 0:
            both = dot(table, jnp.concatenate([part_cos, part_sin], axis=1))
            of_cos, of_sin = both[:, :lanes], both[:, lanes:]
        else:
            of_cos, of_sin = dot(table, part_cos), dot(table, part_sin)
        real = of_cos[:half] - of_sin[half:]
        imag = of_cos[half:] + of_sin[:half]
        twisted[:, m * SUB : (m + 1) * SUB, :] = real.astype(BF).reshape(2 * fields, SUB, lanes)
        twisted[:, A + m * SUB : A + (m + 1) * SUB, :] = imag.astype(BF).reshape(
            2 * fields, SUB, lanes
        )
    for d in range(fields):
        lines = twisted[2 * d : 2 * d + 2].reshape(4 * A, lanes)
        out[d, 0] = dot(dot(last[0, d], lines).astype(BF), perm[...]).astype(BF)


def forward_x(sel, pot, section, last, fields, part):
    groups = pot.shape[0] // A
    lanes = groups * SUB
    steps = HIGH // PARTS
    return pl.pallas_call(
        forward_x_kernel,
        grid_spec=pltpu.PrefetchScalarGridSpec(
            num_scalar_prefetch=1,
            grid=(steps,),
            in_specs=[
                pl.BlockSpec((groups, 1, SUB, N), lambda i, s: (0, part * steps + i, 0, 0)),
                pl.BlockSpec((1,) + section.shape[1:], lambda i, s: (s[0], 0, 0)),
                pl.BlockSpec((1,) + last.shape[1:], lambda i, s: (s[0], 0, 0, 0)),
                pl.BlockSpec((lanes, lanes), lambda i, s: (0, 0)),
            ],
            out_specs=pl.BlockSpec((fields, 1, ROWS, lanes), lambda i, s: (0, i, 0, 0)),
            scratch_shapes=[
                pltpu.VMEM((A, A, lanes), BF),
                pltpu.VMEM((A, A, lanes), BF),
                pltpu.VMEM((2 * fields, 2 * A, lanes), BF),
            ],
        ),
        out_shape=jax.ShapeDtypeStruct((fields, steps, ROWS, lanes), BF),
        compiler_params=pltpu.CompilerParams(vmem_limit_bytes=VMEM),
        cost_estimate=SMALL,
        name="forward_x",
    )(sel, pot.reshape(groups, HIGH, SUB, N), section, last, line_order(lanes))


def first_section_y(lines, section, gathered, held):
    groups, steps = lines.shape[:2]
    span = LANES * FEW // SUB
    zeros = jnp.zeros((LANES - PART, LANES), F32)
    for g in range(groups):
        for h in range(steps):
            block = lines[g, h].astype(F32)
            both = jnp.concatenate([block[:PART], zeros, block[PART:], zeros], axis=0)
            turned = both.astype(BF).T
            columns = slice(2 * h * LANES, 2 * (h + 1) * LANES)
            for a in range(SUB // FEW):
                gathered[a, g * span : (g + 1) * span, columns] = turned[a * span : (a + 1) * span]
    half = A * FEW
    for a in range(SUB // FEW):
        both = dot(section[...], gathered[a])
        for h in range(steps):
            re = slice(2 * h * LANES, (2 * h + 1) * LANES)
            im = slice((2 * h + 1) * LANES, (2 * h + 2) * LANES)
            real = both[:half, re] - both[half:, im]
            imag = both[:half, im] + both[half:, re]
            for b in range(FEW):
                n2 = h * SUB + a * FEW + b
                rows = slice(b * A, (b + 1) * A)
                held[pl.ds(n2, A, stride=PITCH_Y), :] = real[rows]
                held[pl.ds(A * PITCH_Y + n2, A, stride=PITCH_Y), :] = imag[rows]


def first_section_scratch(lines):
    return [
        pltpu.VMEM((SUB // FEW, A * FEW, 2 * lines.shape[1] * LANES), BF),
        pltpu.VMEM(((2 * A + 1) * PITCH_Y, LANES), F32),
    ]


def forward_y_first_kernel(lines, section, twisted, gathered, held):
    first_section_y(lines, section, gathered, held)

    def digit(k, carry):
        for part in range(2):
            start = (part * A + k) * PITCH_Y
            twisted[k, part] = held[pl.ds(start, A // PARTS), :].astype(BF)
        return carry

    lax.fori_loop(0, A, digit, 0, unroll=8)


def forward_y_first(lines, section):
    return pl.pallas_call(
        forward_y_first_kernel,
        grid=(1,),
        in_specs=[
            pl.BlockSpec(lines.shape, lambda i: (0, 0, 0, 0)),
            pl.BlockSpec(section.shape, lambda i: (0, 0)),
        ],
        out_specs=pl.BlockSpec((A, 2, A // PARTS, LANES), lambda i: (0, 0, 0, 0)),
        out_shape=jax.ShapeDtypeStruct((A, 2, A // PARTS, LANES), BF),
        scratch_shapes=first_section_scratch(lines),
        compiler_params=pltpu.CompilerParams(vmem_limit_bytes=VMEM),
        cost_estimate=SMALL,
        name="forward_y_first",
    )(lines, section)


def forward_y_kernel(lines, section, earlier, last, *rest):
    out, gathered, held = rest[-3:]
    step = pl.program_id(0)

    @pl.when(step == 0)
    def _():
        first_section_y(lines, section, gathered, held)

    @pl.when(step > 0)
    def _():
        count = out.shape[0]
        base = (step - 1) * count
        for q in range(count):
            rows = []
            for e in range(2):
                for part in range(2):
                    k = 2 * (base + q) + e
                    rows.append(earlier[k, part])
                    start = (part * A + k) * PITCH_Y
                    rows.append(held[pl.ds(start, A // PARTS), :].astype(BF))
            out[q] = dot(last[q], jnp.concatenate(rows, axis=0)).astype(BF)


def forward_y(lines, section, earlier, last, after):
    steps = 2
    count = PAIRS // steps

    def late(i):
        return (jnp.maximum(i - 1, 0), 0, 0)

    return pl.pallas_call(
        forward_y_kernel,
        grid=(1 + steps,),
        in_specs=[
            pl.BlockSpec(lines.shape, lambda i: (0, 0, 0, 0)),
            pl.BlockSpec(section.shape, lambda i: (0, 0)),
            pl.BlockSpec(earlier.shape, lambda i: (0, 0, 0, 0)),
            pl.BlockSpec((count, ROWS, 4 * A), late),
        ]
        + [pl.BlockSpec(memory_space=pl.ANY)] * len(after),
        out_specs=pl.BlockSpec((count, ROWS, LANES), late),
        out_shape=jax.ShapeDtypeStruct((PAIRS, ROWS, LANES), BF),
        scratch_shapes=first_section_scratch(lines),
        compiler_params=pltpu.CompilerParams(vmem_limit_bytes=VMEM),
        cost_estimate=SMALL,
        name="forward_y",
    )(lines, section, earlier, last, *after)


def order_kernel(value, *rest):
    pass


def order(value, after):
    return pl.pallas_call(
        order_kernel,
        in_specs=[pl.BlockSpec(memory_space=pl.ANY)] * (1 + len(after)),
        out_specs=pl.BlockSpec(memory_space=pl.ANY),
        out_shape=jax.ShapeDtypeStruct(value.shape, value.dtype),
        input_output_aliases={0: 0},
        name="order",
    )(value, *after)


def inverse_kernel(steps, which, near, sel, *refs):
    specs = refs[:near]
    freq_y, square_x, table_y = refs[near : near + 3]
    tables_x = refs[near + 3 : 2 * near + 3]
    out, mid = refs[-2:]
    step = pl.program_id(0)
    count = PAIRS // steps
    each = HALF // steps
    limit = F32(LIMIT * LIMIT)
    whole = 2 * A * PITCH

    @pl.when(step < steps)
    def _():
        def pair(q, carry):
            pair_id = step * count + q
            offset = (2 * pair_id + sel[3 * which + 2]).astype(F32)
            row_freq = freq_y[...] + offset
            row_square = row_freq * row_freq
            values = []
            for x in range(near):
                inside = row_square + square_x[x] <= limit
                values.append(jnp.where(inside, specs[x][q].astype(F32), 0.0))
            for e in range(2):
                half = [v[e * PART : (e + 1) * PART].astype(BF) for v in values]
                half = half[0] if near == 1 else jnp.concatenate(half, axis=1)
                mixed = dot(table_y[q, e], half)
                for x in range(near):
                    for part in range(2):
                        spot = x * whole + part * A * PITCH + 2 * pair_id + e
                        mid[pl.ds(spot, A, stride=PITCH), :] = mixed[
                            part * A : (part + 1) * A, x * LANES : (x + 1) * LANES
                        ]
            return carry

        lax.fori_loop(0, count, pair, 0, unroll=16)

    @pl.when(step >= steps)
    def _():
        def line(i, carry):
            by = (step - steps) * each + i
            for x in range(near):
                rows = []
                for b in range(2):
                    start = x * whole + (by + b * HALF) * PITCH
                    real = mid[pl.ds(start, A), :].astype(BF)
                    imag = mid[pl.ds(start + A * PITCH, A), :].astype(BF)
                    rows.append(jnp.concatenate([real, imag], axis=1))
                product = dot(jnp.concatenate(rows, axis=0), tables_x[x][0, 0]).astype(BF)
                for b in range(2):
                    for part in range(2):
                        low_row = 2 * A * x + A * part
                        out[i, low_row : low_row + A, b * LANES : (b + 1) * LANES] = product[
                            b * A : (b + 1) * A, part * LANES : (part + 1) * LANES
                        ]
            return carry

        lax.fori_loop(0, each, line, 0, unroll=16)


def inverse(which, sel, specs, freq_y, square_x, table_y, table_x, after):
    near = len(specs)
    steps = 2
    count = PAIRS // steps
    each = HALF // steps

    def early(i, s):
        return jnp.minimum(i, steps - 1)

    def table_spec(x):
        return pl.BlockSpec(
            (1, 1) + table_x.shape[2:],
            lambda i, s: (s[3 * (which + x)], s[3 * (which + x) + 1], 0, 0),
        )

    return pl.pallas_call(
        functools.partial(inverse_kernel, steps, which, near),
        grid_spec=pltpu.PrefetchScalarGridSpec(
            num_scalar_prefetch=1,
            grid=(2 * steps,),
            in_specs=[pl.BlockSpec((count, ROWS, LANES), lambda i, s: (early(i, s), 0, 0))] * near
            + [
                pl.BlockSpec((ROWS, LANES), lambda i, s: (0, 0)),
                pl.BlockSpec((near, 1, LANES), lambda i, s: (which // near, 0, 0)),
                pl.BlockSpec((count, 2, 2 * A, PART), lambda i, s: (early(i, s), 0, 0, 0)),
            ]
            + [table_spec(x) for x in range(near)]
            + [pl.BlockSpec(memory_space=pl.ANY)] * len(after),
            out_specs=pl.BlockSpec(
                (each, 2 * A * near, 2 * LANES), lambda i, s: (jnp.maximum(i - steps, 0), 0, 0)
            ),
            scratch_shapes=[pltpu.VMEM(((near * 2 * A + 1) * PITCH, LANES), F32)],
        ),
        out_shape=jax.ShapeDtypeStruct((HALF, 2 * A * near, 2 * LANES), BF),
        compiler_params=pltpu.CompilerParams(vmem_limit_bytes=VMEM),
        cost_estimate=SMALL,
        name="inverse",
    )(sel, *specs, freq_y, square_x, table_y, *[table_x] * near, *after)


def collect_kernel(count, k1_pairs, *refs):
    sheets, places = refs[:count], refs[count]
    outs = refs[-2 - PARTS : -2]
    weights, held = refs[-2:]
    devices, _, slots, lines, _ = outs[0].shape
    each = sheets[0].shape[0]
    steps = lines // each
    step = pl.program_id(0) % steps
    part_id = pl.program_id(0) // steps
    tiles = devices * slots
    pitch = lines + 1
    lane = lax.broadcasted_iota(jnp.int32, (tiles, LANES), 1)
    lower = lane < A

    @pl.when(step == 0)
    def _():
        quarter = A // 4
        base = places[0, 0, 0] * (lane % A) + quarter * (lane // A)
        for x in range(weights.shape[1] // LANES):
            for ks in range(2):
                winding = base + places[0, 0, 1] * (k1_pairs[x] + ks)
                for part in range(2):
                    angle = ((winding - quarter * part) & (A - 1)) - A // 2
                    angle = angle.astype(F32) * F32(2.0 * math.pi / A)
                    rows = slice((2 * part + ks) * tiles, (2 * part + ks + 1) * tiles)
                    weights[rows, x * LANES : (x + 1) * LANES] = (-cosine(angle * angle)).astype(BF)

    def line(i, carry):
        stacked = sheets[0][i]
        if len(sheets) > 1:
            stacked = jnp.concatenate([sheet[i] for sheet in sheets], axis=0)
        sums = dot(weights[...], stacked)
        for part in range(2):
            even = sums[2 * part * tiles : (2 * part + 1) * tiles]
            odd = sums[(2 * part + 1) * tiles : (2 * part + 2) * tiles]
            keep = jnp.where(lower, even[:, :LANES], odd[:, LANES:])
            move = jnp.where(lower, even[:, LANES:], odd[:, :LANES])
            total = keep + pltpu.roll(move, A, 1)
            spot = part * tiles * pitch + step * each + i
            held[pl.ds(spot, tiles, stride=pitch), :] = total
        return carry

    lax.fori_loop(0, each, line, 0, unroll=8)

    for p, out in enumerate(outs):

        def device(d, carry, out=out):
            for part in range(2):
                for slot in range(slots):
                    start = (part * tiles + d * slots + slot) * pitch
                    out[d, part, slot] = held[pl.ds(start, lines), :].astype(BF)
            return carry

        @pl.when((step == steps - 1) & (part_id == p))
        def _(device=device):
            lax.fori_loop(0, devices, device, 0, unroll=4)


def collect(sheets, k1_pairs, places, devices, which, after):
    tiles = places.shape[3]
    lines = HALF // PARTS
    steps = 2
    shape = (devices, 2, tiles // devices, lines, LANES)
    depth = sum(sheet.shape[1] for sheet in sheets)
    sheet_spec = pl.BlockSpec((lines // steps,) + sheets[0].shape[1:], lambda i, s: (i, 0, 0))
    block = pl.BlockSpec(shape, lambda i, s: (0, 0, 0, 0, 0))
    return pl.pallas_call(
        functools.partial(collect_kernel, len(sheets)),
        grid_spec=pltpu.PrefetchScalarGridSpec(
            num_scalar_prefetch=1,
            grid=(PARTS * steps,),
            in_specs=[sheet_spec] * len(sheets)
            + [
                pl.BlockSpec(
                    (1, 1) + places.shape[2:], lambda i, s: (which, i // steps, 0, 0, 0)
                )
            ]
            + [pl.BlockSpec(memory_space=pl.ANY)] * len(after),
            out_specs=[block] * PARTS,
            scratch_shapes=[
                pltpu.VMEM((4 * tiles, depth), BF),
                pltpu.VMEM(((2 * tiles + 1) * (lines + 1), LANES), F32),
            ],
        ),
        out_shape=[jax.ShapeDtypeStruct(shape, BF)] * PARTS,
        compiler_params=pltpu.CompilerParams(vmem_limit_bytes=VMEM),
        cost_estimate=SMALL,
        name="collect",
    )(k1_pairs, *sheets, places, *after)


def crop_kernel(rows, cols, odd, mine, pot, after, out, held, sems):
    slots = out.shape[0]

    def copy(i):
        return pltpu.make_async_copy(
            pot.at[
                pl.ds(pl.multiple_of(rows[i] * A, A), A),
                pl.ds(pl.multiple_of(cols[i] * LANES, LANES), LANES),
            ],
            held.at[i],
            sems.at[i],
        )

    def begin(i, carry):
        copy(i).start()
        return carry

    def finish(i, carry):
        copy(i).wait()
        block = held[i].astype(F32)
        block = jnp.where(odd[i] == 1, pltpu.roll(block, A, 1), block)
        lane = lax.broadcasted_iota(jnp.int32, (HALF, LANES), 1)
        packed = jnp.where(lane < A, block[:HALF], pltpu.roll(block[HALF:], A, 1))
        out[i] = jnp.where(mine[i] == 1, packed, 0.0).astype(BF)
        return carry

    lax.fori_loop(0, slots, begin, 0)
    lax.fori_loop(0, slots, finish, 0)


def crop(rows, cols, odd, mine, pot, after):
    slots = rows.shape[0]
    return pl.pallas_call(
        crop_kernel,
        in_specs=[pl.BlockSpec(memory_space=pltpu.SMEM)] * 4
        + [pl.BlockSpec(memory_space=pl.ANY)] * 2,
        out_specs=pl.BlockSpec(memory_space=pltpu.VMEM),
        out_shape=jax.ShapeDtypeStruct((slots, HALF, LANES), BF),
        scratch_shapes=[pltpu.VMEM((slots, A, LANES), BF), pltpu.SemaphoreType.DMA((slots,))],
        compiler_params=pltpu.CompilerParams(vmem_limit_bytes=VMEM),
        cost_estimate=SMALL,
        name="crop",
    )(rows, cols, odd, mine, pot, after)


def detect_kernel(parts, alpha, counts, *refs):
    fields = refs[:parts]
    pot, plane, across, down, bins, out, lines, held = refs[parts:]
    beams, _, slots = fields[0].shape[:3]
    for s in range(slots):
        waves = []
        for j in range(beams):
            re, im = (
                jnp.concatenate([half[j, part, s] for half in fields], axis=0).astype(F32)
                for part in range(2)
            )
            cos, sin = plane[j, 0], plane[j, 1]
            waves.append((re * cos - im * sin, re * sin + im * cos))
        turned, level = sine_cosine(pot[s].astype(F32))
        for g in range(G):
            real = jnp.zeros((HALF, LANES), F32)
            imag = jnp.zeros((HALF, LANES), F32)
            for j in range(beams):
                cos, sin = alpha[0, j, s * G + g], alpha[1, j, s * G + g]
                re, im = waves[j]
                real = real + cos * re - sin * im
                imag = imag + cos * im + sin * re
            lines[2 * (s * G + g)] = (real * level - imag * turned).astype(BF)
            lines[2 * (s * G + g) + 1] = (real * turned + imag * level).astype(BF)
    total = slots * G
    first = dot(lines[...].reshape(2 * total * HALF, LANES), across[...])
    first = first.reshape(total, 2, HALF, 2 * LANES)
    real = (first[:, 0, :, :LANES] + first[:, 1, :, LANES:]).astype(BF)
    imag = (first[:, 1, :, :LANES] - first[:, 0, :, LANES:]).astype(BF)
    lane = lax.broadcasted_iota(jnp.int32, (A, LANES), 1)
    for i in range(total):
        both = jnp.concatenate([real[i], imag[i]], axis=1)
        mixed = dot(down[...], both)
        even, odd = mixed[: 2 * A], mixed[2 * A :]
        re_cos = even[:A, :LANES] + pltpu.roll(odd[:A, :LANES], A, 1)
        re_sin = even[A:, :LANES] + pltpu.roll(odd[A:, :LANES], A, 1)
        im_cos = even[:A, LANES:] + pltpu.roll(odd[:A, LANES:], A, 1)
        im_sin = even[A:, LANES:] + pltpu.roll(odd[A:, LANES:], A, 1)
        re = re_cos + im_sin
        im = im_cos - re_sin
        power = jnp.where(lane < A, re * re + im * im, 0.0)
        sums = jnp.sum(power[None] * bins[...], axis=1)
        block, slot = divmod(i // G, slots // counts.shape[0])
        active = slot < counts[block]
        held[i * NDET : (i + 1) * NDET, :] = jnp.where(active, sums, 0.0)
    sums = jnp.sum(held[...].T, axis=0, keepdims=True)
    each = slots // counts.shape[0]
    for i in range(total):
        block, slot = divmod(i // G, each)
        out[block, slot, i % G : i % G + 1, :] = sums[:, i * NDET : (i + 1) * NDET]


def detect(alpha, counts, fields, pot, plane, across, down, bins):
    slots = fields[0].shape[2]
    rows = -(-slots * G * NDET // LANES) * LANES
    blocks = counts.shape[0]
    smem = pl.BlockSpec(memory_space=pltpu.SMEM)
    vmem = pl.BlockSpec(memory_space=pltpu.VMEM)
    return pl.pallas_call(
        functools.partial(detect_kernel, len(fields)),
        in_specs=[smem, smem] + [vmem] * (5 + len(fields)),
        out_specs=vmem,
        out_shape=jax.ShapeDtypeStruct((blocks, slots // blocks, G, NDET), F32),
        scratch_shapes=[
            pltpu.VMEM((2 * slots * G, HALF, LANES), BF),
            pltpu.VMEM((rows, LANES), F32),
        ],
        compiler_params=pltpu.CompilerParams(vmem_limit_bytes=VMEM),
        name="detect",
    )(alpha, counts, *fields, pot, plane, across, down, bins)


def detect_tables(beam_total):
    n = np.arange(A)
    table = turn(n[:, None] * n[None, :], A) / A
    cos, sin = table.real, table.imag
    zero = np.zeros((A, A))
    across = np.block([[cos, zero, sin, zero], [zero, cos, zero, sin]])
    rows = np.concatenate([cos, sin], axis=0)
    down = np.concatenate([rows[:, :HALF], rows[:, HALF:]], axis=0)
    signed = np.where(n < A // 2, n, n - A)
    radius = signed[:, None] ** 2 + signed[None, :] ** 2
    width = A // (2 * NDET)
    bins = np.zeros((NDET, A, LANES))
    for d in range(NDET):
        member = (radius >= (width * d) ** 2) & (radius < (width * (d + 1)) ** 2)
        bins[d, :, :A] = member * (A * A / (beam_total * member.sum()))
    return low(across), low(down), bins.astype(np.float32)


def coefficients(tile_ids, beam_rows, shifts):
    across = N // A
    offsets = jnp.arange(G, dtype=jnp.int32)
    spot_y = (tile_ids // across)[:, None] * A + A // 2 + offsets[None, :]
    spot_x = (tile_ids % across)[:, None] * A + A // 2 + 2 * offsets[None, :]
    wave_y = jnp.remainder(F * beam_rows[:, 0], N)[:, None, None]
    wave_x = jnp.remainder(F * beam_rows[:, 1], N)[:, None, None]
    windings = (wave_y * spot_y[None] % N + wave_x * spot_x[None] % N) % N
    phases = shifts[:, None, None] + 2.0 * math.pi / N * windings.astype(F32)
    return jnp.stack([jnp.cos(phases), -jnp.sin(phases)])


def plane_waves(beam_index):
    by = jnp.arange(HALF, dtype=jnp.int32)[:, None] + HALF * (jnp.arange(LANES) // A)[None, :]
    bx = jnp.broadcast_to((jnp.arange(LANES, dtype=jnp.int32) % A)[None, :], by.shape)
    row_y = beam_index[:, 0][:, None, None]
    row_x = beam_index[:, 1][:, None, None]
    winding = (row_y * by[None] + row_x * bx[None] + HALF * (row_y + row_x)) % A
    angle = 2.0 * math.pi / A * winding.astype(F32)
    return jnp.stack([jnp.cos(angle), jnp.sin(angle)], axis=1)


def shards(pot_first, pot_second, beam_index, aberration, tile_table, tile_count):
    field_count = lax.axis_size("beam")
    hold_count = lax.axis_size("slab")
    field_pos = lax.axis_index("beam")
    hold_pos = lax.axis_index("slab")
    band_rows = pot_first.shape[0]
    band_tiles = band_rows // A
    width_k = A // field_count
    sheets = width_k // 2
    across = N // A
    beam_total = beam_index.shape[0]
    share = hold_pos % sheets

    section_x = np.stack(
        [
            first_forward_x(
                np.array(
                    [width_k * p + 2 * t + ks for p in range(field_count) for ks in range(2)]
                )
            )
            for t in range(sheets)
        ]
    )
    last_x = np.stack(
        [
            np.stack(
                [
                    last_forward_x([width_k * p + 2 * t, width_k * p + 2 * t + 1])
                    for p in range(field_count)
                ]
            )
            for t in range(sheets)
        ]
    )
    section_y = first_forward_y()
    last_y = np.stack([last_forward_y([2 * q, 2 * q + 1]) for q in range(PAIRS)])
    inverse_y = np.stack([first_inverse_y([2 * q, 2 * q + 1]) for q in range(PAIRS)])
    inverse_x = np.stack(
        [
            np.stack(
                [
                    first_inverse_x([width_k * p + 2 * t, width_k * p + 2 * t + 1])
                    for t in range(sheets)
                ]
            )
            for p in range(field_count)
        ]
    )

    blocks_dev = tile_table.shape[0] // (field_count * hold_count)
    slot_count = tile_table.shape[1]
    own_slots = blocks_dev * slot_count
    table = tile_table.reshape(field_count, hold_count, own_slots)

    def trade(value, axis):
        return lax.all_to_all(value, axis, split_axis=0, concat_axis=0, tiled=True)

    near = min(sheets, 2)
    far = sheets // near

    def swap(value, x):
        return lax.ppermute(value, "slab", [(i, i ^ x) for i in range(hold_count)])

    ids = lax.dynamic_index_in_dim(table, hold_pos, 1, keepdims=False).reshape(-1)
    tile_y, tile_x = ids // across, ids % across
    mine = (tile_y // band_tiles == field_pos).astype(jnp.int32)
    rows = jnp.clip(tile_y - field_pos * band_tiles, 0, band_tiles - 1)
    columns, odd = tile_x // 2, tile_x % 2

    beam_row = lax.dynamic_index_in_dim(beam_index, hold_pos, 0, keepdims=False)
    pair_ids = share ^ jnp.arange(sheets, dtype=jnp.int32)
    k1_pairs = field_pos * width_k + 2 * pair_ids
    near_bit, far_bit = (jnp.stack([1 - v, v]) for v in (field_pos % 2, field_pos // 2 % 2))
    corners = table.reshape(field_count // 4, 2, 2, hold_count, own_slots)
    corners = corners.transpose(2, 1, 0, 3, 4)[near_bit][:, far_bit]
    sets = jnp.stack([corners, corners.transpose(1, 0, 2, 3, 4)], axis=1)
    sets = sets.reshape(2, PARTS, -1)
    places = jnp.stack([sets // across - beam_row[0], sets % across - beam_row[1]], axis=2)
    places = jnp.broadcast_to(places[..., None], places.shape + (LANES,))
    row = np.arange(ROWS)
    base = row // PART + A * (K2_LOW + row % PART % K2_COUNT)
    freq_y = np.broadcast_to(base[:, None], (ROWS, LANES)).astype(np.float32)
    lane = np.arange(LANES)
    base = np.where(lane < 2 * K2_COUNT, lane // K2_COUNT + A * (K2_LOW + lane % K2_COUNT), N)
    freq_x = (k1_pairs + F * beam_row[1])[:, None, None] + base.astype(np.int32)
    square_x = (freq_x * freq_x).astype(F32)
    scalars = jnp.stack(
        jnp.broadcast_arrays(field_pos, pair_ids, F * beam_row[0]), axis=-1
    )
    scalars = scalars.astype(jnp.int32).reshape(-1)

    sel = share.reshape(1).astype(jnp.int32)
    received = [[] for _ in range(far)]
    earlier = []
    for part in range(PARTS):
        lines = forward_x(sel, pot_first, section_x, last_x, field_count, part)
        if part:
            lines = order(lines, [places, scalars, square_x, rows, columns, odd, mine])
        lines = trade(lines, "beam")
        if lines.shape[3] != LANES:
            ratio = LANES // lines.shape[3]
            lines = lines.reshape(
                field_count // ratio, ratio, HIGH // PARTS, ROWS, SUB // FEW, -1
            )
            lines = lines.transpose(0, 2, 3, 4, 1, 5).reshape(-1, HIGH // PARTS, ROWS, LANES)
        if part:
            crops = crop(rows, columns, odd, mine, pot_second, earlier[0])
            lines = order(lines, [crops] + [r[0] for r in received[1:]])
        for f in range(far):
            received[f].append(swap(lines, f * near) if f else lines)
        if part == 0:
            earlier = [forward_y_first(received[f][0], section_y) for f in range(far)]
    crops = order(crops.reshape(field_count, own_slots, HALF, LANES), received[0][1:])
    crops = trade(crops, "beam")
    waves = []
    for f in range(far):
        spec = forward_y(received[f][1], section_y, earlier[f], last_y, [crops] if f else [])
        ready = [spec] + [swap(spec, x) for x in range(1, near)]
        waves.append(
            inverse(
                f * near, scalars, ready, freq_y, square_x, inverse_y, inverse_x, waves[-1:]
            )
        )
    owners = field_count // 2 * hold_count
    other = collect(waves, k1_pairs, places, owners, 0, [crops])
    partial = other + collect(waves, k1_pairs, places, owners, 1, other[:1])

    def hop(value, bit):
        return lax.ppermute(value, "beam", [(i, i ^ (1 << bit)) for i in range(field_count)])

    def total(arrays, span):
        return functools.reduce(jnp.add, [array[span].astype(F32) for array in arrays])

    moving, staying = slice(0, owners // 2), slice(owners // 2, owners)
    arrived = [hop(partial[part], part) for part in range(PARTS)]
    halves = [[partial[PARTS + part], arrived[part]] for part in range(PARTS)]
    passed = [hop(total(halves[part], moving).astype(BF), 1 - part) for part in range(PARTS)]
    tiles = jnp.concatenate(
        [total(halves[part], staying) + passed[part].astype(F32) for part in range(PARTS)], axis=3
    ).astype(BF)
    groups = [
        [b * hold_count + h for b in range(g, field_count, 4) for h in range(hold_count)]
        for g in range(4)
    ]
    tiles = lax.all_to_all(
        tiles,
        ("beam", "slab"),
        split_axis=0,
        concat_axis=0,
        axis_index_groups=groups,
        tiled=True,
    )
    tiles = tiles.reshape((field_count // 4, hold_count) + tiles.shape[1:]).astype(F32)
    fields = [jnp.sum(tiles, axis=0).astype(BF)]
    crops = jnp.sum(crops.astype(F32), axis=0).astype(BF)

    own = lax.dynamic_index_in_dim(
        lax.dynamic_index_in_dim(table, field_pos, 0, keepdims=False), hold_pos, 0, keepdims=False
    )
    alpha = coefficients(own, beam_index, aberration).reshape(2, beam_total, own_slots * G)
    first_block = (field_pos * hold_count + hold_pos) * blocks_dev
    counts = lax.dynamic_slice_in_dim(tile_count, first_block, blocks_dev, 0)
    bins = detect_tables(beam_total)
    return detect(alpha, counts, fields, crops, plane_waves(beam_index), *bins)


def solution(mesh):
    return jax.shard_map(
        shards,
        mesh=mesh,
        in_specs=(P("beam", None), P("beam", None), P(), P(), P(), P()),
        out_specs=P(("beam", "slab"), None, None, None),
        check_vma=False,
    )
```

```python
import functools
import math

import jax
import jax.numpy as jnp
import ml_dtypes
import numpy as np
from jax import lax
from jax.experimental import pallas as pl
from jax.experimental.pallas import tpu as pltpu
from jax.sharding import PartitionSpec as P

A = 64
N = 4096
F = 64
G = 3
NDET = 16
QMAX = 3
LIMIT = N // 3
K2_LOW = -(LIMIT // A + 1 + QMAX)
K2_COUNT = 2 * (LIMIT // A + 1 + QMAX)
PART = 104
ROWS = 2 * PART
LANES = 128
SUB = 16
FEW = 4
HIGH = A // SUB
HALF = A // 2
PAIRS = A // 2
PARTS = 2
VMEM = 60 * 1024 * 1024
PITCH = A + 1
PITCH_Y = A // PARTS + 1
SMALL = pl.CostEstimate(flops=1 << 20, bytes_accessed=0, transcendentals=0)
BF = jnp.bfloat16
F32 = jnp.float32


def low(values):
    return np.asarray(values, dtype=np.float32).astype(ml_dtypes.bfloat16)


def turn(numerator, period):
    return np.exp(2j * np.pi * (numerator % period) / period)


def digits_k2():
    return K2_LOW + np.arange(K2_COUNT)


def spread(table, sub):
    both = np.stack([table.real, table.imag])
    return both[:, :, None, :, None] * np.eye(sub)[None, None, :, None, :]


def real_rows(table):
    return np.block([[table.real, -table.imag], [table.imag, table.real]])


def section_forward(k1):
    n1 = np.arange(A)
    return np.conj(turn(k1[:, None] * n1[None, :], A)) / A


def first_forward_x(k1):
    return low(spread(section_forward(k1), SUB).reshape(2 * len(k1) * SUB, A * SUB))


def first_forward_y():
    table = spread(section_forward(np.arange(A)), FEW).transpose(0, 2, 1, 3, 4)
    return low(table.reshape(2 * A * FEW, A * FEW))


def line_order(lanes):
    order = np.arange(lanes).reshape(-1, SUB // FEW, FEW).transpose(1, 0, 2).reshape(-1)
    out = np.zeros((lanes, lanes))
    out[order, np.arange(lanes)] = 1
    return low(out)


def last_forward_x(k1_pair):
    n2 = np.arange(A)
    out = np.zeros((2, PART, 2, 2, A))
    for ks, k1 in enumerate(k1_pair):
        freq = k1 + A * digits_k2()
        table = np.conj(turn(freq[:, None] * n2[None, :], N)) / A
        block = real_rows(table).reshape(2, K2_COUNT, 2, A)
        out[:, ks * K2_COUNT : (ks + 1) * K2_COUNT, ks] = block
    return low(out.reshape(ROWS, 4 * A))


def last_forward_y(k1_pair):
    n2 = np.arange(A)
    out = np.zeros((ROWS, 2, 2 * A))
    for e, k1 in enumerate(k1_pair):
        freq = k1 + A * digits_k2()
        table = np.conj(turn(freq[:, None] * n2[None, :], N)) / A
        out[e * PART : e * PART + 2 * K2_COUNT, e] = real_rows(table)
    return low(out.reshape(ROWS, 4 * A))


def first_inverse(k1):
    n2 = np.arange(A)
    freq = k1 + A * digits_k2()
    return turn(n2[:, None] * freq[None, :], N) * np.conj(turn(freq * freq, 2 * N))[None, :]


def first_inverse_y(k1_pair):
    out = np.zeros((2, 2 * A, PART))
    for e, k1 in enumerate(k1_pair):
        out[e, :, : 2 * K2_COUNT] = real_rows(first_inverse(k1))
    return low(out)


def first_inverse_x(k1_pair):
    out = np.zeros((2, LANES, 2, 2, A))
    for ks, k1 in enumerate(k1_pair):
        table = first_inverse(k1).T
        rows = slice(ks * K2_COUNT, (ks + 1) * K2_COUNT)
        out[0, rows, 0, ks] = table.real
        out[0, rows, 1, ks] = table.imag
        out[1, rows, 0, ks] = -table.imag
        out[1, rows, 1, ks] = table.real
    return low(out.reshape(2 * LANES, 4 * A))


def cosine(u):
    q = F32(COS_FIT[-1])
    for c in COS_FIT[-2::-1]:
        q = q * u + F32(c)
    return q


def sine_cosine(x):
    u = x * x
    s = F32(SIN_FIT[-1])
    for c in SIN_FIT[-2::-1]:
        s = s * u + F32(c)
    return s * x, cosine(u)


def fit(function, degree):
    top = 3.1421**2
    nodes = 0.5 * top * (1 - np.cos(np.pi * (np.arange(64) + 0.5) / 64))
    cheb = np.polynomial.chebyshev.Chebyshev.fit(
        nodes, function(np.sqrt(nodes)), degree, domain=[0, top]
    )
    return [float(c) for c in cheb.convert(kind=np.polynomial.Polynomial).coef]


SIN_FIT = fit(lambda x: np.sinc(x / np.pi), 5)
COS_FIT = fit(np.cos, 5)


def dot(a, b):
    return jnp.dot(a, b, preferred_element_type=F32)


def forward_x_kernel(sel, pot, section, last, perm, out, cos_ref, sin_ref, twisted):
    fields = out.shape[0]
    lanes = out.shape[3]
    half = section.shape[1] // 2

    def chunk(t, carry):
        block = pot[:, 0, :, pl.ds(pl.multiple_of(t * LANES, LANES), LANES)]
        values = block.reshape(lanes, LANES).T.astype(F32)
        sine, cosine = sine_cosine(values)
        cos_ref[pl.ds(2 * t, 2)] = cosine.astype(BF).reshape(2, A, lanes)
        sin_ref[pl.ds(2 * t, 2)] = sine.astype(BF).reshape(2, A, lanes)
        return carry

    lax.fori_loop(0, N // LANES, chunk, 0, unroll=16)
    table = section[0]
    for m in range(HIGH):
        span = slice(m * SUB, (m + 1) * SUB)
        part_cos = cos_ref[:, span, :].reshape(A * SUB, lanes)
        part_sin = sin_ref[:, span, :].reshape(A * SUB, lanes)
        if lanes % LANES == 0:
            both = dot(table, jnp.concatenate([part_cos, part_sin], axis=1))
            of_cos, of_sin = both[:, :lanes], both[:, lanes:]
        else:
            of_cos, of_sin = dot(table, part_cos), dot(table, part_sin)
        real = of_cos[:half] - of_sin[half:]
        imag = of_cos[half:] + of_sin[:half]
        twisted[:, m * SUB : (m + 1) * SUB, :] = real.astype(BF).reshape(2 * fields, SUB, lanes)
        twisted[:, A + m * SUB : A + (m + 1) * SUB, :] = imag.astype(BF).reshape(
            2 * fields, SUB, lanes
        )
    for d in range(fields):
        lines = twisted[2 * d : 2 * d + 2].reshape(4 * A, lanes)
        out[d, 0] = dot(dot(last[0, d], lines).astype(BF), perm[...]).astype(BF)


def forward_x(sel, pot, section, last, fields, part):
    groups = pot.shape[0] // A
    lanes = groups * SUB
    steps = HIGH // PARTS
    return pl.pallas_call(
        forward_x_kernel,
        grid_spec=pltpu.PrefetchScalarGridSpec(
            num_scalar_prefetch=1,
            grid=(steps,),
            in_specs=[
                pl.BlockSpec((groups, 1, SUB, N), lambda i, s: (0, part * steps + i, 0, 0)),
                pl.BlockSpec((1,) + section.shape[1:], lambda i, s: (s[0], 0, 0)),
                pl.BlockSpec((1,) + last.shape[1:], lambda i, s: (s[0], 0, 0, 0)),
                pl.BlockSpec((lanes, lanes), lambda i, s: (0, 0)),
            ],
            out_specs=pl.BlockSpec((fields, 1, ROWS, lanes), lambda i, s: (0, i, 0, 0)),
            scratch_shapes=[
                pltpu.VMEM((A, A, lanes), BF),
                pltpu.VMEM((A, A, lanes), BF),
                pltpu.VMEM((2 * fields, 2 * A, lanes), BF),
            ],
        ),
        out_shape=jax.ShapeDtypeStruct((fields, steps, ROWS, lanes), BF),
        compiler_params=pltpu.CompilerParams(vmem_limit_bytes=VMEM),
        cost_estimate=SMALL,
        name="forward_x",
    )(sel, pot.reshape(groups, HIGH, SUB, N), section, last, line_order(lanes))


def first_section_y(lines, section, gathered, held):
    groups, steps = lines.shape[:2]
    span = LANES * FEW // SUB
    zeros = jnp.zeros((LANES - PART, LANES), F32)
    for g in range(groups):
        for h in range(steps):
            block = lines[g, h].astype(F32)
            both = jnp.concatenate([block[:PART], zeros, block[PART:], zeros], axis=0)
            turned = both.astype(BF).T
            columns = slice(2 * h * LANES, 2 * (h + 1) * LANES)
            for a in range(SUB // FEW):
                gathered[a, g * span : (g + 1) * span, columns] = turned[a * span : (a + 1) * span]
    half = A * FEW
    for a in range(SUB // FEW):
        both = dot(section[...], gathered[a])
        for h in range(steps):
            re = slice(2 * h * LANES, (2 * h + 1) * LANES)
            im = slice((2 * h + 1) * LANES, (2 * h + 2) * LANES)
            real = both[:half, re] - both[half:, im]
            imag = both[:half, im] + both[half:, re]
            for b in range(FEW):
                n2 = h * SUB + a * FEW + b
                rows = slice(b * A, (b + 1) * A)
                held[pl.ds(n2, A, stride=PITCH_Y), :] = real[rows]
                held[pl.ds(A * PITCH_Y + n2, A, stride=PITCH_Y), :] = imag[rows]


def first_section_scratch(lines):
    return [
        pltpu.VMEM((SUB // FEW, A * FEW, 2 * lines.shape[1] * LANES), BF),
        pltpu.VMEM(((2 * A + 1) * PITCH_Y, LANES), F32),
    ]


def forward_y_first_kernel(lines, section, twisted, gathered, held):
    first_section_y(lines, section, gathered, held)

    def digit(k, carry):
        for part in range(2):
            start = (part * A + k) * PITCH_Y
            twisted[k, part] = held[pl.ds(start, A // PARTS), :].astype(BF)
        return carry

    lax.fori_loop(0, A, digit, 0, unroll=8)


def forward_y_first(lines, section):
    return pl.pallas_call(
        forward_y_first_kernel,
        grid=(1,),
        in_specs=[
            pl.BlockSpec(lines.shape, lambda i: (0, 0, 0, 0)),
            pl.BlockSpec(section.shape, lambda i: (0, 0)),
        ],
        out_specs=pl.BlockSpec((A, 2, A // PARTS, LANES), lambda i: (0, 0, 0, 0)),
        out_shape=jax.ShapeDtypeStruct((A, 2, A // PARTS, LANES), BF),
        scratch_shapes=first_section_scratch(lines),
        compiler_params=pltpu.CompilerParams(vmem_limit_bytes=VMEM),
        cost_estimate=SMALL,
        name="forward_y_first",
    )(lines, section)


def forward_y_kernel(lines, section, earlier, last, *rest):
    out, gathered, held = rest[-3:]
    step = pl.program_id(0)

    @pl.when(step == 0)
    def _():
        first_section_y(lines, section, gathered, held)

    @pl.when(step > 0)
    def _():
        count = out.shape[0]
        base = (step - 1) * count
        for q in range(count):
            rows = []
            for e in range(2):
                for part in range(2):
                    k = 2 * (base + q) + e
                    rows.append(earlier[k, part])
                    start = (part * A + k) * PITCH_Y
                    rows.append(held[pl.ds(start, A // PARTS), :].astype(BF))
            out[q] = dot(last[q], jnp.concatenate(rows, axis=0)).astype(BF)


def forward_y(lines, section, earlier, last, after):
    steps = 2
    count = PAIRS // steps

    def late(i):
        return (jnp.maximum(i - 1, 0), 0, 0)

    return pl.pallas_call(
        forward_y_kernel,
        grid=(1 + steps,),
        in_specs=[
            pl.BlockSpec(lines.shape, lambda i: (0, 0, 0, 0)),
            pl.BlockSpec(section.shape, lambda i: (0, 0)),
            pl.BlockSpec(earlier.shape, lambda i: (0, 0, 0, 0)),
            pl.BlockSpec((count, ROWS, 4 * A), late),
        ]
        + [pl.BlockSpec(memory_space=pl.ANY)] * len(after),
        out_specs=pl.BlockSpec((count, ROWS, LANES), late),
        out_shape=jax.ShapeDtypeStruct((PAIRS, ROWS, LANES), BF),
        scratch_shapes=first_section_scratch(lines),
        compiler_params=pltpu.CompilerParams(vmem_limit_bytes=VMEM),
        cost_estimate=SMALL,
        name="forward_y",
    )(lines, section, earlier, last, *after)


def order_kernel(value, *rest):
    pass


def order(value, after):
    return pl.pallas_call(
        order_kernel,
        in_specs=[pl.BlockSpec(memory_space=pl.ANY)] * (1 + len(after)),
        out_specs=pl.BlockSpec(memory_space=pl.ANY),
        out_shape=jax.ShapeDtypeStruct(value.shape, value.dtype),
        input_output_aliases={0: 0},
        name="order",
    )(value, *after)


def inverse_kernel(steps, which, near, sel, *refs):
    specs = refs[:near]
    freq_y, square_x, table_y = refs[near : near + 3]
    tables_x = refs[near + 3 : 2 * near + 3]
    out, mid = refs[-2:]
    step = pl.program_id(0)
    count = PAIRS // steps
    each = HALF // steps
    limit = F32(LIMIT * LIMIT)
    whole = 2 * A * PITCH

    @pl.when(step < steps)
    def _():
        def pair(q, carry):
            pair_id = step * count + q
            offset = (2 * pair_id + sel[3 * which + 2]).astype(F32)
            row_freq = freq_y[...] + offset
            row_square = row_freq * row_freq
            values = []
            for x in range(near):
                inside = row_square + square_x[x] <= limit
                values.append(jnp.where(inside, specs[x][q].astype(F32), 0.0))
            for e in range(2):
                half = [v[e * PART : (e + 1) * PART].astype(BF) for v in values]
                half = half[0] if near == 1 else jnp.concatenate(half, axis=1)
                mixed = dot(table_y[q, e], half)
                for x in range(near):
                    for part in range(2):
                        spot = x * whole + part * A * PITCH + 2 * pair_id + e
                        mid[pl.ds(spot, A, stride=PITCH), :] = mixed[
                            part * A : (part + 1) * A, x * LANES : (x + 1) * LANES
                        ]
            return carry

        lax.fori_loop(0, count, pair, 0, unroll=16)

    @pl.when(step >= steps)
    def _():
        def line(i, carry):
            by = (step - steps) * each + i
            for x in range(near):
                rows = []
                for b in range(2):
                    start = x * whole + (by + b * HALF) * PITCH
                    real = mid[pl.ds(start, A), :].astype(BF)
                    imag = mid[pl.ds(start + A * PITCH, A), :].astype(BF)
                    rows.append(jnp.concatenate([real, imag], axis=1))
                product = dot(jnp.concatenate(rows, axis=0), tables_x[x][0, 0]).astype(BF)
                for b in range(2):
                    for part in range(2):
                        low_row = 2 * A * x + A * part
                        out[i, low_row : low_row + A, b * LANES : (b + 1) * LANES] = product[
                            b * A : (b + 1) * A, part * LANES : (part + 1) * LANES
                        ]
            return carry

        lax.fori_loop(0, each, line, 0, unroll=16)


def inverse(which, sel, specs, freq_y, square_x, table_y, table_x, after):
    near = len(specs)
    steps = 2
    count = PAIRS // steps
    each = HALF // steps

    def early(i, s):
        return jnp.minimum(i, steps - 1)

    def table_spec(x):
        return pl.BlockSpec(
            (1, 1) + table_x.shape[2:],
            lambda i, s: (s[3 * (which + x)], s[3 * (which + x) + 1], 0, 0),
        )

    return pl.pallas_call(
        functools.partial(inverse_kernel, steps, which, near),
        grid_spec=pltpu.PrefetchScalarGridSpec(
            num_scalar_prefetch=1,
            grid=(2 * steps,),
            in_specs=[pl.BlockSpec((count, ROWS, LANES), lambda i, s: (early(i, s), 0, 0))] * near
            + [
                pl.BlockSpec((ROWS, LANES), lambda i, s: (0, 0)),
                pl.BlockSpec((near, 1, LANES), lambda i, s: (0, 0, 0)),
                pl.BlockSpec((count, 2, 2 * A, PART), lambda i, s: (early(i, s), 0, 0, 0)),
            ]
            + [table_spec(x) for x in range(near)]
            + [pl.BlockSpec(memory_space=pl.ANY)] * len(after),
            out_specs=pl.BlockSpec(
                (each, 2 * A * near, 2 * LANES), lambda i, s: (jnp.maximum(i - steps, 0), 0, 0)
            ),
            scratch_shapes=[pltpu.VMEM(((near * 2 * A + 1) * PITCH, LANES), F32)],
        ),
        out_shape=jax.ShapeDtypeStruct((HALF, 2 * A * near, 2 * LANES), BF),
        compiler_params=pltpu.CompilerParams(vmem_limit_bytes=VMEM),
        cost_estimate=SMALL,
        name="inverse",
    )(sel, *specs, freq_y, square_x, table_y, *[table_x] * near, *after)


def collect_kernel(count, k1_pairs, *refs):
    sheets, places = refs[:count], refs[count]
    outs = refs[-2 - PARTS : -2]
    weights, held = refs[-2:]
    devices, _, slots, lines, _ = outs[0].shape
    each = sheets[0].shape[0]
    steps = lines // each
    step = pl.program_id(0) % steps
    part_id = pl.program_id(0) // steps
    tiles = devices * slots
    pitch = lines + 1
    lane = lax.broadcasted_iota(jnp.int32, (tiles, LANES), 1)
    lower = lane < A

    @pl.when(step == 0)
    def _():
        quarter = A // 4
        base = places[0, 0, 0] * (lane % A) + quarter * (lane // A)
        for x in range(weights.shape[1] // LANES):
            for ks in range(2):
                winding = base + places[0, 0, 1] * (k1_pairs[x] + ks)
                for part in range(2):
                    angle = ((winding - quarter * part) & (A - 1)) - A // 2
                    angle = angle.astype(F32) * F32(2.0 * math.pi / A)
                    rows = slice((2 * part + ks) * tiles, (2 * part + ks + 1) * tiles)
                    weights[rows, x * LANES : (x + 1) * LANES] = (-cosine(angle * angle)).astype(BF)

    def line(i, carry):
        stacked = sheets[0][i]
        if len(sheets) > 1:
            stacked = jnp.concatenate([sheet[i] for sheet in sheets], axis=0)
        sums = dot(weights[...], stacked)
        for part in range(2):
            even = sums[2 * part * tiles : (2 * part + 1) * tiles]
            odd = sums[(2 * part + 1) * tiles : (2 * part + 2) * tiles]
            keep = jnp.where(lower, even[:, :LANES], odd[:, LANES:])
            move = jnp.where(lower, even[:, LANES:], odd[:, :LANES])
            total = keep + pltpu.roll(move, A, 1)
            spot = part * tiles * pitch + step * each + i
            held[pl.ds(spot, tiles, stride=pitch), :] = total
        return carry

    lax.fori_loop(0, each, line, 0, unroll=8)

    for p, out in enumerate(outs):

        def device(d, carry, out=out):
            for part in range(2):
                for slot in range(slots):
                    start = (part * tiles + d * slots + slot) * pitch
                    out[d, part, slot] = held[pl.ds(start, lines), :].astype(BF)
            return carry

        @pl.when((step == steps - 1) & (part_id == p))
        def _(device=device):
            lax.fori_loop(0, devices, device, 0, unroll=4)


def collect(sheets, k1_pairs, places, devices, which, after):
    tiles = places.shape[3]
    lines = HALF // PARTS
    steps = 2
    shape = (devices, 2, tiles // devices, lines, LANES)
    depth = sum(sheet.shape[1] for sheet in sheets)
    sheet_specs = [
        pl.BlockSpec((lines // steps,) + sheet.shape[1:], lambda i, s: (i, 0, 0))
        for sheet in sheets
    ]
    block = pl.BlockSpec(shape, lambda i, s: (0, 0, 0, 0, 0))
    return pl.pallas_call(
        functools.partial(collect_kernel, len(sheets)),
        grid_spec=pltpu.PrefetchScalarGridSpec(
            num_scalar_prefetch=1,
            grid=(PARTS * steps,),
            in_specs=sheet_specs
            + [
                pl.BlockSpec(
                    (1, 1) + places.shape[2:], lambda i, s: (which, i // steps, 0, 0, 0)
                )
            ]
            + [pl.BlockSpec(memory_space=pl.ANY)] * len(after),
            out_specs=[block] * PARTS,
            scratch_shapes=[
                pltpu.VMEM((4 * tiles, depth), BF),
                pltpu.VMEM(((2 * tiles + 1) * (lines + 1), LANES), F32),
            ],
        ),
        out_shape=[jax.ShapeDtypeStruct(shape, BF)] * PARTS,
        compiler_params=pltpu.CompilerParams(vmem_limit_bytes=VMEM),
        cost_estimate=SMALL,
        name="collect",
    )(k1_pairs, *sheets, places, *after)


def crop_kernel(rows, cols, odd, mine, pot, after, out, held, sems):
    slots = out.shape[0]

    def copy(i):
        return pltpu.make_async_copy(
            pot.at[
                pl.ds(pl.multiple_of(rows[i] * A, A), A),
                pl.ds(pl.multiple_of(cols[i] * LANES, LANES), LANES),
            ],
            held.at[i],
            sems.at[i],
        )

    def begin(i, carry):
        copy(i).start()
        return carry

    def finish(i, carry):
        copy(i).wait()
        block = held[i].astype(F32)
        block = jnp.where(odd[i] == 1, pltpu.roll(block, A, 1), block)
        lane = lax.broadcasted_iota(jnp.int32, (HALF, LANES), 1)
        packed = jnp.where(lane < A, block[:HALF], pltpu.roll(block[HALF:], A, 1))
        out[i] = jnp.where(mine[i] == 1, packed, 0.0).astype(BF)
        return carry

    lax.fori_loop(0, slots, begin, 0)
    lax.fori_loop(0, slots, finish, 0)


def crop(rows, cols, odd, mine, pot, after):
    slots = rows.shape[0]
    return pl.pallas_call(
        crop_kernel,
        in_specs=[pl.BlockSpec(memory_space=pltpu.SMEM)] * 4
        + [pl.BlockSpec(memory_space=pl.ANY)] * 2,
        out_specs=pl.BlockSpec(memory_space=pltpu.VMEM),
        out_shape=jax.ShapeDtypeStruct((slots, HALF, LANES), BF),
        scratch_shapes=[pltpu.VMEM((slots, A, LANES), BF), pltpu.SemaphoreType.DMA((slots,))],
        compiler_params=pltpu.CompilerParams(vmem_limit_bytes=VMEM),
        cost_estimate=SMALL,
        name="crop",
    )(rows, cols, odd, mine, pot, after)


def detect_kernel(parts, alpha, counts, *refs):
    fields = refs[:parts]
    pot, plane, across, down, bins, out, lines, held = refs[parts:]
    beams, _, slots = fields[0].shape[:3]
    for s in range(slots):
        waves = []
        for j in range(beams):
            re, im = (
                jnp.concatenate([half[j, part, s] for half in fields], axis=0).astype(F32)
                for part in range(2)
            )
            cos, sin = plane[j, 0], plane[j, 1]
            waves.append((re * cos - im * sin, re * sin + im * cos))
        turned, level = sine_cosine(pot[s].astype(F32))
        for g in range(G):
            real = jnp.zeros((HALF, LANES), F32)
            imag = jnp.zeros((HALF, LANES), F32)
            for j in range(beams):
                cos, sin = alpha[0, j, s * G + g], alpha[1, j, s * G + g]
                re, im = waves[j]
                real = real + cos * re - sin * im
                imag = imag + cos * im + sin * re
            lines[2 * (s * G + g)] = (real * level - imag * turned).astype(BF)
            lines[2 * (s * G + g) + 1] = (real * turned + imag * level).astype(BF)
    total = slots * G
    first = dot(lines[...].reshape(2 * total * HALF, LANES), across[...])
    first = first.reshape(total, 2, HALF, 2 * LANES)
    real = (first[:, 0, :, :LANES] + first[:, 1, :, LANES:]).astype(BF)
    imag = (first[:, 1, :, :LANES] - first[:, 0, :, LANES:]).astype(BF)
    lane = lax.broadcasted_iota(jnp.int32, (A, LANES), 1)
    for i in range(total):
        both = jnp.concatenate([real[i], imag[i]], axis=1)
        mixed = dot(down[...], both)
        even, odd = mixed[: 2 * A], mixed[2 * A :]
        re_cos = even[:A, :LANES] + pltpu.roll(odd[:A, :LANES], A, 1)
        re_sin = even[A:, :LANES] + pltpu.roll(odd[A:, :LANES], A, 1)
        im_cos = even[:A, LANES:] + pltpu.roll(odd[:A, LANES:], A, 1)
        im_sin = even[A:, LANES:] + pltpu.roll(odd[A:, LANES:], A, 1)
        re = re_cos + im_sin
        im = im_cos - re_sin
        power = jnp.where(lane < A, re * re + im * im, 0.0)
        sums = jnp.sum(power[None] * bins[...], axis=1)
        block, slot = divmod(i // G, slots // counts.shape[0])
        active = slot < counts[block]
        held[i * NDET : (i + 1) * NDET, :] = jnp.where(active, sums, 0.0)
    sums = jnp.sum(held[...].T, axis=0, keepdims=True)
    each = slots // counts.shape[0]
    for i in range(total):
        block, slot = divmod(i // G, each)
        out[block, slot, i % G : i % G + 1, :] = sums[:, i * NDET : (i + 1) * NDET]


def detect(alpha, counts, fields, pot, plane, across, down, bins):
    slots = fields[0].shape[2]
    rows = -(-slots * G * NDET // LANES) * LANES
    blocks = counts.shape[0]
    smem = pl.BlockSpec(memory_space=pltpu.SMEM)
    vmem = pl.BlockSpec(memory_space=pltpu.VMEM)
    return pl.pallas_call(
        functools.partial(detect_kernel, len(fields)),
        in_specs=[smem, smem] + [vmem] * (5 + len(fields)),
        out_specs=vmem,
        out_shape=jax.ShapeDtypeStruct((blocks, slots // blocks, G, NDET), F32),
        scratch_shapes=[
            pltpu.VMEM((2 * slots * G, HALF, LANES), BF),
            pltpu.VMEM((rows, LANES), F32),
        ],
        compiler_params=pltpu.CompilerParams(vmem_limit_bytes=VMEM),
        name="detect",
    )(alpha, counts, *fields, pot, plane, across, down, bins)


def detect_tables(beam_total):
    n = np.arange(A)
    table = turn(n[:, None] * n[None, :], A) / A
    cos, sin = table.real, table.imag
    zero = np.zeros((A, A))
    across = np.block([[cos, zero, sin, zero], [zero, cos, zero, sin]])
    rows = np.concatenate([cos, sin], axis=0)
    down = np.concatenate([rows[:, :HALF], rows[:, HALF:]], axis=0)
    signed = np.where(n < A // 2, n, n - A)
    radius = signed[:, None] ** 2 + signed[None, :] ** 2
    width = A // (2 * NDET)
    bins = np.zeros((NDET, A, LANES))
    for d in range(NDET):
        member = (radius >= (width * d) ** 2) & (radius < (width * (d + 1)) ** 2)
        bins[d, :, :A] = member * (A * A / (beam_total * member.sum()))
    return low(across), low(down), bins.astype(np.float32)


def coefficients(tile_ids, beam_rows, shifts):
    across = N // A
    offsets = jnp.arange(G, dtype=jnp.int32)
    spot_y = (tile_ids // across)[:, None] * A + A // 2 + offsets[None, :]
    spot_x = (tile_ids % across)[:, None] * A + A // 2 + 2 * offsets[None, :]
    wave_y = jnp.remainder(F * beam_rows[:, 0], N)[:, None, None]
    wave_x = jnp.remainder(F * beam_rows[:, 1], N)[:, None, None]
    windings = (wave_y * spot_y[None] % N + wave_x * spot_x[None] % N) % N
    phases = shifts[:, None, None] + 2.0 * math.pi / N * windings.astype(F32)
    return jnp.stack([jnp.cos(phases), -jnp.sin(phases)])


def plane_waves(beam_index):
    by = jnp.arange(HALF, dtype=jnp.int32)[:, None] + HALF * (jnp.arange(LANES) // A)[None, :]
    bx = jnp.broadcast_to((jnp.arange(LANES, dtype=jnp.int32) % A)[None, :], by.shape)
    row_y = beam_index[:, 0][:, None, None]
    row_x = beam_index[:, 1][:, None, None]
    winding = (row_y * by[None] + row_x * bx[None] + HALF * (row_y + row_x)) % A
    angle = 2.0 * math.pi / A * winding.astype(F32)
    return jnp.stack([jnp.cos(angle), jnp.sin(angle)], axis=1)


def shards(pot_first, pot_second, beam_index, aberration, tile_table, tile_count):
    field_count = lax.axis_size("beam")
    hold_count = lax.axis_size("slab")
    field_pos = lax.axis_index("beam")
    hold_pos = lax.axis_index("slab")
    band_rows = pot_first.shape[0]
    band_tiles = band_rows // A
    width_k = A // field_count
    sheets = width_k // 2
    across = N // A
    beam_total = beam_index.shape[0]
    share = hold_pos % sheets

    section_x = np.stack(
        [
            first_forward_x(
                np.array(
                    [width_k * p + 2 * t + ks for p in range(field_count) for ks in range(2)]
                )
            )
            for t in range(sheets)
        ]
    )
    last_x = np.stack(
        [
            np.stack(
                [
                    last_forward_x([width_k * p + 2 * t, width_k * p + 2 * t + 1])
                    for p in range(field_count)
                ]
            )
            for t in range(sheets)
        ]
    )
    section_y = first_forward_y()
    last_y = np.stack([last_forward_y([2 * q, 2 * q + 1]) for q in range(PAIRS)])
    inverse_y = np.stack([first_inverse_y([2 * q, 2 * q + 1]) for q in range(PAIRS)])
    inverse_x = np.stack(
        [
            np.stack(
                [
                    first_inverse_x([width_k * p + 2 * t, width_k * p + 2 * t + 1])
                    for t in range(sheets)
                ]
            )
            for p in range(field_count)
        ]
    )

    blocks_dev = tile_table.shape[0] // (field_count * hold_count)
    slot_count = tile_table.shape[1]
    own_slots = blocks_dev * slot_count
    table = tile_table.reshape(field_count, hold_count, own_slots)

    def trade(value, axis):
        return lax.all_to_all(value, axis, split_axis=0, concat_axis=0, tiled=True)

    near = min(sheets, 2)
    far = sheets // near

    def swap(value, x):
        return lax.ppermute(value, "slab", [(i, i ^ x) for i in range(hold_count)])

    ids = lax.dynamic_index_in_dim(table, hold_pos, 1, keepdims=False).reshape(-1)
    tile_y, tile_x = ids // across, ids % across
    mine = (tile_y // band_tiles == field_pos).astype(jnp.int32)
    rows = jnp.clip(tile_y - field_pos * band_tiles, 0, band_tiles - 1)
    columns, odd = tile_x // 2, tile_x % 2

    beam_row = lax.dynamic_index_in_dim(beam_index, hold_pos, 0, keepdims=False)
    pair_ids = share ^ jnp.arange(sheets, dtype=jnp.int32)
    k1_pairs = field_pos * width_k + 2 * pair_ids
    near_bit, far_bit = (jnp.stack([1 - v, v]) for v in (field_pos % 2, field_pos // 2 % 2))
    corners = table.reshape(field_count // 4, 2, 2, hold_count, own_slots)
    corners = corners.transpose(2, 1, 0, 3, 4)[near_bit][:, far_bit]
    sets = jnp.stack([corners, corners.transpose(1, 0, 2, 3, 4)], axis=1)
    sets = sets.reshape(2, PARTS, -1)
    places = jnp.stack([sets // across - beam_row[0], sets % across - beam_row[1]], axis=2)
    places = jnp.broadcast_to(places[..., None], places.shape + (LANES,))
    row = np.arange(ROWS)
    base = row // PART + A * (K2_LOW + row % PART % K2_COUNT)
    freq_y = np.broadcast_to(base[:, None], (ROWS, LANES)).astype(np.float32)
    lane = np.arange(LANES)
    base = np.where(lane < 2 * K2_COUNT, lane // K2_COUNT + A * (K2_LOW + lane % K2_COUNT), N)
    freq_x = (k1_pairs + F * beam_row[1])[:, None, None] + base.astype(np.int32)
    square_x = (freq_x * freq_x).astype(F32)
    scalars = jnp.stack(
        jnp.broadcast_arrays(field_pos, pair_ids, F * beam_row[0]), axis=-1
    )
    scalars = scalars.astype(jnp.int32).reshape(-1)

    sel = share.reshape(1).astype(jnp.int32)
    received = [[] for _ in range(far)]
    earlier = []
    for part in range(PARTS):
        lines = forward_x(sel, pot_first, section_x, last_x, field_count, part)
        if part:
            lines = order(lines, [places, scalars, square_x, rows, columns, odd, mine])
        lines = trade(lines, "beam")
        if lines.shape[3] != LANES:
            ratio = LANES // lines.shape[3]
            lines = lines.reshape(
                field_count // ratio, ratio, HIGH // PARTS, ROWS, SUB // FEW, -1
            )
            lines = lines.transpose(0, 2, 3, 4, 1, 5).reshape(-1, HIGH // PARTS, ROWS, LANES)
        if part:
            crops = crop(rows, columns, odd, mine, pot_second, earlier[0])
            lines = order(lines, [crops] + [r[0] for r in received[1:]])
        for f in range(far):
            received[f].append(swap(lines, f * near) if f else lines)
        if part == 0:
            earlier = [forward_y_first(received[f][0], section_y) for f in range(far)]
    crops = order(crops.reshape(field_count, own_slots, HALF, LANES), received[0][1:])
    crops = trade(crops, "beam")
    waves = []
    ready = []

    def invert(stop, after):
        start = stop - len(ready)
        limits = square_x[start:stop]
        waves.append(
            inverse(start, scalars, ready[:], freq_y, limits, inverse_y, inverse_x, after)
        )
        ready.clear()

    for f in range(far):
        spec = forward_y(received[f][1], section_y, earlier[f], last_y, [crops] + waves if f else [])
        for x in range(near):
            ready.append(swap(spec, x) if x else spec)
            if x == 0:
                invert(f * near + 1, waves[1:])
    if ready:
        invert(sheets, waves[-1:])
    owners = field_count // 2 * hold_count
    other = collect(waves, k1_pairs, places, owners, 0, [crops])
    partial = other + collect(waves, k1_pairs, places, owners, 1, other[:1])

    def hop(value, bit):
        return lax.ppermute(value, "beam", [(i, i ^ (1 << bit)) for i in range(field_count)])

    def total(arrays, span):
        return functools.reduce(jnp.add, [array[span].astype(F32) for array in arrays])

    moving, staying = slice(0, owners // 2), slice(owners // 2, owners)
    arrived = [hop(partial[part], part) for part in range(PARTS)]
    halves = [[partial[PARTS + part], arrived[part]] for part in range(PARTS)]
    passed = [hop(total(halves[part], moving).astype(BF), 1 - part) for part in range(PARTS)]
    tiles = jnp.concatenate(
        [total(halves[part], staying) + passed[part].astype(F32) for part in range(PARTS)], axis=3
    ).astype(BF)
    groups = [
        [b * hold_count + h for b in range(g, field_count, 4) for h in range(hold_count)]
        for g in range(4)
    ]
    tiles = lax.all_to_all(
        tiles,
        ("beam", "slab"),
        split_axis=0,
        concat_axis=0,
        axis_index_groups=groups,
        tiled=True,
    )
    tiles = tiles.reshape((field_count // 4, hold_count) + tiles.shape[1:]).astype(F32)
    fields = [jnp.sum(tiles, axis=0).astype(BF)]
    crops = jnp.sum(crops.astype(F32), axis=0).astype(BF)

    own = lax.dynamic_index_in_dim(
        lax.dynamic_index_in_dim(table, field_pos, 0, keepdims=False), hold_pos, 0, keepdims=False
    )
    alpha = coefficients(own, beam_index, aberration).reshape(2, beam_total, own_slots * G)
    first_block = (field_pos * hold_count + hold_pos) * blocks_dev
    counts = lax.dynamic_slice_in_dim(tile_count, first_block, blocks_dev, 0)
    bins = detect_tables(beam_total)
    return detect(alpha, counts, fields, crops, plane_waves(beam_index), *bins)


def solution(mesh):
    return jax.shard_map(
        shards,
        mesh=mesh,
        in_specs=(P("beam", None), P("beam", None), P(), P(), P(), P()),
        out_specs=P(("beam", "slab"), None, None, None),
        check_vma=False,
    )
```

```python
import functools
import math

import jax
import jax.numpy as jnp
import ml_dtypes
import numpy as np
from jax import lax
from jax.experimental import pallas as pl
from jax.experimental.pallas import tpu as pltpu
from jax.sharding import PartitionSpec as P

A = 64
N = 4096
F = 64
G = 3
NDET = 16
QMAX = 3
LIMIT = N // 3
K2_LOW = -(LIMIT // A + 1 + QMAX)
K2_COUNT = 2 * (LIMIT // A + 1 + QMAX)
PART = 104
ROWS = 2 * PART
LANES = 128
SUB = 16
FEW = 4
HIGH = A // SUB
HALF = A // 2
PAIRS = A // 2
PARTS = 2
VMEM = 60 * 1024 * 1024
PITCH = A + 1
PITCH_Y = A // PARTS + 1
SMALL = pl.CostEstimate(flops=1 << 20, bytes_accessed=0, transcendentals=0)
BF = jnp.bfloat16
F32 = jnp.float32


def low(values):
    return np.asarray(values, dtype=np.float32).astype(ml_dtypes.bfloat16)


def turn(numerator, period):
    return np.exp(2j * np.pi * (numerator % period) / period)


def digits_k2():
    return K2_LOW + np.arange(K2_COUNT)


def spread(table, sub):
    both = np.stack([table.real, table.imag])
    return both[:, :, None, :, None] * np.eye(sub)[None, None, :, None, :]


def real_rows(table):
    return np.block([[table.real, -table.imag], [table.imag, table.real]])


def section_forward(k1):
    n1 = np.arange(A)
    return np.conj(turn(k1[:, None] * n1[None, :], A)) / A


def first_forward_x(k1):
    return low(spread(section_forward(k1), SUB).reshape(2 * len(k1) * SUB, A * SUB))


def first_forward_y():
    table = spread(section_forward(np.arange(A)), FEW).transpose(0, 2, 1, 3, 4)
    return low(table.reshape(2 * A * FEW, A * FEW))


def line_order(lanes):
    order = np.arange(lanes).reshape(-1, SUB // FEW, FEW).transpose(1, 0, 2).reshape(-1)
    out = np.zeros((lanes, lanes))
    out[order, np.arange(lanes)] = 1
    return low(out)


def last_forward_x(k1_pair):
    n2 = np.arange(A)
    out = np.zeros((2, PART, 2, 2, A))
    for ks, k1 in enumerate(k1_pair):
        freq = k1 + A * digits_k2()
        table = np.conj(turn(freq[:, None] * n2[None, :], N)) / A
        block = real_rows(table).reshape(2, K2_COUNT, 2, A)
        out[:, ks * K2_COUNT : (ks + 1) * K2_COUNT, ks] = block
    return low(out.reshape(ROWS, 4 * A))


def last_forward_y(k1_pair):
    n2 = np.arange(A)
    out = np.zeros((ROWS, 2, 2 * A))
    for e, k1 in enumerate(k1_pair):
        freq = k1 + A * digits_k2()
        table = np.conj(turn(freq[:, None] * n2[None, :], N)) / A
        out[e * PART : e * PART + 2 * K2_COUNT, e] = real_rows(table)
    return low(out.reshape(ROWS, 4 * A))


def first_inverse(k1):
    n2 = np.arange(A)
    freq = k1 + A * digits_k2()
    return turn(n2[:, None] * freq[None, :], N) * np.conj(turn(freq * freq, 2 * N))[None, :]


def first_inverse_y(k1_pair):
    out = np.zeros((2, 2 * A, PART))
    for e, k1 in enumerate(k1_pair):
        out[e, :, : 2 * K2_COUNT] = real_rows(first_inverse(k1))
    return low(out)


def first_inverse_x(k1_pair):
    out = np.zeros((2, LANES, 2, 2, A))
    for ks, k1 in enumerate(k1_pair):
        table = first_inverse(k1).T
        rows = slice(ks * K2_COUNT, (ks + 1) * K2_COUNT)
        out[0, rows, 0, ks] = table.real
        out[0, rows, 1, ks] = table.imag
        out[1, rows, 0, ks] = -table.imag
        out[1, rows, 1, ks] = table.real
    return low(out.reshape(2 * LANES, 4 * A))


def cosine(u):
    q = F32(COS_FIT[-1])
    for c in COS_FIT[-2::-1]:
        q = q * u + F32(c)
    return q


def sine_cosine(x):
    u = x * x
    s = F32(SIN_FIT[-1])
    for c in SIN_FIT[-2::-1]:
        s = s * u + F32(c)
    return s * x, cosine(u)


def fit(function, degree):
    top = 3.1421**2
    nodes = 0.5 * top * (1 - np.cos(np.pi * (np.arange(64) + 0.5) / 64))
    cheb = np.polynomial.chebyshev.Chebyshev.fit(
        nodes, function(np.sqrt(nodes)), degree, domain=[0, top]
    )
    return [float(c) for c in cheb.convert(kind=np.polynomial.Polynomial).coef]


SIN_FIT = fit(lambda x: np.sinc(x / np.pi), 5)
COS_FIT = fit(np.cos, 5)


def dot(a, b):
    return jnp.dot(a, b, preferred_element_type=F32)


def forward_x_kernel(sel, pot, section, last, perm, out, cos_ref, sin_ref, twisted):
    fields = out.shape[0]
    lanes = out.shape[3]
    half = section.shape[1] // 2

    def chunk(t, carry):
        block = pot[:, 0, :, pl.ds(pl.multiple_of(t * LANES, LANES), LANES)]
        values = block.reshape(lanes, LANES).T.astype(F32)
        sine, cosine = sine_cosine(values)
        cos_ref[pl.ds(2 * t, 2)] = cosine.astype(BF).reshape(2, A, lanes)
        sin_ref[pl.ds(2 * t, 2)] = sine.astype(BF).reshape(2, A, lanes)
        return carry

    lax.fori_loop(0, N // LANES, chunk, 0, unroll=16)
    table = section[0]
    for m in range(HIGH):
        span = slice(m * SUB, (m + 1) * SUB)
        part_cos = cos_ref[:, span, :].reshape(A * SUB, lanes)
        part_sin = sin_ref[:, span, :].reshape(A * SUB, lanes)
        if lanes % LANES == 0:
            both = dot(table, jnp.concatenate([part_cos, part_sin], axis=1))
            of_cos, of_sin = both[:, :lanes], both[:, lanes:]
        else:
            of_cos, of_sin = dot(table, part_cos), dot(table, part_sin)
        real = of_cos[:half] - of_sin[half:]
        imag = of_cos[half:] + of_sin[:half]
        twisted[:, m * SUB : (m + 1) * SUB, :] = real.astype(BF).reshape(2 * fields, SUB, lanes)
        twisted[:, A + m * SUB : A + (m + 1) * SUB, :] = imag.astype(BF).reshape(
            2 * fields, SUB, lanes
        )
    for d in range(fields):
        lines = twisted[2 * d : 2 * d + 2].reshape(4 * A, lanes)
        out[d, 0] = dot(dot(last[0, d], lines).astype(BF), perm[...]).astype(BF)


def forward_x(sel, pot, section, last, fields, part):
    groups = pot.shape[0] // A
    lanes = groups * SUB
    steps = HIGH // PARTS
    return pl.pallas_call(
        forward_x_kernel,
        grid_spec=pltpu.PrefetchScalarGridSpec(
            num_scalar_prefetch=1,
            grid=(steps,),
            in_specs=[
                pl.BlockSpec((groups, 1, SUB, N), lambda i, s: (0, part * steps + i, 0, 0)),
                pl.BlockSpec((1,) + section.shape[1:], lambda i, s: (s[0], 0, 0)),
                pl.BlockSpec((1,) + last.shape[1:], lambda i, s: (s[0], 0, 0, 0)),
                pl.BlockSpec((lanes, lanes), lambda i, s: (0, 0)),
            ],
            out_specs=pl.BlockSpec((fields, 1, ROWS, lanes), lambda i, s: (0, i, 0, 0)),
            scratch_shapes=[
                pltpu.VMEM((A, A, lanes), BF),
                pltpu.VMEM((A, A, lanes), BF),
                pltpu.VMEM((2 * fields, 2 * A, lanes), BF),
            ],
        ),
        out_shape=jax.ShapeDtypeStruct((fields, steps, ROWS, lanes), BF),
        compiler_params=pltpu.CompilerParams(vmem_limit_bytes=VMEM),
        cost_estimate=SMALL,
        name="forward_x",
    )(sel, pot.reshape(groups, HIGH, SUB, N), section, last, line_order(lanes))


def first_section_y(lines, section, gathered, held):
    groups, steps = lines.shape[:2]
    span = LANES * FEW // SUB
    zeros = jnp.zeros((LANES - PART, LANES), F32)
    for g in range(groups):
        for h in range(steps):
            block = lines[g, h].astype(F32)
            both = jnp.concatenate([block[:PART], zeros, block[PART:], zeros], axis=0)
            turned = both.astype(BF).T
            columns = slice(2 * h * LANES, 2 * (h + 1) * LANES)
            for a in range(SUB // FEW):
                gathered[a, g * span : (g + 1) * span, columns] = turned[a * span : (a + 1) * span]
    half = A * FEW
    for a in range(SUB // FEW):
        both = dot(section[...], gathered[a])
        for h in range(steps):
            re = slice(2 * h * LANES, (2 * h + 1) * LANES)
            im = slice((2 * h + 1) * LANES, (2 * h + 2) * LANES)
            real = both[:half, re] - both[half:, im]
            imag = both[:half, im] + both[half:, re]
            for b in range(FEW):
                n2 = h * SUB + a * FEW + b
                rows = slice(b * A, (b + 1) * A)
                held[pl.ds(n2, A, stride=PITCH_Y), :] = real[rows]
                held[pl.ds(A * PITCH_Y + n2, A, stride=PITCH_Y), :] = imag[rows]


def first_section_scratch(lines):
    return [
        pltpu.VMEM((SUB // FEW, A * FEW, 2 * lines.shape[1] * LANES), BF),
        pltpu.VMEM(((2 * A + 1) * PITCH_Y, LANES), F32),
    ]


def forward_y_first_kernel(lines, section, twisted, gathered, held):
    first_section_y(lines, section, gathered, held)

    def digit(k, carry):
        for part in range(2):
            start = (part * A + k) * PITCH_Y
            twisted[k, part] = held[pl.ds(start, A // PARTS), :].astype(BF)
        return carry

    lax.fori_loop(0, A, digit, 0, unroll=8)


def forward_y_first(lines, section):
    return pl.pallas_call(
        forward_y_first_kernel,
        grid=(1,),
        in_specs=[
            pl.BlockSpec(lines.shape, lambda i: (0, 0, 0, 0)),
            pl.BlockSpec(section.shape, lambda i: (0, 0)),
        ],
        out_specs=pl.BlockSpec((A, 2, A // PARTS, LANES), lambda i: (0, 0, 0, 0)),
        out_shape=jax.ShapeDtypeStruct((A, 2, A // PARTS, LANES), BF),
        scratch_shapes=first_section_scratch(lines),
        compiler_params=pltpu.CompilerParams(vmem_limit_bytes=VMEM),
        cost_estimate=SMALL,
        name="forward_y_first",
    )(lines, section)


def forward_y_kernel(lines, section, earlier, last, *rest):
    out, gathered, held = rest[-3:]
    step = pl.program_id(0)

    @pl.when(step == 0)
    def _():
        first_section_y(lines, section, gathered, held)

    @pl.when(step > 0)
    def _():
        count = out.shape[0]
        base = (step - 1) * count
        for q in range(count):
            rows = []
            for e in range(2):
                for part in range(2):
                    k = 2 * (base + q) + e
                    rows.append(earlier[k, part])
                    start = (part * A + k) * PITCH_Y
                    rows.append(held[pl.ds(start, A // PARTS), :].astype(BF))
            out[q] = dot(last[q], jnp.concatenate(rows, axis=0)).astype(BF)


def forward_y(lines, section, earlier, last, after):
    steps = 2
    count = PAIRS // steps

    def late(i):
        return (jnp.maximum(i - 1, 0), 0, 0)

    return pl.pallas_call(
        forward_y_kernel,
        grid=(1 + steps,),
        in_specs=[
            pl.BlockSpec(lines.shape, lambda i: (0, 0, 0, 0)),
            pl.BlockSpec(section.shape, lambda i: (0, 0)),
            pl.BlockSpec(earlier.shape, lambda i: (0, 0, 0, 0)),
            pl.BlockSpec((count, ROWS, 4 * A), late),
        ]
        + [pl.BlockSpec(memory_space=pl.ANY)] * len(after),
        out_specs=pl.BlockSpec((count, ROWS, LANES), late),
        out_shape=jax.ShapeDtypeStruct((PAIRS, ROWS, LANES), BF),
        scratch_shapes=first_section_scratch(lines),
        compiler_params=pltpu.CompilerParams(vmem_limit_bytes=VMEM),
        cost_estimate=SMALL,
        name="forward_y",
    )(lines, section, earlier, last, *after)


def order_kernel(value, *rest):
    pass


def order(value, after):
    return pl.pallas_call(
        order_kernel,
        in_specs=[pl.BlockSpec(memory_space=pl.ANY)] * (1 + len(after)),
        out_specs=pl.BlockSpec(memory_space=pl.ANY),
        out_shape=jax.ShapeDtypeStruct(value.shape, value.dtype),
        input_output_aliases={0: 0},
        name="order",
    )(value, *after)


def inverse_kernel(steps, which, near, sel, *refs):
    specs = refs[:near]
    freq_y, square_x, table_y = refs[near : near + 3]
    tables_x = refs[near + 3 : 2 * near + 3]
    out, mid = refs[-2:]
    step = pl.program_id(0)
    count = PAIRS // steps
    each = HALF // steps
    limit = F32(LIMIT * LIMIT)
    whole = 2 * A * PITCH

    @pl.when(step < steps)
    def _():
        def pair(q, carry):
            pair_id = step * count + q
            offset = (2 * pair_id + sel[3 * which + 2]).astype(F32)
            row_freq = freq_y[...] + offset
            row_square = row_freq * row_freq
            values = []
            for x in range(near):
                inside = row_square + square_x[which + x] <= limit
                values.append(jnp.where(inside, specs[x][q].astype(F32), 0.0))
            for e in range(2):
                half = [v[e * PART : (e + 1) * PART].astype(BF) for v in values]
                half = half[0] if near == 1 else jnp.concatenate(half, axis=1)
                mixed = dot(table_y[q, e], half)
                for x in range(near):
                    for part in range(2):
                        spot = x * whole + part * A * PITCH + 2 * pair_id + e
                        mid[pl.ds(spot, A, stride=PITCH), :] = mixed[
                            part * A : (part + 1) * A, x * LANES : (x + 1) * LANES
                        ]
            return carry

        lax.fori_loop(0, count, pair, 0, unroll=16)

    @pl.when(step >= steps)
    def _():
        def line(i, carry):
            by = (step - steps) * each + i
            for x in range(near):
                rows = []
                for b in range(2):
                    start = x * whole + (by + b * HALF) * PITCH
                    real = mid[pl.ds(start, A), :].astype(BF)
                    imag = mid[pl.ds(start + A * PITCH, A), :].astype(BF)
                    rows.append(jnp.concatenate([real, imag], axis=1))
                product = dot(jnp.concatenate(rows, axis=0), tables_x[x][0, 0]).astype(BF)
                for b in range(2):
                    for part in range(2):
                        low_row = 2 * A * x + A * part
                        out[i, low_row : low_row + A, b * LANES : (b + 1) * LANES] = product[
                            b * A : (b + 1) * A, part * LANES : (part + 1) * LANES
                        ]
            return carry

        lax.fori_loop(0, each, line, 0, unroll=16)


def inverse(which, sel, specs, freq_y, square_x, table_y, table_x, after):
    near = len(specs)
    steps = 2
    count = PAIRS // steps
    each = HALF // steps

    def early(i, s):
        return jnp.minimum(i, steps - 1)

    def table_spec(x):
        return pl.BlockSpec(
            (1, 1) + table_x.shape[2:],
            lambda i, s: (s[3 * (which + x)], s[3 * (which + x) + 1], 0, 0),
        )

    return pl.pallas_call(
        functools.partial(inverse_kernel, steps, which, near),
        grid_spec=pltpu.PrefetchScalarGridSpec(
            num_scalar_prefetch=1,
            grid=(2 * steps,),
            in_specs=[pl.BlockSpec((count, ROWS, LANES), lambda i, s: (early(i, s), 0, 0))] * near
            + [
                pl.BlockSpec((ROWS, LANES), lambda i, s: (0, 0)),
                pl.BlockSpec(square_x.shape, lambda i, s: (0, 0, 0)),
                pl.BlockSpec((count, 2, 2 * A, PART), lambda i, s: (early(i, s), 0, 0, 0)),
            ]
            + [table_spec(x) for x in range(near)]
            + [pl.BlockSpec(memory_space=pl.ANY)] * len(after),
            out_specs=pl.BlockSpec(
                (each, 2 * A * near, 2 * LANES), lambda i, s: (jnp.maximum(i - steps, 0), 0, 0)
            ),
            scratch_shapes=[pltpu.VMEM(((near * 2 * A + 1) * PITCH, LANES), F32)],
        ),
        out_shape=jax.ShapeDtypeStruct((HALF, 2 * A * near, 2 * LANES), BF),
        compiler_params=pltpu.CompilerParams(vmem_limit_bytes=VMEM),
        cost_estimate=SMALL,
        name="inverse",
    )(sel, *specs, freq_y, square_x, table_y, *[table_x] * near, *after)


def collect_kernel(count, k1_pairs, *refs):
    sheets, places = refs[:count], refs[count]
    outs = refs[-2 - PARTS : -2]
    weights, held = refs[-2:]
    devices, _, slots, lines, _ = outs[0].shape
    each = sheets[0].shape[0]
    steps = lines // each
    step = pl.program_id(0) % steps
    part_id = pl.program_id(0) // steps
    tiles = devices * slots
    pitch = lines + 1
    lane = lax.broadcasted_iota(jnp.int32, (tiles, LANES), 1)
    lower = lane < A

    @pl.when(step == 0)
    def _():
        quarter = A // 4
        base = places[0, 0, 0] * (lane % A) + quarter * (lane // A)
        for x in range(weights.shape[1] // LANES):
            for ks in range(2):
                winding = base + places[0, 0, 1] * (k1_pairs[x] + ks)
                for part in range(2):
                    angle = ((winding - quarter * part) & (A - 1)) - A // 2
                    angle = angle.astype(F32) * F32(2.0 * math.pi / A)
                    rows = slice((2 * part + ks) * tiles, (2 * part + ks + 1) * tiles)
                    weights[rows, x * LANES : (x + 1) * LANES] = (-cosine(angle * angle)).astype(BF)

    def line(i, carry):
        stacked = sheets[0][i]
        if len(sheets) > 1:
            stacked = jnp.concatenate([sheet[i] for sheet in sheets], axis=0)
        sums = dot(weights[...], stacked)
        for part in range(2):
            even = sums[2 * part * tiles : (2 * part + 1) * tiles]
            odd = sums[(2 * part + 1) * tiles : (2 * part + 2) * tiles]
            keep = jnp.where(lower, even[:, :LANES], odd[:, LANES:])
            move = jnp.where(lower, even[:, LANES:], odd[:, :LANES])
            total = keep + pltpu.roll(move, A, 1)
            spot = part * tiles * pitch + step * each + i
            held[pl.ds(spot, tiles, stride=pitch), :] = total
        return carry

    lax.fori_loop(0, each, line, 0, unroll=8)

    for p, out in enumerate(outs):

        def device(d, carry, out=out):
            for part in range(2):
                for slot in range(slots):
                    start = (part * tiles + d * slots + slot) * pitch
                    out[d, part, slot] = held[pl.ds(start, lines), :].astype(BF)
            return carry

        @pl.when((step == steps - 1) & (part_id == p))
        def _(device=device):
            lax.fori_loop(0, devices, device, 0, unroll=16)


def collect(sheets, k1_pairs, places, devices, which, after):
    tiles = places.shape[3]
    lines = HALF // PARTS
    steps = 2
    shape = (devices, 2, tiles // devices, lines, LANES)
    depth = sum(sheet.shape[1] for sheet in sheets)
    sheet_specs = [
        pl.BlockSpec((lines // steps,) + sheet.shape[1:], lambda i, s: (i, 0, 0))
        for sheet in sheets
    ]
    block = pl.BlockSpec(shape, lambda i, s: (0, 0, 0, 0, 0))
    return pl.pallas_call(
        functools.partial(collect_kernel, len(sheets)),
        grid_spec=pltpu.PrefetchScalarGridSpec(
            num_scalar_prefetch=1,
            grid=(PARTS * steps,),
            in_specs=sheet_specs
            + [
                pl.BlockSpec(
                    (1, 1) + places.shape[2:], lambda i, s: (which, i // steps, 0, 0, 0)
                )
            ]
            + [pl.BlockSpec(memory_space=pl.ANY)] * len(after),
            out_specs=[block] * PARTS,
            scratch_shapes=[
                pltpu.VMEM((4 * tiles, depth), BF),
                pltpu.VMEM(((2 * tiles + 1) * (lines + 1), LANES), F32),
            ],
        ),
        out_shape=[jax.ShapeDtypeStruct(shape, BF)] * PARTS,
        compiler_params=pltpu.CompilerParams(vmem_limit_bytes=VMEM),
        cost_estimate=SMALL,
        name="collect",
    )(k1_pairs, *sheets, places, *after)


def crop_kernel(rows, cols, odd, mine, pot, after, out, held, sems):
    slots = out.shape[0]

    def copy(i):
        return pltpu.make_async_copy(
            pot.at[
                pl.ds(pl.multiple_of(rows[i] * A, A), A),
                pl.ds(pl.multiple_of(cols[i] * LANES, LANES), LANES),
            ],
            held.at[i],
            sems.at[i],
        )

    def begin(i, carry):
        copy(i).start()
        return carry

    def finish(i, carry):
        copy(i).wait()
        block = held[i].astype(F32)
        block = jnp.where(odd[i] == 1, pltpu.roll(block, A, 1), block)
        lane = lax.broadcasted_iota(jnp.int32, (HALF, LANES), 1)
        packed = jnp.where(lane < A, block[:HALF], pltpu.roll(block[HALF:], A, 1))
        out[i] = jnp.where(mine[i] == 1, packed, 0.0).astype(BF)
        return carry

    lax.fori_loop(0, slots, begin, 0)
    lax.fori_loop(0, slots, finish, 0)


def crop(rows, cols, odd, mine, pot, after):
    slots = rows.shape[0]
    return pl.pallas_call(
        crop_kernel,
        in_specs=[pl.BlockSpec(memory_space=pltpu.SMEM)] * 4
        + [pl.BlockSpec(memory_space=pl.ANY)] * 2,
        out_specs=pl.BlockSpec(memory_space=pltpu.VMEM),
        out_shape=jax.ShapeDtypeStruct((slots, HALF, LANES), BF),
        scratch_shapes=[pltpu.VMEM((slots, A, LANES), BF), pltpu.SemaphoreType.DMA((slots,))],
        compiler_params=pltpu.CompilerParams(vmem_limit_bytes=VMEM),
        cost_estimate=SMALL,
        name="crop",
    )(rows, cols, odd, mine, pot, after)


def detect_kernel(parts, alpha, counts, *refs):
    fields = refs[:parts]
    pot, plane, across, down, bins, out, lines, held = refs[parts:]
    beams, _, slots = fields[0].shape[:3]
    for s in range(slots):
        waves = []
        for j in range(beams):
            re, im = (
                jnp.concatenate([half[j, part, s] for half in fields], axis=0).astype(F32)
                for part in range(2)
            )
            cos, sin = plane[j, 0], plane[j, 1]
            waves.append((re * cos - im * sin, re * sin + im * cos))
        turned, level = sine_cosine(pot[s].astype(F32))
        for g in range(G):
            real = jnp.zeros((HALF, LANES), F32)
            imag = jnp.zeros((HALF, LANES), F32)
            for j in range(beams):
                cos, sin = alpha[0, j, s * G + g], alpha[1, j, s * G + g]
                re, im = waves[j]
                real = real + cos * re - sin * im
                imag = imag + cos * im + sin * re
            lines[2 * (s * G + g)] = (real * level - imag * turned).astype(BF)
            lines[2 * (s * G + g) + 1] = (real * turned + imag * level).astype(BF)
    total = slots * G
    first = dot(lines[...].reshape(2 * total * HALF, LANES), across[...])
    first = first.reshape(total, 2, HALF, 2 * LANES)
    real = (first[:, 0, :, :LANES] + first[:, 1, :, LANES:]).astype(BF)
    imag = (first[:, 1, :, :LANES] - first[:, 0, :, LANES:]).astype(BF)
    lane = lax.broadcasted_iota(jnp.int32, (A, LANES), 1)
    for i in range(total):
        both = jnp.concatenate([real[i], imag[i]], axis=1)
        mixed = dot(down[...], both)
        even, odd = mixed[: 2 * A], mixed[2 * A :]
        re_cos = even[:A, :LANES] + pltpu.roll(odd[:A, :LANES], A, 1)
        re_sin = even[A:, :LANES] + pltpu.roll(odd[A:, :LANES], A, 1)
        im_cos = even[:A, LANES:] + pltpu.roll(odd[:A, LANES:], A, 1)
        im_sin = even[A:, LANES:] + pltpu.roll(odd[A:, LANES:], A, 1)
        re = re_cos + im_sin
        im = im_cos - re_sin
        power = jnp.where(lane < A, re * re + im * im, 0.0)
        sums = jnp.sum(power[None] * bins[...], axis=1)
        block, slot = divmod(i // G, slots // counts.shape[0])
        active = slot < counts[block]
        held[i * NDET : (i + 1) * NDET, :] = jnp.where(active, sums, 0.0)
    sums = jnp.sum(held[...].T, axis=0, keepdims=True)
    each = slots // counts.shape[0]
    for i in range(total):
        block, slot = divmod(i // G, each)
        out[block, slot, i % G : i % G + 1, :] = sums[:, i * NDET : (i + 1) * NDET]


def detect(alpha, counts, fields, pot, plane, across, down, bins):
    slots = fields[0].shape[2]
    rows = -(-slots * G * NDET // LANES) * LANES
    blocks = counts.shape[0]
    smem = pl.BlockSpec(memory_space=pltpu.SMEM)
    vmem = pl.BlockSpec(memory_space=pltpu.VMEM)
    return pl.pallas_call(
        functools.partial(detect_kernel, len(fields)),
        in_specs=[smem, smem] + [vmem] * (5 + len(fields)),
        out_specs=vmem,
        out_shape=jax.ShapeDtypeStruct((blocks, slots // blocks, G, NDET), F32),
        scratch_shapes=[
            pltpu.VMEM((2 * slots * G, HALF, LANES), BF),
            pltpu.VMEM((rows, LANES), F32),
        ],
        compiler_params=pltpu.CompilerParams(vmem_limit_bytes=VMEM),
        name="detect",
    )(alpha, counts, *fields, pot, plane, across, down, bins)


def detect_tables(beam_total):
    n = np.arange(A)
    table = turn(n[:, None] * n[None, :], A) / A
    cos, sin = table.real, table.imag
    zero = np.zeros((A, A))
    across = np.block([[cos, zero, sin, zero], [zero, cos, zero, sin]])
    rows = np.concatenate([cos, sin], axis=0)
    down = np.concatenate([rows[:, :HALF], rows[:, HALF:]], axis=0)
    signed = np.where(n < A // 2, n, n - A)
    radius = signed[:, None] ** 2 + signed[None, :] ** 2
    width = A // (2 * NDET)
    bins = np.zeros((NDET, A, LANES))
    for d in range(NDET):
        member = (radius >= (width * d) ** 2) & (radius < (width * (d + 1)) ** 2)
        bins[d, :, :A] = member * (A * A / (beam_total * member.sum()))
    return low(across), low(down), bins.astype(np.float32)


def coefficients(tile_ids, beam_rows, shifts):
    across = N // A
    offsets = jnp.arange(G, dtype=jnp.int32)
    spot_y = (tile_ids // across)[:, None] * A + A // 2 + offsets[None, :]
    spot_x = (tile_ids % across)[:, None] * A + A // 2 + 2 * offsets[None, :]
    wave_y = jnp.remainder(F * beam_rows[:, 0], N)[:, None, None]
    wave_x = jnp.remainder(F * beam_rows[:, 1], N)[:, None, None]
    windings = (wave_y * spot_y[None] % N + wave_x * spot_x[None] % N) % N
    phases = shifts[:, None, None] + 2.0 * math.pi / N * windings.astype(F32)
    return jnp.stack([jnp.cos(phases), -jnp.sin(phases)])


def plane_waves(beam_index):
    by = jnp.arange(HALF, dtype=jnp.int32)[:, None] + HALF * (jnp.arange(LANES) // A)[None, :]
    bx = jnp.broadcast_to((jnp.arange(LANES, dtype=jnp.int32) % A)[None, :], by.shape)
    row_y = beam_index[:, 0][:, None, None]
    row_x = beam_index[:, 1][:, None, None]
    winding = (row_y * by[None] + row_x * bx[None] + HALF * (row_y + row_x)) % A
    angle = 2.0 * math.pi / A * winding.astype(F32)
    return jnp.stack([jnp.cos(angle), jnp.sin(angle)], axis=1)


def shards(pot_first, pot_second, beam_index, aberration, tile_table, tile_count):
    field_count = lax.axis_size("beam")
    hold_count = lax.axis_size("slab")
    field_pos = lax.axis_index("beam")
    hold_pos = lax.axis_index("slab")
    band_rows = pot_first.shape[0]
    band_tiles = band_rows // A
    width_k = A // field_count
    sheets = width_k // 2
    across = N // A
    beam_total = beam_index.shape[0]
    share = hold_pos % sheets

    section_x = np.stack(
        [
            first_forward_x(
                np.array(
                    [width_k * p + 2 * t + ks for p in range(field_count) for ks in range(2)]
                )
            )
            for t in range(sheets)
        ]
    )
    last_x = np.stack(
        [
            np.stack(
                [
                    last_forward_x([width_k * p + 2 * t, width_k * p + 2 * t + 1])
                    for p in range(field_count)
                ]
            )
            for t in range(sheets)
        ]
    )
    section_y = first_forward_y()
    last_y = np.stack([last_forward_y([2 * q, 2 * q + 1]) for q in range(PAIRS)])
    inverse_y = np.stack([first_inverse_y([2 * q, 2 * q + 1]) for q in range(PAIRS)])
    inverse_x = np.stack(
        [
            np.stack(
                [
                    first_inverse_x([width_k * p + 2 * t, width_k * p + 2 * t + 1])
                    for t in range(sheets)
                ]
            )
            for p in range(field_count)
        ]
    )

    blocks_dev = tile_table.shape[0] // (field_count * hold_count)
    slot_count = tile_table.shape[1]
    own_slots = blocks_dev * slot_count
    table = tile_table.reshape(field_count, hold_count, own_slots)

    def trade(value, axis):
        return lax.all_to_all(value, axis, split_axis=0, concat_axis=0, tiled=True)

    near = min(sheets, 2)
    far = sheets // near

    def swap(value, x):
        return lax.ppermute(value, "slab", [(i, i ^ x) for i in range(hold_count)])

    ids = lax.dynamic_index_in_dim(table, hold_pos, 1, keepdims=False).reshape(-1)
    tile_y, tile_x = ids // across, ids % across
    mine = (tile_y // band_tiles == field_pos).astype(jnp.int32)
    rows = jnp.clip(tile_y - field_pos * band_tiles, 0, band_tiles - 1)
    columns, odd = tile_x // 2, tile_x % 2

    beam_row = lax.dynamic_index_in_dim(beam_index, hold_pos, 0, keepdims=False)
    pair_ids = share ^ jnp.arange(sheets, dtype=jnp.int32)
    k1_pairs = field_pos * width_k + 2 * pair_ids
    near_bit, far_bit = (jnp.stack([1 - v, v]) for v in (field_pos % 2, field_pos // 2 % 2))
    corners = table.reshape(field_count // 4, 2, 2, hold_count, own_slots)
    corners = corners.transpose(2, 1, 0, 3, 4)[near_bit][:, far_bit]
    sets = jnp.stack([corners, corners.transpose(1, 0, 2, 3, 4)], axis=1)
    sets = sets.reshape(2, PARTS, -1)
    places = jnp.stack([sets // across - beam_row[0], sets % across - beam_row[1]], axis=2)
    places = jnp.broadcast_to(places[..., None], places.shape + (LANES,))
    row = np.arange(ROWS)
    base = row // PART + A * (K2_LOW + row % PART % K2_COUNT)
    freq_y = np.broadcast_to(base[:, None], (ROWS, LANES)).astype(np.float32)
    lane = np.arange(LANES)
    base = np.where(lane < 2 * K2_COUNT, lane // K2_COUNT + A * (K2_LOW + lane % K2_COUNT), N)
    freq_x = (k1_pairs + F * beam_row[1])[:, None, None] + base.astype(np.int32)
    square_x = (freq_x * freq_x).astype(F32)
    scalars = jnp.stack(
        jnp.broadcast_arrays(field_pos, pair_ids, F * beam_row[0]), axis=-1
    )
    scalars = scalars.astype(jnp.int32).reshape(-1)

    sel = share.reshape(1).astype(jnp.int32)
    received = [[] for _ in range(far)]
    earlier = []
    for part in range(PARTS):
        lines = forward_x(sel, pot_first, section_x, last_x, field_count, part)
        if part:
            lines = order(lines, [places, scalars, square_x, rows, columns, odd, mine])
        lines = trade(lines, "beam")
        if lines.shape[3] != LANES:
            ratio = LANES // lines.shape[3]
            lines = lines.reshape(
                field_count // ratio, ratio, HIGH // PARTS, ROWS, SUB // FEW, -1
            )
            lines = lines.transpose(0, 2, 3, 4, 1, 5).reshape(-1, HIGH // PARTS, ROWS, LANES)
        if part:
            crops = crop(rows, columns, odd, mine, pot_second, earlier[0])
            lines = order(lines, [crops] + [r[0] for r in received[1:]])
        for f in range(far):
            received[f].append(swap(lines, f * near) if f else lines)
        if part == 0:
            earlier = [forward_y_first(received[f][0], section_y) for f in range(far)]
    crops = order(crops.reshape(field_count, own_slots, HALF, LANES), received[0][1:])
    crops = trade(crops, "beam")
    waves = []
    ready = []

    def invert(stop, after):
        start = stop - len(ready)
        waves.append(
            inverse(start, scalars, ready[:], freq_y, square_x, inverse_y, inverse_x, after)
        )
        ready.clear()

    for f in range(far):
        spec = forward_y(received[f][1], section_y, earlier[f], last_y, [crops] + waves if f else [])
        for x in range(near):
            ready.append(swap(spec, x) if x else spec)
            if x == 0:
                invert(f * near + 1, waves[1:])
    if ready:
        invert(sheets, waves[-1:])
    owners = field_count // 2 * hold_count
    other = collect(waves, k1_pairs, places, owners, 0, [crops])
    partial = other + collect(waves, k1_pairs, places, owners, 1, other[:1])

    def hop(value, bit):
        return lax.ppermute(value, "beam", [(i, i ^ (1 << bit)) for i in range(field_count)])

    def total(arrays, span):
        return functools.reduce(jnp.add, [array[span].astype(F32) for array in arrays])

    moving, staying = slice(0, owners // 2), slice(owners // 2, owners)
    arrived = [hop(partial[part], part) for part in range(PARTS)]
    halves = [[partial[PARTS + part], arrived[part]] for part in range(PARTS)]
    passed = [hop(total(halves[part], moving).astype(BF), 1 - part) for part in range(PARTS)]
    tiles = jnp.concatenate(
        [total(halves[part], staying) + passed[part].astype(F32) for part in range(PARTS)], axis=3
    ).astype(BF)
    groups = [
        [b * hold_count + h for b in range(g, field_count, 4) for h in range(hold_count)]
        for g in range(4)
    ]
    tiles = lax.all_to_all(
        tiles,
        ("beam", "slab"),
        split_axis=0,
        concat_axis=0,
        axis_index_groups=groups,
        tiled=True,
    )
    tiles = tiles.reshape((field_count // 4, hold_count) + tiles.shape[1:]).astype(F32)
    fields = [jnp.sum(tiles, axis=0).astype(BF)]
    crops = jnp.sum(crops.astype(F32), axis=0).astype(BF)

    own = lax.dynamic_index_in_dim(
        lax.dynamic_index_in_dim(table, field_pos, 0, keepdims=False), hold_pos, 0, keepdims=False
    )
    alpha = coefficients(own, beam_index, aberration).reshape(2, beam_total, own_slots * G)
    first_block = (field_pos * hold_count + hold_pos) * blocks_dev
    counts = lax.dynamic_slice_in_dim(tile_count, first_block, blocks_dev, 0)
    bins = detect_tables(beam_total)
    return detect(alpha, counts, fields, crops, plane_waves(beam_index), *bins)


def solution(mesh):
    return jax.shard_map(
        shards,
        mesh=mesh,
        in_specs=(P("beam", None), P("beam", None), P(), P(), P(), P()),
        out_specs=P(("beam", "slab"), None, None, None),
        check_vma=False,
    )
```
